32 devices in a mesh: dp: 4 (over y, core), fsdp: 8 (over z, x).
Axes of the slice: x: 2, y: 2, z: 4, core: 2. Of those that a mesh axis runs over, the one named last changes fastest.
Arguments:
- patches: bfloat16 [32, 8, 196, 768], P(('dp', 'fsdp')), may hold values from -10 to 10
- patch_keep_mask: int32 [32, 8, 196], P(('dp', 'fsdp')), may hold values from 0 to 1, as said below
- partner: int32 [32], replicated, may hold values from 0 to 31, as said below
- matrices: float32 [18, 768, 768], P(None, 'fsdp'), may hold values from -3 to 3
- matrix_first: float32 [18, 768, 768], P(None, 'fsdp'), may hold values from -9.536743e-06 to 9.536743e-06
- matrix_second: float32 [18, 768, 768], P(None, 'fsdp'), may hold values from 1.201335e-11 to 4.787138e-11
- matrix_average: float32 [18, 768, 768], P(None, 'fsdp'), may hold values from -0.21875 to 0.21875
- head_weight: float32 [768, 256], P('fsdp'), may hold values from -0.21875 to 0.21875
- head_first: float32 [768, 256], P('fsdp'), may hold values from -3.8146973e-05 to 3.8146973e-05
- head_second: float32 [768, 256], P('fsdp'), may hold values from 1.9112148e-10 to 7.644859e-10
- head_average: float32 [768, 256], P('fsdp'), may hold values from -0.21875 to 0.21875
- vectors: float32 [227, 768], P(None, 'fsdp'), may hold values from -3 to 3
- array_running_mean: float32 [227, 768], P(None, 'fsdp'), may hold values from -3.8146973e-05 to 3.8146973e-05
- vector_second: float32 [227, 768], P(None, 'fsdp'), may hold values from 1.9112148e-11 to 7.644859e-11
- vector_average: float32 [227, 768], P(None, 'fsdp'), may hold values from -1.75 to 1.75
Outputs:
- contrastive_loss: float32 [], replicated
- squared_norm: float32 [], replicated
- new_matrices: float32 [18, 768, 768], P(None, 'fsdp')
- new_matrix_first: float32 [18, 768, 768], P(None, 'fsdp')
- revised_grid_variance: float32 [18, 768, 768], P(None, 'fsdp')
- new_matrix_average: float32 [18, 768, 768], P(None, 'fsdp')
- new_head_weight: float32 [768, 256], P('fsdp')
- new_head_first: float32 [768, 256], P('fsdp')
- new_head_second: float32 [768, 256], P('fsdp')
- new_head_average: float32 [768, 256], P('fsdp')
- new_vectors: float32 [227, 768], P(None, 'fsdp')
- new_vector_first: float32 [227, 768], P(None, 'fsdp')
- new_vector_second: float32 [227, 768], P(None, 'fsdp')
- new_vector_average: float32 [227, 768], P(None, 'fsdp')
The draws below stay inside these ranges and needn't reach their ends.
Inputs may be any that keep to these rules, and one draw needn't show every extreme that they name: `patch_keep_mask`: frame 0 of every clip keeps all 196 patches; the other frames keep shares that differ from frame to frame. partner[partner[i]] = i and partner[i] != i for every clip i.
All inputs are finite; a program needn't handle non-finite values.
Results may differ from the reference program's by a relative error of at most 0.0055.
The reference program's roundings to bfloat16 on the way count: a program that leaves them out, or rounds other values in their place, can miss the bound.
Values may be sent and summed in bfloat16 or wider, within the bound.
A program may use at most 448 MiB of HBM per device.

```python
import math
import jax
import jax.numpy as jnp
from jax import lax

D = 768
H = 12
HD = 64
FF = 3072
F = 8
S = 196
PIX = 768
PROJ = 256
NMAT = 18
STEP = 10
NVEC = 227
CLIPS = 32


def draw_patches(key, part):
    shared = jax.random.normal(jax.random.fold_in(key, 102), (CLIPS, 1, 1, PIX), jnp.float32)
    rough = jax.random.normal(jax.random.fold_in(key, 101), (CLIPS, F, S, PIX), jnp.float32)
    return jnp.clip(0.7 * rough + 0.7 * shared, -10.0, 10.0).astype(jnp.bfloat16)


def draw_patch_keep_mask(key, part):
    level = jax.random.randint(jax.random.fold_in(key, 401), (CLIPS, F, 1), 2, 9)
    roll = jax.random.randint(jax.random.fold_in(key, 402), (CLIPS, F, S), 0, 8)
    leading = jnp.arange(F)[None, :, None] == 0
    return jnp.where(leading | (roll < level), 1, 0).astype(jnp.int32)


def draw_partner(key, part):
    order = jax.random.permutation(jax.random.fold_in(key, 501), CLIPS).astype(jnp.int32)
    place = jnp.argsort(order).astype(jnp.int32)
    mate = place + 1 - 2 * (place % 2)
    return order[mate].astype(jnp.int32)


def draw_matrices(key, part):
    raw = jax.random.normal(jax.random.fold_in(key, 201), (NMAT, D, D), jnp.float32)
    block = jnp.arange(NMAT)[:, None, None]
    factor = jnp.where(block == 4, 2.0, jnp.where(block == 9, 8.0, jnp.where(block >= 14, 0.5, 1.0)))
    return jnp.clip(raw * factor * D ** (-0.5), -3.0, 3.0)


def draw_vectors(key, part):
    raw = jax.random.normal(jax.random.fold_in(key, 301), (NVEC, D), jnp.float32)
    row = jnp.arange(NVEC)[:, None]
    gains = (row == 22) | (row == 24) | (row == 26) | (row == 28)
    return jnp.clip(jnp.where(gains, 1.0 + 0.1 * raw, 0.3 * raw), -3.0, 3.0)


def block_scale(stream_key, dims, split, low, largest):
    def one(position, blocks):
        draws = jax.random.uniform(jax.random.fold_in(jax.random.fold_in(stream_key, 6), position), (blocks,), jnp.float32, low / len(split), largest / len(split))
        return jnp.repeat(jnp.exp(draws), dims[position] // blocks).reshape((-1,) + (1,) * (len(dims) - position - 1))

    loudness = one(*split[0])
    for cut in split[1:]:
        loudness = loudness * one(*cut)
    return loudness


def scatter_about(key, shape, scale, bound, cuts=(), kind=jnp.bfloat16):
    array = jax.random.normal(key, shape, jnp.float32) * scale
    if len(cuts) > 0:
        array = block_scale(key, shape, cuts, -0.22, 0.18) * array
    return jnp.clip(array, min=-bound, max=bound).astype(kind)


def setup_inputs(seed: int = 0) -> dict:
    key_list = jax.random.split(jax.random.key(seed), 16)
    patches = draw_patches(jax.random.fold_in(key_list[15], 71), 0)
    patch_keep_mask = draw_patch_keep_mask(jax.random.fold_in(key_list[15], 71), 0)
    partner = draw_partner(jax.random.fold_in(key_list[15], 71), 0)
    matrices = draw_matrices(jax.random.fold_in(key_list[15], 71), 0)
    matrix_first = scatter_about(key_list[4], (NMAT, D, D), (0.0056 * (NMAT * D * D + D * PROJ + NVEC * D) ** -0.5), 9.5367431640625e-06, ((1, 8),), jnp.float32)
    matrix_second = jnp.clip(jnp.exp(math.log(4.787138047079864e-11) - 1.3824992775232334 * jax.random.uniform(key_list[5], (NMAT, D, D), jnp.float32) ** block_scale(key_list[5], (NMAT, D, D), ((1, 8),), -0.2, 0.2)), 1.2013350383921484e-11, 4.787138047079864e-11)
    matrix_average = scatter_about(key_list[6], (NMAT, D, D), (D ** -0.5), 0.21875, ((1, 8),), jnp.float32)
    head_weight = scatter_about(key_list[7], (D, PROJ), D ** -0.5, 0.21875, ((0, 8),), jnp.float32)
    head_first = scatter_about(key_list[8], (D, PROJ), (0.0222 * (NMAT * D * D + D * PROJ + NVEC * D) ** -0.5), 3.814697265625e-05, ((0, 8),), jnp.float32)
    head_second = jnp.clip(jnp.exp(math.log(7.644859190136799e-10) - 1.3862944 * jax.random.uniform(key_list[9], (D, PROJ), jnp.float32) ** block_scale(key_list[9], (D, PROJ), ((0, 8),), -0.2, 0.2)), 1.9112147975341998e-10, 7.644859190136799e-10)
    head_average = scatter_about(key_list[10], (D, PROJ), D ** -0.5, 0.21875, ((0, 8),), jnp.float32)
    vectors = draw_vectors(jax.random.fold_in(key_list[15], 71), 0)
    array_running_mean = scatter_about(key_list[12], (NVEC, D), (0.0222 * (NMAT * D * D + D * PROJ + NVEC * D) ** -0.5), 3.814697265625e-05, ((1, 8),), jnp.float32)
    vector_second = jnp.clip(jnp.exp(math.log(7.644859051358921e-11) - 1.3862944 * jax.random.uniform(key_list[13], (NVEC, D), jnp.float32) ** block_scale(key_list[13], (NVEC, D), ((1, 8),), -0.2, 0.2)), 1.9112147628397302e-11, 7.644859051358921e-11)
    vector_average = scatter_about(key_list[14], (NVEC, D), 0.3, 1.75, ((1, 8),), jnp.float32)
    return dict(patches=patches, patch_keep_mask=patch_keep_mask, partner=partner, matrices=matrices, matrix_first=matrix_first, matrix_second=matrix_second, matrix_average=matrix_average, head_weight=head_weight, head_first=head_first, head_second=head_second, head_average=head_average, vectors=vectors, array_running_mean=array_running_mean, vector_second=vector_second, vector_average=vector_average)


@jax.custom_vjp
def low(v):
    return lax.optimization_barrier(v.astype(jnp.bfloat16)).astype(jnp.float32)

@jax.custom_vjp
def low_back(v):
    return v

def low_keep(v):
    return (low(v), None)

def low_pass(kept, grad):
    return (grad,)

def back_keep(v):
    return (v, None)

def back_low(kept, grad):
    return (low(grad),)
low.defvjp(low_keep, low_pass)
low_back.defvjp(back_keep, back_low)
PRECISE = lax.Precision.HIGHEST
NORM_EPS = 1e-06
SCORE_SHARPNESS = 0.07
CLIP_AT = 0.05
RATE = 0.01
VECTOR_RATE = 0.1
BETA_ONE = 0.9
BETA_TWO = 0.95
ADAM_EPSILON = 1e-08
DECAY = 0.05
AVERAGE_KEEP = 0.9

def layer_norm(inputs, gain, shift):
    centred = inputs - lax.optimization_barrier(jnp.mean(inputs, -1, keepdims=True))
    spread = lax.optimization_barrier(jnp.mean(centred * centred, -1, keepdims=True))
    return centred * lax.rsqrt(spread + NORM_EPS) * gain + shift

def linear_map_compose(left, right):
    return jnp.matmul(left, right, precision=PRECISE)

def round_both(value):
    return low(low_back(value))

def attend(query, keys, values, allowed):
    scores = low_back(jnp.einsum('blhd,bmhd->bhlm', query, keys, precision=PRECISE) * HD ** (-0.5))
    scores = jnp.where(allowed[:, None, None, :], scores, -1000000000.0)
    probabilities = low(jax.nn.softmax(scores, axis=-1))
    return jnp.einsum('bhlm,bmhd->blhd', probabilities, values, precision=PRECISE)

def per_patch(tensor):
    return tensor.reshape(F, S, H, HD).transpose(1, 0, 2, 3)

def per_frame(tensor):
    leading = jnp.broadcast_to(tensor[0][None, None], (F, 1, D))
    return jnp.concatenate([leading, tensor[1:].reshape(F, S, D)], 1).reshape(F, S + 1, H, HD)

def clip_net(mats16, head16, vecs16, pixels, kept_mask):
    alive = kept_mask > 0
    embedded = low_back(linear_map_compose(pixels, mats16[0]) + vecs16[9])
    start_rows = embedded + vecs16[31:31 + S][None] + vecs16[1:1 + F][:, None]
    normed_time = low(layer_norm(start_rows, vecs16[22], vecs16[23]))
    query_time = round_both(linear_map_compose(normed_time, mats16[1]) + vecs16[10])
    keys_time = round_both(linear_map_compose(normed_time, mats16[2]))
    values_time = round_both(linear_map_compose(normed_time, mats16[3]) + vecs16[11])
    mixed_time = attend(per_patch(query_time), per_patch(keys_time), per_patch(values_time), alive.T)
    mixed_time = round_both(mixed_time.transpose(1, 0, 2, 3).reshape(F, S, D))
    moved_time = round_both(linear_map_compose(mixed_time, mats16[4]) + vecs16[12])
    after_time = start_rows + low_back(linear_map_compose(moved_time, mats16[5]) + vecs16[13])
    joined = jnp.concatenate([(vecs16[0] + vecs16[30])[None], after_time.reshape(F * S, D)], 0)
    normed_space = low(layer_norm(joined, vecs16[24], vecs16[25]))
    query_space = round_both(linear_map_compose(normed_space, mats16[6]) + vecs16[14])
    keys_space = round_both(linear_map_compose(normed_space, mats16[7]))
    values_space = round_both(linear_map_compose(normed_space, mats16[8]) + vecs16[15])
    allowed = jnp.concatenate([jnp.ones((F, 1), jnp.bool_), alive], 1)
    mixed_space = attend(per_frame(query_space), per_frame(keys_space), per_frame(values_space), allowed)
    mixed_space = mixed_space.reshape(F, S + 1, D)
    mixed_space = round_both(jnp.concatenate([lax.optimization_barrier(jnp.mean(mixed_space[:, 0], 0))[None], mixed_space[:, 1:].reshape(F * S, D)], 0))
    after_space = joined + low_back(linear_map_compose(mixed_space, mats16[9]) + vecs16[16])
    normed_mlp = low(layer_norm(after_space, vecs16[26], vecs16[27]))
    weight_in = mats16[10:14].transpose(1, 0, 2).reshape(D, FF)
    hidden = low_back(linear_map_compose(normed_mlp, weight_in) + vecs16[17:21].reshape(FF))
    activated = low(jax.nn.gelu(hidden, approximate=False))
    after_mlp = after_space + low_back(linear_map_compose(activated, mats16[14:18].reshape(FF, D)) + vecs16[21])
    pooled = low(lax.optimization_barrier(jnp.mean(layer_norm(after_mlp, vecs16[28], vecs16[29]), 0)))
    return low_back(linear_map_compose(pooled, head16))

def total_loss(matrices, head_weight, vectors, pixels, patch_keep_mask, partner):
    mats16 = low(matrices)
    head16 = low(head_weight)
    vecs16 = low(vectors)

    def one_clip(item):
        return clip_net(mats16, head16, vecs16, item[0], item[1])
    projected = lax.map(jax.checkpoint(one_clip), (pixels, patch_keep_mask))
    unit_length_lines = projected * lax.rsqrt(lax.optimization_barrier(jnp.sum(projected * projected, -1, keepdims=True)) + 1e-06)
    pairwise_affinity_scores_raw = linear_map_compose(unit_length_lines, unit_length_lines.T) / SCORE_SHARPNESS
    clip_count = pairwise_affinity_scores_raw.shape[0]
    diagonal = jnp.arange(clip_count)[:, None] == jnp.arange(clip_count)[None, :]
    pairwise_affinity_scores_raw = jnp.where(diagonal, -1000000000.0, pairwise_affinity_scores_raw)
    positive = jnp.take_along_axis(pairwise_affinity_scores_raw, partner[:, None].astype(jnp.int32), 1)[:, 0]
    return jnp.mean(jax.nn.logsumexp(pairwise_affinity_scores_raw, -1) - positive)

def adamw_step(weight, first, second, average, gradient, factor, rate):
    clipped = gradient * factor
    first = BETA_ONE * first + (1.0 - BETA_ONE) * clipped
    second = BETA_TWO * second + (1.0 - BETA_TWO) * clipped * clipped
    first_hat = first / (1.0 - BETA_ONE ** STEP)
    second_hat = second / (1.0 - BETA_TWO ** STEP)
    weight = weight - rate * (first_hat / (jnp.sqrt(second_hat) + ADAM_EPSILON) + DECAY * weight)
    average = AVERAGE_KEEP * average + (1.0 - AVERAGE_KEEP) * weight
    return (weight, first, second, average)

def reference(patches, patch_keep_mask, partner, matrices, matrix_first, matrix_second, matrix_average, head_weight, head_first, head_second, head_average, vectors, array_running_mean, vector_second, vector_average):
    pixels = patches.astype(jnp.float32)

    def objective(mats_in, head_in, vecs_in):
        return total_loss(mats_in, head_in, vecs_in, pixels, patch_keep_mask, partner)
    contrastive_loss, pull_back = jax.vjp(objective, matrices, head_weight, vectors)
    grad_mats, grad_head, grad_vecs = pull_back(jnp.ones_like(contrastive_loss))
    squared_norm = jnp.sum(grad_mats * grad_mats) + jnp.sum(grad_head * grad_head) + jnp.sum(grad_vecs * grad_vecs)
    factor = CLIP_AT / jnp.maximum(jnp.sqrt(squared_norm), CLIP_AT)
    mats_out = adamw_step(matrices, matrix_first, matrix_second, matrix_average, grad_mats, factor, RATE)
    head_out = adamw_step(head_weight, head_first, head_second, head_average, grad_head, factor, RATE)
    vecs_out = adamw_step(vectors, array_running_mean, vector_second, vector_average, grad_vecs, factor, VECTOR_RATE)
    return (contrastive_loss, squared_norm, mats_out[0], mats_out[1], mats_out[2], mats_out[3], head_out[0], head_out[1], head_out[2], head_out[3], vecs_out[0], vecs_out[1], vecs_out[2], vecs_out[3])
```

```python
import functools
import jax
import jax.numpy as jnp
from jax import lax
from jax.experimental import pallas as pl
from jax.experimental.pallas import tpu as pltpu
from jax.sharding import PartitionSpec as P

D = 768
H = 12
HD = 64
F = 8
S = 196
NVEC = 227
STEP = 10


NORM_EPS = 1e-06
SCORE_SHARPNESS = 0.07
CLIP_AT = 0.05
RATE = 0.01
VECTOR_RATE = 0.1
BETA_ONE = 0.9
BETA_TWO = 0.95
ADAM_EPSILON = 1e-08
DECAY = 0.05
AVERAGE_KEEP = 0.9


NMAT = 18
MESH = pl.DeviceIdType.MESH
ANY = pl.BlockSpec(memory_space=pl.ANY)


class Layout:
    def __init__(self, dp, fsdp, split):
        self.dp, self.n = dp, fsdp
        self.outer = 4 if fsdp % 4 == 0 else 1
        self.inner = fsdp // self.outer
        self.planes = dp // 2
        self.half = NMAT // 2
        self.split = split
        self.common = self.half - split * self.planes
        self.handled = self.common + split
        self.rows = D // fsdp

    def place(self):
        i = lax.axis_index("fsdp")
        d = lax.axis_index("dp")
        return i, lax.div(i, self.inner), lax.rem(i, self.inner), lax.div(d, 2), lax.rem(d, 2)

    def peer(self, i, y, c):
        return {"fsdp": i, "dp": y * 2 + c}

    def matrix(self, c, y, k):
        if k < self.common:
            return c * self.half + k
        return c * self.half + self.common + y * self.split + (k - self.common)


def turn(x, t, size):
    return lax.rem(x + t + size, size)


def greet(lay, i, a, b, y, c):
    barrier = pltpu.get_barrier_semaphore()
    others = [lay.peer(turn(a, t, lay.outer) * lay.inner + b, y, c) for t in range(1, lay.outer)]
    others += [lay.peer(a * lay.inner + turn(b, u, lay.inner), y, c) for u in range(1, lay.inner)]
    others += [lay.peer(i, turn(y, v, lay.planes), c) for v in range(1, lay.planes)]
    others += [lay.peer(i, y, 1 - c)]
    for other in others:
        pl.semaphore_signal(barrier, inc=1, device_id=other, device_id_type=MESH)
    pl.semaphore_wait(barrier, len(others))


def gather_kernel(lay, w_ref, s_ref, ow_ref, os_ref, own_sem, zs, zr, xs, xr, ys, yr, cs, cr, small):
    i, a, b, y, c = lay.place()
    A, B = lay.outer, lay.inner
    greet(lay, i, a, b, y, c)
    pending = []

    def remote(src, dst, ssem, rsem, dev):
        copy = pltpu.make_async_remote_copy(
            src_ref=src, dst_ref=dst, send_sem=ssem, recv_sem=rsem, device_id=dev, device_id_type=MESH
        )
        copy.start()
        pending.append(copy)
        return copy

    def landed(dst, ssem, rsem, dev):
        pltpu.make_async_remote_copy(
            src_ref=dst, dst_ref=dst, send_sem=ssem, recv_sem=rsem, device_id=dev, device_id_type=MESH
        ).wait_recv()

    K = lay.handled
    here = lay.peer(i, y, 1 - c)
    local_small = pltpu.make_async_copy(s_ref, os_ref.at[i], own_sem.at[0])
    local_small.start()
    for k in [-1] + list(range(lay.common, K)) + list(range(lay.common)):
        src = s_ref if k < 0 else w_ref.at[lay.matrix(c, y, k)]
        dst = os_ref.at[i] if k < 0 else ow_ref.at[lay.matrix(c, y, k), i]
        for t in range(1, A):
            remote(src, dst, zs.at[k + 1, t], zr.at[k + 1, t], lay.peer(turn(a, t, A) * B + b, y, c))
        for u in range(1, B):
            remote(src, dst, xs.at[k + 1, u, 0], xr.at[k + 1, u, 0], lay.peer(a * B + turn(b, u, B), y, c))
    locals_ = []
    for first, count in ((lay.matrix(c, y, 0), lay.common), (lay.matrix(c, y, lay.common), lay.split)):
        if count:
            span = pl.ds(first, count)
            locals_.append(pltpu.make_async_copy(w_ref.at[span], ow_ref.at[span, i], own_sem.at[1 + len(locals_)]))
            locals_[-1].start()
    order = [-1] + list(range(lay.common, K)) + list(range(lay.common))

    def at(k, j):
        return os_ref.at[j] if k < 0 else ow_ref.at[lay.matrix(c, y, k), j]

    def cross(k):
        for t in range(1, A):
            j = turn(a, -t, A) * B + b
            landed(at(k, j), zs.at[k + 1, t], zr.at[k + 1, t], here)
            for u in range(1, B):
                remote(at(k, j), at(k, j), xs.at[k + 1, u, t], xr.at[k + 1, u, t], lay.peer(a * B + turn(b, u, B), y, c))

    def share(k):
        for u in range(1, B):
            for t in range(A):
                j = turn(a, -t, A) * B + turn(b, -u, B)
                landed(at(k, j), xs.at[k + 1, u, t], xr.at[k + 1, u, t], here)
        if k >= 0:
            m = lay.matrix(c, y, k)
            if k >= lay.common:
                for v in range(1, lay.planes):
                    q = k - lay.common
                    remote(ow_ref.at[m], ow_ref.at[m], ys.at[q, v], yr.at[q, v], lay.peer(i, turn(y, v, lay.planes), c))
            remote(ow_ref.at[m], ow_ref.at[m], cs.at[k], cr.at[k], here)

    for step in range(len(order) + 1):
        if step < len(order):
            cross(order[step])
        if step == 2:
            for local in locals_:
                local.wait()
        if step >= 1:
            share(order[step - 1])
    slot = K
    for v in range(1, lay.planes):
        for q in range(lay.split):
            m = lay.matrix(c, turn(y, -v, lay.planes), lay.common + q)
            landed(ow_ref.at[m], ys.at[q, v], yr.at[q, v], here)
            remote(ow_ref.at[m], ow_ref.at[m], cs.at[slot], cr.at[slot], here)
            slot += 1
    slot = K
    for k in range(K):
        m = lay.matrix(1 - c, y, k)
        landed(ow_ref.at[m], cs.at[k], cr.at[k], here)
    for v in range(1, lay.planes):
        for q in range(lay.split):
            m = lay.matrix(1 - c, turn(y, -v, lay.planes), lay.common + q)
            landed(ow_ref.at[m], cs.at[slot], cr.at[slot], here)
            slot += 1
    local_small.wait()
    for copy in pending:
        copy.wait_send()


def gather(lay, shard, small):
    A, B, K = lay.outer, lay.inner, lay.handled
    dma = pltpu.SemaphoreType.DMA
    kept = max(lay.split, 1)
    return pl.pallas_call(
        functools.partial(gather_kernel, lay),
        out_shape=(
            jax.ShapeDtypeStruct((NMAT, lay.n) + shard.shape[1:], shard.dtype),
            jax.ShapeDtypeStruct((lay.n,) + small.shape, small.dtype),
        ),
        in_specs=[ANY, ANY],
        out_specs=(ANY, ANY),
        scratch_shapes=[
            dma((3,)), dma((K + 1, A)), dma((K + 1, A)), dma((K + 1, B, A)), dma((K + 1, B, A)),
            dma((kept, lay.planes)), dma((kept, lay.planes)), dma((lay.half,)), dma((lay.half,)),
            dma((1,)),
        ],
        compiler_params=pltpu.CompilerParams(collective_id=0, has_side_effects=True),
    )(shard, small)


def reduce_kernel(lay, g_ref, s_ref, og_ref, os_ref, *scratch):
    i, a, b, y, c = lay.place()
    A, B, Y = lay.outer, lay.inner, lay.planes
    greet(lay, i, a, b, y, c)
    big, little, out_sem = scratch[:20], scratch[20:40], scratch[40]
    pending = []
    here = lay.peer(i, y, 1 - c)

    def remote(src, dst, ssem, rsem, dev):
        copy = pltpu.make_async_remote_copy(
            src_ref=src, dst_ref=dst, send_sem=ssem, recv_sem=rsem, device_id=dev, device_id_type=MESH
        )
        copy.start()
        pending.append(copy.wait_send)

    def landed(dst, sems, *at):
        pltpu.make_async_remote_copy(
            src_ref=dst, dst_ref=dst, send_sem=sems.at[at], recv_sem=sems.at[at], device_id=here, device_id_type=MESH
        ).wait_recv()

    class Set:
        def __init__(self, refs, common, split, source, target):
            (self.g, self.r, self.ys, self.yr, self.xs, self.xr, self.zs, self.zr, self.fin, self.all_) = refs[:10]
            (self.lsem, self.rs, self.rr, self.yss, self.yrs, self.xss, self.xrs, self.zss, self.zrs, self.fsem) = refs[10:]
            self.common, self.split = common, split
            self.source, self.target = source, target
            self.blocks = self.g.shape[1]

        def slots(self):
            found = [(v, q) for v in range(1, Y) for q in range(self.split)]
            return found + [(None, k) for k in range(self.common)] + [(0, q) for q in range(self.split)]

        def slot(self, v, q):
            return self.slots().index((v, q))

    def big_at(core, v, q):
        if v is None:
            return core * lay.half + q
        return core * lay.half + lay.common + turn(y, v, Y) * lay.split + q

    mats = Set(big, lay.common, lay.split, lambda core, v, q: g_ref.at[big_at(core, v, q)], lambda core, v, q: og_ref.at[big_at(core, v, q)])
    rest = Set(little, 1, 0, lambda core, v, q: s_ref.at[core], lambda core, v, q: os_ref.at[core])

    work = [(rest, None, 0)] + [(mats, None, k) for k in range(mats.common)] + [(mats, 0, q) for q in range(mats.split)]
    starts = [(mats, v, q) for v in range(1, Y) for q in range(mats.split)] + work
    for st, v, q in starts:
        n = st.slot(v, q)
        remote(st.source(1 - c, v, q), st.r.at[n], st.rs.at[n], st.rr.at[n], here)
        pltpu.make_async_copy(st.source(c, v, q), st.g.at[n], st.lsem.at[n]).start()

    def ready(st, v, q):
        n = st.slot(v, q)
        pltpu.make_async_copy(st.source(c, v, q), st.g.at[n], st.lsem.at[n]).wait()
        landed(st.r.at[n], st.rr, n)

    def base(st, n, v, q, j):
        total = st.g[n, j].astype(jnp.float32) + st.r[n, j].astype(jnp.float32)
        if v == 0:
            for w in range(1, Y):
                total = total + st.yr[w - 1, q, j].astype(jnp.float32)
        return total

    def pass_on(st, v, q):
        n = st.slot(v, q)
        ready(st, v, q)

        @pl.loop(0, st.blocks)
        def _(j):
            st.ys[v - 1, q, j] = base(st, n, None, q, j).astype(jnp.bfloat16)

        remote(st.ys.at[v - 1, q], st.yr.at[v - 1, q], st.yss.at[v - 1, q], st.yrs.at[v - 1, q], lay.peer(i, turn(y, v, Y), c))

    def item(st, v, q):
        return q if v is None else st.common + q

    def cross(st, v, q):
        n, k = st.slot(v, q), item(st, v, q)
        ready(st, v, q)
        if v == 0:
            for w in range(1, Y):
                landed(st.yr.at[w - 1, q], st.yrs, w - 1, q)
        for u in range(1, B):
            other = turn(b, u, B)

            @pl.loop(0, A)
            def _(e):
                st.xs[k, u - 1, e] = base(st, n, v, q, e * B + other).astype(jnp.bfloat16)

            remote(st.xs.at[k, u - 1], st.xr.at[k, u - 1], st.xss.at[k, u - 1], st.xrs.at[k, u - 1], lay.peer(a * B + other, y, c))

    def along(st, v, q):
        n, k = st.slot(v, q), item(st, v, q)
        for u in range(1, B):
            landed(st.xr.at[k, u - 1], st.xrs, k, u - 1)

        def total(e):
            value = base(st, n, v, q, e * B + b)
            for u in range(1, B):
                value = value + st.xr[k, u - 1, e].astype(jnp.float32)
            return value

        for t in range(1, A):
            e = turn(a, t, A)
            st.zs[k, t - 1] = total(e).astype(jnp.bfloat16)
            remote(st.zs.at[k, t - 1], st.zr.at[k, t - 1], st.zss.at[k, t - 1], st.zrs.at[k, t - 1], lay.peer(e * B + b, y, c))
        st.fin[k] = total(a)

    def close(st, v, q):
        k = item(st, v, q)
        for t in range(1, A):
            landed(st.zr.at[k, t - 1], st.zrs, k, t - 1)
        value = st.fin[k]
        for t in range(1, A):
            value = value + st.zr[k, t - 1].astype(jnp.float32)
        st.fin[k] = value
        if v is None:
            st.all_[y, k] = value
            for w in range(1, Y):
                remote(st.all_.at[y, k], st.all_.at[y, k], st.fsem.at[0, k, w], st.fsem.at[1, k, w], lay.peer(i, turn(y, w, Y), c))
        else:
            target = st.target(c, v, q)
            for w in range(1, Y):
                remote(st.fin.at[k], target, st.fsem.at[0, k, w], st.fsem.at[1, k, w], lay.peer(i, turn(y, w, Y), c))
            finish(st, k, target)

    def finish(st, k, target):
        copy = pltpu.make_async_copy(st.fin.at[k], target, st.fsem.at[2, k, 0])
        copy.start()
        pending.append(copy.wait)
        remote(st.fin.at[k], target, st.fsem.at[3, k, 0], st.fsem.at[4, k, 0], here)

    def merge(st, v, q):
        k = item(st, v, q)
        if v is None:
            for w in range(1, Y):
                landed(st.all_.at[turn(y, -w, Y), k], st.fsem, 1, k, w)
            value = st.all_[0, k]
            for w in range(1, Y):
                value = value + st.all_[w, k]
            st.fin[k] = value
            finish(st, k, st.target(c, v, q))
        else:
            for w in range(1, Y):
                back = st.target(c, -w, q)
                landed(back, st.fsem, 1, k, w)
                remote(back, back, st.fsem.at[3, k, w], st.fsem.at[4, k, w], here)

    others = [(mats, v, q) for v in range(1, Y) for q in range(mats.split)]
    for job in others:
        pass_on(*job)
    for step in range(len(work) + 3):
        if step < len(work):
            cross(*work[step])
        if 0 <= step - 1 < len(work):
            along(*work[step - 1])
        if 0 <= step - 2 < len(work):
            close(*work[step - 2])
        if 0 <= step - 3 < len(work):
            merge(*work[step - 3])
    for st, v, q in work:
        k = item(st, v, q)
        landed(st.target(1 - c, v, q), st.fsem, 4, k, 0)
        if v is not None:
            for w in range(1, Y):
                landed(st.target(1 - c, -w, q), st.fsem, 4, k, w)
    for wait in pending:
        wait()


def reduce_scratch(lay, rows, common, split):
    A, B, Y, n = lay.outer, lay.inner, lay.planes, lay.n
    slots, kept, passed, K = common + split * Y, max(split, 1), max(Y - 1, 1), common + split
    half = jnp.bfloat16
    dma = pltpu.SemaphoreType.DMA
    width = rows if split else 16
    depth = n if split else 1
    crossed, along = max(B - 1, 1), max(A - 1, 1)
    return [
        pltpu.VMEM((slots, n, rows, D), half), pltpu.VMEM((slots, n, rows, D), half),
        pltpu.VMEM((passed, kept, depth, width, D), half), pltpu.VMEM((passed, kept, depth, width, D), half),
        pltpu.VMEM((K, crossed, A, rows, D), half), pltpu.VMEM((K, crossed, A, rows, D), half),
        pltpu.VMEM((K, along, rows, D), half), pltpu.VMEM((K, along, rows, D), half),
        pltpu.VMEM((K, rows, D), jnp.float32), pltpu.VMEM((Y, K if not split else common, rows, D), jnp.float32),
        dma((slots,)), dma((slots,)), dma((slots,)), dma((passed, kept)), dma((passed, kept)),
        dma((K, crossed)), dma((K, crossed)), dma((K, along)), dma((K, along)), dma((5, K, Y)),
    ]


def reduce(lay, grads, small):
    rows, rest = grads.shape[2], small.shape[2]
    return pl.pallas_call(
        functools.partial(reduce_kernel, lay),
        out_shape=(
            jax.ShapeDtypeStruct((NMAT, rows, D), jnp.float32),
            jax.ShapeDtypeStruct((2, rest, D), jnp.float32),
        ),
        in_specs=[ANY, ANY],
        out_specs=(ANY, ANY),
        scratch_shapes=reduce_scratch(lay, rows, lay.common, lay.split) + reduce_scratch(lay, rest, 1, 0) + [pltpu.SemaphoreType.DMA((1,))],
        compiler_params=pltpu.CompilerParams(collective_id=1, has_side_effects=True, vmem_limit_bytes=58 * 2**20),
    )(grads, small)


def spread_kernel(dp, n, x_ref, o_ref, ssem, rsem):
    i, d = lax.axis_index("fsdp"), lax.axis_index("dp")
    me = d * n + i
    total = dp * n
    barrier = pltpu.get_barrier_semaphore()

    def other(t):
        j = lax.rem(me + t, total)
        return {"fsdp": lax.rem(j, n), "dp": lax.div(j, n)}

    @pl.loop(1, total)
    def _(t):
        pl.semaphore_signal(barrier, inc=1, device_id=other(t), device_id_type=MESH)

    pl.semaphore_wait(barrier, total - 1)

    @pl.loop(1, total)
    def _(t):
        pltpu.make_async_remote_copy(
            src_ref=x_ref, dst_ref=o_ref.at[me], send_sem=ssem.at[t], recv_sem=rsem.at[t], device_id=other(t), device_id_type=MESH
        ).start()

    o_ref[me] = x_ref[...]

    @pl.loop(1, total)
    def _(t):
        pltpu.make_async_remote_copy(
            src_ref=x_ref, dst_ref=o_ref.at[lax.rem(me - t + total, total)], send_sem=ssem.at[t], recv_sem=rsem.at[t], device_id=other(t), device_id_type=MESH
        ).wait()


def spread(dp, n, tile, number):
    vmem = pl.BlockSpec(memory_space=pltpu.VMEM)
    return pl.pallas_call(
        functools.partial(spread_kernel, dp, n),
        out_shape=jax.ShapeDtypeStruct((dp * n,) + tile.shape, tile.dtype),
        in_specs=[vmem],
        out_specs=vmem,
        scratch_shapes=[pltpu.SemaphoreType.DMA((dp * n,)), pltpu.SemaphoreType.DMA((dp * n,))],
        compiler_params=pltpu.CompilerParams(collective_id=number, has_side_effects=True),
    )(tile)

def layer_norm(inputs, gain, shift):
    centred = inputs - jnp.mean(inputs, -1, keepdims=True)
    spread = jnp.mean(centred * centred, -1, keepdims=True)
    return centred * lax.rsqrt(spread + NORM_EPS) * gain + shift


def gelu_exact(values):
    return jax.nn.gelu(values, approximate=False)


def project(inputs, weight):
    return jnp.einsum("...a,ab->...b", inputs, weight, preferred_element_type=jnp.float32)


def project_back(inputs, weight, cotangent):
    rounded = cotangent.astype(jnp.bfloat16)
    back_in = jnp.einsum("...b,ab->...a", rounded, weight, preferred_element_type=jnp.float32)
    flat_in = inputs.reshape(-1, inputs.shape[-1])
    flat_back = rounded.reshape(-1, rounded.shape[-1])
    grad_weight = jnp.einsum("na,nb->ab", flat_in, flat_back, preferred_element_type=jnp.float32)
    return (back_in, grad_weight, jnp.sum(flat_back, 0, dtype=jnp.float32))


def project_many(inputs, weights):
    return jnp.einsum("...a,kab->k...b", inputs, weights, preferred_element_type=jnp.float32)


def project_many_back(inputs, weights, cotangent):
    rounded = cotangent.astype(jnp.bfloat16)
    back_in = jnp.einsum("k...b,kab->...a", rounded, weights, preferred_element_type=jnp.float32)
    flat_in = inputs.reshape(-1, inputs.shape[-1])
    flat_back = rounded.reshape(rounded.shape[0], -1, rounded.shape[-1])
    grad_weight = jnp.einsum("na,knb->kab", flat_in, flat_back, preferred_element_type=jnp.float32)
    return (back_in, grad_weight, jnp.sum(flat_back, 1, dtype=jnp.float32))


def stacked_bias(first_row, last_row, rank):
    rows = jnp.stack([first_row, jnp.zeros_like(first_row), last_row])
    return rows.reshape((3,) + (1,) * (rank - 2) + (first_row.shape[-1],))


def scores_of(query, keys, allowed):
    raw_scores = jnp.einsum(
        "blhd,bmhd->bhlm", query, keys, preferred_element_type=jnp.float32
    ) * HD ** (-0.5)
    return jnp.where(allowed[:, None, None, :], raw_scores, -1000000000.0)


def attend(query, keys, values, allowed):
    scores = scores_of(query, keys, allowed)
    highest = jnp.max(scores, -1, keepdims=True)
    expanded = jnp.exp(scores - highest)
    summed = jnp.sum(expanded, -1, keepdims=True)
    probabilities = (expanded / summed).astype(jnp.bfloat16)
    mixed = jnp.einsum("bhlm,bmhd->blhd", probabilities, values, preferred_element_type=jnp.float32)
    return (mixed, (highest + jnp.log(summed))[..., 0])


def attend_back(query, keys, values, allowed, logsum, back_out):
    scores = scores_of(query, keys, allowed)
    probabilities = jnp.exp(scores - logsum[..., None])
    back_probs = jnp.einsum("blhd,bmhd->bhlm", back_out, values, preferred_element_type=jnp.float32)
    inner = jnp.sum(back_probs * probabilities, -1, keepdims=True)
    back_scores = (probabilities * (back_probs - inner)).astype(jnp.bfloat16)
    factor = HD ** (-0.5)
    back_query = (
        jnp.einsum("bhlm,bmhd->blhd", back_scores, keys, preferred_element_type=jnp.float32)
        * factor
    )
    back_keys = (
        jnp.einsum("bhlm,blhd->bmhd", back_scores, query, preferred_element_type=jnp.float32)
        * factor
    )
    back_values = jnp.einsum(
        "bhlm,blhd->bmhd",
        probabilities.astype(jnp.bfloat16),
        back_out,
        preferred_element_type=jnp.float32,
    )
    return (back_query, back_keys, back_values)


def per_patch(tensor, clip_count):
    return (
        tensor.reshape(clip_count, F, S, H, HD)
        .transpose(0, 2, 1, 3, 4)
        .reshape(clip_count * S, F, H, HD)
    )


def from_patch(tensor, clip_count):
    return (
        tensor.reshape(clip_count, S, F, H, HD)
        .transpose(0, 2, 1, 3, 4)
        .reshape(clip_count, F, S, H * HD)
    )


def per_frame(tensor, clip_count):
    width = tensor.shape[-1]
    leading = jnp.broadcast_to(tensor[:, None, :1], (clip_count, F, 1, width))
    framed = jnp.concatenate([leading, tensor[:, 1:].reshape(clip_count, F, S, width)], 2)
    return framed.reshape(clip_count * F, S + 1, H, HD)


def from_frame(tensor, clip_count):
    framed = tensor.reshape(clip_count, F, S + 1, H * HD)
    return jnp.concatenate(
        [jnp.sum(framed[:, :, :1], 1), framed[:, :, 1:].reshape(clip_count, F * S, H * HD)], 1
    )


def forward(mats16, head16, vectors, patches, patch_keep_mask):
    clip_count = patches.shape[0]
    alive = patch_keep_mask > 0
    embedded = project(patches, mats16[0]) + vectors[9]
    start_rows = embedded + vectors[31 : 31 + S][None, None] + vectors[1 : 1 + F][None, :, None]
    normed_time = layer_norm(start_rows, vectors[22], vectors[23]).astype(jnp.bfloat16)
    triple_time = (
        project_many(normed_time, mats16[1:4]) + stacked_bias(vectors[10], vectors[11], 5)
    ).astype(jnp.bfloat16)
    live_time = alive.transpose(0, 2, 1).reshape(clip_count * S, F)
    mixed_time, logsum_time = attend(
        per_patch(triple_time[0], clip_count),
        per_patch(triple_time[1], clip_count),
        per_patch(triple_time[2], clip_count),
        live_time,
    )
    mixed_time = from_patch(mixed_time, clip_count).astype(jnp.bfloat16)
    moved_time = (project(mixed_time, mats16[4]) + vectors[12]).astype(jnp.bfloat16)
    after_time = start_rows + project(moved_time, mats16[5]) + vectors[13]
    leading = jnp.broadcast_to(vectors[0] + vectors[30], (clip_count, 1, D))
    joined = jnp.concatenate([leading, after_time.reshape(clip_count, F * S, D)], 1)
    normed_space = layer_norm(joined, vectors[24], vectors[25]).astype(jnp.bfloat16)
    triple_space = (
        project_many(normed_space, mats16[6:9]) + stacked_bias(vectors[14], vectors[15], 4)
    ).astype(jnp.bfloat16)
    live_space = jnp.concatenate([jnp.ones((clip_count, F, 1), jnp.bool_), alive], 2).reshape(
        clip_count * F, S + 1
    )
    mixed_space, logsum_space = attend(
        per_frame(triple_space[0], clip_count),
        per_frame(triple_space[1], clip_count),
        per_frame(triple_space[2], clip_count),
        live_space,
    )
    mixed_space = mixed_space.reshape(clip_count, F, S + 1, D)
    mixed_space = jnp.concatenate(
        [jnp.mean(mixed_space[:, :, :1], 1), mixed_space[:, :, 1:].reshape(clip_count, F * S, D)], 1
    ).astype(jnp.bfloat16)
    after_space = joined + project(mixed_space, mats16[9]) + vectors[16]
    normed_mlp = layer_norm(after_space, vectors[26], vectors[27]).astype(jnp.bfloat16)
    hidden = project_many(normed_mlp, mats16[10:14]) + vectors[17:21][:, None, None, :]
    activated = gelu_exact(hidden).astype(jnp.bfloat16)
    after_mlp = (
        after_space
        + jnp.einsum("kcna,kab->cnb", activated, mats16[14:18], preferred_element_type=jnp.float32)
        + vectors[21]
    )
    pooled = jnp.mean(layer_norm(after_mlp, vectors[28], vectors[29]), 1).astype(jnp.bfloat16)
    projected = project(pooled, head16)
    saved = (
        start_rows,
        normed_time,
        triple_time,
        live_time,
        logsum_time,
        mixed_time,
        moved_time,
        joined,
        normed_space,
        triple_space,
        live_space,
        logsum_space,
        mixed_space,
        after_space,
        normed_mlp,
        hidden,
        activated,
        after_mlp,
        pooled,
    )
    return (projected, saved)


def backward(mats16, head16, vectors, patches, saved, back_projected):
    (
        start_rows,
        normed_time,
        triple_time,
        live_time,
        logsum_time,
        mixed_time,
        moved_time,
        joined,
        normed_space,
        triple_space,
        live_space,
        logsum_space,
        mixed_space,
        after_space,
        normed_mlp,
        hidden,
        activated,
        after_mlp,
        pooled,
    ) = saved
    clip_count = start_rows.shape[0]
    rows_clip = joined.shape[1]
    back_pooled, grad_head, unused_bias = project_back(pooled, head16, back_projected)
    unused_out, norm_back = jax.vjp(layer_norm, after_mlp, vectors[28], vectors[29])
    reverse_perceptron, gain_final, shift_final = norm_back(
        jnp.broadcast_to(back_pooled[:, None] / rows_clip, after_mlp.shape)
    )
    rounded = reverse_perceptron.astype(jnp.bfloat16)
    back_activated = jnp.einsum(
        "cnb,kab->kcna", rounded, mats16[14:18], preferred_element_type=jnp.float32
    )
    grad_down = jnp.einsum("kcna,cnb->kab", activated, rounded, preferred_element_type=jnp.float32)
    bias_down = jnp.sum(rounded, (0, 1), dtype=jnp.float32)
    unused_out, gelu_back = jax.vjp(gelu_exact, hidden)
    (back_hidden,) = gelu_back(back_activated)
    back_normed, grad_up, bias_up = project_many_back(normed_mlp, mats16[10:14], back_hidden)
    unused_out, norm_back = jax.vjp(layer_norm, after_space, vectors[26], vectors[27])
    back_norm_in, gain_mlp, shift_mlp = norm_back(back_normed)
    back_space = reverse_perceptron + back_norm_in
    back_mixed, grad_proj_space, bias_proj_space = project_back(mixed_space, mats16[9], back_space)
    back_mixed = back_mixed.astype(jnp.bfloat16)
    head_rows = (back_mixed[:, None, :1].astype(jnp.float32) / F).astype(jnp.bfloat16)
    back_frames = jnp.concatenate(
        [
            jnp.broadcast_to(head_rows, (clip_count, F, 1, D)),
            back_mixed[:, 1:].reshape(clip_count, F, S, D),
        ],
        2,
    ).reshape(clip_count * F, S + 1, H, HD)
    back_query, back_keys, back_values = attend_back(
        per_frame(triple_space[0], clip_count),
        per_frame(triple_space[1], clip_count),
        per_frame(triple_space[2], clip_count),
        live_space,
        logsum_space,
        back_frames,
    )
    back_triple = jnp.stack(
        [
            from_frame(back_query, clip_count),
            from_frame(back_keys, clip_count),
            from_frame(back_values, clip_count),
        ]
    )
    back_normed, grad_triple_space, bias_triple_space = project_many_back(
        normed_space, mats16[6:9], back_triple
    )
    unused_out, norm_back = jax.vjp(layer_norm, joined, vectors[24], vectors[25])
    back_norm_in, gain_space, shift_space = norm_back(back_normed)
    back_joined = back_space + back_norm_in
    back_class = jnp.sum(back_joined[:, 0], 0)
    back_after = back_joined[:, 1:].reshape(clip_count, F, S, D)
    back_moved, grad_fc_time, bias_fc_time = project_back(moved_time, mats16[5], back_after)
    back_mixed, grad_proj_time, bias_proj_time = project_back(mixed_time, mats16[4], back_moved)
    back_mixed = per_patch(back_mixed.astype(jnp.bfloat16), clip_count)
    back_query, back_keys, back_values = attend_back(
        per_patch(triple_time[0], clip_count),
        per_patch(triple_time[1], clip_count),
        per_patch(triple_time[2], clip_count),
        live_time,
        logsum_time,
        back_mixed,
    )
    back_triple = jnp.stack(
        [
            from_patch(back_query, clip_count),
            from_patch(back_keys, clip_count),
            from_patch(back_values, clip_count),
        ]
    )
    back_normed, grad_triple_time, bias_triple_time = project_many_back(
        normed_time, mats16[1:4], back_triple
    )
    unused_out, norm_back = jax.vjp(layer_norm, start_rows, vectors[22], vectors[23])
    back_norm_in, gain_time, shift_time = norm_back(back_normed)
    back_start = back_after + back_norm_in
    rounded = back_start.astype(jnp.bfloat16).reshape(-1, D)
    grad_embed = jnp.einsum(
        "na,nb->ab",
        patches.reshape(-1, patches.shape[-1]),
        rounded,
        preferred_element_type=jnp.float32,
    )
    embedding_bias = jnp.sum(rounded, 0, dtype=jnp.float32)
    grad_mats = jnp.concatenate(
        [
            grad_embed[None],
            grad_triple_time,
            grad_proj_time[None],
            grad_fc_time[None],
            grad_triple_space,
            grad_proj_space[None],
            grad_up,
            grad_down,
        ],
        0,
    )
    grad_vecs = jnp.concatenate(
        [
            back_class[None],
            jnp.sum(back_start, (0, 2)),
            embedding_bias[None],
            bias_triple_time[0][None],
            bias_triple_time[2][None],
            bias_proj_time[None],
            bias_fc_time[None],
            bias_triple_space[0][None],
            bias_triple_space[2][None],
            bias_proj_space[None],
            bias_up,
            bias_down[None],
            jnp.stack(
                [
                    gain_time,
                    shift_time,
                    gain_space,
                    shift_space,
                    gain_mlp,
                    shift_mlp,
                    gain_final,
                    shift_final,
                ]
            ),
            back_class[None],
            jnp.sum(back_start, (0, 1)),
        ],
        0,
    )
    return (grad_mats, grad_head, grad_vecs)


def normalize(projected):
    return projected * lax.rsqrt(jnp.sum(projected * projected, -1, keepdims=True) + 1e-06)


def adamw_step(weight, first, second, average, gradient, factor, rate):
    clipped = gradient * factor
    first = BETA_ONE * first + (1.0 - BETA_ONE) * clipped
    second = BETA_TWO * second + (1.0 - BETA_TWO) * clipped * clipped
    first_hat = first / (1.0 - BETA_ONE**STEP)
    second_hat = second / (1.0 - BETA_TWO**STEP)
    weight = weight - rate * (first_hat / (jnp.sqrt(second_hat) + ADAM_EPSILON) + DECAY * weight)
    average = AVERAGE_KEEP * average + (1.0 - AVERAGE_KEEP) * weight
    return (weight, first, second, average)


def pack(head, vecs):
    rows = head.shape[0] // 3
    first = jnp.concatenate([head[:rows], head[rows : 2 * rows], head[2 * rows :]], 1)
    tall = jnp.pad(vecs, ((0, D // 3 - vecs.shape[0]), (0, 0)))
    second = tall.reshape(D // head.shape[0], rows, head.shape[0]).transpose(1, 0, 2).reshape(rows, D)
    fill = -rows % 16
    return jnp.pad(jnp.stack([first, second]), ((0, 0), (0, fill), (0, 0)))


def unpack(blocks, rows):
    n = blocks.shape[0]
    kept = blocks[:, :, : rows // 3]
    head = kept[:, 0].reshape(n, rows // 3, 3, D // 3).transpose(0, 2, 1, 3).reshape(D, D // 3)
    vecs = kept[:, 1].reshape(n, rows // 3, n, rows).transpose(2, 1, 0, 3).reshape(D // 3, D)
    return head, vecs[:NVEC]


def pack_all(head, vecs, n):
    rows = D // n
    first = head.reshape(n, 3, rows // 3, D // 3).transpose(0, 2, 1, 3).reshape(n, rows // 3, D)
    tall = jnp.pad(vecs, ((0, D // 3 - vecs.shape[0]), (0, 0)))
    second = tall.reshape(n, rows // 3, n, rows).transpose(2, 1, 0, 3).reshape(n, rows // 3, D)
    fill = -(rows // 3) % 16
    return jnp.pad(jnp.stack([first, second]), ((0, 0), (0, 0), (0, fill), (0, 0)))


def unpack_shard(blocks, n):
    rows = D // n
    first, second = blocks[0, : rows // 3], blocks[1, : rows // 3]
    head = jnp.concatenate([first[:, : D // 3], first[:, D // 3 : 2 * D // 3], first[:, 2 * D // 3 :]], 0)
    vecs = second.reshape(rows // 3, n, rows).transpose(1, 0, 2).reshape(D // 3, rows)
    return head, vecs[:NVEC]


def local(
    lay,
    patches,
    patch_keep_mask,
    partner,
    matrices,
    matrix_first,
    matrix_second,
    matrix_average,
    head_weight,
    head_first,
    head_second,
    head_average,
    vectors,
    array_running_mean,
    vector_second,
    vector_average,
):
    n = lay.n
    gathered_mats, gathered_small = gather(
        lay,
        matrices.astype(jnp.bfloat16),
        pack(head_weight.astype(jnp.bfloat16), vectors.astype(jnp.bfloat16)),
    )
    mats16 = gathered_mats.reshape(NMAT, D, D)
    head16, vecs16 = unpack(gathered_small, lay.rows)
    projected, saved = forward(mats16, head16, vecs16.astype(jnp.float32), patches, patch_keep_mask)
    unit_length_lines, unit_back = jax.vjp(normalize, projected)
    clip_count, width = unit_length_lines.shape
    lines = unit_length_lines.reshape(-1, 128)
    tile = jnp.pad(lines, ((0, -lines.shape[0] % 8), (0, 0)))
    everyone = spread(lay.dp, n, tile, 2)
    gathered = everyone[:, : lines.shape[0]].reshape(-1, width)

    def contrast(gathered_rows):
        pairwise_affinity_scores_raw = (
            jnp.dot(gathered_rows, gathered_rows.T, precision=lax.Precision.HIGHEST)
            / SCORE_SHARPNESS
        )
        clip_total = pairwise_affinity_scores_raw.shape[0]
        column = jnp.arange(clip_total)[None, :]
        pairwise_affinity_scores_raw = jnp.where(
            jnp.arange(clip_total)[:, None] == column, -1000000000.0, pairwise_affinity_scores_raw
        )
        positive = jnp.sum(
            jnp.where(column == partner[:, None], pairwise_affinity_scores_raw, 0.0), -1
        )
        return jnp.mean(jax.nn.logsumexp(pairwise_affinity_scores_raw, -1) - positive)

    contrastive_loss, objective_cotangent_flow = jax.vjp(contrast, gathered)
    (back_gathered,) = objective_cotangent_flow(jnp.ones_like(contrastive_loss))
    clip_count = projected.shape[0]
    offset = lax.axis_index(("dp", "fsdp")) * clip_count
    back_unit = lax.dynamic_slice_in_dim(back_gathered, offset, clip_count, 0)
    (back_projected,) = unit_back(back_unit)
    grad_mats, grad_head, grad_vecs = backward(
        mats16,
        head16,
        vecs16.astype(jnp.float32),
        patches,
        saved,
        back_projected,
    )
    grad_mats, grad_small = reduce(
        lay,
        grad_mats.astype(jnp.bfloat16).reshape(NMAT, n, lay.rows, D),
        pack_all(grad_head, grad_vecs, n).astype(jnp.bfloat16),
    )
    grad_head, grad_vecs = unpack_shard(grad_small, n)
    partial_squares = (
        jnp.sum(grad_mats * grad_mats)
        + jnp.sum(grad_head * grad_head)
        + jnp.sum(grad_vecs * grad_vecs)
    )
    squares = spread(lay.dp, n, jnp.broadcast_to(partial_squares, (8, 128)), 3)
    squared_norm = jnp.sum(squares[:, 0, 0]) / lay.dp
    factor = CLIP_AT / jnp.maximum(jnp.sqrt(squared_norm), CLIP_AT)
    mats_out = adamw_step(
        matrices, matrix_first, matrix_second, matrix_average, grad_mats, factor, RATE
    )
    head_out = adamw_step(
        head_weight, head_first, head_second, head_average, grad_head, factor, RATE
    )
    vecs_out = adamw_step(
        vectors, array_running_mean, vector_second, vector_average, grad_vecs, factor, VECTOR_RATE
    )
    return (
        contrastive_loss,
        squared_norm,
        mats_out[0],
        mats_out[1],
        mats_out[2],
        mats_out[3],
        head_out[0],
        head_out[1],
        head_out[2],
        head_out[3],
        vecs_out[0],
        vecs_out[1],
        vecs_out[2],
        vecs_out[3],
    )


def solution(mesh):
    lay = Layout(mesh.shape["dp"], mesh.shape["fsdp"], 2)
    placed = (
        P(("dp", "fsdp"), None, None, None),
        P(("dp", "fsdp"), None, None),
        P(),
        P(None, "fsdp", None),
        P(None, "fsdp", None),
        P(None, "fsdp", None),
        P(None, "fsdp", None),
        P("fsdp", None),
        P("fsdp", None),
        P("fsdp", None),
        P("fsdp", None),
        P(None, "fsdp"),
        P(None, "fsdp"),
        P(None, "fsdp"),
        P(None, "fsdp"),
    )
    return jax.shard_map(
        functools.partial(local, lay),
        mesh=mesh,
        in_specs=placed,
        out_specs=(
            P(),
            P(),
            P(None, "fsdp", None),
            P(None, "fsdp", None),
            P(None, "fsdp", None),
            P(None, "fsdp", None),
            P("fsdp", None),
            P("fsdp", None),
            P("fsdp", None),
            P("fsdp", None),
            P(None, "fsdp"),
            P(None, "fsdp"),
            P(None, "fsdp"),
            P(None, "fsdp"),
        ),
        check_vma=False,
    )
```

```python
import functools
import jax
import jax.numpy as jnp
from jax import lax
from jax.experimental import pallas as pl
from jax.experimental.pallas import tpu as pltpu
from jax.sharding import PartitionSpec as P

D = 768
H = 12
HD = 64
F = 8
S = 196
SP = 208
NMAT = 18
NVEC = 227
STEP = 10

SCORE_SHARPNESS = 0.07
CLIP_AT = 0.05
RATE = 0.01
VECTOR_RATE = 0.1
BETA_ONE = 0.9
BETA_TWO = 0.95
ADAM_EPSILON = 1e-08
DECAY = 0.05
AVERAGE_KEEP = 0.9

MESH = pl.DeviceIdType.MESH
ANY = pl.BlockSpec(memory_space=pl.ANY)


class Layout:
    def __init__(self, dp, fsdp, split):
        self.dp, self.n = dp, fsdp
        self.outer = 4 if fsdp % 4 == 0 else 1
        self.inner = fsdp // self.outer
        self.planes = dp // 2
        self.half = NMAT // 2
        self.split = split
        self.common = self.half - split * self.planes
        self.handled = self.common + split
        self.rows = D // fsdp

    def place(self):
        i = lax.axis_index("fsdp")
        d = lax.axis_index("dp")
        return i, lax.div(i, self.inner), lax.rem(i, self.inner), lax.div(d, 2), lax.rem(d, 2)

    def peer(self, i, y, c):
        return {"fsdp": i, "dp": y * 2 + c}

    def matrix(self, c, y, k):
        if k < self.common:
            return c * self.half + k
        return c * self.half + self.common + y * self.split + (k - self.common)


def turn(x, t, size):
    return lax.rem(x + t + size, size)


def greet(lay, i, a, b, y, c):
    barrier = pltpu.get_barrier_semaphore()
    others = [lay.peer(turn(a, t, lay.outer) * lay.inner + b, y, c) for t in range(1, lay.outer)]
    others += [lay.peer(a * lay.inner + turn(b, u, lay.inner), y, c) for u in range(1, lay.inner)]
    others += [lay.peer(i, turn(y, v, lay.planes), c) for v in range(1, lay.planes)]
    others += [lay.peer(i, y, 1 - c)]
    for other in others:
        pl.semaphore_signal(barrier, inc=1, device_id=other, device_id_type=MESH)
    pl.semaphore_wait(barrier, len(others))


def gather_kernel(lay, w_ref, s_ref, ow_ref, os_ref, own_sem, zs, zr, xs, xr, ys, yr, cs, cr, small):
    i, a, b, y, c = lay.place()
    A, B = lay.outer, lay.inner
    greet(lay, i, a, b, y, c)
    pending = []

    def remote(src, dst, ssem, rsem, dev):
        copy = pltpu.make_async_remote_copy(
            src_ref=src, dst_ref=dst, send_sem=ssem, recv_sem=rsem, device_id=dev, device_id_type=MESH
        )
        copy.start()
        pending.append(copy)
        return copy

    def landed(dst, ssem, rsem, dev):
        pltpu.make_async_remote_copy(
            src_ref=dst, dst_ref=dst, send_sem=ssem, recv_sem=rsem, device_id=dev, device_id_type=MESH
        ).wait_recv()

    K = lay.handled
    here = lay.peer(i, y, 1 - c)
    local_small = pltpu.make_async_copy(s_ref, os_ref.at[i], own_sem.at[0])
    local_small.start()
    for k in [-1] + list(range(lay.common, K)) + list(range(lay.common)):
        src = s_ref if k < 0 else w_ref.at[lay.matrix(c, y, k)]
        dst = os_ref.at[i] if k < 0 else ow_ref.at[lay.matrix(c, y, k), i]
        for t in range(1, A):
            remote(src, dst, zs.at[k + 1, t], zr.at[k + 1, t], lay.peer(turn(a, t, A) * B + b, y, c))
        for u in range(1, B):
            remote(src, dst, xs.at[k + 1, u, 0], xr.at[k + 1, u, 0], lay.peer(a * B + turn(b, u, B), y, c))
    locals_ = []
    for first, count in ((lay.matrix(c, y, 0), lay.common), (lay.matrix(c, y, lay.common), lay.split)):
        if count:
            span = pl.ds(first, count)
            locals_.append(pltpu.make_async_copy(w_ref.at[span], ow_ref.at[span, i], own_sem.at[1 + len(locals_)]))
            locals_[-1].start()
    order = [-1] + list(range(lay.common, K)) + list(range(lay.common))

    def at(k, j):
        return os_ref.at[j] if k < 0 else ow_ref.at[lay.matrix(c, y, k), j]

    def cross(k):
        for t in range(1, A):
            j = turn(a, -t, A) * B + b
            landed(at(k, j), zs.at[k + 1, t], zr.at[k + 1, t], here)
            for u in range(1, B):
                remote(at(k, j), at(k, j), xs.at[k + 1, u, t], xr.at[k + 1, u, t], lay.peer(a * B + turn(b, u, B), y, c))

    def share(k):
        for u in range(1, B):
            for t in range(A):
                j = turn(a, -t, A) * B + turn(b, -u, B)
                landed(at(k, j), xs.at[k + 1, u, t], xr.at[k + 1, u, t], here)
        if k >= 0:
            m = lay.matrix(c, y, k)
            if k >= lay.common:
                for v in range(1, lay.planes):
                    q = k - lay.common
                    remote(ow_ref.at[m], ow_ref.at[m], ys.at[q, v], yr.at[q, v], lay.peer(i, turn(y, v, lay.planes), c))
            remote(ow_ref.at[m], ow_ref.at[m], cs.at[k], cr.at[k], here)

    for step in range(len(order) + 1):
        if step < len(order):
            cross(order[step])
        if step == 2:
            for local in locals_:
                local.wait()
        if step >= 1:
            share(order[step - 1])
    slot = K
    for v in range(1, lay.planes):
        for q in range(lay.split):
            m = lay.matrix(c, turn(y, -v, lay.planes), lay.common + q)
            landed(ow_ref.at[m], ys.at[q, v], yr.at[q, v], here)
            remote(ow_ref.at[m], ow_ref.at[m], cs.at[slot], cr.at[slot], here)
            slot += 1
    slot = K
    for k in range(K):
        m = lay.matrix(1 - c, y, k)
        landed(ow_ref.at[m], cs.at[k], cr.at[k], here)
    for v in range(1, lay.planes):
        for q in range(lay.split):
            m = lay.matrix(1 - c, turn(y, -v, lay.planes), lay.common + q)
            landed(ow_ref.at[m], cs.at[slot], cr.at[slot], here)
            slot += 1
    local_small.wait()
    for copy in pending:
        copy.wait_send()


def gather(lay, shard, small):
    A, B, K = lay.outer, lay.inner, lay.handled
    dma = pltpu.SemaphoreType.DMA
    kept = max(lay.split, 1)
    return pl.pallas_call(
        functools.partial(gather_kernel, lay),
        out_shape=(
            jax.ShapeDtypeStruct((NMAT, lay.n) + shard.shape[1:], shard.dtype),
            jax.ShapeDtypeStruct((lay.n,) + small.shape, small.dtype),
        ),
        in_specs=[ANY, ANY],
        out_specs=(ANY, ANY),
        scratch_shapes=[
            dma((3,)), dma((K + 1, A)), dma((K + 1, A)), dma((K + 1, B, A)), dma((K + 1, B, A)),
            dma((kept, lay.planes)), dma((kept, lay.planes)), dma((lay.half,)), dma((lay.half,)),
            dma((1,)),
        ],
        compiler_params=pltpu.CompilerParams(collective_id=0, has_side_effects=True),
    )(shard, small)


def reduce_kernel(lay, g_ref, s_ref, og_ref, os_ref, *scratch):
    i, a, b, y, c = lay.place()
    A, B, Y = lay.outer, lay.inner, lay.planes
    greet(lay, i, a, b, y, c)
    big, little, out_sem = scratch[:20], scratch[20:40], scratch[40]
    pending = []
    here = lay.peer(i, y, 1 - c)

    def remote(src, dst, ssem, rsem, dev):
        copy = pltpu.make_async_remote_copy(
            src_ref=src, dst_ref=dst, send_sem=ssem, recv_sem=rsem, device_id=dev, device_id_type=MESH
        )
        copy.start()
        pending.append(copy.wait_send)

    def landed(dst, sems, *at):
        pltpu.make_async_remote_copy(
            src_ref=dst, dst_ref=dst, send_sem=sems.at[at], recv_sem=sems.at[at], device_id=here, device_id_type=MESH
        ).wait_recv()

    class Set:
        def __init__(self, refs, common, split, source, target):
            (self.g, self.r, self.ys, self.yr, self.xs, self.xr, self.zs, self.zr, self.fin, self.all_) = refs[:10]
            (self.lsem, self.rs, self.rr, self.yss, self.yrs, self.xss, self.xrs, self.zss, self.zrs, self.fsem) = refs[10:]
            self.common, self.split = common, split
            self.source, self.target = source, target
            self.blocks = self.g.shape[1]

        def slots(self):
            found = [(v, q) for v in range(1, Y) for q in range(self.split)]
            return found + [(None, k) for k in range(self.common)] + [(0, q) for q in range(self.split)]

        def slot(self, v, q):
            return self.slots().index((v, q))

    def big_at(core, v, q):
        if v is None:
            return core * lay.half + q
        return core * lay.half + lay.common + turn(y, v, Y) * lay.split + q

    mats = Set(big, lay.common, lay.split, lambda core, v, q: g_ref.at[big_at(core, v, q)], lambda core, v, q: og_ref.at[big_at(core, v, q)])
    rest = Set(little, 1, 0, lambda core, v, q: s_ref.at[core], lambda core, v, q: os_ref.at[core])

    work = [(rest, None, 0)] + [(mats, None, k) for k in range(mats.common)] + [(mats, 0, q) for q in range(mats.split)]
    starts = [(mats, v, q) for v in range(1, Y) for q in range(mats.split)] + work
    for st, v, q in starts:
        n = st.slot(v, q)
        remote(st.source(1 - c, v, q), st.r.at[n], st.rs.at[n], st.rr.at[n], here)
        pltpu.make_async_copy(st.source(c, v, q), st.g.at[n], st.lsem.at[n]).start()

    def ready(st, v, q):
        n = st.slot(v, q)
        pltpu.make_async_copy(st.source(c, v, q), st.g.at[n], st.lsem.at[n]).wait()
        landed(st.r.at[n], st.rr, n)

    def base(st, n, v, q, j):
        total = st.g[n, j].astype(jnp.float32) + st.r[n, j].astype(jnp.float32)
        if v == 0:
            for w in range(1, Y):
                total = total + st.yr[w - 1, q, j].astype(jnp.float32)
        return total

    def pass_on(st, v, q):
        n = st.slot(v, q)
        ready(st, v, q)

        @pl.loop(0, st.blocks)
        def _(j):
            st.ys[v - 1, q, j] = base(st, n, None, q, j).astype(jnp.bfloat16)

        remote(st.ys.at[v - 1, q], st.yr.at[v - 1, q], st.yss.at[v - 1, q], st.yrs.at[v - 1, q], lay.peer(i, turn(y, v, Y), c))

    def item(st, v, q):
        return q if v is None else st.common + q

    def cross(st, v, q):
        n, k = st.slot(v, q), item(st, v, q)
        ready(st, v, q)
        if v == 0:
            for w in range(1, Y):
                landed(st.yr.at[w - 1, q], st.yrs, w - 1, q)
        for u in range(1, B):
            other = turn(b, u, B)

            @pl.loop(0, A)
            def _(e):
                st.xs[k, u - 1, e] = base(st, n, v, q, e * B + other).astype(jnp.bfloat16)

            remote(st.xs.at[k, u - 1], st.xr.at[k, u - 1], st.xss.at[k, u - 1], st.xrs.at[k, u - 1], lay.peer(a * B + other, y, c))

    def along(st, v, q):
        n, k = st.slot(v, q), item(st, v, q)
        for u in range(1, B):
            landed(st.xr.at[k, u - 1], st.xrs, k, u - 1)

        def total(e):
            value = base(st, n, v, q, e * B + b)
            for u in range(1, B):
                value = value + st.xr[k, u - 1, e].astype(jnp.float32)
            return value

        for t in range(1, A):
            e = turn(a, t, A)
            st.zs[k, t - 1] = total(e).astype(jnp.bfloat16)
            remote(st.zs.at[k, t - 1], st.zr.at[k, t - 1], st.zss.at[k, t - 1], st.zrs.at[k, t - 1], lay.peer(e * B + b, y, c))
        st.fin[k] = total(a)

    def close(st, v, q):
        k = item(st, v, q)
        for t in range(1, A):
            landed(st.zr.at[k, t - 1], st.zrs, k, t - 1)
        value = st.fin[k]
        for t in range(1, A):
            value = value + st.zr[k, t - 1].astype(jnp.float32)
        st.fin[k] = value
        if v is None:
            st.all_[y, k] = value
            for w in range(1, Y):
                remote(st.all_.at[y, k], st.all_.at[y, k], st.fsem.at[0, k, w], st.fsem.at[1, k, w], lay.peer(i, turn(y, w, Y), c))
        else:
            target = st.target(c, v, q)
            for w in range(1, Y):
                remote(st.fin.at[k], target, st.fsem.at[0, k, w], st.fsem.at[1, k, w], lay.peer(i, turn(y, w, Y), c))
            finish(st, k, target)

    def finish(st, k, target):
        copy = pltpu.make_async_copy(st.fin.at[k], target, st.fsem.at[2, k, 0])
        copy.start()
        pending.append(copy.wait)
        remote(st.fin.at[k], target, st.fsem.at[3, k, 0], st.fsem.at[4, k, 0], here)

    def merge(st, v, q):
        k = item(st, v, q)
        if v is None:
            for w in range(1, Y):
                landed(st.all_.at[turn(y, -w, Y), k], st.fsem, 1, k, w)
            value = st.all_[0, k]
            for w in range(1, Y):
                value = value + st.all_[w, k]
            st.fin[k] = value
            finish(st, k, st.target(c, v, q))
        else:
            for w in range(1, Y):
                back = st.target(c, -w, q)
                landed(back, st.fsem, 1, k, w)
                remote(back, back, st.fsem.at[3, k, w], st.fsem.at[4, k, w], here)

    others = [(mats, v, q) for v in range(1, Y) for q in range(mats.split)]
    for job in others:
        pass_on(*job)
    for step in range(len(work) + 3):
        if step < len(work):
            cross(*work[step])
        if 0 <= step - 1 < len(work):
            along(*work[step - 1])
        if 0 <= step - 2 < len(work):
            close(*work[step - 2])
        if 0 <= step - 3 < len(work):
            merge(*work[step - 3])
    for st, v, q in work:
        k = item(st, v, q)
        landed(st.target(1 - c, v, q), st.fsem, 4, k, 0)
        if v is not None:
            for w in range(1, Y):
                landed(st.target(1 - c, -w, q), st.fsem, 4, k, w)
    for wait in pending:
        wait()


def reduce_scratch(lay, rows, common, split):
    A, B, Y, n = lay.outer, lay.inner, lay.planes, lay.n
    slots, kept, passed, K = common + split * Y, max(split, 1), max(Y - 1, 1), common + split
    half = jnp.bfloat16
    dma = pltpu.SemaphoreType.DMA
    width = rows if split else 16
    depth = n if split else 1
    crossed, along = max(B - 1, 1), max(A - 1, 1)
    return [
        pltpu.VMEM((slots, n, rows, D), half), pltpu.VMEM((slots, n, rows, D), half),
        pltpu.VMEM((passed, kept, depth, width, D), half), pltpu.VMEM((passed, kept, depth, width, D), half),
        pltpu.VMEM((K, crossed, A, rows, D), half), pltpu.VMEM((K, crossed, A, rows, D), half),
        pltpu.VMEM((K, along, rows, D), half), pltpu.VMEM((K, along, rows, D), half),
        pltpu.VMEM((K, rows, D), jnp.float32), pltpu.VMEM((Y, K if not split else common, rows, D), jnp.float32),
        dma((slots,)), dma((slots,)), dma((slots,)), dma((passed, kept)), dma((passed, kept)),
        dma((K, crossed)), dma((K, crossed)), dma((K, along)), dma((K, along)), dma((5, K, Y)),
    ]


def reduce(lay, grads, small):
    rows, rest = grads.shape[2], small.shape[2]
    return pl.pallas_call(
        functools.partial(reduce_kernel, lay),
        out_shape=(
            jax.ShapeDtypeStruct((NMAT, rows, D), jnp.float32),
            jax.ShapeDtypeStruct((2, rest, D), jnp.float32),
        ),
        in_specs=[ANY, ANY],
        out_specs=(ANY, ANY),
        scratch_shapes=reduce_scratch(lay, rows, lay.common, lay.split) + reduce_scratch(lay, rest, 1, 0) + [pltpu.SemaphoreType.DMA((1,))],
        compiler_params=pltpu.CompilerParams(collective_id=1, has_side_effects=True, vmem_limit_bytes=58 * 2**20),
    )(grads, small)


def spread_kernel(dp, n, x_ref, o_ref, ssem, rsem):
    i, d = lax.axis_index("fsdp"), lax.axis_index("dp")
    me = d * n + i
    total = dp * n
    barrier = pltpu.get_barrier_semaphore()

    def other(t):
        j = lax.rem(me + t, total)
        return {"fsdp": lax.rem(j, n), "dp": lax.div(j, n)}

    @pl.loop(1, total)
    def _(t):
        pl.semaphore_signal(barrier, inc=1, device_id=other(t), device_id_type=MESH)

    pl.semaphore_wait(barrier, total - 1)

    @pl.loop(1, total)
    def _(t):
        pltpu.make_async_remote_copy(
            src_ref=x_ref, dst_ref=o_ref.at[me], send_sem=ssem.at[t], recv_sem=rsem.at[t], device_id=other(t), device_id_type=MESH
        ).start()

    o_ref[me] = x_ref[...]

    @pl.loop(1, total)
    def _(t):
        pltpu.make_async_remote_copy(
            src_ref=x_ref, dst_ref=o_ref.at[lax.rem(me - t + total, total)], send_sem=ssem.at[t], recv_sem=rsem.at[t], device_id=other(t), device_id_type=MESH
        ).wait()


def spread(dp, n, tile, number):
    vmem = pl.BlockSpec(memory_space=pltpu.VMEM)
    return pl.pallas_call(
        functools.partial(spread_kernel, dp, n),
        out_shape=jax.ShapeDtypeStruct((dp * n,) + tile.shape, tile.dtype),
        in_specs=[vmem],
        out_specs=vmem,
        scratch_shapes=[pltpu.SemaphoreType.DMA((dp * n,)), pltpu.SemaphoreType.DMA((dp * n,))],
        compiler_params=pltpu.CompilerParams(collective_id=number, has_side_effects=True),
    )(tile)


FB = 2
GROUP = 16
HALF = jnp.bfloat16
FULL = jnp.float32
NORM_EPS = 1e-06
MASKED = -1000000000.0
NEVER = -3e38


def dot(a, b):
    return lax.dot_general(a, b, (((1,), (0,)), ((), ())), preferred_element_type=FULL)


def dot_back(a, b):
    return lax.dot_general(a, b, (((1,), (1,)), ((), ())), preferred_element_type=FULL)


def dot_rows(a, b):
    return lax.dot_general(a, b, (((0,), (0,)), ((), ())), preferred_element_type=FULL)


def mean(x):
    return jnp.sum(x, -1, keepdims=True) * (1.0 / D)


def norm(x, gain, shift):
    centred = x - mean(x)
    scale = lax.rsqrt(mean(centred * centred) + NORM_EPS)
    return centred * scale * gain + shift


def norm_back(x, gain, back):
    centred = x - mean(x)
    scale = lax.rsqrt(mean(centred * centred) + NORM_EPS)
    unit = centred * scale
    inner = back * gain
    return scale * (inner - mean(inner) - unit * mean(inner * unit)), back * unit


def normal_cdf(x):
    size = jnp.abs(x) * 0.7071067811865476
    t = pl.reciprocal(1.0 + 0.3275911 * size)
    bell = jnp.exp(-0.5 * x * x)
    poly = ((((1.061405429 * t - 1.453152027) * t + 1.421413741) * t - 0.284496736) * t + 0.254829592) * t
    tail = 0.5 * poly * bell
    return jnp.where(x < 0, tail, 1.0 - tail), bell


def gelu(x):
    return x * normal_cdf(x)[0]


def gelu_slope(x):
    below, bell = normal_cdf(x)
    return below + x * bell * 0.3989422804014327


def column_sum(x):
    return jnp.sum(x.astype(FULL), 0, keepdims=True)


def flat(ref):
    x = ref[...]
    return x.reshape(-1, x.shape[-1])


def row_of(rows):
    return lax.rem(lax.broadcasted_iota(jnp.int32, (rows, 1), 0), SP)


def first_step():
    return pl.program_id(0) == 0


def add_rows(ref, values):
    @pl.when(first_step())
    def _():
        ref[...] = jnp.zeros_like(ref)

    for k, value in enumerate(values):
        if value is not None:
            ref[k : k + 1, :] += value


def pair_lanes(x, low):
    zero = jnp.zeros_like(x)
    return jnp.concatenate([jnp.where(low, x, zero), jnp.where(low, zero, x)], 0)


def attend(q, k, v, fill):
    rows = q.shape[0]
    low = lax.broadcasted_iota(jnp.int32, (rows, 128), 1) < HD
    stacked = pair_lanes(q * jnp.asarray(HD ** (-0.5), HALF), low)
    scores = dot_back(stacked, k)
    if fill.shape[0] != 1:
        fill = jnp.concatenate([fill, fill], 0)
    scores = jnp.where(fill == 0.0, scores, fill)
    expanded = jnp.exp(scores - jnp.max(scores, -1, keepdims=True))
    share = pl.reciprocal(jnp.sum(expanded, -1, keepdims=True))
    mixed = dot((expanded * share).astype(HALF), v)
    return jnp.where(low, mixed[:rows], mixed[rows:])


def attend_back(q, k, v, back, fill):
    rows = q.shape[0]
    low = lax.broadcasted_iota(jnp.int32, (rows, 128), 1) < HD
    stacked = pair_lanes(q * jnp.asarray(HD ** (-0.5), HALF), low)
    backs = pair_lanes(back, low)
    scores = dot_back(k, stacked)
    scores = jnp.where(fill == 0.0, scores, fill)
    expanded = jnp.exp(scores - jnp.max(scores, 0, keepdims=True))
    chances = expanded * pl.reciprocal(jnp.sum(expanded, 0, keepdims=True))
    back_chances = dot_back(v, backs)
    inner = jnp.sum(back_chances * chances, 0, keepdims=True)
    back_scores = (chances * (back_chances - inner)).astype(HALF)
    back_keys = dot(back_scores, stacked)
    back_values = dot(chances.astype(HALF), backs)
    queries = dot_rows(back_scores, k) * HD ** (-0.5)
    return jnp.where(low, queries[:rows], queries[rows:]), back_keys, back_values


def embed_kernel(p_ref, w0, w1, w2, w3, v_ref, pos_ref, time_ref, pad_ref, x_ref, a_ref, q_ref, k_ref, b_ref):
    pad_ref[:, SP - GROUP :, :] = jnp.zeros((FB, GROUP, D), HALF)
    for f in range(FB):
        pad_ref[f, :S, :] = p_ref[0, f]
    pos = pos_ref[...]
    here = jnp.concatenate([pos + time_ref[f] for f in range(FB)], 0)
    x = dot(flat(pad_ref), w0[0]) + v_ref[9:10] + here
    x_ref[...] = x.reshape(FB, SP, D)
    a = norm(x, v_ref[22:23], v_ref[23:24]).astype(HALF)
    a_ref[...] = a.reshape(FB, SP, D)
    q_ref[...] = (dot(a, w1[0]) + v_ref[10:11]).astype(HALF).reshape(FB, SP, D)
    k_ref[...] = dot(a, w2[0]).astype(HALF).reshape(FB, SP, D)
    b_ref[...] = (dot(a, w3[0]) + v_ref[11:12]).astype(HALF).reshape(FB, SP, D)


def time_kernel(q_ref, k_ref, v_ref, fill_ref, o_ref):
    rows = F * GROUP
    for p in range(H // 2):
        lanes = slice(128 * p, 128 * p + 128)
        q, k, v = (ref[:, :, lanes].reshape(rows, 128) for ref in (q_ref, k_ref, v_ref))
        o_ref[:, :, lanes] = attend(q, k, v, fill_ref[0]).astype(HALF).reshape(F, GROUP, 128)


def space_kernel(o_ref, x_ref, w0, w1, w2, w3, w4, v_ref, fill_ref, y_ref, xs_ref, a_ref, q_ref, k_ref, b_ref, os_ref, cls_ref):
    rows = FB * SP
    y = (dot(flat(o_ref), w0[0]) + v_ref[12:13]).astype(HALF)
    y_ref[...] = y.reshape(FB, SP, D)
    x = flat(x_ref) + dot(y, w1[0]) + v_ref[13:14]
    x = jnp.where(row_of(rows) == S, v_ref[0:1] + v_ref[30:31], x)
    xs_ref[...] = x.reshape(FB, SP, D)
    a = norm(x, v_ref[24:25], v_ref[25:26]).astype(HALF)
    a_ref[...] = a.reshape(FB, SP, D)
    q_ref[...] = (dot(a, w2[0]) + v_ref[14:15]).astype(HALF).reshape(FB, SP, D)
    k_ref[...] = dot(a, w3[0]).astype(HALF).reshape(FB, SP, D)
    b_ref[...] = (dot(a, w4[0]) + v_ref[15:16]).astype(HALF).reshape(FB, SP, D)
    for f in range(FB):
        for p in range(H // 2):
            lanes = slice(128 * p, 128 * p + 128)
            mixed = attend(q_ref[f, :, lanes], k_ref[f, :, lanes], b_ref[f, :, lanes], fill_ref[f])
            os_ref[f, :, lanes] = mixed.astype(HALF)
            cls_ref[f, :, lanes] = mixed[S : S + 8]


def mlp_kernel(o_ref, cls_ref, xs_ref, wp_ref, u0, u1, u2, u3, e0, e1, e2, e3, v_ref, share_ref, of_ref, x2_ref, a_ref, g_ref, e_ref, x3_ref, pool_ref):
    rows = FB * SP
    o = jnp.where(row_of(rows) == S, cls_ref[...], flat(o_ref).astype(FULL)).astype(HALF)
    of_ref[...] = o.reshape(FB, SP, D)
    x2 = flat(xs_ref) + dot(o, wp_ref[0]) + v_ref[16:17]
    x2_ref[...] = x2.reshape(FB, SP, D)
    a = norm(x2, v_ref[26:27], v_ref[27:28]).astype(HALF)
    a_ref[...] = a.reshape(FB, SP, D)
    x3 = x2 + v_ref[21:22]
    for k in range(4):
        g = dot(a, (u0, u1, u2, u3)[k][0]) + v_ref[17 + k : 18 + k]
        g_ref[k] = g.reshape(FB, SP, D)
        e = gelu(g).astype(HALF)
        e_ref[k] = e.reshape(FB, SP, D)
        x3 = x3 + dot(e, (e0, e1, e2, e3)[k][0])
    x3_ref[...] = x3.reshape(FB, SP, D)
    final = norm(x3, v_ref[28:29], v_ref[29:30]) * share_ref[...]
    add_rows(pool_ref, [column_sum(final)])


def mlp_back_kernel(x3_ref, x2_ref, g_ref, d_ref, wp_ref, u0, u1, u2, u3, e0, e1, e2, e3, v_ref, share_ref, q_ref, k_ref, b_ref, fill_ref,
                    r3_ref, dg_ref, d2_ref, r2_ref, dq_ref, dk_ref, dv_ref, cq_ref, ck_ref, cv_ref, sum_ref, do_ref):
    top = d_ref[0:1] * share_ref[...]
    d3, unit = norm_back(flat(x3_ref), v_ref[28:29], top)
    sums = [column_sum(unit), column_sum(top)]
    r3 = d3.astype(HALF)
    r3_ref[...] = r3.reshape(FB, SP, D)
    sums.append(column_sum(r3))
    back = None
    for k in range(4):
        dg = (dot_back(r3, (e0, e1, e2, e3)[k][0]) * gelu_slope(flat(g_ref.at[k]))).astype(HALF)
        dg_ref[k] = dg.reshape(FB, SP, D)
        sums.append(column_sum(dg))
        part = dot_back(dg, (u0, u1, u2, u3)[k][0])
        back = part if back is None else back + part
    d2, unit = norm_back(flat(x2_ref), v_ref[26:27], back)
    sums += [column_sum(unit), column_sum(back)]
    d2 = d2 + d3
    d2_ref[...] = d2.reshape(FB, SP, D)
    r2 = d2.astype(HALF)
    r2_ref[...] = r2.reshape(FB, SP, D)
    sums.append(column_sum(r2))
    add_rows(sum_ref, sums)
    do_ref[...] = dot_back(r2, wp_ref[0]).astype(HALF).reshape(FB, SP, D)
    for f in range(FB):
        for p in range(H // 2):
            lanes = slice(128 * p, 128 * p + 128)
            outs = attend_back(q_ref[f, :, lanes], k_ref[f, :, lanes], b_ref[f, :, lanes], do_ref[f, :, lanes], fill_ref[f][:, 0:1])
            for value, ref, cls in zip(outs, (dq_ref, dk_ref, dv_ref), (cq_ref, ck_ref, cv_ref)):
                ref[f, :, lanes] = value.astype(HALF)
                cls[f, :, lanes] = value[S : S + 8]


def space_back_kernel(dq_ref, dk_ref, dv_ref, cls_ref, xs_ref, d2_ref, w0, w1, w2, w3, w4, v_ref, fq_ref, fk_ref, fv_ref, d1_ref, r1_ref, dy_ref, do_ref, sum_ref):
    rows = FB * SP
    is_class = row_of(rows) == S
    grads = []
    for k, (ref, out) in enumerate(zip((dq_ref, dk_ref, dv_ref), (fq_ref, fk_ref, fv_ref))):
        grad = jnp.where(is_class, cls_ref[k : k + 1], flat(ref).astype(FULL)).astype(HALF)
        out[...] = grad.reshape(FB, SP, D)
        grads.append(grad)
    back = dot_back(grads[0], w2[0]) + dot_back(grads[1], w3[0]) + dot_back(grads[2], w4[0])
    d, unit = norm_back(flat(xs_ref), v_ref[24:25], back)
    sums = [column_sum(grads[0]), column_sum(grads[2]), column_sum(unit), column_sum(back)]
    d = d + flat(d2_ref)
    kept = jnp.where(is_class, d, 0.0)
    sums.append(column_sum(kept))
    d = d - kept
    d1_ref[...] = d.reshape(FB, SP, D)
    r1 = d.astype(HALF)
    r1_ref[...] = r1.reshape(FB, SP, D)
    sums.append(column_sum(r1))
    dy = dot_back(r1, w1[0]).astype(HALF)
    dy_ref[...] = dy.reshape(FB, SP, D)
    sums.append(column_sum(dy))
    do_ref[...] = dot_back(dy, w0[0]).astype(HALF).reshape(FB, SP, D)
    add_rows(sum_ref, sums)


def time_back_kernel(q_ref, k_ref, v_ref, d_ref, fill_ref, dq_ref, dk_ref, dv_ref):
    rows = F * GROUP
    fill = jnp.concatenate([fill_ref[0], fill_ref[0]], 1)
    for p in range(H // 2):
        lanes = slice(128 * p, 128 * p + 128)
        q, k, v, d = (ref[:, :, lanes].reshape(rows, 128) for ref in (q_ref, k_ref, v_ref, d_ref))
        for value, ref in zip(attend_back(q, k, v, d, fill), (dq_ref, dk_ref, dv_ref)):
            ref[:, :, lanes] = value.astype(HALF).reshape(F, GROUP, 128)


def embed_back_kernel(dq_ref, dk_ref, dv_ref, x_ref, d1_ref, w1, w2, w3, v_ref, r_ref, pos_ref, time_ref, sum_ref):
    q, v = flat(dq_ref), flat(dv_ref)
    back = dot_back(q, w1[0]) + dot_back(flat(dk_ref), w2[0]) + dot_back(v, w3[0])
    d, unit = norm_back(flat(x_ref), v_ref[22:23], back)
    d = d + flat(d1_ref)
    rounded = d.astype(HALF)
    r_ref[...] = rounded.reshape(FB, SP, D)
    add_rows(sum_ref, [column_sum(q), column_sum(v), column_sum(unit), column_sum(back), column_sum(rounded)])

    @pl.when(first_step())
    def _():
        pos_ref[...] = jnp.zeros_like(pos_ref)

    total = jnp.zeros((SP, D), FULL)
    for f in range(FB):
        part = d[f * SP : (f + 1) * SP]
        time_ref[f] = column_sum(part)
        total = total + part
    pos_ref[...] += total


def shape(*dims, dtype=HALF):
    return jax.ShapeDtypeStruct(dims, dtype)


FRAMES = pl.BlockSpec((FB, SP, D), lambda i: (i, 0, 0))
HIDDEN = pl.BlockSpec((4, FB, SP, D), lambda i: (0, i, 0, 0))
SLAB = pl.BlockSpec((F, GROUP, D), lambda i: (0, i, 0))
ROWS16 = shape(F, SP, D)
ROWS32 = shape(F, SP, D, dtype=FULL)
HIDDEN16 = shape(4, F, SP, D)
HIDDEN32 = shape(4, F, SP, D, dtype=FULL)


def whole(*dims):
    return pl.BlockSpec(dims, lambda i: (0,) * len(dims), pipeline_mode=pl.Buffered(1))


def matrix(m):
    return pl.BlockSpec((1, D, D), lambda i: (m, 0, 0), pipeline_mode=pl.Buffered(1))


def matrices(first, count):
    return [matrix(m) for m in range(first, first + count)]


def summed(rows):
    return pl.BlockSpec((rows, D), lambda i: (0, 0))


def call(kernel, steps, in_specs, out_specs, out_shape, scratch=()):
    return pl.pallas_call(
        kernel,
        grid=(steps,),
        in_specs=in_specs,
        out_specs=out_specs,
        out_shape=out_shape,
        scratch_shapes=list(scratch),
        compiler_params=pltpu.CompilerParams(vmem_limit_bytes=60 * 2**20),
    )


def per_frame(*tail):
    return pl.BlockSpec((FB,) + tail, lambda i: (i,) + (0,) * len(tail))


def forward(mats, table, patches, mask):
    alive = jnp.pad(mask[0] > 0, ((0, 0), (0, SP - S)))
    kept = jnp.where(alive, 0.0, MASKED).astype(FULL)
    places = jnp.arange(SP)[None]
    space_fill = jnp.where(places < S, kept, jnp.where(places == S, 0.0, NEVER))
    time_keys = kept.reshape(F, SP // GROUP, GROUP).transpose(1, 0, 2).reshape(SP // GROUP, F * GROUP)
    spot = jnp.arange(F * GROUP) % GROUP
    same = spot[:, None] == spot[None]
    time_fill = jnp.where(same[None], time_keys[:, None, :], NEVER)
    time_fill_back = jnp.where(same[None], time_keys[:, :, None], NEVER)
    table = jnp.pad(table, ((0, -table.shape[0] % 8), (0, 0)))
    pos = jnp.pad(table[31 : 31 + S], ((0, SP - S), (0, 0)))
    time = table[1 : 1 + F][:, None]
    one = jnp.where(places[0] < S, 1.0, jnp.where(places[0] == S, 1.0 / F, 0.0)).astype(FULL)
    share = jnp.broadcast_to(jnp.tile(one, FB)[:, None], (FB * SP, 1))
    tab = whole(*table.shape)
    steps = F // FB
    padded, x0, at, qt, kt, vt = call(
        embed_kernel, steps,
        [pl.BlockSpec((1, FB, S, D), lambda i: (0, i, 0, 0))] + matrices(0, 4) + [tab, whole(SP, D), per_frame(1, D)],
        [FRAMES] * 6, [ROWS16, ROWS32] + [ROWS16] * 4,
    )(patches, *[mats] * 4, table, pos, time)
    ot = call(
        time_kernel, SP // GROUP, [SLAB] * 3 + [pl.BlockSpec((1, F * GROUP, F * GROUP), lambda i: (i, 0, 0))], SLAB, ROWS16,
    )(qt, kt, vt, time_fill)
    yt, xs, as_, qs, ks, vs, os_, cls = call(
        space_kernel, steps, [FRAMES, FRAMES] + matrices(4, 5) + [tab, per_frame(1, SP)],
        [FRAMES] * 7 + [per_frame(8, D)], [ROWS16, ROWS32] + [ROWS16] * 5 + [shape(F, 8, D, dtype=FULL)],
    )(ot, x0, *[mats] * 5, table, space_fill[:, None])
    cls = jnp.mean(cls[:, 0], 0, keepdims=True)
    of, x2, a2, g, e, x3, pool = call(
        mlp_kernel, steps,
        [FRAMES, whole(1, D), FRAMES] + matrices(9, 9) + [tab, whole(FB * SP, 1)],
        [FRAMES] * 3 + [HIDDEN] * 2 + [FRAMES, summed(8)],
        [ROWS16, ROWS32, ROWS16, HIDDEN32, HIDDEN16, ROWS32, shape(8, D, dtype=FULL)],
    )(os_, cls, xs, *[mats] * 9, table, share)
    pooled = (pool[:1] / (F * S + 1)).astype(HALF)
    saved = (table, share, space_fill, time_fill_back, padded, x0, at, qt, kt, vt, ot, yt, xs, as_, qs, ks, vs, of, x2, a2, g, e, x3)
    return pooled, saved


def backward(mats, saved, back_pooled):
    (table, share, space_fill, time_fill, padded, x0, at, qt, kt, vt, ot, yt, xs, as_, qs, ks, vs, of, x2, a2, g, e, x3) = saved
    tab = whole(*table.shape)
    steps = F // FB
    top = back_pooled / (F * S + 1)
    column = jnp.broadcast_to(space_fill[:, :, None], (F, SP, 128))
    r3, dg, d2, r2, dq, dk, dv, cq, ck, cv, sums1 = call(
        mlp_back_kernel, steps,
        [FRAMES, FRAMES, HIDDEN, whole(1, D)] + matrices(9, 9) + [tab, whole(FB * SP, 1), FRAMES, FRAMES, FRAMES, per_frame(SP, 128)],
        [FRAMES, HIDDEN] + [FRAMES] * 5 + [per_frame(8, D)] * 3 + [summed(16)],
        [ROWS16, HIDDEN16, ROWS32] + [ROWS16] * 4 + [shape(F, 8, D, dtype=FULL)] * 3 + [shape(16, D, dtype=FULL)],
        [pltpu.VMEM((FB, SP, D), HALF)],
    )(x3, x2, g, top, *[mats] * 9, table, share, qs, ks, vs, column)
    cls = jnp.concatenate([jnp.sum(part[:, 0], 0, keepdims=True) for part in (cq, ck, cv)], 0)
    cls = cls.astype(HALF).astype(FULL) / F
    fq, fk, fv, d1, r1, dy, do, sums2 = call(
        space_back_kernel, steps,
        [FRAMES] * 3 + [whole(3, D), FRAMES, FRAMES] + matrices(4, 5) + [tab],
        [FRAMES] * 7 + [summed(16)],
        [ROWS16] * 3 + [ROWS32] + [ROWS16] * 3 + [shape(16, D, dtype=FULL)],
    )(dq, dk, dv, cls, xs, d2, *[mats] * 5, table)
    tq, tk, tv = call(
        time_back_kernel, SP // GROUP, [SLAB] * 4 + [pl.BlockSpec((1, F * GROUP, F * GROUP), lambda i: (i, 0, 0))], [SLAB] * 3, [ROWS16] * 3,
    )(qt, kt, vt, do, time_fill)
    rp, pos, time, sums3 = call(
        embed_back_kernel, steps,
        [FRAMES] * 5 + matrices(1, 3) + [tab],
        [FRAMES, summed(SP), per_frame(1, D), summed(16)],
        [ROWS16, shape(SP, D, dtype=FULL), shape(F, 1, D, dtype=FULL), shape(16, D, dtype=FULL)],
    )(tq, tk, tv, x0, d1, *[mats] * 3, table)

    def product(a, b):
        return dot_rows(a.reshape(-1, D), b.reshape(-1, D)).astype(HALF)

    pairs = [(padded, rp), (at, tq), (at, tk), (at, tv), (ot, dy), (yt, r1), (as_, fq), (as_, fk), (as_, fv), (of, r2)]
    pairs += [(a2, dg[k]) for k in range(4)] + [(e[k], r3) for k in range(4)]
    grad_mats = jnp.stack([product(*pair) for pair in pairs])
    class_grad = sums2[4:5]
    grad_vecs = jnp.concatenate(
        [
            class_grad, time[:, 0], sums3[4:5], sums3[0:2], sums2[6:7], sums2[5:6], sums2[0:2], sums1[9:10], sums1[3:7], sums1[2:3],
            sums3[2:4], sums2[2:4], sums1[7:9], sums1[0:2], class_grad, pos[:S],
        ],
        0,
    )
    return grad_mats, grad_vecs


def project(inputs, weight):
    return jnp.einsum("...a,ab->...b", inputs, weight, preferred_element_type=jnp.float32)


def project_back(inputs, weight, cotangent):
    rounded = cotangent.astype(jnp.bfloat16)
    back_in = jnp.einsum("...b,ab->...a", rounded, weight, preferred_element_type=jnp.float32)
    flat_in = inputs.reshape(-1, inputs.shape[-1])
    flat_back = rounded.reshape(-1, rounded.shape[-1])
    grad_weight = jnp.einsum("na,nb->ab", flat_in, flat_back, preferred_element_type=jnp.float32)
    return (back_in, grad_weight, jnp.sum(flat_back, 0, dtype=jnp.float32))


def normalize(projected):
    return projected * lax.rsqrt(jnp.sum(projected * projected, -1, keepdims=True) + 1e-06)


def adamw_step(weight, first, second, average, gradient, factor, rate):
    clipped = gradient * factor
    first = BETA_ONE * first + (1.0 - BETA_ONE) * clipped
    second = BETA_TWO * second + (1.0 - BETA_TWO) * clipped * clipped
    first_hat = first / (1.0 - BETA_ONE**STEP)
    second_hat = second / (1.0 - BETA_TWO**STEP)
    weight = weight - rate * (first_hat / (jnp.sqrt(second_hat) + ADAM_EPSILON) + DECAY * weight)
    average = AVERAGE_KEEP * average + (1.0 - AVERAGE_KEEP) * weight
    return (weight, first, second, average)


def pack(head, vecs):
    rows = head.shape[0] // 3
    first = jnp.concatenate([head[:rows], head[rows : 2 * rows], head[2 * rows :]], 1)
    tall = jnp.pad(vecs, ((0, D // 3 - vecs.shape[0]), (0, 0)))
    second = tall.reshape(D // head.shape[0], rows, head.shape[0]).transpose(1, 0, 2).reshape(rows, D)
    fill = -rows % 16
    return jnp.pad(jnp.stack([first, second]), ((0, 0), (0, fill), (0, 0)))


def unpack(blocks, rows):
    n = blocks.shape[0]
    kept = blocks[:, :, : rows // 3]
    head = kept[:, 0].reshape(n, rows // 3, 3, D // 3).transpose(0, 2, 1, 3).reshape(D, D // 3)
    vecs = kept[:, 1].reshape(n, rows // 3, n, rows).transpose(2, 1, 0, 3).reshape(D // 3, D)
    return head, vecs[:NVEC]


def pack_all(head, vecs, n):
    rows = D // n
    first = head.reshape(n, 3, rows // 3, D // 3).transpose(0, 2, 1, 3).reshape(n, rows // 3, D)
    tall = jnp.pad(vecs, ((0, D // 3 - vecs.shape[0]), (0, 0)))
    second = tall.reshape(n, rows // 3, n, rows).transpose(2, 1, 0, 3).reshape(n, rows // 3, D)
    fill = -(rows // 3) % 16
    return jnp.pad(jnp.stack([first, second]), ((0, 0), (0, 0), (0, fill), (0, 0)))


def unpack_shard(blocks, n):
    rows = D // n
    first, second = blocks[0, : rows // 3], blocks[1, : rows // 3]
    head = jnp.concatenate([first[:, : D // 3], first[:, D // 3 : 2 * D // 3], first[:, 2 * D // 3 :]], 0)
    vecs = second.reshape(rows // 3, n, rows).transpose(1, 0, 2).reshape(D // 3, rows)
    return head, vecs[:NVEC]


def local(
    lay,
    patches,
    patch_keep_mask,
    partner,
    matrices,
    matrix_first,
    matrix_second,
    matrix_average,
    head_weight,
    head_first,
    head_second,
    head_average,
    vectors,
    array_running_mean,
    vector_second,
    vector_average,
):
    n = lay.n
    gathered_mats, gathered_small = gather(
        lay,
        matrices.astype(jnp.bfloat16),
        pack(head_weight.astype(jnp.bfloat16), vectors.astype(jnp.bfloat16)),
    )
    mats16 = gathered_mats.reshape(NMAT, D, D)
    head16, vecs16 = unpack(gathered_small, lay.rows)
    pooled, saved = forward(mats16, vecs16.astype(jnp.float32), patches, patch_keep_mask)
    projected = project(pooled, head16)
    unit_length_lines, unit_back = jax.vjp(normalize, projected)
    clip_count, width = unit_length_lines.shape
    lines = unit_length_lines.reshape(-1, 128)
    tile = jnp.pad(lines, ((0, -lines.shape[0] % 8), (0, 0)))
    everyone = spread(lay.dp, n, tile, 2)
    gathered = everyone[:, : lines.shape[0]].reshape(-1, width)

    def contrast(gathered_rows):
        pairwise_affinity_scores_raw = (
            jnp.dot(gathered_rows, gathered_rows.T, precision=lax.Precision.HIGHEST)
            / SCORE_SHARPNESS
        )
        clip_total = pairwise_affinity_scores_raw.shape[0]
        column = jnp.arange(clip_total)[None, :]
        pairwise_affinity_scores_raw = jnp.where(
            jnp.arange(clip_total)[:, None] == column, -1000000000.0, pairwise_affinity_scores_raw
        )
        positive = jnp.sum(
            jnp.where(column == partner[:, None], pairwise_affinity_scores_raw, 0.0), -1
        )
        return jnp.mean(jax.nn.logsumexp(pairwise_affinity_scores_raw, -1) - positive)

    contrastive_loss, objective_cotangent_flow = jax.vjp(contrast, gathered)
    (back_gathered,) = objective_cotangent_flow(jnp.ones_like(contrastive_loss))
    clip_count = projected.shape[0]
    offset = lax.axis_index(("dp", "fsdp")) * clip_count
    back_unit = lax.dynamic_slice_in_dim(back_gathered, offset, clip_count, 0)
    (back_projected,) = unit_back(back_unit)
    back_pooled, grad_head, unused_bias = project_back(pooled, head16, back_projected)
    grad_mats, grad_vecs = backward(mats16, saved, back_pooled)
    grad_mats, grad_small = reduce(
        lay,
        grad_mats.reshape(NMAT, n, lay.rows, D),
        pack_all(grad_head, grad_vecs, n).astype(jnp.bfloat16),
    )
    grad_head, grad_vecs = unpack_shard(grad_small, n)
    partial_squares = (
        jnp.sum(grad_mats * grad_mats)
        + jnp.sum(grad_head * grad_head)
        + jnp.sum(grad_vecs * grad_vecs)
    )
    squares = spread(lay.dp, n, jnp.broadcast_to(partial_squares, (8, 128)), 3)
    squared_norm = jnp.sum(squares[:, 0, 0]) / lay.dp
    factor = CLIP_AT / jnp.maximum(jnp.sqrt(squared_norm), CLIP_AT)
    mats_out = adamw_step(
        matrices, matrix_first, matrix_second, matrix_average, grad_mats, factor, RATE
    )
    head_out = adamw_step(
        head_weight, head_first, head_second, head_average, grad_head, factor, RATE
    )
    vecs_out = adamw_step(
        vectors, array_running_mean, vector_second, vector_average, grad_vecs, factor, VECTOR_RATE
    )
    return (
        contrastive_loss,
        squared_norm,
        mats_out[0],
        mats_out[1],
        mats_out[2],
        mats_out[3],
        head_out[0],
        head_out[1],
        head_out[2],
        head_out[3],
        vecs_out[0],
        vecs_out[1],
        vecs_out[2],
        vecs_out[3],
    )


def solution(mesh):
    lay = Layout(mesh.shape["dp"], mesh.shape["fsdp"], 2)
    placed = (
        P(("dp", "fsdp"), None, None, None),
        P(("dp", "fsdp"), None, None),
        P(),
        P(None, "fsdp", None),
        P(None, "fsdp", None),
        P(None, "fsdp", None),
        P(None, "fsdp", None),
        P("fsdp", None),
        P("fsdp", None),
        P("fsdp", None),
        P("fsdp", None),
        P(None, "fsdp"),
        P(None, "fsdp"),
        P(None, "fsdp"),
        P(None, "fsdp"),
    )
    return jax.shard_map(
        functools.partial(local, lay),
        mesh=mesh,
        in_specs=placed,
        out_specs=(
            P(),
            P(),
            P(None, "fsdp", None),
            P(None, "fsdp", None),
            P(None, "fsdp", None),
            P(None, "fsdp", None),
            P("fsdp", None),
            P("fsdp", None),
            P("fsdp", None),
            P("fsdp", None),
            P(None, "fsdp"),
            P(None, "fsdp"),
            P(None, "fsdp"),
            P(None, "fsdp"),
        ),
        check_vma=False,
    )
```

```python
import functools
import jax
import jax.numpy as jnp
from jax import lax
from jax.experimental import pallas as pl
from jax.experimental.pallas import tpu as pltpu
from jax.sharding import PartitionSpec as P

D = 768
H = 12
HD = 64
F = 8
S = 196
SP = 208
NMAT = 18
NVEC = 227
STEP = 10

SCORE_SHARPNESS = 0.07
CLIP_AT = 0.05
RATE = 0.01
VECTOR_RATE = 0.1
BETA_ONE = 0.9
BETA_TWO = 0.95
ADAM_EPSILON = 1e-08
DECAY = 0.05
AVERAGE_KEEP = 0.9

MESH = pl.DeviceIdType.MESH
ANY = pl.BlockSpec(memory_space=pl.ANY)


class Layout:
    def __init__(self, dp, fsdp, split):
        self.dp, self.n = dp, fsdp
        self.outer = 4 if fsdp % 4 == 0 else 1
        self.inner = fsdp // self.outer
        self.planes = dp // 2
        self.half = NMAT // 2
        self.split = split
        self.common = self.half - split * self.planes
        self.handled = self.common + split
        self.rows = D // fsdp

    def place(self):
        i = lax.axis_index("fsdp")
        d = lax.axis_index("dp")
        return i, lax.div(i, self.inner), lax.rem(i, self.inner), lax.div(d, 2), lax.rem(d, 2)

    def peer(self, i, y, c):
        return {"fsdp": i, "dp": y * 2 + c}

    def matrix(self, c, y, k):
        if k < self.common:
            return c * self.half + k
        return c * self.half + self.common + y * self.split + (k - self.common)


def turn(x, t, size):
    return lax.rem(x + t + size, size)


def greet(lay, i, a, b, y, c):
    barrier = pltpu.get_barrier_semaphore()
    others = [lay.peer(turn(a, t, lay.outer) * lay.inner + b, y, c) for t in range(1, lay.outer)]
    others += [lay.peer(a * lay.inner + turn(b, u, lay.inner), y, c) for u in range(1, lay.inner)]
    others += [lay.peer(i, turn(y, v, lay.planes), c) for v in range(1, lay.planes)]
    others += [lay.peer(i, y, 1 - c)]
    for other in others:
        pl.semaphore_signal(barrier, inc=1, device_id=other, device_id_type=MESH)
    pl.semaphore_wait(barrier, len(others))


def gather_kernel(lay, w_ref, s_ref, ow_ref, os_ref, own_sem, zs, zr, xs, xr, ys, yr, cs, cr, small):
    i, a, b, y, c = lay.place()
    A, B = lay.outer, lay.inner
    greet(lay, i, a, b, y, c)
    pending = []

    def remote(src, dst, ssem, rsem, dev):
        copy = pltpu.make_async_remote_copy(
            src_ref=src, dst_ref=dst, send_sem=ssem, recv_sem=rsem, device_id=dev, device_id_type=MESH
        )
        copy.start()
        pending.append(copy)
        return copy

    def landed(dst, ssem, rsem, dev):
        pltpu.make_async_remote_copy(
            src_ref=dst, dst_ref=dst, send_sem=ssem, recv_sem=rsem, device_id=dev, device_id_type=MESH
        ).wait_recv()

    K = lay.handled
    here = lay.peer(i, y, 1 - c)
    local_small = pltpu.make_async_copy(s_ref, os_ref.at[i], own_sem.at[0])
    local_small.start()
    for k in [-1] + list(range(lay.common, K)) + list(range(lay.common)):
        src = s_ref if k < 0 else w_ref.at[lay.matrix(c, y, k)]
        dst = os_ref.at[i] if k < 0 else ow_ref.at[lay.matrix(c, y, k), i]
        for t in range(1, A):
            remote(src, dst, zs.at[k + 1, t], zr.at[k + 1, t], lay.peer(turn(a, t, A) * B + b, y, c))
        for u in range(1, B):
            remote(src, dst, xs.at[k + 1, u, 0], xr.at[k + 1, u, 0], lay.peer(a * B + turn(b, u, B), y, c))
    locals_ = []
    for first, count in ((lay.matrix(c, y, 0), lay.common), (lay.matrix(c, y, lay.common), lay.split)):
        if count:
            span = pl.ds(first, count)
            locals_.append(pltpu.make_async_copy(w_ref.at[span], ow_ref.at[span, i], own_sem.at[1 + len(locals_)]))
            locals_[-1].start()
    order = [-1] + list(range(lay.common, K)) + list(range(lay.common))

    def at(k, j):
        return os_ref.at[j] if k < 0 else ow_ref.at[lay.matrix(c, y, k), j]

    def cross(k):
        for t in range(1, A):
            j = turn(a, -t, A) * B + b
            landed(at(k, j), zs.at[k + 1, t], zr.at[k + 1, t], here)
            for u in range(1, B):
                remote(at(k, j), at(k, j), xs.at[k + 1, u, t], xr.at[k + 1, u, t], lay.peer(a * B + turn(b, u, B), y, c))

    def share(k):
        for u in range(1, B):
            for t in range(A):
                j = turn(a, -t, A) * B + turn(b, -u, B)
                landed(at(k, j), xs.at[k + 1, u, t], xr.at[k + 1, u, t], here)
        if k >= 0:
            m = lay.matrix(c, y, k)
            if k >= lay.common:
                for v in range(1, lay.planes):
                    q = k - lay.common
                    remote(ow_ref.at[m], ow_ref.at[m], ys.at[q, v], yr.at[q, v], lay.peer(i, turn(y, v, lay.planes), c))
            remote(ow_ref.at[m], ow_ref.at[m], cs.at[k], cr.at[k], here)

    for step in range(len(order) + 1):
        if step < len(order):
            cross(order[step])
        if step == 2:
            for local in locals_:
                local.wait()
        if step >= 1:
            share(order[step - 1])
    slot = K
    for v in range(1, lay.planes):
        for q in range(lay.split):
            m = lay.matrix(c, turn(y, -v, lay.planes), lay.common + q)
            landed(ow_ref.at[m], ys.at[q, v], yr.at[q, v], here)
            remote(ow_ref.at[m], ow_ref.at[m], cs.at[slot], cr.at[slot], here)
            slot += 1
    slot = K
    for k in range(K):
        m = lay.matrix(1 - c, y, k)
        landed(ow_ref.at[m], cs.at[k], cr.at[k], here)
    for v in range(1, lay.planes):
        for q in range(lay.split):
            m = lay.matrix(1 - c, turn(y, -v, lay.planes), lay.common + q)
            landed(ow_ref.at[m], cs.at[slot], cr.at[slot], here)
            slot += 1
    local_small.wait()
    for copy in pending:
        copy.wait_send()


def gather(lay, shard, small):
    A, B, K = lay.outer, lay.inner, lay.handled
    dma = pltpu.SemaphoreType.DMA
    kept = max(lay.split, 1)
    return pl.pallas_call(
        functools.partial(gather_kernel, lay),
        out_shape=(
            jax.ShapeDtypeStruct((NMAT, lay.n) + shard.shape[1:], shard.dtype),
            jax.ShapeDtypeStruct((lay.n,) + small.shape, small.dtype),
        ),
        in_specs=[ANY, ANY],
        out_specs=(ANY, ANY),
        scratch_shapes=[
            dma((3,)), dma((K + 1, A)), dma((K + 1, A)), dma((K + 1, B, A)), dma((K + 1, B, A)),
            dma((kept, lay.planes)), dma((kept, lay.planes)), dma((lay.half,)), dma((lay.half,)),
            dma((1,)),
        ],
        compiler_params=pltpu.CompilerParams(collective_id=0, has_side_effects=True),
    )(shard, small)


def spread_kernel(dp, n, x_ref, o_ref, ssem, rsem):
    i, d = lax.axis_index("fsdp"), lax.axis_index("dp")
    me = d * n + i
    total = dp * n
    barrier = pltpu.get_barrier_semaphore()

    def other(t):
        j = lax.rem(me + t, total)
        return {"fsdp": lax.rem(j, n), "dp": lax.div(j, n)}

    @pl.loop(1, total)
    def _(t):
        pl.semaphore_signal(barrier, inc=1, device_id=other(t), device_id_type=MESH)

    pl.semaphore_wait(barrier, total - 1)

    @pl.loop(1, total)
    def _(t):
        pltpu.make_async_remote_copy(
            src_ref=x_ref, dst_ref=o_ref.at[me], send_sem=ssem.at[t], recv_sem=rsem.at[t], device_id=other(t), device_id_type=MESH
        ).start()

    o_ref[me] = x_ref[...]

    @pl.loop(1, total)
    def _(t):
        pltpu.make_async_remote_copy(
            src_ref=x_ref, dst_ref=o_ref.at[lax.rem(me - t + total, total)], send_sem=ssem.at[t], recv_sem=rsem.at[t], device_id=other(t), device_id_type=MESH
        ).wait()


def spread(dp, n, tile, number):
    vmem = pl.BlockSpec(memory_space=pltpu.VMEM)
    return pl.pallas_call(
        functools.partial(spread_kernel, dp, n),
        out_shape=jax.ShapeDtypeStruct((dp * n,) + tile.shape, tile.dtype),
        in_specs=[vmem],
        out_specs=vmem,
        scratch_shapes=[pltpu.SemaphoreType.DMA((dp * n,)), pltpu.SemaphoreType.DMA((dp * n,))],
        compiler_params=pltpu.CompilerParams(collective_id=number, has_side_effects=True),
    )(tile)


FB = 2
GROUP = 16
HALF = jnp.bfloat16
FULL = jnp.float32
NORM_EPS = 1e-06
MASKED = -1000000000.0
NEVER = -3e38


def dot(a, b):
    return lax.dot_general(a, b, (((1,), (0,)), ((), ())), preferred_element_type=FULL)


def dot_back(a, b):
    return lax.dot_general(a, b, (((1,), (1,)), ((), ())), preferred_element_type=FULL)


def dot_rows(a, b):
    return lax.dot_general(a, b, (((0,), (0,)), ((), ())), preferred_element_type=FULL)


def mean(x):
    return jnp.sum(x, -1, keepdims=True) * (1.0 / D)


def norm(x, gain, shift):
    centred = x - mean(x)
    scale = lax.rsqrt(mean(centred * centred) + NORM_EPS)
    return centred * scale * gain + shift


def norm_back(x, gain, back):
    centred = x - mean(x)
    scale = lax.rsqrt(mean(centred * centred) + NORM_EPS)
    unit = centred * scale
    inner = back * gain
    return scale * (inner - mean(inner) - unit * mean(inner * unit)), back * unit


def normal_cdf(x):
    size = jnp.abs(x) * 0.7071067811865476
    t = pl.reciprocal(1.0 + 0.3275911 * size)
    bell = jnp.exp(-0.5 * x * x)
    poly = ((((1.061405429 * t - 1.453152027) * t + 1.421413741) * t - 0.284496736) * t + 0.254829592) * t
    tail = 0.5 * poly * bell
    return jnp.where(x < 0, tail, 1.0 - tail), bell


def gelu(x):
    return x * normal_cdf(x)[0]


def gelu_slope(x):
    below, bell = normal_cdf(x)
    return below + x * bell * 0.3989422804014327


def column_sum(x):
    return jnp.sum(x.astype(FULL), 0, keepdims=True)


def flat(ref):
    x = ref[...]
    return x.reshape(-1, x.shape[-1])


def row_of(rows):
    return lax.rem(lax.broadcasted_iota(jnp.int32, (rows, 1), 0), SP)


def first_step():
    return pl.program_id(0) == 0


def add_rows(ref, values):
    @pl.when(first_step())
    def _():
        ref[...] = jnp.zeros_like(ref)

    for k, value in enumerate(values):
        if value is not None:
            ref[k : k + 1, :] += value


def pair_lanes(x, low):
    zero = jnp.zeros_like(x)
    return jnp.concatenate([jnp.where(low, x, zero), jnp.where(low, zero, x)], 0)


def attend(q, k, v, fill):
    rows = q.shape[0]
    low = lax.broadcasted_iota(jnp.int32, (rows, 128), 1) < HD
    stacked = pair_lanes(q * jnp.asarray(HD ** (-0.5), HALF), low)
    scores = dot_back(stacked, k)
    if fill.shape[0] != 1:
        fill = jnp.concatenate([fill, fill], 0)
    scores = jnp.where(fill == 0.0, scores, fill)
    expanded = jnp.exp(scores - jnp.max(scores, -1, keepdims=True))
    share = pl.reciprocal(jnp.sum(expanded, -1, keepdims=True))
    mixed = dot((expanded * share).astype(HALF), v)
    return jnp.where(low, mixed[:rows], mixed[rows:])


def attend_back(q, k, v, back, fill):
    rows = q.shape[0]
    low = lax.broadcasted_iota(jnp.int32, (rows, 128), 1) < HD
    stacked = pair_lanes(q * jnp.asarray(HD ** (-0.5), HALF), low)
    backs = pair_lanes(back, low)
    scores = dot_back(k, stacked)
    scores = jnp.where(fill == 0.0, scores, fill)
    expanded = jnp.exp(scores - jnp.max(scores, 0, keepdims=True))
    chances = expanded * pl.reciprocal(jnp.sum(expanded, 0, keepdims=True))
    back_chances = dot_back(v, backs)
    inner = jnp.sum(back_chances * chances, 0, keepdims=True)
    back_scores = (chances * (back_chances - inner)).astype(HALF)
    back_keys = dot(back_scores, stacked)
    back_values = dot(chances.astype(HALF), backs)
    queries = dot_rows(back_scores, k) * HD ** (-0.5)
    return jnp.where(low, queries[:rows], queries[rows:]), back_keys, back_values


def embed_kernel(p_ref, w0, w1, w2, w3, v_ref, pos_ref, time_ref, pad_ref, x_ref, a_ref, q_ref, k_ref, b_ref):
    pad_ref[:, SP - GROUP :, :] = jnp.zeros((FB, GROUP, D), HALF)
    for f in range(FB):
        pad_ref[f, :S, :] = p_ref[0, f]
    pos = pos_ref[...]
    here = jnp.concatenate([pos + time_ref[f] for f in range(FB)], 0)
    x = dot(flat(pad_ref), w0[0]) + v_ref[9:10] + here
    x_ref[...] = x.reshape(FB, SP, D)
    a = norm(x, v_ref[22:23], v_ref[23:24]).astype(HALF)
    a_ref[...] = a.reshape(FB, SP, D)
    q_ref[...] = (dot(a, w1[0]) + v_ref[10:11]).astype(HALF).reshape(FB, SP, D)
    k_ref[...] = dot(a, w2[0]).astype(HALF).reshape(FB, SP, D)
    b_ref[...] = (dot(a, w3[0]) + v_ref[11:12]).astype(HALF).reshape(FB, SP, D)


def time_kernel(q_ref, k_ref, v_ref, fill_ref, o_ref):
    rows = F * GROUP
    for p in range(H // 2):
        lanes = slice(128 * p, 128 * p + 128)
        q, k, v = (ref[:, :, lanes].reshape(rows, 128) for ref in (q_ref, k_ref, v_ref))
        o_ref[:, :, lanes] = attend(q, k, v, fill_ref[0]).astype(HALF).reshape(F, GROUP, 128)


def space_kernel(o_ref, x_ref, w0, w1, w2, w3, w4, v_ref, fill_ref, y_ref, xs_ref, a_ref, q_ref, k_ref, b_ref, os_ref, cls_ref):
    rows = FB * SP
    y = (dot(flat(o_ref), w0[0]) + v_ref[12:13]).astype(HALF)
    y_ref[...] = y.reshape(FB, SP, D)
    x = flat(x_ref) + dot(y, w1[0]) + v_ref[13:14]
    x = jnp.where(row_of(rows) == S, v_ref[0:1] + v_ref[30:31], x)
    xs_ref[...] = x.reshape(FB, SP, D)
    a = norm(x, v_ref[24:25], v_ref[25:26]).astype(HALF)
    a_ref[...] = a.reshape(FB, SP, D)
    q_ref[...] = (dot(a, w2[0]) + v_ref[14:15]).astype(HALF).reshape(FB, SP, D)
    k_ref[...] = dot(a, w3[0]).astype(HALF).reshape(FB, SP, D)
    b_ref[...] = (dot(a, w4[0]) + v_ref[15:16]).astype(HALF).reshape(FB, SP, D)
    for f in range(FB):
        for p in range(H // 2):
            lanes = slice(128 * p, 128 * p + 128)
            mixed = attend(q_ref[f, :, lanes], k_ref[f, :, lanes], b_ref[f, :, lanes], fill_ref[f])
            os_ref[f, :, lanes] = mixed.astype(HALF)
            cls_ref[f, :, lanes] = mixed[S : S + 8]


def mlp_kernel(o_ref, cls_ref, xs_ref, wp_ref, u0, u1, u2, u3, e0, e1, e2, e3, v_ref, share_ref, of_ref, x2_ref, a_ref, g_ref, e_ref, x3_ref, pool_ref):
    rows = FB * SP
    o = jnp.where(row_of(rows) == S, cls_ref[...], flat(o_ref).astype(FULL)).astype(HALF)
    of_ref[...] = o.reshape(FB, SP, D)
    x2 = flat(xs_ref) + dot(o, wp_ref[0]) + v_ref[16:17]
    x2_ref[...] = x2.reshape(FB, SP, D)
    a = norm(x2, v_ref[26:27], v_ref[27:28]).astype(HALF)
    a_ref[...] = a.reshape(FB, SP, D)
    x3 = x2 + v_ref[21:22]
    for k in range(4):
        g = dot(a, (u0, u1, u2, u3)[k][0]) + v_ref[17 + k : 18 + k]
        g_ref[k] = g.reshape(FB, SP, D)
        e = gelu(g).astype(HALF)
        e_ref[k] = e.reshape(FB, SP, D)
        x3 = x3 + dot(e, (e0, e1, e2, e3)[k][0])
    x3_ref[...] = x3.reshape(FB, SP, D)
    final = norm(x3, v_ref[28:29], v_ref[29:30]) * share_ref[...]
    add_rows(pool_ref, [column_sum(final)])


def mlp_back_kernel(x3_ref, x2_ref, g_ref, d_ref, wp_ref, u0, u1, u2, u3, e0, e1, e2, e3, v_ref, share_ref, q_ref, k_ref, b_ref, fill_ref,
                    r3_ref, dg_ref, d2_ref, r2_ref, dq_ref, dk_ref, dv_ref, cq_ref, ck_ref, cv_ref, sum_ref, do_ref):
    top = d_ref[0:1] * share_ref[...]
    d3, unit = norm_back(flat(x3_ref), v_ref[28:29], top)
    sums = [column_sum(unit), column_sum(top)]
    r3 = d3.astype(HALF)
    r3_ref[...] = r3.reshape(FB, SP, D)
    sums.append(column_sum(r3))
    back = None
    for k in range(4):
        dg = (dot_back(r3, (e0, e1, e2, e3)[k][0]) * gelu_slope(flat(g_ref.at[k]))).astype(HALF)
        dg_ref[k] = dg.reshape(FB, SP, D)
        sums.append(column_sum(dg))
        part = dot_back(dg, (u0, u1, u2, u3)[k][0])
        back = part if back is None else back + part
    d2, unit = norm_back(flat(x2_ref), v_ref[26:27], back)
    sums += [column_sum(unit), column_sum(back)]
    d2 = d2 + d3
    d2_ref[...] = d2.reshape(FB, SP, D)
    r2 = d2.astype(HALF)
    r2_ref[...] = r2.reshape(FB, SP, D)
    sums.append(column_sum(r2))
    add_rows(sum_ref, sums)
    do_ref[...] = dot_back(r2, wp_ref[0]).astype(HALF).reshape(FB, SP, D)
    for f in range(FB):
        for p in range(H // 2):
            lanes = slice(128 * p, 128 * p + 128)
            outs = attend_back(q_ref[f, :, lanes], k_ref[f, :, lanes], b_ref[f, :, lanes], do_ref[f, :, lanes], fill_ref[f][:, 0:1])
            for value, ref, cls in zip(outs, (dq_ref, dk_ref, dv_ref), (cq_ref, ck_ref, cv_ref)):
                ref[f, :, lanes] = value.astype(HALF)
                cls[f, :, lanes] = value[S : S + 8]


def space_back_kernel(dq_ref, dk_ref, dv_ref, cls_ref, xs_ref, d2_ref, w0, w1, w2, w3, w4, v_ref, fq_ref, fk_ref, fv_ref, d1_ref, r1_ref, dy_ref, do_ref, sum_ref):
    rows = FB * SP
    is_class = row_of(rows) == S
    grads = []
    for k, (ref, out) in enumerate(zip((dq_ref, dk_ref, dv_ref), (fq_ref, fk_ref, fv_ref))):
        grad = jnp.where(is_class, cls_ref[k : k + 1], flat(ref).astype(FULL)).astype(HALF)
        out[...] = grad.reshape(FB, SP, D)
        grads.append(grad)
    back = dot_back(grads[0], w2[0]) + dot_back(grads[1], w3[0]) + dot_back(grads[2], w4[0])
    d, unit = norm_back(flat(xs_ref), v_ref[24:25], back)
    sums = [column_sum(grads[0]), column_sum(grads[2]), column_sum(unit), column_sum(back)]
    d = d + flat(d2_ref)
    kept = jnp.where(is_class, d, 0.0)
    sums.append(column_sum(kept))
    d = d - kept
    d1_ref[...] = d.reshape(FB, SP, D)
    r1 = d.astype(HALF)
    r1_ref[...] = r1.reshape(FB, SP, D)
    sums.append(column_sum(r1))
    dy = dot_back(r1, w1[0]).astype(HALF)
    dy_ref[...] = dy.reshape(FB, SP, D)
    sums.append(column_sum(dy))
    do_ref[...] = dot_back(dy, w0[0]).astype(HALF).reshape(FB, SP, D)
    add_rows(sum_ref, sums)


def time_back_kernel(q_ref, k_ref, v_ref, d_ref, fill_ref, dq_ref, dk_ref, dv_ref):
    rows = F * GROUP
    fill = jnp.concatenate([fill_ref[0], fill_ref[0]], 1)
    for p in range(H // 2):
        lanes = slice(128 * p, 128 * p + 128)
        q, k, v, d = (ref[:, :, lanes].reshape(rows, 128) for ref in (q_ref, k_ref, v_ref, d_ref))
        for value, ref in zip(attend_back(q, k, v, d, fill), (dq_ref, dk_ref, dv_ref)):
            ref[:, :, lanes] = value.astype(HALF).reshape(F, GROUP, 128)


def embed_back_kernel(dq_ref, dk_ref, dv_ref, x_ref, d1_ref, w1, w2, w3, v_ref, r_ref, pos_ref, time_ref, sum_ref):
    q, v = flat(dq_ref), flat(dv_ref)
    back = dot_back(q, w1[0]) + dot_back(flat(dk_ref), w2[0]) + dot_back(v, w3[0])
    d, unit = norm_back(flat(x_ref), v_ref[22:23], back)
    d = d + flat(d1_ref)
    rounded = d.astype(HALF)
    r_ref[...] = rounded.reshape(FB, SP, D)
    add_rows(sum_ref, [column_sum(q), column_sum(v), column_sum(unit), column_sum(back), column_sum(rounded)])

    @pl.when(first_step())
    def _():
        pos_ref[...] = jnp.zeros_like(pos_ref)

    total = jnp.zeros((SP, D), FULL)
    for f in range(FB):
        part = d[f * SP : (f + 1) * SP]
        time_ref[f] = column_sum(part)
        total = total + part
    pos_ref[...] += total


def shape(*dims, dtype=HALF):
    return jax.ShapeDtypeStruct(dims, dtype)


FRAMES = pl.BlockSpec((FB, SP, D), lambda i: (i, 0, 0))
HIDDEN = pl.BlockSpec((4, FB, SP, D), lambda i: (0, i, 0, 0))
SLAB = pl.BlockSpec((F, GROUP, D), lambda i: (0, i, 0))
ROWS16 = shape(F, SP, D)
ROWS32 = shape(F, SP, D, dtype=FULL)
HIDDEN16 = shape(4, F, SP, D)
HIDDEN32 = shape(4, F, SP, D, dtype=FULL)


def whole(*dims):
    return pl.BlockSpec(dims, lambda i: (0,) * len(dims), pipeline_mode=pl.Buffered(1))


def matrix(m):
    return pl.BlockSpec((1, D, D), lambda i: (m, 0, 0), pipeline_mode=pl.Buffered(1))


def matrices(first, count):
    return [matrix(m) for m in range(first, first + count)]


def summed(rows):
    return pl.BlockSpec((rows, D), lambda i: (0, 0))


def call(kernel, steps, in_specs, out_specs, out_shape, scratch=()):
    return pl.pallas_call(
        kernel,
        grid=(steps,),
        in_specs=in_specs,
        out_specs=out_specs,
        out_shape=out_shape,
        scratch_shapes=list(scratch),
        compiler_params=pltpu.CompilerParams(vmem_limit_bytes=60 * 2**20),
    )


def per_frame(*tail):
    return pl.BlockSpec((FB,) + tail, lambda i: (i,) + (0,) * len(tail))


class Part:
    def __init__(self, lay, first, half, split):
        self.first, self.half, self.split = first, half, split
        self.common = half - split * lay.planes

    def order(self):
        return list(range(self.common, self.half)) + list(range(self.common))


class Sums:
    def __init__(self, refs, common, split):
        (self.g, self.r, self.ys, self.yr, self.xs, self.xr, self.zs, self.zr, self.fin, self.every) = refs[:10]
        (self.rs, self.rr, self.yss, self.yrs, self.xss, self.xrs, self.zss, self.zrs, self.fsem) = refs[10:]
        self.common, self.split = common, split


SUMS = 19


def sums_scratch(lay, rows, common, split):
    A, B, Y, n = lay.outer, lay.inner, lay.planes, lay.n
    slots, kept, passed, K = common + split * Y, max(split, 1), max(Y - 1, 1), common + split
    dma = pltpu.SemaphoreType.DMA
    width, depth = (rows, n) if split else (16, 1)
    crossed, along = max(B - 1, 1), max(A - 1, 1)
    return [
        pltpu.VMEM((slots, 2, n, rows, D), HALF), pltpu.VMEM((slots, n, rows, D), HALF),
        pltpu.VMEM((passed, kept, depth, width, D), HALF), pltpu.VMEM((passed, kept, depth, width, D), HALF),
        pltpu.VMEM((K, crossed, A, rows, D), HALF), pltpu.VMEM((K, crossed, A, rows, D), HALF),
        pltpu.VMEM((K, along, rows, D), HALF), pltpu.VMEM((K, along, rows, D), HALF),
        pltpu.VMEM((K, rows, D), FULL), pltpu.VMEM((Y, common, rows, D), FULL),
        dma((slots,)), dma((slots,)), dma((passed, kept)), dma((passed, kept)),
        dma((K, crossed)), dma((K, crossed)), dma((K, along)), dma((K, along)), dma((5, K, Y)),
    ]


class Reducer:
    def __init__(self, lay):
        self.lay = lay
        self.i, self.a, self.b, self.y, self.c = lay.place()
        self.here = lay.peer(self.i, self.y, 1 - self.c)
        self.pending = []
        greet(lay, self.i, self.a, self.b, self.y, self.c)

    def remote(self, src, dst, sends, at, recvs, dev, like):
        pltpu.make_async_remote_copy(
            src_ref=src, dst_ref=dst, send_sem=sends.at[at], recv_sem=recvs[0].at[recvs[1]], device_id=dev, device_id_type=MESH
        ).start()
        self.pending.append((like, sends, at, True))

    def wait_all(self):
        for make, sems, at, remote in self.pending:
            like = make()
            if remote:
                pltpu.make_async_remote_copy(
                    src_ref=like, dst_ref=like, send_sem=sems.at[at], recv_sem=sems.at[at], device_id=self.here, device_id_type=MESH
                ).wait_send()
            else:
                pltpu.make_async_copy(like, like, sems.at[at]).wait()

    def landed(self, dst, sems, *at):
        pltpu.make_async_remote_copy(
            src_ref=dst, dst_ref=dst, send_sem=sems.at[at], recv_sem=sems.at[at], device_id=self.here, device_id_type=MESH
        ).wait_recv()

    def slot(self, st, v, q):
        if v is None:
            return q
        return st.common + turn(self.y, v, self.lay.planes) * st.split + q

    def hand(self, st, h):
        self.remote(st.g.at[h, 1 - self.c], st.r.at[h], st.rs, (h,), (st.rr, (h,)), self.here, lambda: st.r.at[h])

    def base(self, st, v, q, j):
        n = self.slot(st, v, q)
        total = st.g[n, self.c, j].astype(FULL) + st.r[n, j].astype(FULL)
        if v == 0:
            for w in range(1, self.lay.planes):
                total = total + st.yr[w - 1, q, j].astype(FULL)
        return total

    def pass_on(self, st, v, q):
        n = self.slot(st, v, q)
        self.landed(st.r.at[n], st.rr, n)

        @pl.loop(0, self.lay.n)
        def _(j):
            st.ys[v - 1, q, j] = self.base(st, v, q, j).astype(HALF)

        self.remote(
            st.ys.at[v - 1, q], st.yr.at[v - 1, q], st.yss, (v - 1, q), (st.yrs, (v - 1, q)),
            self.lay.peer(self.i, turn(self.y, v, self.lay.planes), self.c), lambda: st.ys.at[v - 1, q],
        )

    def item(self, st, v, q):
        return q if v is None else st.common + q

    def cross(self, st, target, v, q):
        k, n = self.item(st, v, q), self.slot(st, v, q)
        self.landed(st.r.at[n], st.rr, n)
        if v == 0:
            for w in range(1, self.lay.planes):
                self.landed(st.yr.at[w - 1, q], st.yrs, w - 1, q)
        for u in range(1, self.lay.inner):
            other = turn(self.b, u, self.lay.inner)

            @pl.loop(0, self.lay.outer)
            def _(e):
                st.xs[k, u - 1, e] = self.base(st, v, q, e * self.lay.inner + other).astype(HALF)

            self.remote(
                st.xs.at[k, u - 1], st.xr.at[k, u - 1], st.xss, (k, u - 1), (st.xrs, (k, u - 1)),
                self.lay.peer(self.a * self.lay.inner + other, self.y, self.c), lambda u=u: st.xs.at[k, u - 1],
            )

    def along(self, st, target, v, q):
        k = self.item(st, v, q)
        inner, outer = self.lay.inner, self.lay.outer
        for u in range(1, inner):
            self.landed(st.xr.at[k, u - 1], st.xrs, k, u - 1)

        def total(e):
            value = self.base(st, v, q, e * inner + self.b)
            for u in range(1, inner):
                value = value + st.xr[k, u - 1, e].astype(FULL)
            return value

        for t in range(1, outer):
            e = turn(self.a, t, outer)
            st.zs[k, t - 1] = total(e).astype(HALF)
            self.remote(
                st.zs.at[k, t - 1], st.zr.at[k, t - 1], st.zss, (k, t - 1), (st.zrs, (k, t - 1)),
                self.lay.peer(e * inner + self.b, self.y, self.c), lambda t=t: st.zs.at[k, t - 1],
            )
        st.fin[k] = total(self.a)

    def close(self, st, target, v, q):
        k, Y = self.item(st, v, q), self.lay.planes
        for t in range(1, self.lay.outer):
            self.landed(st.zr.at[k, t - 1], st.zrs, k, t - 1)
        value = st.fin[k]
        for t in range(1, self.lay.outer):
            value = value + st.zr[k, t - 1].astype(FULL)
        if v is None:
            st.every[self.y, k] = value
            source, landing = st.every.at[self.y, k], st.every.at[self.y, k]
            like = lambda: st.every.at[0, k]
        else:
            st.fin[k] = value
            source = st.fin.at[k]
            like = lambda: st.fin.at[k]
            landing = target(self.c, self.slot(st, v, q))
        for w in range(1, Y):
            self.remote(source, landing, st.fsem, (0, k, w), (st.fsem, (1, k, w)), self.lay.peer(self.i, turn(self.y, w, Y), self.c), like)
        if v is not None:
            self.finish(st, k, landing)

    def finish(self, st, k, landing):
        pltpu.make_async_copy(st.fin.at[k], landing, st.fsem.at[2, k, 0]).start()
        self.pending.append((lambda: st.fin.at[k], st.fsem, (2, k, 0), False))
        self.remote(st.fin.at[k], landing, st.fsem, (3, k, 0), (st.fsem, (4, k, 0)), self.here, lambda: st.fin.at[k])

    def merge(self, st, target, v, q):
        k, Y = self.item(st, v, q), self.lay.planes
        if v is None:
            for w in range(1, Y):
                self.landed(st.every.at[turn(self.y, -w, Y), k], st.fsem, 1, k, w)
            value = st.every[0, k]
            for w in range(1, Y):
                value = value + st.every[w, k]
            st.fin[k] = value
            self.finish(st, k, target(self.c, q))
        else:
            for w in range(1, Y):
                back = target(self.c, self.slot(st, -w, q))
                self.landed(back, st.fsem, 1, k, w)
                self.remote(back, back, st.fsem, (3, k, w), (st.fsem, (4, k, w)), self.here, lambda: target(0, 0))

    def last(self, st, target, v, q):
        k = self.item(st, v, q)
        self.landed(target(1 - self.c, self.slot(st, v, q)), st.fsem, 4, k, 0)
        if v is not None:
            for w in range(1, self.lay.planes):
                self.landed(target(1 - self.c, self.slot(st, -w, q)), st.fsem, 4, k, w)

    def progress(self, work, step):
        for lag, stage in enumerate((self.cross, self.along, self.close, self.merge)):
            if 0 <= step - lag < len(work):
                stage(*work[step - lag])

    def done(self, work):
        for job in work:
            self.last(*job)
        self.wait_all()


def outer_products(rows, operands, jobs, st, after, a_buf, b_buf, sems):
    n = st.g.shape[2]
    lefts, rights, plan = [], [], []
    for slot, core, left, right in jobs:
        fresh = [not lefts or lefts[-1] != left, not rights or rights[-1] != right]
        if fresh[0]:
            lefts.append(left)
        if fresh[1]:
            rights.append(right)
        plan.append((slot, core, len(lefts) - 1, len(rights) - 1, fresh))

    def load(kind, loads, k):
        number, block = loads[k]
        buf = (a_buf, b_buf)[kind]
        return pltpu.make_async_copy(operands[number].at[pl.ds(block * rows, rows)], buf.at[k % 2], sems.at[kind, k % 2])

    load(0, lefts, 0).start()
    load(1, rights, 0).start()
    for slot, core, left, right, fresh in plan:
        if fresh[0]:
            load(0, lefts, left).wait()
        if fresh[1]:
            load(1, rights, right).wait()
        if fresh[0] and left + 1 < len(lefts):
            load(0, lefts, left + 1).start()
        if fresh[1] and right + 1 < len(rights):
            load(1, rights, right + 1).start()
        value = dot_rows(a_buf[left % 2], b_buf[right % 2])
        st.g[slot, core] = value.reshape(n, -1, D).astype(HALF)
        if core == 1:
            after(slot)


def product_buffers(rows):
    return [
        pltpu.VMEM((2, rows, D), HALF), pltpu.VMEM((2, rows, D), HALF), pltpu.SemaphoreType.DMA((2, 2)),
    ]


def product_jobs(part, pairs):
    return [(h, core, *pairs[2 * h + core]) for h in part.order() for core in range(2)]


def part_work(lay, part, st, target):
    return [(st, target, None, k) for k in range(part.common)] + [(st, target, 0, q) for q in range(part.split)]


def products_and_hand(red, part, st, work, operands, jobs, buffers):
    passed = [(v, q) for v in range(1, red.lay.planes) for q in range(part.split)]
    order = part.order()
    ahead = len(work) - part.common - part.split

    def after(h):
        red.hand(st, h)
        place = order.index(h) - (part.half - part.common)
        if place == 0 or part.common == 0 and h == order[-1]:
            for v, q in passed:
                red.pass_on(st, v, q)
        if place >= 1 - ahead and place + ahead - 1 < steps_beside(part, ahead):
            red.progress(work, place + ahead - 1)

    outer_products(F * SP, operands, jobs, st, after, *buffers)


def steps_beside(part, ahead):
    return max(part.common + ahead - 1, 0)


def early_kernel(lay, part, pairs, *refs):
    (e_ref, r3_ref, a2_ref, dg_ref, dq_ref, dk_ref, dv_ref, cls_ref, xs_ref, d2_ref, qt_ref, kt_ref, vt_ref, fill_ref, x0_ref, mats_ref, v_ref) = refs[:17]
    (og_ref, fq_ref, fk_ref, fv_ref, d1_ref, r1_ref, dy_ref, do_ref, tq_ref, tk_ref, tv_ref, rp_ref, sum2_ref, pos_ref, time_ref, sum3_ref) = refs[17:33]
    red = Reducer(lay)
    st = Sums(refs[33 : 33 + SUMS], part.common, part.split)
    w_buf, w_sem = refs[33 + SUMS :]
    load = pltpu.make_async_copy(mats_ref.at[pl.ds(1, 8)], w_buf, w_sem.at[0])
    load.start()

    def target(core, h):
        return og_ref.at[2 * h + core]

    work = part_work(lay, part, st, target)
    rows = F * SP
    jobs = product_jobs(part, pairs)
    pl.run_scoped(lambda *buffers: products_and_hand(red, part, st, work, (e_ref, r3_ref, a2_ref, dg_ref), jobs, buffers), *product_buffers(rows))
    begun = steps_beside(part, 0)
    load.wait()
    ws = [w_buf.at[pl.ds(k, 1)] for k in range(8)]

    steps = F // FB

    def space(dq, dk, dv, xs, d2, fq, fk, fv, d1, r1, dy, do):
        space_back_kernel(dq, dk, dv, cls_ref, xs, d2, ws[3], ws[4], ws[5], ws[6], ws[7], v_ref, fq, fk, fv, d1, r1, dy, do, sum2_ref)
        for s in range(steps):
            @pl.when(pl.program_id(0) == s)
            def _():
                red.progress(work, begun + s)

    pltpu.emit_pipeline(space, grid=(steps,), in_specs=[FRAMES] * 5, out_specs=[FRAMES] * 7)(
        dq_ref, dk_ref, dv_ref, xs_ref, d2_ref, fq_ref, fk_ref, fv_ref, d1_ref, r1_ref, dy_ref, do_ref
    )

    def time(q, k, v, d, fill, dq, dk, dv):
        time_back_kernel(q, k, v, d, fill, dq, dk, dv)

        @pl.when(pl.program_id(0) == 6)
        def _():
            red.progress(work, begun + steps)

    pltpu.emit_pipeline(time, grid=(SP // GROUP,), in_specs=[SLAB] * 4 + [FILL], out_specs=[SLAB] * 3)(
        qt_ref, kt_ref, vt_ref, do_ref, fill_ref, tq_ref, tk_ref, tv_ref
    )
    red.progress(work, begun + steps + 1)

    def embed(dq, dk, dv, x, d1, r, time):
        embed_back_kernel(dq, dk, dv, x, d1, ws[0], ws[1], ws[2], v_ref, r, pos_ref, time, sum3_ref)

    pltpu.emit_pipeline(embed, grid=(steps,), in_specs=[FRAMES] * 5, out_specs=[FRAMES, per_frame(1, D)])(
        tq_ref, tk_ref, tv_ref, x0_ref, d1_ref, rp_ref, time_ref
    )
    for s in range(begun + steps + 2, len(work) + 3):
        red.progress(work, s)
    red.done(work)


FILL = pl.BlockSpec((1, F * GROUP, F * GROUP), lambda i: (i, 0, 0))


def early(lay, part, pairs, arrays, cls, table):
    vmem = pl.BlockSpec(memory_space=pltpu.VMEM)
    e, r3, a2, dg, dq, dk, dv, xs, d2, qt, kt, vt, fill, x0, mats = arrays
    two = lambda x: x.reshape(-1, D)
    full = functools.partial(shape, dtype=FULL)
    return pl.pallas_call(
        functools.partial(early_kernel, lay, part, pairs),
        in_specs=[ANY] * 7 + [vmem] + [ANY] * 8 + [vmem],
        out_specs=[ANY] * 12 + [vmem, vmem, ANY, vmem],
        out_shape=[full(2 * part.half, lay.rows, D), ROWS16, ROWS16, ROWS16, ROWS32] + [ROWS16] * 7 + [full(16, D), full(SP, D), full(F, 1, D), full(16, D)],
        scratch_shapes=sums_scratch(lay, lay.rows, part.common, part.split) + [pltpu.VMEM((8, D, D), HALF), pltpu.SemaphoreType.DMA((1,))],
        compiler_params=pltpu.CompilerParams(collective_id=1, has_side_effects=True, vmem_limit_bytes=62 * 2**20),
    )(two(e), two(r3), two(a2), two(dg), dq, dk, dv, cls, xs, d2, qt, kt, vt, fill, x0, mats, table)


def late_kernel(lay, part, pairs, count, *refs):
    s_ref, operands = refs[0], refs[1 : 1 + count]
    og_ref, os_ref = refs[1 + count : 3 + count]
    red = Reducer(lay)
    rest = refs[3 + count :]
    st = Sums(rest[:SUMS], part.common, part.split)
    little = Sums(rest[SUMS : 2 * SUMS], 1, 0)
    small_sem = rest[2 * SUMS]
    load = pltpu.make_async_copy(s_ref, little.g.at[0], small_sem.at[0])
    load.start()

    def target(core, h):
        return og_ref.at[2 * h + core]

    work = part_work(lay, part, st, target)
    work = [(little, lambda core, h: os_ref.at[core], None, 0)] + work
    rows = F * SP
    jobs = product_jobs(part, pairs)
    load.wait()
    red.hand(little, 0)
    pl.run_scoped(lambda *buffers: products_and_hand(red, part, st, work, operands, jobs, buffers), *product_buffers(rows))
    for s in range(steps_beside(part, 1), len(work) + 3):
        red.progress(work, s)
    red.done(work)


def late(lay, part, pairs, small, arrays):
    full = functools.partial(shape, dtype=FULL)
    return pl.pallas_call(
        functools.partial(late_kernel, lay, part, pairs, len(arrays)),
        in_specs=[ANY] * (1 + len(arrays)),
        out_specs=[ANY, ANY],
        out_shape=[full(2 * part.half, lay.rows, D), full(2, small.shape[2], D)],
        scratch_shapes=sums_scratch(lay, lay.rows, part.common, part.split) + sums_scratch(lay, small.shape[2], 1, 0) + [pltpu.SemaphoreType.DMA((1,))],
        compiler_params=pltpu.CompilerParams(collective_id=4, has_side_effects=True, vmem_limit_bytes=62 * 2**20),
    )(small, *[x.reshape(-1, D) for x in arrays])


def forward(mats, table, patches, mask):
    alive = jnp.pad(mask[0] > 0, ((0, 0), (0, SP - S)))
    kept = jnp.where(alive, 0.0, MASKED).astype(FULL)
    places = jnp.arange(SP)[None]
    space_fill = jnp.where(places < S, kept, jnp.where(places == S, 0.0, NEVER))
    time_keys = kept.reshape(F, SP // GROUP, GROUP).transpose(1, 0, 2).reshape(SP // GROUP, F * GROUP)
    spot = jnp.arange(F * GROUP) % GROUP
    same = spot[:, None] == spot[None]
    time_fill = jnp.where(same[None], time_keys[:, None, :], NEVER)
    time_fill_back = jnp.where(same[None], time_keys[:, :, None], NEVER)
    table = jnp.pad(table, ((0, -table.shape[0] % 8), (0, 0)))
    pos = jnp.pad(table[31 : 31 + S], ((0, SP - S), (0, 0)))
    time = table[1 : 1 + F][:, None]
    one = jnp.where(places[0] < S, 1.0, jnp.where(places[0] == S, 1.0 / F, 0.0)).astype(FULL)
    share = jnp.broadcast_to(jnp.tile(one, FB)[:, None], (FB * SP, 1))
    tab = whole(*table.shape)
    steps = F // FB
    padded, x0, at, qt, kt, vt = call(
        embed_kernel, steps,
        [pl.BlockSpec((1, FB, S, D), lambda i: (0, i, 0, 0))] + matrices(0, 4) + [tab, whole(SP, D), per_frame(1, D)],
        [FRAMES] * 6, [ROWS16, ROWS32] + [ROWS16] * 4,
    )(patches, *[mats] * 4, table, pos, time)
    ot = call(
        time_kernel, SP // GROUP, [SLAB] * 3 + [pl.BlockSpec((1, F * GROUP, F * GROUP), lambda i: (i, 0, 0))], SLAB, ROWS16,
    )(qt, kt, vt, time_fill)
    yt, xs, as_, qs, ks, vs, os_, cls = call(
        space_kernel, steps, [FRAMES, FRAMES] + matrices(4, 5) + [tab, per_frame(1, SP)],
        [FRAMES] * 7 + [per_frame(8, D)], [ROWS16, ROWS32] + [ROWS16] * 5 + [shape(F, 8, D, dtype=FULL)],
    )(ot, x0, *[mats] * 5, table, space_fill[:, None])
    cls = jnp.mean(cls[:, 0], 0, keepdims=True)
    of, x2, a2, g, e, x3, pool = call(
        mlp_kernel, steps,
        [FRAMES, whole(1, D), FRAMES] + matrices(9, 9) + [tab, whole(FB * SP, 1)],
        [FRAMES] * 3 + [HIDDEN] * 2 + [FRAMES, summed(8)],
        [ROWS16, ROWS32, ROWS16, HIDDEN32, HIDDEN16, ROWS32, shape(8, D, dtype=FULL)],
    )(os_, cls, xs, *[mats] * 9, table, share)
    pooled = (pool[:1] / (F * S + 1)).astype(HALF)
    saved = (table, share, space_fill, time_fill_back, padded, x0, at, qt, kt, vt, ot, yt, xs, as_, qs, ks, vs, of, x2, a2, g, e, x3)
    return pooled, saved


def backward(lay, mats, saved, back_pooled):
    (table, share, space_fill, time_fill, padded, x0, at, qt, kt, vt, ot, yt, xs, as_, qs, ks, vs, of, x2, a2, g, e, x3) = saved
    tab = whole(*table.shape)
    steps = F // FB
    top = back_pooled / (F * S + 1)
    column = jnp.broadcast_to(space_fill[:, :, None], (F, SP, 128))
    r3, dg, d2, r2, dq, dk, dv, cq, ck, cv, sums1 = call(
        mlp_back_kernel, steps,
        [FRAMES, FRAMES, HIDDEN, whole(1, D)] + matrices(9, 9) + [tab, whole(FB * SP, 1), FRAMES, FRAMES, FRAMES, per_frame(SP, 128)],
        [FRAMES, HIDDEN] + [FRAMES] * 5 + [per_frame(8, D)] * 3 + [summed(16)],
        [ROWS16, HIDDEN16, ROWS32] + [ROWS16] * 4 + [shape(F, 8, D, dtype=FULL)] * 3 + [shape(16, D, dtype=FULL)],
        [pltpu.VMEM((FB, SP, D), HALF)],
    )(x3, x2, g, top, *[mats] * 9, table, share, qs, ks, vs, column)
    cls = jnp.concatenate([jnp.sum(part[:, 0], 0, keepdims=True) for part in (cq, ck, cv)], 0)
    cls = cls.astype(HALF).astype(FULL) / F
    first = Part(lay, 10, 4, 1 if lay.planes <= 4 else 0)
    pairs = [((2, 0), (3, k)) for k in range(4)] + [((0, k), (1, 0)) for k in range(4)]
    upper, fq, fk, fv, d1, r1, dy, do, tq, tk, tv, rp, sums2, pos, time, sums3 = early(
        lay, first, pairs, (e, r3, a2, dg, dq, dk, dv, xs, d2, qt, kt, vt, time_fill, x0, mats), cls, table
    )
    class_grad = sums2[4:5]
    grad_vecs = jnp.concatenate(
        [
            class_grad, time[:, 0], sums3[4:5], sums3[0:2], sums2[6:7], sums2[5:6], sums2[0:2], sums1[9:10], sums1[3:7], sums1[2:3],
            sums3[2:4], sums2[2:4], sums1[7:9], sums1[0:2], class_grad, pos[:S],
        ],
        0,
    )
    second = Part(lay, 0, 5, 1 if lay.planes <= 4 else 0)
    operands = (padded, rp, at, tq, tk, tv, ot, dy, yt, r1, as_, fq, fk, fv, of, r2)
    pairs = [(0, 1), (2, 3), (2, 4), (2, 5), (6, 7), (8, 9), (10, 11), (10, 12), (10, 13), (14, 15)]
    pairs = [((left, 0), (right, 0)) for left, right in pairs]

    def finish(small):
        lower, rest = late(lay, second, pairs, small, operands)
        return jnp.concatenate([lower, upper], 0), rest

    return finish, grad_vecs


def project(inputs, weight):
    return jnp.einsum("...a,ab->...b", inputs, weight, preferred_element_type=jnp.float32)


def project_back(inputs, weight, cotangent):
    rounded = cotangent.astype(jnp.bfloat16)
    back_in = jnp.einsum("...b,ab->...a", rounded, weight, preferred_element_type=jnp.float32)
    flat_in = inputs.reshape(-1, inputs.shape[-1])
    flat_back = rounded.reshape(-1, rounded.shape[-1])
    grad_weight = jnp.einsum("na,nb->ab", flat_in, flat_back, preferred_element_type=jnp.float32)
    return (back_in, grad_weight, jnp.sum(flat_back, 0, dtype=jnp.float32))


def normalize(projected):
    return projected * lax.rsqrt(jnp.sum(projected * projected, -1, keepdims=True) + 1e-06)


def adamw_step(weight, first, second, average, gradient, factor, rate):
    clipped = gradient * factor
    first = BETA_ONE * first + (1.0 - BETA_ONE) * clipped
    second = BETA_TWO * second + (1.0 - BETA_TWO) * clipped * clipped
    first_hat = first / (1.0 - BETA_ONE**STEP)
    second_hat = second / (1.0 - BETA_TWO**STEP)
    weight = weight - rate * (first_hat / (jnp.sqrt(second_hat) + ADAM_EPSILON) + DECAY * weight)
    average = AVERAGE_KEEP * average + (1.0 - AVERAGE_KEEP) * weight
    return (weight, first, second, average)


def pack(head, vecs):
    rows = head.shape[0] // 3
    first = jnp.concatenate([head[:rows], head[rows : 2 * rows], head[2 * rows :]], 1)
    tall = jnp.pad(vecs, ((0, D // 3 - vecs.shape[0]), (0, 0)))
    second = tall.reshape(D // head.shape[0], rows, head.shape[0]).transpose(1, 0, 2).reshape(rows, D)
    fill = -rows % 16
    return jnp.pad(jnp.stack([first, second]), ((0, 0), (0, fill), (0, 0)))


def unpack(blocks, rows):
    n = blocks.shape[0]
    kept = blocks[:, :, : rows // 3]
    head = kept[:, 0].reshape(n, rows // 3, 3, D // 3).transpose(0, 2, 1, 3).reshape(D, D // 3)
    vecs = kept[:, 1].reshape(n, rows // 3, n, rows).transpose(2, 1, 0, 3).reshape(D // 3, D)
    return head, vecs[:NVEC]


def pack_all(head, vecs, n):
    rows = D // n
    first = head.reshape(n, 3, rows // 3, D // 3).transpose(0, 2, 1, 3).reshape(n, rows // 3, D)
    tall = jnp.pad(vecs, ((0, D // 3 - vecs.shape[0]), (0, 0)))
    second = tall.reshape(n, rows // 3, n, rows).transpose(2, 1, 0, 3).reshape(n, rows // 3, D)
    fill = -(rows // 3) % 16
    return jnp.pad(jnp.stack([first, second]), ((0, 0), (0, 0), (0, fill), (0, 0)))


def unpack_shard(blocks, n):
    rows = D // n
    first, second = blocks[0, : rows // 3], blocks[1, : rows // 3]
    head = jnp.concatenate([first[:, : D // 3], first[:, D // 3 : 2 * D // 3], first[:, 2 * D // 3 :]], 0)
    vecs = second.reshape(rows // 3, n, rows).transpose(1, 0, 2).reshape(D // 3, rows)
    return head, vecs[:NVEC]


def local(
    lay,
    patches,
    patch_keep_mask,
    partner,
    matrices,
    matrix_first,
    matrix_second,
    matrix_average,
    head_weight,
    head_first,
    head_second,
    head_average,
    vectors,
    array_running_mean,
    vector_second,
    vector_average,
):
    n = lay.n
    gathered_mats, gathered_small = gather(
        lay,
        matrices.astype(jnp.bfloat16),
        pack(head_weight.astype(jnp.bfloat16), vectors.astype(jnp.bfloat16)),
    )
    mats16 = gathered_mats.reshape(NMAT, D, D)
    head16, vecs16 = unpack(gathered_small, lay.rows)
    pooled, saved = forward(mats16, vecs16.astype(jnp.float32), patches, patch_keep_mask)
    projected = project(pooled, head16)
    unit_length_lines, unit_back = jax.vjp(normalize, projected)
    clip_count, width = unit_length_lines.shape
    lines = unit_length_lines.reshape(-1, 128)
    tile = jnp.pad(lines, ((0, -lines.shape[0] % 8), (0, 0)))
    everyone = spread(lay.dp, n, tile, 2)
    gathered = everyone[:, : lines.shape[0]].reshape(-1, width)

    def contrast(gathered_rows):
        pairwise_affinity_scores_raw = (
            jnp.dot(gathered_rows, gathered_rows.T, precision=lax.Precision.HIGHEST)
            / SCORE_SHARPNESS
        )
        clip_total = pairwise_affinity_scores_raw.shape[0]
        column = jnp.arange(clip_total)[None, :]
        pairwise_affinity_scores_raw = jnp.where(
            jnp.arange(clip_total)[:, None] == column, -1000000000.0, pairwise_affinity_scores_raw
        )
        positive = jnp.sum(
            jnp.where(column == partner[:, None], pairwise_affinity_scores_raw, 0.0), -1
        )
        return jnp.mean(jax.nn.logsumexp(pairwise_affinity_scores_raw, -1) - positive)

    contrastive_loss, objective_cotangent_flow = jax.vjp(contrast, gathered)
    (back_gathered,) = objective_cotangent_flow(jnp.ones_like(contrastive_loss))
    clip_count = projected.shape[0]
    offset = lax.axis_index(("dp", "fsdp")) * clip_count
    back_unit = lax.dynamic_slice_in_dim(back_gathered, offset, clip_count, 0)
    (back_projected,) = unit_back(back_unit)
    back_pooled, grad_head, unused_bias = project_back(pooled, head16, back_projected)
    finish, grad_vecs = backward(lay, mats16, saved, back_pooled)
    small = pack_all(grad_head, grad_vecs, n).astype(jnp.bfloat16)
    grad_mats, grad_small = finish(small)
    grad_head, grad_vecs = unpack_shard(grad_small, n)
    partial_squares = (
        jnp.sum(grad_mats * grad_mats)
        + jnp.sum(grad_head * grad_head)
        + jnp.sum(grad_vecs * grad_vecs)
    )
    squares = spread(lay.dp, n, jnp.broadcast_to(partial_squares, (8, 128)), 3)
    squared_norm = jnp.sum(squares[:, 0, 0]) / lay.dp
    factor = CLIP_AT / jnp.maximum(jnp.sqrt(squared_norm), CLIP_AT)
    mats_out = adamw_step(
        matrices, matrix_first, matrix_second, matrix_average, grad_mats, factor, RATE
    )
    head_out = adamw_step(
        head_weight, head_first, head_second, head_average, grad_head, factor, RATE
    )
    vecs_out = adamw_step(
        vectors, array_running_mean, vector_second, vector_average, grad_vecs, factor, VECTOR_RATE
    )
    return (
        contrastive_loss,
        squared_norm,
        mats_out[0],
        mats_out[1],
        mats_out[2],
        mats_out[3],
        head_out[0],
        head_out[1],
        head_out[2],
        head_out[3],
        vecs_out[0],
        vecs_out[1],
        vecs_out[2],
        vecs_out[3],
    )


def solution(mesh):
    lay = Layout(mesh.shape["dp"], mesh.shape["fsdp"], 2)
    placed = (
        P(("dp", "fsdp"), None, None, None),
        P(("dp", "fsdp"), None, None),
        P(),
        P(None, "fsdp", None),
        P(None, "fsdp", None),
        P(None, "fsdp", None),
        P(None, "fsdp", None),
        P("fsdp", None),
        P("fsdp", None),
        P("fsdp", None),
        P("fsdp", None),
        P(None, "fsdp"),
        P(None, "fsdp"),
        P(None, "fsdp"),
        P(None, "fsdp"),
    )
    return jax.shard_map(
        functools.partial(local, lay),
        mesh=mesh,
        in_specs=placed,
        out_specs=(
            P(),
            P(),
            P(None, "fsdp", None),
            P(None, "fsdp", None),
            P(None, "fsdp", None),
            P(None, "fsdp", None),
            P("fsdp", None),
            P("fsdp", None),
            P("fsdp", None),
            P("fsdp", None),
            P(None, "fsdp"),
            P(None, "fsdp"),
            P(None, "fsdp"),
            P(None, "fsdp"),
        ),
        check_vma=False,
    )
```

```python
import functools
import jax
import jax.numpy as jnp
from jax import lax
from jax.experimental import pallas as pl
from jax.experimental.pallas import tpu as pltpu
from jax.sharding import PartitionSpec as P

D = 768
H = 12
HD = 64
F = 8
S = 196
SP = 208
NMAT = 18
NVEC = 227
STEP = 10

SCORE_SHARPNESS = 0.07
CLIP_AT = 0.05
RATE = 0.01
VECTOR_RATE = 0.1
BETA_ONE = 0.9
BETA_TWO = 0.95
ADAM_EPSILON = 1e-08
DECAY = 0.05
AVERAGE_KEEP = 0.9

MESH = pl.DeviceIdType.MESH
ANY = pl.BlockSpec(memory_space=pl.ANY)


class Layout:
    def __init__(self, dp, fsdp, split):
        self.dp, self.n = dp, fsdp
        self.outer = 4 if fsdp % 4 == 0 else 1
        self.inner = fsdp // self.outer
        self.planes = dp // 2
        self.half = NMAT // 2
        self.split = split
        self.common = self.half - split * self.planes
        self.handled = self.common + split
        self.rows = D // fsdp

    def place(self):
        i = lax.axis_index("fsdp")
        d = lax.axis_index("dp")
        return i, lax.div(i, self.inner), lax.rem(i, self.inner), lax.div(d, 2), lax.rem(d, 2)

    def peer(self, i, y, c):
        return {"fsdp": i, "dp": y * 2 + c}

    def matrix(self, c, y, k):
        if k < self.common:
            return c * self.half + k
        return c * self.half + self.common + y * self.split + (k - self.common)


def turn(x, t, size):
    return lax.rem(x + t + size, size)


def greet(lay, i, a, b, y, c):
    barrier = pltpu.get_barrier_semaphore()
    others = [lay.peer(turn(a, t, lay.outer) * lay.inner + b, y, c) for t in range(1, lay.outer)]
    others += [lay.peer(a * lay.inner + turn(b, u, lay.inner), y, c) for u in range(1, lay.inner)]
    others += [lay.peer(i, turn(y, v, lay.planes), c) for v in range(1, lay.planes)]
    others += [lay.peer(i, y, 1 - c)]
    for other in others:
        pl.semaphore_signal(barrier, inc=1, device_id=other, device_id_type=MESH)
    pl.semaphore_wait(barrier, len(others))


def spread_kernel(dp, n, x_ref, o_ref, ssem, rsem):
    i, d = lax.axis_index("fsdp"), lax.axis_index("dp")
    me = d * n + i
    total = dp * n
    barrier = pltpu.get_barrier_semaphore()

    def other(t):
        j = lax.rem(me + t, total)
        return {"fsdp": lax.rem(j, n), "dp": lax.div(j, n)}

    @pl.loop(1, total)
    def _(t):
        pl.semaphore_signal(barrier, inc=1, device_id=other(t), device_id_type=MESH)

    pl.semaphore_wait(barrier, total - 1)

    @pl.loop(1, total)
    def _(t):
        pltpu.make_async_remote_copy(
            src_ref=x_ref, dst_ref=o_ref.at[me], send_sem=ssem.at[t], recv_sem=rsem.at[t], device_id=other(t), device_id_type=MESH
        ).start()

    o_ref[me] = x_ref[...]

    @pl.loop(1, total)
    def _(t):
        pltpu.make_async_remote_copy(
            src_ref=x_ref, dst_ref=o_ref.at[lax.rem(me - t + total, total)], send_sem=ssem.at[t], recv_sem=rsem.at[t], device_id=other(t), device_id_type=MESH
        ).wait()


def spread(dp, n, tile, number):
    vmem = pl.BlockSpec(memory_space=pltpu.VMEM)
    return pl.pallas_call(
        functools.partial(spread_kernel, dp, n),
        out_shape=jax.ShapeDtypeStruct((dp * n,) + tile.shape, tile.dtype),
        in_specs=[vmem],
        out_specs=vmem,
        scratch_shapes=[pltpu.SemaphoreType.DMA((dp * n,)), pltpu.SemaphoreType.DMA((dp * n,))],
        compiler_params=pltpu.CompilerParams(collective_id=number, has_side_effects=True),
    )(tile)


FB = 2
GROUP = 16
HALF = jnp.bfloat16
FULL = jnp.float32
NORM_EPS = 1e-06
MASKED = -1000000000.0
NEVER = -3e38


def dot(a, b):
    return lax.dot_general(a, b, (((1,), (0,)), ((), ())), preferred_element_type=FULL)


def dot_back(a, b):
    return lax.dot_general(a, b, (((1,), (1,)), ((), ())), preferred_element_type=FULL)


def dot_rows(a, b):
    return lax.dot_general(a, b, (((0,), (0,)), ((), ())), preferred_element_type=FULL)


def mean(x):
    return jnp.sum(x, -1, keepdims=True) * (1.0 / D)


def norm(x, gain, shift):
    centred = x - mean(x)
    scale = lax.rsqrt(mean(centred * centred) + NORM_EPS)
    return centred * scale * gain + shift


def norm_back(x, gain, back):
    centred = x - mean(x)
    scale = lax.rsqrt(mean(centred * centred) + NORM_EPS)
    unit = centred * scale
    inner = back * gain
    return scale * (inner - mean(inner) - unit * mean(inner * unit)), back * unit


def normal_cdf(x):
    size = jnp.abs(x) * 0.7071067811865476
    t = pl.reciprocal(1.0 + 0.3275911 * size)
    bell = jnp.exp(-0.5 * x * x)
    poly = ((((1.061405429 * t - 1.453152027) * t + 1.421413741) * t - 0.284496736) * t + 0.254829592) * t
    tail = 0.5 * poly * bell
    return jnp.where(x < 0, tail, 1.0 - tail), bell


def gelu(x):
    return x * normal_cdf(x)[0]


def gelu_slope(x):
    below, bell = normal_cdf(x)
    return below + x * bell * 0.3989422804014327


def column_sum(x):
    return jnp.sum(x.astype(FULL), 0, keepdims=True)


def flat(ref):
    x = ref[...]
    return x.reshape(-1, x.shape[-1])


def row_of(rows):
    return lax.rem(lax.broadcasted_iota(jnp.int32, (rows, 1), 0), SP)


def first_step():
    return pl.program_id(0) == 0


def add_rows(ref, values):
    @pl.when(first_step())
    def _():
        ref[...] = jnp.zeros_like(ref)

    for k, value in enumerate(values):
        if value is not None:
            ref[k : k + 1, :] += value


def pair_lanes(x, low):
    zero = jnp.zeros_like(x)
    return jnp.concatenate([jnp.where(low, x, zero), jnp.where(low, zero, x)], 0)


def attend(q, k, v, fill):
    rows = q.shape[0]
    low = lax.broadcasted_iota(jnp.int32, (rows, 128), 1) < HD
    stacked = pair_lanes(q * jnp.asarray(HD ** (-0.5), HALF), low)
    scores = dot_back(stacked, k)
    if fill.shape[0] != 1:
        fill = jnp.concatenate([fill, fill], 0)
    scores = jnp.where(fill == 0.0, scores, fill)
    expanded = jnp.exp(scores - jnp.max(scores, -1, keepdims=True))
    share = pl.reciprocal(jnp.sum(expanded, -1, keepdims=True))
    mixed = dot((expanded * share).astype(HALF), v)
    return jnp.where(low, mixed[:rows], mixed[rows:])


def attend_back(q, k, v, back, fill):
    rows = q.shape[0]
    low = lax.broadcasted_iota(jnp.int32, (rows, 128), 1) < HD
    stacked = pair_lanes(q * jnp.asarray(HD ** (-0.5), HALF), low)
    backs = pair_lanes(back, low)
    scores = dot_back(k, stacked)
    scores = jnp.where(fill == 0.0, scores, fill)
    expanded = jnp.exp(scores - jnp.max(scores, 0, keepdims=True))
    chances = expanded * pl.reciprocal(jnp.sum(expanded, 0, keepdims=True))
    back_chances = dot_back(v, backs)
    inner = jnp.sum(back_chances * chances, 0, keepdims=True)
    back_scores = (chances * (back_chances - inner)).astype(HALF)
    back_keys = dot(back_scores, stacked)
    back_values = dot(chances.astype(HALF), backs)
    queries = dot_rows(back_scores, k) * HD ** (-0.5)
    return jnp.where(low, queries[:rows], queries[rows:]), back_keys, back_values


def embed_kernel(p_ref, w0, w1, w2, w3, v_ref, pos_ref, time_ref, pad_ref, x_ref, a_ref, q_ref, k_ref, b_ref):
    pad_ref[:, SP - GROUP :, :] = jnp.zeros((FB, GROUP, D), HALF)
    for f in range(FB):
        pad_ref[f, :S, :] = p_ref[0, f]
    pos = pos_ref[...]
    here = jnp.concatenate([pos + time_ref[f] for f in range(FB)], 0)
    x = dot(flat(pad_ref), w0[0]) + v_ref[9:10] + here
    x_ref[...] = x.reshape(FB, SP, D)
    a = norm(x, v_ref[22:23], v_ref[23:24]).astype(HALF)
    a_ref[...] = a.reshape(FB, SP, D)
    q_ref[...] = (dot(a, w1[0]) + v_ref[10:11]).astype(HALF).reshape(FB, SP, D)
    k_ref[...] = dot(a, w2[0]).astype(HALF).reshape(FB, SP, D)
    b_ref[...] = (dot(a, w3[0]) + v_ref[11:12]).astype(HALF).reshape(FB, SP, D)


def time_kernel(q_ref, k_ref, v_ref, fill_ref, o_ref):
    rows = F * GROUP
    for p in range(H // 2):
        lanes = slice(128 * p, 128 * p + 128)
        q, k, v = (ref[:, :, lanes].reshape(rows, 128) for ref in (q_ref, k_ref, v_ref))
        o_ref[:, :, lanes] = attend(q, k, v, fill_ref[0]).astype(HALF).reshape(F, GROUP, 128)


def space_kernel(o_ref, x_ref, w0, w1, w2, w3, w4, v_ref, fill_ref, y_ref, xs_ref, a_ref, q_ref, k_ref, b_ref, os_ref, cls_ref):
    rows = FB * SP
    y = (dot(flat(o_ref), w0[0]) + v_ref[12:13]).astype(HALF)
    y_ref[...] = y.reshape(FB, SP, D)
    x = flat(x_ref) + dot(y, w1[0]) + v_ref[13:14]
    x = jnp.where(row_of(rows) == S, v_ref[0:1] + v_ref[30:31], x)
    xs_ref[...] = x.reshape(FB, SP, D)
    a = norm(x, v_ref[24:25], v_ref[25:26]).astype(HALF)
    a_ref[...] = a.reshape(FB, SP, D)
    q_ref[...] = (dot(a, w2[0]) + v_ref[14:15]).astype(HALF).reshape(FB, SP, D)
    k_ref[...] = dot(a, w3[0]).astype(HALF).reshape(FB, SP, D)
    b_ref[...] = (dot(a, w4[0]) + v_ref[15:16]).astype(HALF).reshape(FB, SP, D)
    for f in range(FB):
        for p in range(H // 2):
            lanes = slice(128 * p, 128 * p + 128)
            mixed = attend(q_ref[f, :, lanes], k_ref[f, :, lanes], b_ref[f, :, lanes], fill_ref[f])
            os_ref[f, :, lanes] = mixed.astype(HALF)
            cls_ref[f, :, lanes] = mixed[S : S + 8]


def mlp_kernel(o_ref, cls_ref, xs_ref, wp_ref, u0, u1, u2, u3, e0, e1, e2, e3, v_ref, share_ref, of_ref, x2_ref, a_ref, g_ref, e_ref, x3_ref, pool_ref):
    rows = FB * SP
    o = jnp.where(row_of(rows) == S, cls_ref[...], flat(o_ref).astype(FULL)).astype(HALF)
    of_ref[...] = o.reshape(FB, SP, D)
    x2 = flat(xs_ref) + dot(o, wp_ref[0]) + v_ref[16:17]
    x2_ref[...] = x2.reshape(FB, SP, D)
    a = norm(x2, v_ref[26:27], v_ref[27:28]).astype(HALF)
    a_ref[...] = a.reshape(FB, SP, D)
    x3 = x2 + v_ref[21:22]
    for k in range(4):
        g = dot(a, (u0, u1, u2, u3)[k][0]) + v_ref[17 + k : 18 + k]
        g_ref[k] = g.reshape(FB, SP, D)
        e = gelu(g).astype(HALF)
        e_ref[k] = e.reshape(FB, SP, D)
        x3 = x3 + dot(e, (e0, e1, e2, e3)[k][0])
    x3_ref[...] = x3.reshape(FB, SP, D)
    final = norm(x3, v_ref[28:29], v_ref[29:30]) * share_ref[...]
    add_rows(pool_ref, [column_sum(final)])


def mlp_back_kernel(x3_ref, x2_ref, g_ref, d_ref, wp_ref, u0, u1, u2, u3, e0, e1, e2, e3, v_ref, share_ref, q_ref, k_ref, b_ref, fill_ref,
                    r3_ref, dg_ref, d2_ref, r2_ref, dq_ref, dk_ref, dv_ref, cq_ref, ck_ref, cv_ref, sum_ref, do_ref):
    top = d_ref[0:1] * share_ref[...]
    d3, unit = norm_back(flat(x3_ref), v_ref[28:29], top)
    sums = [column_sum(unit), column_sum(top)]
    r3 = d3.astype(HALF)
    r3_ref[...] = r3.reshape(FB, SP, D)
    sums.append(column_sum(r3))
    back = None
    for k in range(4):
        dg = (dot_back(r3, (e0, e1, e2, e3)[k][0]) * gelu_slope(flat(g_ref.at[k]))).astype(HALF)
        dg_ref[k] = dg.reshape(FB, SP, D)
        sums.append(column_sum(dg))
        part = dot_back(dg, (u0, u1, u2, u3)[k][0])
        back = part if back is None else back + part
    d2, unit = norm_back(flat(x2_ref), v_ref[26:27], back)
    sums += [column_sum(unit), column_sum(back)]
    d2 = d2 + d3
    d2_ref[...] = d2.reshape(FB, SP, D)
    r2 = d2.astype(HALF)
    r2_ref[...] = r2.reshape(FB, SP, D)
    sums.append(column_sum(r2))
    add_rows(sum_ref, sums)
    do_ref[...] = dot_back(r2, wp_ref[0]).astype(HALF).reshape(FB, SP, D)
    for f in range(FB):
        for p in range(H // 2):
            lanes = slice(128 * p, 128 * p + 128)
            outs = attend_back(q_ref[f, :, lanes], k_ref[f, :, lanes], b_ref[f, :, lanes], do_ref[f, :, lanes], fill_ref[f][:, 0:1])
            for value, ref, cls in zip(outs, (dq_ref, dk_ref, dv_ref), (cq_ref, ck_ref, cv_ref)):
                ref[f, :, lanes] = value.astype(HALF)
                cls[f, :, lanes] = value[S : S + 8]


def space_back_kernel(dq_ref, dk_ref, dv_ref, cls_ref, xs_ref, d2_ref, w0, w1, w2, w3, w4, v_ref, fq_ref, fk_ref, fv_ref, d1_ref, r1_ref, dy_ref, do_ref, sum_ref):
    rows = FB * SP
    is_class = row_of(rows) == S
    grads = []
    for k, (ref, out) in enumerate(zip((dq_ref, dk_ref, dv_ref), (fq_ref, fk_ref, fv_ref))):
        grad = jnp.where(is_class, cls_ref[k : k + 1], flat(ref).astype(FULL)).astype(HALF)
        out[...] = grad.reshape(FB, SP, D)
        grads.append(grad)
    back = dot_back(grads[0], w2[0]) + dot_back(grads[1], w3[0]) + dot_back(grads[2], w4[0])
    d, unit = norm_back(flat(xs_ref), v_ref[24:25], back)
    sums = [column_sum(grads[0]), column_sum(grads[2]), column_sum(unit), column_sum(back)]
    d = d + flat(d2_ref)
    kept = jnp.where(is_class, d, 0.0)
    sums.append(column_sum(kept))
    d = d - kept
    d1_ref[...] = d.reshape(FB, SP, D)
    r1 = d.astype(HALF)
    r1_ref[...] = r1.reshape(FB, SP, D)
    sums.append(column_sum(r1))
    dy = dot_back(r1, w1[0]).astype(HALF)
    dy_ref[...] = dy.reshape(FB, SP, D)
    sums.append(column_sum(dy))
    do_ref[...] = dot_back(dy, w0[0]).astype(HALF).reshape(FB, SP, D)
    add_rows(sum_ref, sums)


def time_back_kernel(q_ref, k_ref, v_ref, d_ref, fill_ref, dq_ref, dk_ref, dv_ref):
    rows = F * GROUP
    fill = jnp.concatenate([fill_ref[0], fill_ref[0]], 1)
    for p in range(H // 2):
        lanes = slice(128 * p, 128 * p + 128)
        q, k, v, d = (ref[:, :, lanes].reshape(rows, 128) for ref in (q_ref, k_ref, v_ref, d_ref))
        for value, ref in zip(attend_back(q, k, v, d, fill), (dq_ref, dk_ref, dv_ref)):
            ref[:, :, lanes] = value.astype(HALF).reshape(F, GROUP, 128)


def embed_back_kernel(dq_ref, dk_ref, dv_ref, x_ref, d1_ref, w1, w2, w3, v_ref, r_ref, pos_ref, time_ref, sum_ref):
    q, v = flat(dq_ref), flat(dv_ref)
    back = dot_back(q, w1[0]) + dot_back(flat(dk_ref), w2[0]) + dot_back(v, w3[0])
    d, unit = norm_back(flat(x_ref), v_ref[22:23], back)
    d = d + flat(d1_ref)
    rounded = d.astype(HALF)
    r_ref[...] = rounded.reshape(FB, SP, D)
    add_rows(sum_ref, [column_sum(q), column_sum(v), column_sum(unit), column_sum(back), column_sum(rounded)])

    @pl.when(first_step())
    def _():
        pos_ref[...] = jnp.zeros_like(pos_ref)

    total = jnp.zeros((SP, D), FULL)
    for f in range(FB):
        part = d[f * SP : (f + 1) * SP]
        time_ref[f] = column_sum(part)
        total = total + part
    pos_ref[...] += total


def shape(*dims, dtype=HALF):
    return jax.ShapeDtypeStruct(dims, dtype)


FRAMES = pl.BlockSpec((FB, SP, D), lambda i: (i, 0, 0))
HIDDEN = pl.BlockSpec((4, FB, SP, D), lambda i: (0, i, 0, 0))
SLAB = pl.BlockSpec((F, GROUP, D), lambda i: (0, i, 0))
ROWS16 = shape(F, SP, D)
ROWS32 = shape(F, SP, D, dtype=FULL)
HIDDEN16 = shape(4, F, SP, D)
HIDDEN32 = shape(4, F, SP, D, dtype=FULL)


def whole(*dims):
    return pl.BlockSpec(dims, lambda i: (0,) * len(dims), pipeline_mode=pl.Buffered(1))


def matrix(m):
    return pl.BlockSpec((1, D, D), lambda i: (m, 0, 0), pipeline_mode=pl.Buffered(1))


def matrices(first, count):
    return [matrix(m) for m in range(first, first + count)]


def summed(rows):
    return pl.BlockSpec((rows, D), lambda i: (0, 0))


def call(kernel, steps, in_specs, out_specs, out_shape, scratch=()):
    return pl.pallas_call(
        kernel,
        grid=(steps,),
        in_specs=in_specs,
        out_specs=out_specs,
        out_shape=out_shape,
        scratch_shapes=list(scratch),
        compiler_params=pltpu.CompilerParams(vmem_limit_bytes=60 * 2**20),
    )


def per_frame(*tail):
    return pl.BlockSpec((FB,) + tail, lambda i: (i,) + (0,) * len(tail))


class Part:
    def __init__(self, lay, first, half, split):
        self.first, self.half, self.split = first, half, split
        self.common = half - split * lay.planes

    def order(self):
        return list(range(self.common, self.half)) + list(range(self.common))


class Sums:
    def __init__(self, refs, common, split):
        (self.g, self.r, self.ys, self.yr, self.xs, self.xr, self.zs, self.zr, self.fin, self.every) = refs[:10]
        (self.rs, self.rr, self.yss, self.yrs, self.xss, self.xrs, self.zss, self.zrs, self.fsem) = refs[10:]
        self.common, self.split = common, split


SUMS = 19


def sums_scratch(lay, rows, common, split):
    A, B, Y, n = lay.outer, lay.inner, lay.planes, lay.n
    slots, kept, passed, K = common + split * Y, max(split, 1), max(Y - 1, 1), common + split
    dma = pltpu.SemaphoreType.DMA
    width, depth = (rows, n) if split else (16, 1)
    crossed, along = max(B - 1, 1), max(A - 1, 1)
    return [
        pltpu.VMEM((slots, 2, n, rows, D), HALF), pltpu.VMEM((slots, n, rows, D), HALF),
        pltpu.VMEM((passed, kept, depth, width, D), HALF), pltpu.VMEM((passed, kept, depth, width, D), HALF),
        pltpu.VMEM((K, crossed, A, rows, D), HALF), pltpu.VMEM((K, crossed, A, rows, D), HALF),
        pltpu.VMEM((K, along, rows, D), HALF), pltpu.VMEM((K, along, rows, D), HALF),
        pltpu.VMEM((K, rows, D), FULL), pltpu.VMEM((Y, common, rows, D), FULL),
        dma((slots,)), dma((slots,)), dma((passed, kept)), dma((passed, kept)),
        dma((K, crossed, A)), dma((K, crossed, A)), dma((K, along)), dma((K, along)), dma((5, K, Y)),
    ]


class Reducer:
    def __init__(self, lay):
        self.lay = lay
        self.i, self.a, self.b, self.y, self.c = lay.place()
        self.here = lay.peer(self.i, self.y, 1 - self.c)
        self.pending = []
        greet(lay, self.i, self.a, self.b, self.y, self.c)

    def remote(self, src, dst, sends, at, recvs, dev, like):
        pltpu.make_async_remote_copy(
            src_ref=src, dst_ref=dst, send_sem=sends.at[at], recv_sem=recvs[0].at[recvs[1]], device_id=dev, device_id_type=MESH
        ).start()
        self.pending.append((like, sends, at, True))

    def wait_all(self):
        for make, sems, at, remote in self.pending:
            like = make()
            if remote:
                pltpu.make_async_remote_copy(
                    src_ref=like, dst_ref=like, send_sem=sems.at[at], recv_sem=sems.at[at], device_id=self.here, device_id_type=MESH
                ).wait_send()
            else:
                pltpu.make_async_copy(like, like, sems.at[at]).wait()

    def landed(self, dst, sems, *at):
        pltpu.make_async_remote_copy(
            src_ref=dst, dst_ref=dst, send_sem=sems.at[at], recv_sem=sems.at[at], device_id=self.here, device_id_type=MESH
        ).wait_recv()

    def slot(self, st, v, q):
        if v is None:
            return q
        return st.common + turn(self.y, v, self.lay.planes) * st.split + q

    def hand(self, st, h):
        self.remote(st.g.at[h, 1 - self.c], st.r.at[h], st.rs, (h,), (st.rr, (h,)), self.here, lambda: st.r.at[h])

    def base(self, st, v, q, j):
        n = self.slot(st, v, q)
        total = st.g[n, self.c, j].astype(FULL) + st.r[n, j].astype(FULL)
        if v == 0:
            for w in range(1, self.lay.planes):
                total = total + st.yr[w - 1, q, j].astype(FULL)
        return total

    def pass_on(self, st, v, q):
        n = self.slot(st, v, q)
        self.landed(st.r.at[n], st.rr, n)

        @pl.loop(0, self.lay.n)
        def _(j):
            st.ys[v - 1, q, j] = self.base(st, v, q, j).astype(HALF)

        self.remote(
            st.ys.at[v - 1, q], st.yr.at[v - 1, q], st.yss, (v - 1, q), (st.yrs, (v - 1, q)),
            self.lay.peer(self.i, turn(self.y, v, self.lay.planes), self.c), lambda: st.ys.at[v - 1, q],
        )

    def item(self, st, v, q):
        return q if v is None else st.common + q

    def cross(self, st, target, v, q):
        k, n = self.item(st, v, q), self.slot(st, v, q)
        self.landed(st.r.at[n], st.rr, n)
        if v == 0:
            for w in range(1, self.lay.planes):
                self.landed(st.yr.at[w - 1, q], st.yrs, w - 1, q)
        outer, inner = self.lay.outer, self.lay.inner
        for t in list(range(1, outer)) + [0]:
            e = turn(self.a, t, outer)
            for u in range(1, inner):
                other = turn(self.b, u, inner)
                st.xs[k, u - 1, e] = self.base(st, v, q, e * inner + other).astype(HALF)
                self.remote(
                    st.xs.at[k, u - 1, e], st.xr.at[k, u - 1, e], st.xss, (k, u - 1, t), (st.xrs, (k, u - 1, t)),
                    self.lay.peer(self.a * inner + other, self.y, self.c), lambda u=u: st.xs.at[k, u - 1, 0],
                )

    def along(self, st, target, v, q):
        k = self.item(st, v, q)
        inner, outer = self.lay.inner, self.lay.outer
        for t in list(range(1, outer)) + [0]:
            e = turn(self.a, t, outer)
            value = self.base(st, v, q, e * inner + self.b)
            for u in range(1, inner):
                self.landed(st.xr.at[k, u - 1, e], st.xrs, k, u - 1, t)
                value = value + st.xr[k, u - 1, e].astype(FULL)
            if t == 0:
                st.fin[k] = value
                continue
            st.zs[k, t - 1] = value.astype(HALF)
            self.remote(
                st.zs.at[k, t - 1], st.zr.at[k, t - 1], st.zss, (k, t - 1), (st.zrs, (k, t - 1)),
                self.lay.peer(e * inner + self.b, self.y, self.c), lambda t=t: st.zs.at[k, t - 1],
            )

    def close(self, st, target, v, q):
        k, Y = self.item(st, v, q), self.lay.planes
        for t in range(1, self.lay.outer):
            self.landed(st.zr.at[k, t - 1], st.zrs, k, t - 1)
        value = st.fin[k]
        for t in range(1, self.lay.outer):
            value = value + st.zr[k, t - 1].astype(FULL)
        if v is None:
            st.every[self.y, k] = value
            source, landing = st.every.at[self.y, k], st.every.at[self.y, k]
            like = lambda: st.every.at[0, k]
        else:
            st.fin[k] = value
            source = st.fin.at[k]
            like = lambda: st.fin.at[k]
            landing = target(self.c, self.slot(st, v, q))
        for w in range(1, Y):
            self.remote(source, landing, st.fsem, (0, k, w), (st.fsem, (1, k, w)), self.lay.peer(self.i, turn(self.y, w, Y), self.c), like)
        if v is not None:
            self.finish(st, k, landing)

    def finish(self, st, k, landing):
        pltpu.make_async_copy(st.fin.at[k], landing, st.fsem.at[2, k, 0]).start()
        self.pending.append((lambda: st.fin.at[k], st.fsem, (2, k, 0), False))
        self.remote(st.fin.at[k], landing, st.fsem, (3, k, 0), (st.fsem, (4, k, 0)), self.here, lambda: st.fin.at[k])

    def merge(self, st, target, v, q):
        k, Y = self.item(st, v, q), self.lay.planes
        if v is None:
            for w in range(1, Y):
                self.landed(st.every.at[turn(self.y, -w, Y), k], st.fsem, 1, k, w)
            value = st.every[0, k]
            for w in range(1, Y):
                value = value + st.every[w, k]
            st.fin[k] = value
            self.finish(st, k, target(self.c, q))
        else:
            for w in range(1, Y):
                back = target(self.c, self.slot(st, -w, q))
                self.landed(back, st.fsem, 1, k, w)
                self.remote(back, back, st.fsem, (3, k, w), (st.fsem, (4, k, w)), self.here, lambda: target(0, 0))

    def last(self, st, target, v, q):
        k = self.item(st, v, q)
        self.landed(target(1 - self.c, self.slot(st, v, q)), st.fsem, 4, k, 0)
        if v is not None:
            for w in range(1, self.lay.planes):
                self.landed(target(1 - self.c, self.slot(st, -w, q)), st.fsem, 4, k, w)

    def progress(self, work, step):
        for lag, stage in enumerate((self.cross, self.along, self.close, self.merge)):
            if 0 <= step - lag < len(work):
                stage(*work[step - lag])

    def done(self, work):
        for job in work:
            self.last(*job)
        self.wait_all()


def outer_products(rows, operands, jobs, st, after, a_buf, b_buf, sems):
    n = st.g.shape[2]
    lefts, rights, plan = [], [], []
    for slot, core, left, right in jobs:
        fresh = [not lefts or lefts[-1] != left, not rights or rights[-1] != right]
        if fresh[0]:
            lefts.append(left)
        if fresh[1]:
            rights.append(right)
        plan.append((slot, core, len(lefts) - 1, len(rights) - 1, fresh))

    def load(kind, loads, k):
        number, block = loads[k]
        buf = (a_buf, b_buf)[kind]
        return pltpu.make_async_copy(operands[number].at[pl.ds(block * rows, rows)], buf.at[k % 2], sems.at[kind, k % 2])

    load(0, lefts, 0).start()
    load(1, rights, 0).start()
    for slot, core, left, right, fresh in plan:
        if fresh[0]:
            load(0, lefts, left).wait()
        if fresh[1]:
            load(1, rights, right).wait()
        if fresh[0] and left + 1 < len(lefts):
            load(0, lefts, left + 1).start()
        if fresh[1] and right + 1 < len(rights):
            load(1, rights, right + 1).start()
        value = dot_rows(a_buf[left % 2], b_buf[right % 2])
        st.g[slot, core] = value.reshape(n, -1, D).astype(HALF)
        if core == 1:
            after(slot)


def product_buffers(rows):
    return [
        pltpu.VMEM((2, rows, D), HALF), pltpu.VMEM((2, rows, D), HALF), pltpu.SemaphoreType.DMA((2, 2)),
    ]


def product_jobs(part, pairs):
    return [(h, core, *pairs[2 * h + core]) for h in part.order() for core in range(2)]


def part_work(lay, part, st, target):
    return [(st, target, None, k) for k in range(part.common)] + [(st, target, 0, q) for q in range(part.split)]


def products_and_hand(red, part, st, work, operands, jobs, buffers):
    passed = [(v, q) for v in range(1, red.lay.planes) for q in range(part.split)]
    order = part.order()
    ahead = len(work) - part.common - part.split

    def after(h):
        red.hand(st, h)
        place = order.index(h) - (part.half - part.common)
        if place == 0 or part.common == 0 and h == order[-1]:
            for v, q in passed:
                red.pass_on(st, v, q)
        if place >= 1 - ahead and place + ahead - 1 < steps_beside(part, ahead):
            red.progress(work, place + ahead - 1)

    outer_products(F * SP, operands, jobs, st, after, *buffers)


def steps_beside(part, ahead):
    return max(part.common + ahead - 1, 0)


def early_kernel(lay, part, pairs, *refs):
    (e_ref, r3_ref, a2_ref, dg_ref, dq_ref, dk_ref, dv_ref, cls_ref, xs_ref, d2_ref, qt_ref, kt_ref, vt_ref, fill_ref, x0_ref, mats_ref, v_ref) = refs[:17]
    (og_ref, fq_ref, fk_ref, fv_ref, d1_ref, r1_ref, dy_ref, do_ref, tq_ref, tk_ref, tv_ref, rp_ref, sum2_ref, pos_ref, time_ref, sum3_ref) = refs[17:33]
    red = Reducer(lay)
    st = Sums(refs[33 : 33 + SUMS], part.common, part.split)
    w_buf, w_sem = refs[33 + SUMS :]
    load = pltpu.make_async_copy(mats_ref.at[pl.ds(1, 8)], w_buf, w_sem.at[0])
    load.start()

    def target(core, h):
        return og_ref.at[2 * h + core]

    work = part_work(lay, part, st, target)
    rows = F * SP
    jobs = product_jobs(part, pairs)
    pl.run_scoped(lambda *buffers: products_and_hand(red, part, st, work, (e_ref, r3_ref, a2_ref, dg_ref), jobs, buffers), *product_buffers(rows))
    begun = steps_beside(part, 0)
    load.wait()
    ws = [w_buf.at[pl.ds(k, 1)] for k in range(8)]

    steps = F // FB

    def space(dq, dk, dv, xs, d2, fq, fk, fv, d1, r1, dy, do):
        space_back_kernel(dq, dk, dv, cls_ref, xs, d2, ws[3], ws[4], ws[5], ws[6], ws[7], v_ref, fq, fk, fv, d1, r1, dy, do, sum2_ref)
        for s, place in enumerate((1, 3)):
            @pl.when(pl.program_id(0) == place)
            def _():
                red.progress(work, begun + s)

    pltpu.emit_pipeline(space, grid=(steps,), in_specs=[FRAMES] * 5, out_specs=[FRAMES] * 7)(
        dq_ref, dk_ref, dv_ref, xs_ref, d2_ref, fq_ref, fk_ref, fv_ref, d1_ref, r1_ref, dy_ref, do_ref
    )

    def time(q, k, v, d, fill, dq, dk, dv):
        time_back_kernel(q, k, v, d, fill, dq, dk, dv)

        for s, place in enumerate((6, 12)):
            @pl.when(pl.program_id(0) == place)
            def _():
                red.progress(work, begun + 2 + s)

    pltpu.emit_pipeline(time, grid=(SP // GROUP,), in_specs=[SLAB] * 4 + [FILL], out_specs=[SLAB] * 3)(
        qt_ref, kt_ref, vt_ref, do_ref, fill_ref, tq_ref, tk_ref, tv_ref
    )

    def embed(dq, dk, dv, x, d1, r, time):
        embed_back_kernel(dq, dk, dv, x, d1, ws[0], ws[1], ws[2], v_ref, r, pos_ref, time, sum3_ref)

        @pl.when(pl.program_id(0) == 3)
        def _():
            red.progress(work, begun + 4)

    pltpu.emit_pipeline(embed, grid=(steps,), in_specs=[FRAMES] * 5, out_specs=[FRAMES, per_frame(1, D)])(
        tq_ref, tk_ref, tv_ref, x0_ref, d1_ref, rp_ref, time_ref
    )
    for s in range(begun + 5, len(work) + 3):
        red.progress(work, s)
    red.done(work)


FILL = pl.BlockSpec((1, F * GROUP, F * GROUP), lambda i: (i, 0, 0))


def early(lay, part, pairs, arrays, cls, table):
    vmem = pl.BlockSpec(memory_space=pltpu.VMEM)
    e, r3, a2, dg, dq, dk, dv, xs, d2, qt, kt, vt, fill, x0, mats = arrays
    two = lambda x: x.reshape(-1, D)
    full = functools.partial(shape, dtype=FULL)
    return pl.pallas_call(
        functools.partial(early_kernel, lay, part, pairs),
        in_specs=[ANY] * 7 + [vmem] + [ANY] * 8 + [vmem],
        out_specs=[ANY] * 12 + [vmem, vmem, ANY, vmem],
        out_shape=[full(2 * part.half, lay.rows, D), ROWS16, ROWS16, ROWS16, ROWS32] + [ROWS16] * 7 + [full(16, D), full(SP, D), full(F, 1, D), full(16, D)],
        scratch_shapes=sums_scratch(lay, lay.rows, part.common, part.split) + [pltpu.VMEM((8, D, D), HALF), pltpu.SemaphoreType.DMA((1,))],
        compiler_params=pltpu.CompilerParams(collective_id=1, has_side_effects=True, vmem_limit_bytes=62 * 2**20),
    )(two(e), two(r3), two(a2), two(dg), dq, dk, dv, cls, xs, d2, qt, kt, vt, fill, x0, mats, table)


def late_kernel(lay, part, pairs, count, *refs):
    s_ref, operands = refs[0], refs[1 : 1 + count]
    og_ref, os_ref = refs[1 + count : 3 + count]
    red = Reducer(lay)
    rest = refs[3 + count :]
    st = Sums(rest[:SUMS], part.common, part.split)
    little = Sums(rest[SUMS : 2 * SUMS], 1, 0)
    small_sem = rest[2 * SUMS]
    load = pltpu.make_async_copy(s_ref, little.g.at[0], small_sem.at[0])
    load.start()

    def target(core, h):
        return og_ref.at[2 * h + core]

    work = part_work(lay, part, st, target)
    work = [(little, lambda core, h: os_ref.at[core], None, 0)] + work
    rows = F * SP
    jobs = product_jobs(part, pairs)
    load.wait()
    red.hand(little, 0)
    pl.run_scoped(lambda *buffers: products_and_hand(red, part, st, work, operands, jobs, buffers), *product_buffers(rows))
    for s in range(steps_beside(part, 1), len(work) + 3):
        red.progress(work, s)
    red.done(work)


def late(lay, part, pairs, small, arrays):
    full = functools.partial(shape, dtype=FULL)
    return pl.pallas_call(
        functools.partial(late_kernel, lay, part, pairs, len(arrays)),
        in_specs=[ANY] * (1 + len(arrays)),
        out_specs=[ANY, ANY],
        out_shape=[full(2 * part.half, lay.rows, D), full(2, small.shape[2], D)],
        scratch_shapes=sums_scratch(lay, lay.rows, part.common, part.split) + sums_scratch(lay, small.shape[2], 1, 0) + [pltpu.SemaphoreType.DMA((1,))],
        compiler_params=pltpu.CompilerParams(collective_id=4, has_side_effects=True, vmem_limit_bytes=62 * 2**20),
    )(small, *[x.reshape(-1, D) for x in arrays])


def front_kernel(lay, w_ref, s_ref, p_ref, tfill_ref, sfill_ref, *refs):
    (ow_ref, os_ref, pad_ref, x0_ref, at_ref, qt_ref, kt_ref, vt_ref, ot_ref, yt_ref, xs_ref, as_ref, qs_ref, ks_ref, vs_ref, mix_ref, cls_ref, v_ref) = refs[:18]
    (w_buf, piece, pos_buf, time_buf, own, zs, zr, xs, xr, ys, yr, cs, cr, wsem) = refs[18:]
    i, a, b, y, c = lay.place()
    A, B, Y, K = lay.outer, lay.inner, lay.planes, lay.handled
    greet(lay, i, a, b, y, c)
    here = lay.peer(i, y, 1 - c)
    pending = []

    def remote(src, dst, sends, at, recvs, dev, like):
        pltpu.make_async_remote_copy(
            src_ref=src, dst_ref=dst, send_sem=sends.at[at], recv_sem=recvs.at[at], device_id=dev, device_id_type=MESH
        ).start()
        pending.append((like, sends, at))

    def landed(dst, sems, *at):
        pltpu.make_async_remote_copy(
            src_ref=dst, dst_ref=dst, send_sem=sems.at[at], recv_sem=sems.at[at], device_id=here, device_id_type=MESH
        ).wait_recv()

    def matrix_of(core, k, v=0):
        h = k if k < lay.common else lay.common + turn(y, v, Y) * lay.split + (k - lay.common)
        return 2 * h + core

    def source(k):
        return s_ref.at[c] if k < 0 else w_ref.at[matrix_of(c, k)]

    def at(k, j):
        return os_ref.at[c, j] if k < 0 else ow_ref.at[matrix_of(c, k), j]

    def like(k):
        return (lambda: s_ref.at[0]) if k < 0 else (lambda: w_ref.at[0])

    order = [-1] + list(range(K))

    def local(k):
        if k < 0:
            return pltpu.make_async_copy(s_ref.at[c], os_ref.at[c, i], own.at[0])
        m = 2 * k + c
        return pltpu.make_async_copy(w_ref.at[m], ow_ref.at[m, i], own.at[k + 1])

    for k in order:
        for t in range(1, A):
            remote(source(k), at(k, i), zs, (k + 1, t), zr, lay.peer(turn(a, t, A) * B + b, y, c), like(k))
    for k in range(-1, lay.half):
        local(k).start()

    def over(k, j, t, u):
        if k >= lay.common:
            for v in range(1, Y):
                remote(at(k, j), at(k, j), ys, (k - lay.common, v, t, u), yr, lay.peer(i, turn(y, v, Y), c), like(k))

    def cross(k):
        for u in range(1, B):
            remote(source(k), at(k, i), xs, (k + 1, u, 0), xr, lay.peer(a * B + turn(b, u, B), y, c), like(k))
        for t in range(1, A):
            j = turn(a, -t, A) * B + b
            landed(at(k, j), zr, k + 1, t)
            for u in range(1, B):
                remote(at(k, j), at(k, j), xs, (k + 1, u, t), xr, lay.peer(a * B + turn(b, u, B), y, c), like(k))
            over(k, j, t, 0)

    def share(k):
        for t in range(A):
            for u in range(1, B):
                j = turn(a, -t, A) * B + turn(b, -u, B)
                landed(at(k, j), xr, k + 1, u, t)
                over(k, j, t, u)
        if k < 0:
            local(k).wait()
            remote(os_ref.at[c], os_ref.at[c], cs, (0,), cr, here, lambda: os_ref.at[0])
        else:
            if k < lay.common:
                local(k).wait()
            else:
                own_wait(k, 0)
            m = matrix_of(c, k)
            remote(ow_ref.at[m], ow_ref.at[m], cs, (k + 1,), cr, here, lambda: ow_ref.at[0])

    def own_wait(k, v):
        m = matrix_of(c, k, v)
        pltpu.make_async_copy(w_ref.at[m], ow_ref.at[m, i], own.at[lax.div(m, 2) + 1]).wait()

    def slot(q, v):
        return K + 1 + (v - 1) * lay.split + q

    def from_planes():
        for v in range(1, Y):
            for q in range(lay.split):
                k = lay.common + q
                m = matrix_of(c, k, -v)
                for t in range(A):
                    for u in range(B):
                        if t or u:
                            j = turn(a, -t, A) * B + turn(b, -u, B)
                            landed(ow_ref.at[m, j], yr, q, v, t, u)
                own_wait(k, -v)
                remote(ow_ref.at[m], ow_ref.at[m], cs, (slot(q, v),), cr, here, lambda: ow_ref.at[0])

    def paired(k, v=0):
        if k < 0:
            landed(os_ref.at[1 - c], cr, 0)
        else:
            landed(ow_ref.at[matrix_of(1 - c, k, v)], cr, k + 1 if v == 0 else slot(k - lay.common, -v))

    def fetch(first, count):
        span = pl.ds(first, count)
        return pltpu.make_async_copy(ow_ref.at[span], w_buf.at[span], wsem.at[first])

    begun = 0
    for step in range(4):
        cross(order[step])
        if step:
            share(order[step - 1])
        begun = step + 1
    paired(-1)
    paired(0)
    paired(1)
    fetch(0, 4).start()
    table = pltpu.make_async_copy(os_ref.at[0], piece, wsem.at[lay.half])
    table.start()
    v_ref[...] = jnp.zeros_like(v_ref)
    table.wait()
    for j in range(lay.n):
        lane = min(lay.rows * j // 128 * 128, D - 256)
        v_ref[: piece.shape[1], lane : lane + 256] += piece[j].astype(FULL)
    pos_buf[...] = v_ref[31 : 31 + SP, :]
    for f in range(F):
        time_buf[f] = v_ref[1 + f : 2 + f, :]
    fetch(0, 4).wait()
    ws = [Weight(w_buf.at[k]) for k in range(9)]
    steps = F // FB

    def advance(step):
        if step < len(order):
            cross(order[step])
        if step - 1 < len(order):
            share(order[step - 1])

    def embed(p, *outs):
        now = pl.program_id(0)
        embed_kernel(p, *ws[:4], v_ref, pos_buf, time_buf.at[pl.ds(now * FB, FB)], *outs)
        for s, place in enumerate((1, 3)):
            @pl.when(now == place)
            def _():
                advance(begun + s)

    pltpu.emit_pipeline(embed, grid=(steps,), in_specs=[pl.BlockSpec((1, FB, S, D), lambda i: (0, i, 0, 0))], out_specs=[FRAMES] * 6)(
        p_ref, pad_ref, x0_ref, at_ref, qt_ref, kt_ref, vt_ref
    )

    def time(q, k, v, fill, o):
        time_kernel(q, k, v, fill, o)
        for s, place in enumerate((5, 11)):
            @pl.when(pl.program_id(0) == place)
            def _():
                advance(begun + 2 + s)

    pltpu.emit_pipeline(time, grid=(SP // GROUP,), in_specs=[SLAB] * 3 + [FILL], out_specs=[SLAB])(
        qt_ref, kt_ref, vt_ref, tfill_ref, ot_ref
    )
    for k in range(2, 5):
        paired(k)
    fetch(4, 5).start()
    fetch(4, 5).wait()

    def space(o, x, fill, *outs):
        space_kernel(o, x, *ws[4:9], v_ref, fill, *outs)

        @pl.when(pl.program_id(0) == 0)
        def _():
            advance(begun + 4)

    pltpu.emit_pipeline(space, grid=(steps,), in_specs=[FRAMES, FRAMES, per_frame(1, SP)], out_specs=[FRAMES] * 7 + [per_frame(8, D)])(
        ot_ref, x0_ref, sfill_ref, yt_ref, xs_ref, as_ref, qs_ref, ks_ref, vs_ref, mix_ref, cls_ref
    )
    for step in range(begun + 5, len(order) + 1):
        advance(step)
    from_planes()
    for k in range(5, K):
        paired(k)
    for v in range(1, Y):
        for q in range(lay.split):
            paired(lay.common + q, -v)
    for make, sems, at_ in pending:
        ref = make()
        pltpu.make_async_remote_copy(
            src_ref=ref, dst_ref=ref, send_sem=sems.at[at_], recv_sem=sems.at[at_], device_id=here, device_id_type=MESH
        ).wait_send()


class Weight:
    def __init__(self, ref):
        self.ref = ref

    def __getitem__(self, unused):
        value = self.ref[...]
        if value.shape[1] % 16:
            return value.astype(FULL).reshape(D, D).astype(HALF)
        return value.reshape(D, D)


def front(lay, shard, small, patches, time_fill, space_fill):
    A, B, K, Y = lay.outer, lay.inner, lay.handled, lay.planes
    dma = pltpu.SemaphoreType.DMA
    kept = max(lay.split, 1)
    vmem = pl.BlockSpec(memory_space=pltpu.VMEM)
    full = functools.partial(shape, dtype=FULL)
    slots = K + 1 + max(Y - 1, 0) * lay.split
    return pl.pallas_call(
        functools.partial(front_kernel, lay),
        in_specs=[ANY] * 5,
        out_specs=[ANY] * 17 + [vmem],
        out_shape=[
            shape(NMAT, lay.n, lay.rows, D), shape(2, lay.n, *small.shape[1:]),
            ROWS16, ROWS32, ROWS16, ROWS16, ROWS16, ROWS16, ROWS16, ROWS16, ROWS32, ROWS16, ROWS16, ROWS16, ROWS16, ROWS16,
            full(F, 8, D), full(256, D),
        ],
        scratch_shapes=[
            pltpu.VMEM((9, lay.n, lay.rows, D), HALF), pltpu.VMEM((lay.n,) + small.shape[1:], HALF), pltpu.VMEM((SP, D), FULL), pltpu.VMEM((F, 1, D), FULL),
            dma((lay.half + 1,)), dma((K + 1, A)), dma((K + 1, A)), dma((K + 1, B, A)), dma((K + 1, B, A)),
            dma((kept, Y, A, B)), dma((kept, Y, A, B)), dma((slots,)), dma((slots,)), dma((lay.half + 1,)),
        ],
        compiler_params=pltpu.CompilerParams(collective_id=0, has_side_effects=True, vmem_limit_bytes=60 * 2**20),
    )(shard, small, patches, time_fill, space_fill)


def forward(lay, shard, small, patches, mask):
    alive = jnp.pad(mask[0] > 0, ((0, 0), (0, SP - S)))
    kept = jnp.where(alive, 0.0, MASKED).astype(FULL)
    places = jnp.arange(SP)[None]
    space_fill = jnp.where(places < S, kept, jnp.where(places == S, 0.0, NEVER))
    time_keys = kept.reshape(F, SP // GROUP, GROUP).transpose(1, 0, 2).reshape(SP // GROUP, F * GROUP)
    spot = jnp.arange(F * GROUP) % GROUP
    same = spot[:, None] == spot[None]
    time_fill = jnp.where(same[None], time_keys[:, None, :], NEVER)
    time_fill_back = jnp.where(same[None], time_keys[:, :, None], NEVER)
    one = jnp.where(places[0] < S, 1.0, jnp.where(places[0] == S, 1.0 / F, 0.0)).astype(FULL)
    share = jnp.broadcast_to(jnp.tile(one, FB)[:, None], (FB * SP, 1))
    mats, rest, padded, x0, at, qt, kt, vt, ot, yt, xs, as_, qs, ks, vs, os_, cls, table = front(
        lay, shard, small, patches, time_fill, space_fill[:, None]
    )
    mats = mats.reshape(NMAT, D, D)
    tab = whole(*table.shape)
    steps = F // FB
    cls = jnp.mean(cls[:, 0], 0, keepdims=True)
    of, x2, a2, g, e, x3, pool = call(
        mlp_kernel, steps,
        [FRAMES, whole(1, D), FRAMES] + matrices(9, 9) + [tab, whole(FB * SP, 1)],
        [FRAMES] * 3 + [HIDDEN] * 2 + [FRAMES, summed(8)],
        [ROWS16, ROWS32, ROWS16, HIDDEN32, HIDDEN16, ROWS32, shape(8, D, dtype=FULL)],
    )(os_, cls, xs, *[mats] * 9, table, share)
    pooled = (pool[:1] / (F * S + 1)).astype(HALF)
    head = rest[1][:, : lay.rows].reshape(D, -1)
    saved = (table, share, space_fill, time_fill_back, padded, x0, at, qt, kt, vt, ot, yt, xs, as_, qs, ks, vs, of, x2, a2, g, e, x3)
    return pooled, mats, head, saved


def backward(lay, mats, saved, back_pooled):
    (table, share, space_fill, time_fill, padded, x0, at, qt, kt, vt, ot, yt, xs, as_, qs, ks, vs, of, x2, a2, g, e, x3) = saved
    tab = whole(*table.shape)
    steps = F // FB
    top = back_pooled / (F * S + 1)
    column = jnp.broadcast_to(space_fill[:, :, None], (F, SP, 128))
    r3, dg, d2, r2, dq, dk, dv, cq, ck, cv, sums1 = call(
        mlp_back_kernel, steps,
        [FRAMES, FRAMES, HIDDEN, whole(1, D)] + matrices(9, 9) + [tab, whole(FB * SP, 1), FRAMES, FRAMES, FRAMES, per_frame(SP, 128)],
        [FRAMES, HIDDEN] + [FRAMES] * 5 + [per_frame(8, D)] * 3 + [summed(16)],
        [ROWS16, HIDDEN16, ROWS32] + [ROWS16] * 4 + [shape(F, 8, D, dtype=FULL)] * 3 + [shape(16, D, dtype=FULL)],
        [pltpu.VMEM((FB, SP, D), HALF)],
    )(x3, x2, g, top, *[mats] * 9, table, share, qs, ks, vs, column)
    cls = jnp.concatenate([jnp.sum(part[:, 0], 0, keepdims=True) for part in (cq, ck, cv)], 0)
    cls = cls.astype(HALF).astype(FULL) / F
    first = Part(lay, 10, 4, 1 if lay.planes <= 4 else 0)
    pairs = [((2, 0), (3, k)) for k in range(4)] + [((0, k), (1, 0)) for k in range(4)]
    upper, fq, fk, fv, d1, r1, dy, do, tq, tk, tv, rp, sums2, pos, time, sums3 = early(
        lay, first, pairs, (e, r3, a2, dg, dq, dk, dv, xs, d2, qt, kt, vt, time_fill, x0, mats), cls, table
    )
    class_grad = sums2[4:5]
    grad_vecs = jnp.concatenate(
        [
            class_grad, time[:, 0], sums3[4:5], sums3[0:2], sums2[6:7], sums2[5:6], sums2[0:2], sums1[9:10], sums1[3:7], sums1[2:3],
            sums3[2:4], sums2[2:4], sums1[7:9], sums1[0:2], class_grad, pos[:S],
        ],
        0,
    )
    second = Part(lay, 0, 5, 1 if lay.planes <= 4 else 0)
    operands = (padded, rp, at, tq, tk, tv, ot, dy, yt, r1, as_, fq, fk, fv, of, r2)
    pairs = [(0, 1), (2, 3), (2, 4), (2, 5), (6, 7), (8, 9), (10, 11), (10, 12), (10, 13), (14, 15)]
    pairs = [((left, 0), (right, 0)) for left, right in pairs]

    def finish(small):
        lower, rest = late(lay, second, pairs, small, operands)
        return jnp.concatenate([lower, upper], 0), rest

    return finish, grad_vecs


def project(inputs, weight):
    return jnp.einsum("...a,ab->...b", inputs, weight, preferred_element_type=jnp.float32)


def project_back(inputs, weight, cotangent):
    rounded = cotangent.astype(jnp.bfloat16)
    back_in = jnp.einsum("...b,ab->...a", rounded, weight, preferred_element_type=jnp.float32)
    flat_in = inputs.reshape(-1, inputs.shape[-1])
    flat_back = rounded.reshape(-1, rounded.shape[-1])
    grad_weight = jnp.einsum("na,nb->ab", flat_in, flat_back, preferred_element_type=jnp.float32)
    return (back_in, grad_weight, jnp.sum(flat_back, 0, dtype=jnp.float32))


def normalize(projected):
    return projected * lax.rsqrt(jnp.sum(projected * projected, -1, keepdims=True) + 1e-06)


def adamw_step(weight, first, second, average, gradient, factor, rate):
    clipped = gradient * factor
    first = BETA_ONE * first + (1.0 - BETA_ONE) * clipped
    second = BETA_TWO * second + (1.0 - BETA_TWO) * clipped * clipped
    first_hat = first / (1.0 - BETA_ONE**STEP)
    second_hat = second / (1.0 - BETA_TWO**STEP)
    weight = weight - rate * (first_hat / (jnp.sqrt(second_hat) + ADAM_EPSILON) + DECAY * weight)
    average = AVERAGE_KEEP * average + (1.0 - AVERAGE_KEEP) * weight
    return (weight, first, second, average)


def pack(lay, head, vecs):
    first = lay.rows * lax.axis_index("fsdp")
    lane = first - jnp.minimum(first // 128 * 128, D - 256)
    tall = -(-NVEC // 16) * 16
    moved = lax.dynamic_update_slice(jnp.zeros((tall, 256), HALF), vecs, (0, lane))
    return jnp.stack([moved, jnp.pad(head, ((0, tall - head.shape[0]), (0, 0)))])


def pack_all(head, vecs, n):
    rows = D // n
    first = head.reshape(n, 3, rows // 3, D // 3).transpose(0, 2, 1, 3).reshape(n, rows // 3, D)
    tall = jnp.pad(vecs, ((0, D // 3 - vecs.shape[0]), (0, 0)))
    second = tall.reshape(n, rows // 3, n, rows).transpose(2, 1, 0, 3).reshape(n, rows // 3, D)
    fill = -(rows // 3) % 16
    return jnp.pad(jnp.stack([first, second]), ((0, 0), (0, 0), (0, fill), (0, 0)))


def unpack_shard(blocks, n):
    rows = D // n
    first, second = blocks[0, : rows // 3], blocks[1, : rows // 3]
    head = jnp.concatenate([first[:, : D // 3], first[:, D // 3 : 2 * D // 3], first[:, 2 * D // 3 :]], 0)
    vecs = second.reshape(rows // 3, n, rows).transpose(1, 0, 2).reshape(D // 3, rows)
    return head, vecs[:NVEC]


def local(
    lay,
    patches,
    patch_keep_mask,
    partner,
    matrices,
    matrix_first,
    matrix_second,
    matrix_average,
    head_weight,
    head_first,
    head_second,
    head_average,
    vectors,
    array_running_mean,
    vector_second,
    vector_average,
):
    n = lay.n
    pooled, mats16, head16, saved = forward(
        lay,
        matrices.astype(jnp.bfloat16),
        pack(lay, head_weight.astype(jnp.bfloat16), vectors.astype(jnp.bfloat16)),
        patches,
        patch_keep_mask,
    )
    projected = project(pooled, head16)
    unit_length_lines, unit_back = jax.vjp(normalize, projected)
    clip_count, width = unit_length_lines.shape
    lines = unit_length_lines.reshape(-1, 128)
    tile = jnp.pad(lines, ((0, -lines.shape[0] % 8), (0, 0)))
    everyone = spread(lay.dp, n, tile, 2)
    gathered = everyone[:, : lines.shape[0]].reshape(-1, width)

    def contrast(gathered_rows):
        pairwise_affinity_scores_raw = (
            jnp.dot(gathered_rows, gathered_rows.T, precision=lax.Precision.HIGHEST)
            / SCORE_SHARPNESS
        )
        clip_total = pairwise_affinity_scores_raw.shape[0]
        column = jnp.arange(clip_total)[None, :]
        pairwise_affinity_scores_raw = jnp.where(
            jnp.arange(clip_total)[:, None] == column, -1000000000.0, pairwise_affinity_scores_raw
        )
        positive = jnp.sum(
            jnp.where(column == partner[:, None], pairwise_affinity_scores_raw, 0.0), -1
        )
        return jnp.mean(jax.nn.logsumexp(pairwise_affinity_scores_raw, -1) - positive)

    contrastive_loss, objective_cotangent_flow = jax.vjp(contrast, gathered)
    (back_gathered,) = objective_cotangent_flow(jnp.ones_like(contrastive_loss))
    clip_count = projected.shape[0]
    offset = lax.axis_index(("dp", "fsdp")) * clip_count
    back_unit = lax.dynamic_slice_in_dim(back_gathered, offset, clip_count, 0)
    (back_projected,) = unit_back(back_unit)
    back_pooled, grad_head, unused_bias = project_back(pooled, head16, back_projected)
    finish, grad_vecs = backward(lay, mats16, saved, back_pooled)
    small = pack_all(grad_head, grad_vecs, n).astype(jnp.bfloat16)
    grad_mats, grad_small = finish(small)
    grad_head, grad_vecs = unpack_shard(grad_small, n)
    partial_squares = (
        jnp.sum(grad_mats * grad_mats)
        + jnp.sum(grad_head * grad_head)
        + jnp.sum(grad_vecs * grad_vecs)
    )
    squares = spread(lay.dp, n, jnp.broadcast_to(partial_squares, (8, 128)), 3)
    squared_norm = jnp.sum(squares[:, 0, 0]) / lay.dp
    factor = CLIP_AT / jnp.maximum(jnp.sqrt(squared_norm), CLIP_AT)
    mats_out = adamw_step(
        matrices, matrix_first, matrix_second, matrix_average, grad_mats, factor, RATE
    )
    head_out = adamw_step(
        head_weight, head_first, head_second, head_average, grad_head, factor, RATE
    )
    vecs_out = adamw_step(
        vectors, array_running_mean, vector_second, vector_average, grad_vecs, factor, VECTOR_RATE
    )
    return (
        contrastive_loss,
        squared_norm,
        mats_out[0],
        mats_out[1],
        mats_out[2],
        mats_out[3],
        head_out[0],
        head_out[1],
        head_out[2],
        head_out[3],
        vecs_out[0],
        vecs_out[1],
        vecs_out[2],
        vecs_out[3],
    )


def solution(mesh):
    planes = mesh.shape["dp"] // 2
    lay = Layout(mesh.shape["dp"], mesh.shape["fsdp"], 2 if planes == 2 else 0)
    placed = (
        P(("dp", "fsdp"), None, None, None),
        P(("dp", "fsdp"), None, None),
        P(),
        P(None, "fsdp", None),
        P(None, "fsdp", None),
        P(None, "fsdp", None),
        P(None, "fsdp", None),
        P("fsdp", None),
        P("fsdp", None),
        P("fsdp", None),
        P("fsdp", None),
        P(None, "fsdp"),
        P(None, "fsdp"),
        P(None, "fsdp"),
        P(None, "fsdp"),
    )
    return jax.shard_map(
        functools.partial(local, lay),
        mesh=mesh,
        in_specs=placed,
        out_specs=(
            P(),
            P(),
            P(None, "fsdp", None),
            P(None, "fsdp", None),
            P(None, "fsdp", None),
            P(None, "fsdp", None),
            P("fsdp", None),
            P("fsdp", None),
            P("fsdp", None),
            P("fsdp", None),
            P(None, "fsdp"),
            P(None, "fsdp"),
            P(None, "fsdp"),
            P(None, "fsdp"),
        ),
        check_vma=False,
    )
```

```python
import functools
import jax
import jax.numpy as jnp
from jax import lax
from jax.experimental import pallas as pl
from jax.experimental.pallas import tpu as pltpu
from jax.sharding import PartitionSpec as P

D = 768
H = 12
HD = 64
F = 8
S = 196
SP = 208
NMAT = 18
NVEC = 227
STEP = 10

SCORE_SHARPNESS = 0.07
CLIP_AT = 0.05
RATE = 0.01
VECTOR_RATE = 0.1
BETA_ONE = 0.9
BETA_TWO = 0.95
ADAM_EPSILON = 1e-08
DECAY = 0.05
AVERAGE_KEEP = 0.9

MESH = pl.DeviceIdType.MESH
ANY = pl.BlockSpec(memory_space=pl.ANY)


class Layout:
    def __init__(self, dp, fsdp, split):
        self.dp, self.n = dp, fsdp
        self.outer = 4 if fsdp % 4 == 0 else 1
        self.inner = fsdp // self.outer
        self.planes = dp // 2
        self.half = NMAT // 2
        self.split = split
        self.common = self.half - split * self.planes
        self.handled = self.common + split
        self.rows = D // fsdp

    def place(self):
        i = lax.axis_index("fsdp")
        d = lax.axis_index("dp")
        return i, lax.div(i, self.inner), lax.rem(i, self.inner), lax.div(d, 2), lax.rem(d, 2)

    def peer(self, i, y, c):
        return {"fsdp": i, "dp": y * 2 + c}

    def matrix(self, c, y, k):
        if k < self.common:
            return c * self.half + k
        return c * self.half + self.common + y * self.split + (k - self.common)


def turn(x, t, size):
    return lax.rem(x + t + size, size)


def greet(lay, i, a, b, y, c):
    barrier = pltpu.get_barrier_semaphore()
    others = [lay.peer(turn(a, t, lay.outer) * lay.inner + b, y, c) for t in range(1, lay.outer)]
    others += [lay.peer(a * lay.inner + turn(b, u, lay.inner), y, c) for u in range(1, lay.inner)]
    others += [lay.peer(i, turn(y, v, lay.planes), c) for v in range(1, lay.planes)]
    others += [lay.peer(i, y, 1 - c)]
    for other in others:
        pl.semaphore_signal(barrier, inc=1, device_id=other, device_id_type=MESH)
    pl.semaphore_wait(barrier, len(others))


def spread_kernel(dp, n, x_ref, o_ref, ssem, rsem):
    i, d = lax.axis_index("fsdp"), lax.axis_index("dp")
    me = d * n + i
    total = dp * n
    barrier = pltpu.get_barrier_semaphore()

    def other(t):
        j = lax.rem(me + t, total)
        return {"fsdp": lax.rem(j, n), "dp": lax.div(j, n)}

    @pl.loop(1, total)
    def _(t):
        pl.semaphore_signal(barrier, inc=1, device_id=other(t), device_id_type=MESH)

    pl.semaphore_wait(barrier, total - 1)

    @pl.loop(1, total)
    def _(t):
        pltpu.make_async_remote_copy(
            src_ref=x_ref, dst_ref=o_ref.at[me], send_sem=ssem.at[t], recv_sem=rsem.at[t], device_id=other(t), device_id_type=MESH
        ).start()

    o_ref[me] = x_ref[...]

    @pl.loop(1, total)
    def _(t):
        pltpu.make_async_remote_copy(
            src_ref=x_ref, dst_ref=o_ref.at[lax.rem(me - t + total, total)], send_sem=ssem.at[t], recv_sem=rsem.at[t], device_id=other(t), device_id_type=MESH
        ).wait()


def spread(dp, n, tile, number):
    vmem = pl.BlockSpec(memory_space=pltpu.VMEM)
    return pl.pallas_call(
        functools.partial(spread_kernel, dp, n),
        out_shape=jax.ShapeDtypeStruct((dp * n,) + tile.shape, tile.dtype),
        in_specs=[vmem],
        out_specs=vmem,
        scratch_shapes=[pltpu.SemaphoreType.DMA((dp * n,)), pltpu.SemaphoreType.DMA((dp * n,))],
        compiler_params=pltpu.CompilerParams(collective_id=number, has_side_effects=True),
    )(tile)


FB = 2
GROUP = 16
HALF = jnp.bfloat16
FULL = jnp.float32
NORM_EPS = 1e-06
MASKED = -1000000000.0
NEVER = -3e38


def dot(a, b):
    return lax.dot_general(a, b, (((1,), (0,)), ((), ())), preferred_element_type=FULL)


def dot_back(a, b):
    return lax.dot_general(a, b, (((1,), (1,)), ((), ())), preferred_element_type=FULL)


def dot_rows(a, b):
    return lax.dot_general(a, b, (((0,), (0,)), ((), ())), preferred_element_type=FULL)


def mean(x):
    return jnp.sum(x, -1, keepdims=True) * (1.0 / D)


def norm(x, gain, shift):
    centred = x - mean(x)
    scale = lax.rsqrt(mean(centred * centred) + NORM_EPS)
    return centred * scale * gain + shift


def norm_back(x, gain, back):
    centred = x - mean(x)
    scale = lax.rsqrt(mean(centred * centred) + NORM_EPS)
    unit = centred * scale
    inner = back * gain
    return scale * (inner - mean(inner) - unit * mean(inner * unit)), back * unit


def normal_cdf(x):
    size = jnp.abs(x) * 0.7071067811865476
    t = pl.reciprocal(1.0 + 0.3275911 * size)
    bell = jnp.exp(-0.5 * x * x)
    poly = ((((1.061405429 * t - 1.453152027) * t + 1.421413741) * t - 0.284496736) * t + 0.254829592) * t
    tail = 0.5 * poly * bell
    return jnp.where(x < 0, tail, 1.0 - tail), bell


def gelu(x):
    below, bell = normal_cdf(x)
    return x * below, below + x * bell * 0.3989422804014327


def column_sum(x):
    return jnp.sum(x.astype(FULL), 0, keepdims=True)


def flat(ref):
    x = ref[...]
    return x.reshape(-1, x.shape[-1])


def row_of(rows):
    return lax.rem(lax.broadcasted_iota(jnp.int32, (rows, 1), 0), SP)


def first_step():
    return pl.program_id(0) == 0


def add_rows(ref, values):
    @pl.when(first_step())
    def _():
        ref[...] = jnp.zeros_like(ref)

    for k, value in enumerate(values):
        if value is not None:
            ref[k : k + 1, :] += value


def pair_lanes(x, low):
    zero = jnp.zeros_like(x)
    return jnp.concatenate([jnp.where(low, x, zero), jnp.where(low, zero, x)], 0)


def attend(q, k, v, fill):
    rows = q.shape[0]
    low = lax.broadcasted_iota(jnp.int32, (rows, 128), 1) < HD
    stacked = pair_lanes(q * jnp.asarray(HD ** (-0.5), HALF), low)
    scores = dot_back(stacked, k)
    if fill.shape[0] != 1:
        fill = jnp.concatenate([fill, fill], 0)
    scores = jnp.where(fill == 0.0, scores, fill)
    expanded = jnp.exp(scores - jnp.max(scores, -1, keepdims=True))
    share = pl.reciprocal(jnp.sum(expanded, -1, keepdims=True))
    mixed = dot((expanded * share).astype(HALF), v)
    return jnp.where(low, mixed[:rows], mixed[rows:])


def attend_back(q, k, v, back, fill):
    rows = q.shape[0]
    low = lax.broadcasted_iota(jnp.int32, (rows, 128), 1) < HD
    stacked = pair_lanes(q * jnp.asarray(HD ** (-0.5), HALF), low)
    backs = pair_lanes(back, low)
    scores = dot_back(k, stacked)
    scores = jnp.where(fill == 0.0, scores, fill)
    expanded = jnp.exp(scores - jnp.max(scores, 0, keepdims=True))
    chances = expanded * pl.reciprocal(jnp.sum(expanded, 0, keepdims=True))
    back_chances = dot_back(v, backs)
    inner = jnp.sum(back_chances * chances, 0, keepdims=True)
    back_scores = (chances * (back_chances - inner)).astype(HALF)
    back_keys = dot(back_scores, stacked)
    back_values = dot(chances.astype(HALF), backs)
    queries = dot_rows(back_scores, k) * HD ** (-0.5)
    return jnp.where(low, queries[:rows], queries[rows:]), back_keys, back_values


def embed_kernel(p_ref, w0, w1, w2, w3, v_ref, pos_ref, time_ref, pad_ref, x_ref, a_ref, q_ref, k_ref, b_ref):
    pad_ref[:, SP - GROUP :, :] = jnp.zeros((FB, GROUP, D), HALF)
    for f in range(FB):
        pad_ref[f, :S, :] = p_ref[0, f]
    pos = pos_ref[...]
    here = jnp.concatenate([pos + time_ref[f] for f in range(FB)], 0)
    x = dot(flat(pad_ref), w0[0]) + v_ref[9:10] + here
    x_ref[...] = x.reshape(FB, SP, D)
    a = norm(x, v_ref[22:23], v_ref[23:24]).astype(HALF)
    a_ref[...] = a.reshape(FB, SP, D)
    q_ref[...] = (dot(a, w1[0]) + v_ref[10:11]).astype(HALF).reshape(FB, SP, D)
    k_ref[...] = dot(a, w2[0]).astype(HALF).reshape(FB, SP, D)
    b_ref[...] = (dot(a, w3[0]) + v_ref[11:12]).astype(HALF).reshape(FB, SP, D)


def time_kernel(q_ref, k_ref, v_ref, fill_ref, o_ref):
    rows = F * GROUP
    for p in range(H // 2):
        lanes = slice(128 * p, 128 * p + 128)
        q, k, v = (ref[:, :, lanes].reshape(rows, 128) for ref in (q_ref, k_ref, v_ref))
        o_ref[:, :, lanes] = attend(q, k, v, fill_ref[0]).astype(HALF).reshape(F, GROUP, 128)


def space_kernel(o_ref, x_ref, w0, w1, w2, w3, w4, v_ref, fill_ref, y_ref, xs_ref, a_ref, q_ref, k_ref, b_ref, os_ref, cls_ref):
    rows = FB * SP
    y = (dot(flat(o_ref), w0[0]) + v_ref[12:13]).astype(HALF)
    y_ref[...] = y.reshape(FB, SP, D)
    x = flat(x_ref) + dot(y, w1[0]) + v_ref[13:14]
    x = jnp.where(row_of(rows) == S, v_ref[0:1] + v_ref[30:31], x)
    xs_ref[...] = x.reshape(FB, SP, D)
    a = norm(x, v_ref[24:25], v_ref[25:26]).astype(HALF)
    a_ref[...] = a.reshape(FB, SP, D)
    q_ref[...] = (dot(a, w2[0]) + v_ref[14:15]).astype(HALF).reshape(FB, SP, D)
    k_ref[...] = dot(a, w3[0]).astype(HALF).reshape(FB, SP, D)
    b_ref[...] = (dot(a, w4[0]) + v_ref[15:16]).astype(HALF).reshape(FB, SP, D)
    for f in range(FB):
        for p in range(H // 2):
            lanes = slice(128 * p, 128 * p + 128)
            mixed = attend(q_ref[f, :, lanes], k_ref[f, :, lanes], b_ref[f, :, lanes], fill_ref[f])
            os_ref[f, :, lanes] = mixed.astype(HALF)
            cls_ref[f, :, lanes] = mixed[S : S + 8]


def mlp_kernel(o_ref, cls_ref, xs_ref, wp_ref, u0, u1, u2, u3, e0, e1, e2, e3, v_ref, share_ref, of_ref, x2_ref, a_ref, g_ref, e_ref, x3_ref, pool_ref):
    rows = FB * SP
    o = jnp.where(row_of(rows) == S, cls_ref[...], flat(o_ref).astype(FULL)).astype(HALF)
    of_ref[...] = o.reshape(FB, SP, D)
    x2 = flat(xs_ref) + dot(o, wp_ref[0]) + v_ref[16:17]
    x2_ref[...] = x2.reshape(FB, SP, D)
    a = norm(x2, v_ref[26:27], v_ref[27:28]).astype(HALF)
    a_ref[...] = a.reshape(FB, SP, D)
    x3 = x2 + v_ref[21:22]
    for k in range(4):
        g = dot(a, (u0, u1, u2, u3)[k][0]) + v_ref[17 + k : 18 + k]
        e, slope = gelu(g)
        g_ref[k] = slope.reshape(FB, SP, D)
        e = e.astype(HALF)
        e_ref[k] = e.reshape(FB, SP, D)
        x3 = x3 + dot(e, (e0, e1, e2, e3)[k][0])
    x3_ref[...] = x3.reshape(FB, SP, D)
    final = norm(x3, v_ref[28:29], v_ref[29:30]) * share_ref[...]
    add_rows(pool_ref, [column_sum(final)])


def mlp_back_kernel(x3_ref, x2_ref, g_ref, d_ref, wp_ref, u0, u1, u2, u3, e0, e1, e2, e3, v_ref, share_ref, q_ref, k_ref, b_ref, fill_ref,
                    r3_ref, dg_ref, d2_ref, r2_ref, dq_ref, dk_ref, dv_ref, cq_ref, ck_ref, cv_ref, sum_ref, do_ref):
    top = d_ref[0:1] * share_ref[...]
    d3, unit = norm_back(flat(x3_ref), v_ref[28:29], top)
    sums = [column_sum(unit), column_sum(top)]
    r3 = d3.astype(HALF)
    r3_ref[...] = r3.reshape(FB, SP, D)
    sums.append(column_sum(r3))
    back = None
    for k in range(4):
        dg = (dot_back(r3, (e0, e1, e2, e3)[k][0]) * flat(g_ref.at[k])).astype(HALF)
        dg_ref[k] = dg.reshape(FB, SP, D)
        sums.append(column_sum(dg))
        part = dot_back(dg, (u0, u1, u2, u3)[k][0])
        back = part if back is None else back + part
    d2, unit = norm_back(flat(x2_ref), v_ref[26:27], back)
    sums += [column_sum(unit), column_sum(back)]
    d2 = d2 + d3
    d2_ref[...] = d2.reshape(FB, SP, D)
    r2 = d2.astype(HALF)
    r2_ref[...] = r2.reshape(FB, SP, D)
    sums.append(column_sum(r2))
    add_rows(sum_ref, sums)
    do_ref[...] = dot_back(r2, wp_ref[0]).astype(HALF).reshape(FB, SP, D)
    for f in range(FB):
        for p in range(H // 2):
            lanes = slice(128 * p, 128 * p + 128)
            outs = attend_back(q_ref[f, :, lanes], k_ref[f, :, lanes], b_ref[f, :, lanes], do_ref[f, :, lanes], fill_ref[f][:, 0:1])
            for value, ref, cls in zip(outs, (dq_ref, dk_ref, dv_ref), (cq_ref, ck_ref, cv_ref)):
                ref[f, :, lanes] = value.astype(HALF)
                cls[f, :, lanes] = value[S : S + 8]


def space_back_kernel(dq_ref, dk_ref, dv_ref, cls_ref, xs_ref, d2_ref, w0, w1, w2, w3, w4, v_ref, fq_ref, fk_ref, fv_ref, d1_ref, r1_ref, dy_ref, do_ref, sum_ref):
    rows = FB * SP
    is_class = row_of(rows) == S
    grads = []
    for k, (ref, out) in enumerate(zip((dq_ref, dk_ref, dv_ref), (fq_ref, fk_ref, fv_ref))):
        grad = jnp.where(is_class, cls_ref[k : k + 1], flat(ref).astype(FULL)).astype(HALF)
        out[...] = grad.reshape(FB, SP, D)
        grads.append(grad)
    back = dot_back(grads[0], w2[0]) + dot_back(grads[1], w3[0]) + dot_back(grads[2], w4[0])
    d, unit = norm_back(flat(xs_ref), v_ref[24:25], back)
    sums = [column_sum(grads[0]), column_sum(grads[2]), column_sum(unit), column_sum(back)]
    d = d + flat(d2_ref)
    kept = jnp.where(is_class, d, 0.0)
    sums.append(column_sum(kept))
    d = d - kept
    d1_ref[...] = d.reshape(FB, SP, D)
    r1 = d.astype(HALF)
    r1_ref[...] = r1.reshape(FB, SP, D)
    sums.append(column_sum(r1))
    dy = dot_back(r1, w1[0]).astype(HALF)
    dy_ref[...] = dy.reshape(FB, SP, D)
    sums.append(column_sum(dy))
    do_ref[...] = dot_back(dy, w0[0]).astype(HALF).reshape(FB, SP, D)
    add_rows(sum_ref, sums)


def time_back_kernel(q_ref, k_ref, v_ref, d_ref, fill_ref, dq_ref, dk_ref, dv_ref):
    rows = F * GROUP
    fill = jnp.concatenate([fill_ref[0], fill_ref[0]], 1)
    for p in range(H // 2):
        lanes = slice(128 * p, 128 * p + 128)
        q, k, v, d = (ref[:, :, lanes].reshape(rows, 128) for ref in (q_ref, k_ref, v_ref, d_ref))
        for value, ref in zip(attend_back(q, k, v, d, fill), (dq_ref, dk_ref, dv_ref)):
            ref[:, :, lanes] = value.astype(HALF).reshape(F, GROUP, 128)


def embed_back_kernel(dq_ref, dk_ref, dv_ref, x_ref, d1_ref, w1, w2, w3, v_ref, r_ref, pos_ref, time_ref, sum_ref):
    q, v = flat(dq_ref), flat(dv_ref)
    back = dot_back(q, w1[0]) + dot_back(flat(dk_ref), w2[0]) + dot_back(v, w3[0])
    d, unit = norm_back(flat(x_ref), v_ref[22:23], back)
    d = d + flat(d1_ref)
    rounded = d.astype(HALF)
    r_ref[...] = rounded.reshape(FB, SP, D)
    add_rows(sum_ref, [column_sum(q), column_sum(v), column_sum(unit), column_sum(back), column_sum(rounded)])

    @pl.when(first_step())
    def _():
        pos_ref[...] = jnp.zeros_like(pos_ref)

    total = jnp.zeros((SP, D), FULL)
    for f in range(FB):
        part = d[f * SP : (f + 1) * SP]
        time_ref[f] = column_sum(part)
        total = total + part
    pos_ref[...] += total


def shape(*dims, dtype=HALF):
    return jax.ShapeDtypeStruct(dims, dtype)


FRAMES = pl.BlockSpec((FB, SP, D), lambda i: (i, 0, 0))
HIDDEN = pl.BlockSpec((4, FB, SP, D), lambda i: (0, i, 0, 0))
SLAB = pl.BlockSpec((F, GROUP, D), lambda i: (0, i, 0))
ROWS16 = shape(F, SP, D)
ROWS32 = shape(F, SP, D, dtype=FULL)
HIDDEN16 = shape(4, F, SP, D)
HIDDEN32 = shape(4, F, SP, D, dtype=FULL)


def whole(*dims):
    return pl.BlockSpec(dims, lambda i: (0,) * len(dims), pipeline_mode=pl.Buffered(1))


def matrix(m):
    return pl.BlockSpec((1, D, D), lambda i: (m, 0, 0), pipeline_mode=pl.Buffered(1))


def matrices(first, count):
    return [matrix(m) for m in range(first, first + count)]


def summed(rows):
    return pl.BlockSpec((rows, D), lambda i: (0, 0))


def call(kernel, steps, in_specs, out_specs, out_shape, scratch=()):
    return pl.pallas_call(
        kernel,
        grid=(steps,),
        in_specs=in_specs,
        out_specs=out_specs,
        out_shape=out_shape,
        scratch_shapes=list(scratch),
        compiler_params=pltpu.CompilerParams(vmem_limit_bytes=60 * 2**20),
    )


def per_frame(*tail):
    return pl.BlockSpec((FB,) + tail, lambda i: (i,) + (0,) * len(tail))


class Part:
    def __init__(self, lay, first, half, split):
        self.first, self.half, self.split = first, half, split
        self.common = half - split * lay.planes

    def order(self):
        return list(range(self.common, self.half)) + list(range(self.common))


class Sums:
    def __init__(self, refs, common, split):
        (self.g, self.r, self.ys, self.yr, self.xs, self.xr, self.zs, self.zr, self.fin, self.every) = refs[:10]
        (self.rs, self.rr, self.yss, self.yrs, self.xss, self.xrs, self.zss, self.zrs, self.fsem) = refs[10:]
        self.common, self.split = common, split


SUMS = 19


def sums_scratch(lay, rows, common, split):
    A, B, Y, n = lay.outer, lay.inner, lay.planes, lay.n
    slots, kept, passed, K = common + split * Y, max(split, 1), max(Y - 1, 1), common + split
    dma = pltpu.SemaphoreType.DMA
    width, depth = (rows, n) if split else (16, 1)
    crossed, along = max(B - 1, 1), max(A - 1, 1)
    return [
        pltpu.VMEM((slots, 2, n, rows, D), HALF), pltpu.VMEM((slots, n, rows, D), HALF),
        pltpu.VMEM((passed, kept, depth, width, D), HALF), pltpu.VMEM((passed, kept, depth, width, D), HALF),
        pltpu.VMEM((K, crossed, A, rows, D), HALF), pltpu.VMEM((K, crossed, A, rows, D), HALF),
        pltpu.VMEM((K, along, rows, D), HALF), pltpu.VMEM((K, along, rows, D), HALF),
        pltpu.VMEM((K, rows, D), FULL), pltpu.VMEM((Y, common, rows, D), FULL),
        dma((slots,)), dma((slots,)), dma((passed, kept)), dma((passed, kept)),
        dma((K, crossed, A)), dma((K, crossed, A)), dma((K, along)), dma((K, along)), dma((5, K, Y)),
    ]


def other_device(lay, me, t):
    j = lax.rem(me + t, lay.dp * lay.n)
    return {"fsdp": lax.rem(j, lay.n), "dp": lax.div(j, lay.n)}


def greet_all(lay, me):
    barrier = pltpu.get_barrier_semaphore()

    @pl.loop(1, lay.dp * lay.n)
    def _(t):
        pl.semaphore_signal(barrier, inc=1, device_id=other_device(lay, me, t), device_id_type=MESH)

    pl.semaphore_wait(barrier, lay.dp * lay.n - 1)


class Reducer:
    def __init__(self, lay, squares, everyone):
        self.lay = lay
        self.squares = squares
        self.i, self.a, self.b, self.y, self.c = lay.place()
        self.here = lay.peer(self.i, self.y, 1 - self.c)
        self.pending = []
        if everyone:
            greet_all(lay, lax.axis_index("dp") * lay.n + self.i)
        else:
            greet(lay, self.i, self.a, self.b, self.y, self.c)

    def square(self, value, share):
        self.squares[...] += jnp.sum((value * value).reshape(-1, 8, D), 0) * share

    def remote(self, src, dst, sends, at, recvs, dev, like):
        pltpu.make_async_remote_copy(
            src_ref=src, dst_ref=dst, send_sem=sends.at[at], recv_sem=recvs[0].at[recvs[1]], device_id=dev, device_id_type=MESH
        ).start()
        self.pending.append((like, sends, at, True))

    def wait_all(self):
        for make, sems, at, remote in self.pending:
            like = make()
            if remote:
                pltpu.make_async_remote_copy(
                    src_ref=like, dst_ref=like, send_sem=sems.at[at], recv_sem=sems.at[at], device_id=self.here, device_id_type=MESH
                ).wait_send()
            else:
                pltpu.make_async_copy(like, like, sems.at[at]).wait()

    def landed(self, dst, sems, *at):
        pltpu.make_async_remote_copy(
            src_ref=dst, dst_ref=dst, send_sem=sems.at[at], recv_sem=sems.at[at], device_id=self.here, device_id_type=MESH
        ).wait_recv()

    def slot(self, st, v, q):
        if v is None:
            return q
        return st.common + turn(self.y, v, self.lay.planes) * st.split + q

    def hand(self, st, h):
        self.remote(st.g.at[h, 1 - self.c], st.r.at[h], st.rs, (h,), (st.rr, (h,)), self.here, lambda: st.r.at[h])

    def base(self, st, v, q, j):
        n = self.slot(st, v, q)
        total = st.g[n, self.c, j].astype(FULL) + st.r[n, j].astype(FULL)
        if v == 0:
            for w in range(1, self.lay.planes):
                total = total + st.yr[w - 1, q, j].astype(FULL)
        return total

    def pass_on(self, st, v, q):
        n = self.slot(st, v, q)
        self.landed(st.r.at[n], st.rr, n)

        @pl.loop(0, self.lay.n)
        def _(j):
            st.ys[v - 1, q, j] = self.base(st, v, q, j).astype(HALF)

        self.remote(
            st.ys.at[v - 1, q], st.yr.at[v - 1, q], st.yss, (v - 1, q), (st.yrs, (v - 1, q)),
            self.lay.peer(self.i, turn(self.y, v, self.lay.planes), self.c), lambda: st.ys.at[v - 1, q],
        )

    def item(self, st, v, q):
        return q if v is None else st.common + q

    def cross(self, st, target, v, q):
        k, n = self.item(st, v, q), self.slot(st, v, q)
        self.landed(st.r.at[n], st.rr, n)
        if v == 0:
            for w in range(1, self.lay.planes):
                self.landed(st.yr.at[w - 1, q], st.yrs, w - 1, q)
        outer, inner = self.lay.outer, self.lay.inner
        for t in list(range(1, outer)) + [0]:
            e = turn(self.a, t, outer)
            for u in range(1, inner):
                other = turn(self.b, u, inner)
                st.xs[k, u - 1, e] = self.base(st, v, q, e * inner + other).astype(HALF)
                self.remote(
                    st.xs.at[k, u - 1, e], st.xr.at[k, u - 1, e], st.xss, (k, u - 1, t), (st.xrs, (k, u - 1, t)),
                    self.lay.peer(self.a * inner + other, self.y, self.c), lambda u=u: st.xs.at[k, u - 1, 0],
                )

    def along(self, st, target, v, q):
        k = self.item(st, v, q)
        inner, outer = self.lay.inner, self.lay.outer
        for t in list(range(1, outer)) + [0]:
            e = turn(self.a, t, outer)
            value = self.base(st, v, q, e * inner + self.b)
            for u in range(1, inner):
                self.landed(st.xr.at[k, u - 1, e], st.xrs, k, u - 1, t)
                value = value + st.xr[k, u - 1, e].astype(FULL)
            if t == 0:
                st.fin[k] = value
                continue
            st.zs[k, t - 1] = value.astype(HALF)
            self.remote(
                st.zs.at[k, t - 1], st.zr.at[k, t - 1], st.zss, (k, t - 1), (st.zrs, (k, t - 1)),
                self.lay.peer(e * inner + self.b, self.y, self.c), lambda t=t: st.zs.at[k, t - 1],
            )

    def close(self, st, target, v, q):
        k, Y = self.item(st, v, q), self.lay.planes
        for t in range(1, self.lay.outer):
            self.landed(st.zr.at[k, t - 1], st.zrs, k, t - 1)
        value = st.fin[k]
        for t in range(1, self.lay.outer):
            value = value + st.zr[k, t - 1].astype(FULL)
        if v is None:
            st.every[self.y, k] = value
            source, landing = st.every.at[self.y, k], st.every.at[self.y, k]
            like = lambda: st.every.at[0, k]
        else:
            st.fin[k] = value
            self.square(value, 1.0)
            source = st.fin.at[k]
            like = lambda: st.fin.at[k]
            landing = target(self.c, self.slot(st, v, q))
        for w in range(1, Y):
            self.remote(source, landing, st.fsem, (0, k, w), (st.fsem, (1, k, w)), self.lay.peer(self.i, turn(self.y, w, Y), self.c), like)
        if v is not None:
            self.finish(st, k, landing)

    def finish(self, st, k, landing):
        pltpu.make_async_copy(st.fin.at[k], landing, st.fsem.at[2, k, 0]).start()
        self.pending.append((lambda: st.fin.at[k], st.fsem, (2, k, 0), False))
        self.remote(st.fin.at[k], landing, st.fsem, (3, k, 0), (st.fsem, (4, k, 0)), self.here, lambda: st.fin.at[k])

    def merge(self, st, target, v, q):
        k, Y = self.item(st, v, q), self.lay.planes
        if v is None:
            for w in range(1, Y):
                self.landed(st.every.at[turn(self.y, -w, Y), k], st.fsem, 1, k, w)
            value = st.every[0, k]
            for w in range(1, Y):
                value = value + st.every[w, k]
            st.fin[k] = value
            self.square(value, 1.0 / Y)
            self.finish(st, k, target(self.c, q))
        else:
            for w in range(1, Y):
                back = target(self.c, self.slot(st, -w, q))
                self.landed(back, st.fsem, 1, k, w)
                self.remote(back, back, st.fsem, (3, k, w), (st.fsem, (4, k, w)), self.here, lambda: target(0, 0))

    def last(self, st, target, v, q):
        k = self.item(st, v, q)
        self.landed(target(1 - self.c, self.slot(st, v, q)), st.fsem, 4, k, 0)
        if v is not None:
            for w in range(1, self.lay.planes):
                self.landed(target(1 - self.c, self.slot(st, -w, q)), st.fsem, 4, k, w)

    def progress(self, work, step):
        for lag, stage in enumerate((self.cross, self.along, self.close, self.merge)):
            if 0 <= step - lag < len(work):
                stage(*work[step - lag])

    def done(self, work):
        for job in work:
            self.last(*job)
        self.wait_all()


def outer_products(rows, operands, jobs, st, after, a_buf, b_buf, sems):
    n = st.g.shape[2]
    lefts, rights, plan = [], [], []
    for slot, core, left, right in jobs:
        fresh = [not lefts or lefts[-1] != left, not rights or rights[-1] != right]
        if fresh[0]:
            lefts.append(left)
        if fresh[1]:
            rights.append(right)
        plan.append((slot, core, len(lefts) - 1, len(rights) - 1, fresh))

    def load(kind, loads, k):
        number, block = loads[k]
        buf = (a_buf, b_buf)[kind]
        return pltpu.make_async_copy(operands[number].at[pl.ds(block * rows, rows)], buf.at[k % 2], sems.at[kind, k % 2])

    load(0, lefts, 0).start()
    load(1, rights, 0).start()
    for slot, core, left, right, fresh in plan:
        if fresh[0]:
            load(0, lefts, left).wait()
        if fresh[1]:
            load(1, rights, right).wait()
        if fresh[0] and left + 1 < len(lefts):
            load(0, lefts, left + 1).start()
        if fresh[1] and right + 1 < len(rights):
            load(1, rights, right + 1).start()
        value = dot_rows(a_buf[left % 2], b_buf[right % 2])
        st.g[slot, core] = value.reshape(n, -1, D).astype(HALF)
        if core == 1:
            after(slot)


def product_buffers(rows):
    return [
        pltpu.VMEM((2, rows, D), HALF), pltpu.VMEM((2, rows, D), HALF), pltpu.SemaphoreType.DMA((2, 2)),
    ]


def product_jobs(part, pairs):
    return [(h, core, *pairs[2 * h + core]) for h in part.order() for core in range(2)]


def part_work(lay, part, st, target):
    return [(st, target, None, k) for k in range(part.common)] + [(st, target, 0, q) for q in range(part.split)]


def products_and_hand(red, part, st, work, operands, jobs, buffers):
    passed = [(v, q) for v in range(1, red.lay.planes) for q in range(part.split)]
    order = part.order()
    ahead = len(work) - part.common - part.split

    def after(h):
        red.hand(st, h)
        place = order.index(h) - (part.half - part.common)
        if place == 0 or part.common == 0 and h == order[-1]:
            for v, q in passed:
                red.pass_on(st, v, q)
        if place >= 1 - ahead and place + ahead - 1 < steps_beside(part, ahead):
            red.progress(work, place + ahead - 1)

    outer_products(F * SP, operands, jobs, st, after, *buffers)


def steps_beside(part, ahead):
    return max(part.common + ahead - 1, 0)


def early_kernel(lay, part, pairs, *refs):
    (e_ref, r3_ref, a2_ref, dg_ref, dq_ref, dk_ref, dv_ref, cls_ref, xs_ref, d2_ref, qt_ref, kt_ref, vt_ref, fill_ref, x0_ref, mats_ref, v_ref) = refs[:17]
    (og_ref, fq_ref, fk_ref, fv_ref, d1_ref, r1_ref, dy_ref, do_ref, tq_ref, tk_ref, tv_ref, rp_ref, sum2_ref, pos_ref, time_ref, sum3_ref, sq_ref) = refs[17:34]
    red = Reducer(lay, sq_ref, False)
    sq_ref[...] = jnp.zeros_like(sq_ref)
    st = Sums(refs[34 : 34 + SUMS], part.common, part.split)
    w_buf, w_sem = refs[34 + SUMS :]
    load = pltpu.make_async_copy(mats_ref.at[pl.ds(1, 8)], w_buf, w_sem.at[0])
    load.start()

    def target(core, h):
        return og_ref.at[part.first + 2 * h + core]

    work = part_work(lay, part, st, target)
    rows = F * SP
    jobs = product_jobs(part, pairs)
    pl.run_scoped(lambda *buffers: products_and_hand(red, part, st, work, (e_ref, r3_ref, a2_ref, dg_ref), jobs, buffers), *product_buffers(rows))
    begun = steps_beside(part, 0)
    load.wait()
    ws = [w_buf.at[pl.ds(k, 1)] for k in range(8)]

    steps = F // FB

    def space(dq, dk, dv, xs, d2, fq, fk, fv, d1, r1, dy, do):
        space_back_kernel(dq, dk, dv, cls_ref, xs, d2, ws[3], ws[4], ws[5], ws[6], ws[7], v_ref, fq, fk, fv, d1, r1, dy, do, sum2_ref)
        for s, place in enumerate((1, 3)):
            @pl.when(pl.program_id(0) == place)
            def _():
                red.progress(work, begun + s)

    pltpu.emit_pipeline(space, grid=(steps,), in_specs=[FRAMES] * 5, out_specs=[FRAMES] * 7)(
        dq_ref, dk_ref, dv_ref, xs_ref, d2_ref, fq_ref, fk_ref, fv_ref, d1_ref, r1_ref, dy_ref, do_ref
    )

    def time(q, k, v, d, fill, dq, dk, dv):
        time_back_kernel(q, k, v, d, fill, dq, dk, dv)

        for s, place in enumerate((6, 12)):
            @pl.when(pl.program_id(0) == place)
            def _():
                red.progress(work, begun + 2 + s)

    pltpu.emit_pipeline(time, grid=(SP // GROUP,), in_specs=[SLAB] * 4 + [FILL], out_specs=[SLAB] * 3)(
        qt_ref, kt_ref, vt_ref, do_ref, fill_ref, tq_ref, tk_ref, tv_ref
    )

    def embed(dq, dk, dv, x, d1, r, time):
        embed_back_kernel(dq, dk, dv, x, d1, ws[0], ws[1], ws[2], v_ref, r, pos_ref, time, sum3_ref)

        @pl.when(pl.program_id(0) == 3)
        def _():
            red.progress(work, begun + 4)

    pltpu.emit_pipeline(embed, grid=(steps,), in_specs=[FRAMES] * 5, out_specs=[FRAMES, per_frame(1, D)])(
        tq_ref, tk_ref, tv_ref, x0_ref, d1_ref, rp_ref, time_ref
    )
    for s in range(begun + 5, len(work) + 3):
        red.progress(work, s)
    red.done(work)


FILL = pl.BlockSpec((1, F * GROUP, F * GROUP), lambda i: (i, 0, 0))


def early(lay, part, pairs, arrays, cls, table):
    vmem = pl.BlockSpec(memory_space=pltpu.VMEM)
    e, r3, a2, dg, dq, dk, dv, xs, d2, qt, kt, vt, fill, x0, mats = arrays
    two = lambda x: x.reshape(-1, D)
    full = functools.partial(shape, dtype=FULL)
    return pl.pallas_call(
        functools.partial(early_kernel, lay, part, pairs),
        in_specs=[ANY] * 7 + [vmem] + [ANY] * 8 + [vmem],
        out_specs=[ANY] * 12 + [vmem, vmem, ANY, vmem, vmem],
        out_shape=[full(NMAT, lay.rows, D), ROWS16, ROWS16, ROWS16, ROWS32] + [ROWS16] * 7 + [full(16, D), full(SP, D), full(F, 1, D), full(16, D), full(8, D)],
        scratch_shapes=sums_scratch(lay, lay.rows, part.common, part.split) + [pltpu.VMEM((8, D, D), HALF), pltpu.SemaphoreType.DMA((1,))],
        compiler_params=pltpu.CompilerParams(collective_id=1, has_side_effects=True, vmem_limit_bytes=62 * 2**20),
    )(two(e), two(r3), two(a2), two(dg), dq, dk, dv, cls, xs, d2, qt, kt, vt, fill, x0, mats, table)


def late_kernel(lay, part, pairs, count, *refs):
    s_ref, sq_ref, operands = refs[0], refs[1], refs[3 : 3 + count]
    og_ref, os_ref, tiles_ref = refs[3 + count : 6 + count]
    rest = refs[6 + count : -4]
    squares, tile, tile_sent, tile_come = refs[-4:]
    red = Reducer(lay, squares, True)
    squares[...] = sq_ref[...]
    st = Sums(rest[:SUMS], part.common, part.split)
    little = Sums(rest[SUMS : 2 * SUMS], 1, 0)
    small_sem = rest[2 * SUMS]
    load = pltpu.make_async_copy(s_ref, little.g.at[0], small_sem.at[0])
    load.start()

    def target(core, h):
        return og_ref.at[part.first + 2 * h + core]

    work = part_work(lay, part, st, target)
    work = [(little, lambda core, h: os_ref.at[core], None, 0)] + work
    rows = F * SP
    jobs = product_jobs(part, pairs)
    load.wait()
    red.hand(little, 0)
    pl.run_scoped(lambda *buffers: products_and_hand(red, part, st, work, operands, jobs, buffers), *product_buffers(rows))
    for s in range(steps_beside(part, 1), len(work) + 3):
        red.progress(work, s)
    tile[...] = sum(squares[:, e * 128 : e * 128 + 128] for e in range(D // 128))
    me, total = lax.axis_index("dp") * lay.n + red.i, lay.dp * lay.n

    def swap(t, place):
        return pltpu.make_async_remote_copy(
            src_ref=tile, dst_ref=tiles_ref.at[place], send_sem=tile_sent.at[t], recv_sem=tile_come.at[t],
            device_id=other_device(lay, me, t), device_id_type=MESH,
        )

    @pl.loop(1, total)
    def _(t):
        swap(t, me).start()

    tiles_ref[me] = tile[...]
    red.done(work)

    @pl.loop(1, total)
    def _(t):
        swap(t, lax.rem(me - t + total, total)).wait()


def late(lay, part, pairs, small, squares, sums, arrays):
    full = functools.partial(shape, dtype=FULL)
    vmem = pl.BlockSpec(memory_space=pltpu.VMEM)
    everyone = lay.dp * lay.n
    dma = pltpu.SemaphoreType.DMA
    return pl.pallas_call(
        functools.partial(late_kernel, lay, part, pairs, len(arrays)),
        in_specs=[ANY, vmem] + [ANY] * (1 + len(arrays)),
        out_specs=[ANY, ANY, vmem],
        out_shape=[full(NMAT, lay.rows, D), full(2, small.shape[2], D), full(everyone, 8, 128)],
        scratch_shapes=sums_scratch(lay, lay.rows, part.common, part.split) + sums_scratch(lay, small.shape[2], 1, 0)
        + [dma((1,)), pltpu.VMEM((8, D), FULL), pltpu.VMEM((8, 128), FULL), dma((everyone,)), dma((everyone,))],
        input_output_aliases={2: 0},
        compiler_params=pltpu.CompilerParams(collective_id=4, has_side_effects=True, vmem_limit_bytes=62 * 2**20),
    )(small, squares, sums, *[x.reshape(-1, D) for x in arrays])


AHEAD = 1
IN_EMBED = (2,)
IN_TIME = (4, 12)
IN_SPACE = (0, 2)


def front_kernel(lay, w_ref, s_ref, p_ref, tfill_ref, sfill_ref, *refs):
    (ow_ref, os_ref, pad_ref, x0_ref, at_ref, qt_ref, kt_ref, vt_ref, ot_ref, yt_ref, xs_ref, as_ref, qs_ref, ks_ref, vs_ref, mix_ref, cls_ref, v_ref) = refs[:18]
    (w_buf, piece, pos_buf, time_buf, own, zs, zr, xs, xr, ys, yr, cs, cr, wsem) = refs[18:]
    i, a, b, y, c = lay.place()
    A, B, Y, K = lay.outer, lay.inner, lay.planes, lay.handled
    greet(lay, i, a, b, y, c)
    here = lay.peer(i, y, 1 - c)
    pending = []

    def remote(src, dst, sends, at, recvs, dev, like):
        pltpu.make_async_remote_copy(
            src_ref=src, dst_ref=dst, send_sem=sends.at[at], recv_sem=recvs.at[at], device_id=dev, device_id_type=MESH
        ).start()
        pending.append((like, sends, at))

    def landed(dst, sems, *at):
        pltpu.make_async_remote_copy(
            src_ref=dst, dst_ref=dst, send_sem=sems.at[at], recv_sem=sems.at[at], device_id=here, device_id_type=MESH
        ).wait_recv()

    def matrix_of(core, k, v=0):
        h = k * Y + turn(y, v, Y) if k < lay.split else lay.split * (Y - 1) + k
        return 2 * h + core

    def source(k):
        return s_ref.at[c] if k < 0 else w_ref.at[matrix_of(c, k)]

    def at(k, j):
        return os_ref.at[c, j] if k < 0 else ow_ref.at[matrix_of(c, k), j]

    def like(k):
        return (lambda: s_ref.at[0]) if k < 0 else (lambda: w_ref.at[0])

    order = [-1] + list(range(K))

    def local(k):
        if k < 0:
            return pltpu.make_async_copy(s_ref.at[c], os_ref.at[c, i], own.at[0])
        m = 2 * k + c
        return pltpu.make_async_copy(w_ref.at[m], ow_ref.at[m, i], own.at[k + 1])

    def send_along(step):
        if step < len(order):
            k = order[step]
            for t in range(1, A):
                remote(source(k), at(k, i), zs, (k + 1, t), zr, lay.peer(turn(a, t, A) * B + b, y, c), like(k))

    def send_over(k):
        for u in range(1, B):
            remote(source(k), at(k, i), xs, (k + 1, u, 0), xr, lay.peer(a * B + turn(b, u, B), y, c), like(k))

    for step in range(AHEAD):
        send_along(step)
    for k in order:
        send_over(k)
    for k in range(-1, lay.half):
        local(k).start()

    def over(k, j, t, u):
        if 0 <= k < lay.split:
            for v in range(1, Y):
                remote(at(k, j), at(k, j), ys, (k, v, t, u), yr, lay.peer(i, turn(y, v, Y), c), like(k))

    def cross(k):
        send_along(order.index(k) + AHEAD)
        for t in range(1, A):
            j = turn(a, -t, A) * B + b
            landed(at(k, j), zr, k + 1, t)
            for u in range(1, B):
                remote(at(k, j), at(k, j), xs, (k + 1, u, t), xr, lay.peer(a * B + turn(b, u, B), y, c), like(k))
            over(k, j, t, 0)

    def share(k):
        for t in range(A):
            for u in range(1, B):
                j = turn(a, -t, A) * B + turn(b, -u, B)
                landed(at(k, j), xr, k + 1, u, t)
                over(k, j, t, u)
        if k < 0:
            local(k).wait()
            remote(os_ref.at[c], os_ref.at[c], cs, (0,), cr, here, lambda: os_ref.at[0])
        else:
            own_wait(k, 0)
            m = matrix_of(c, k)
            remote(ow_ref.at[m], ow_ref.at[m], cs, (k + 1,), cr, here, lambda: ow_ref.at[0])

    def own_wait(k, v):
        m = matrix_of(c, k, v)
        pltpu.make_async_copy(w_ref.at[m], ow_ref.at[m, i], own.at[lax.div(m, 2) + 1]).wait()

    def slot(q, v):
        return K + 1 + (v - 1) * lay.split + q

    def from_planes(k):
        if k in closed or not 0 <= k < lay.split:
            return
        closed.append(k)
        for v in range(1, Y):
            m = matrix_of(c, k, -v)
            for t in range(A):
                for u in range(B):
                    if t or u:
                        j = turn(a, -t, A) * B + turn(b, -u, B)
                        landed(ow_ref.at[m, j], yr, k, v, t, u)
            own_wait(k, -v)
            remote(ow_ref.at[m], ow_ref.at[m], cs, (slot(k, v),), cr, here, lambda: ow_ref.at[0])

    def paired(k):
        if k < 0:
            landed(os_ref.at[1 - c], cr, 0)
        else:
            landed(ow_ref.at[matrix_of(1 - c, k)], cr, k + 1)
            if k < lay.split:
                for v in range(1, Y):
                    landed(ow_ref.at[matrix_of(1 - c, k, -v)], cr, slot(k, v))

    def fetch(first, count):
        span = pl.ds(first, count)
        return pltpu.make_async_copy(ow_ref.at[span], w_buf.at[span], wsem.at[first])

    closed = []

    def advance(step):
        if step < len(order):
            cross(order[step])
        if 0 <= step - 1 < len(order):
            share(order[step - 1])
        if 0 <= step - 2 < len(order):
            from_planes(order[step - 2])

    first, second = (1, 3) if lay.split else (2, 5)
    begun = first + 2
    for step in range(begun):
        advance(step)
    from_planes(first - 1)
    for k in range(-1, first):
        paired(k)
    fetch(0, 4).start()
    table = pltpu.make_async_copy(os_ref.at[0], piece, wsem.at[lay.half])
    table.start()
    v_ref[...] = jnp.zeros_like(v_ref)
    table.wait()
    for j in range(lay.n):
        lane = min(lay.rows * j // 128 * 128, D - 256)
        wide = jnp.concatenate([piece[j].astype(FULL), jnp.zeros(piece.shape[1:], FULL)], 1)
        v_ref[: piece.shape[1], lane : lane + 256] += pltpu.roll(wide, lay.rows * j - lane, 1)
    pos_buf[...] = v_ref[31 : 31 + SP, :]
    for f in range(F):
        time_buf[f] = v_ref[1 + f : 2 + f, :]
    fetch(0, 4).wait()
    ws = [Weight(w_buf.at[k]) for k in range(9)]
    steps = F // FB

    def embed(p, *outs):
        now = pl.program_id(0)
        embed_kernel(p, *ws[:4], v_ref, pos_buf, time_buf.at[pl.ds(now * FB, FB)], *outs)
        for s, place in enumerate(IN_EMBED):
            @pl.when(now == place)
            def _():
                advance(begun + s)

    pltpu.emit_pipeline(embed, grid=(steps,), in_specs=[pl.BlockSpec((1, FB, S, D), lambda i: (0, i, 0, 0))], out_specs=[FRAMES] * 6)(
        p_ref, pad_ref, x0_ref, at_ref, qt_ref, kt_ref, vt_ref
    )

    def time(q, k, v, fill, o):
        time_kernel(q, k, v, fill, o)
        for s, place in enumerate(IN_TIME):
            @pl.when(pl.program_id(0) == place)
            def _():
                advance(begun + len(IN_EMBED) + s)

    pltpu.emit_pipeline(time, grid=(SP // GROUP,), in_specs=[SLAB] * 3 + [FILL], out_specs=[SLAB])(
        qt_ref, kt_ref, vt_ref, tfill_ref, ot_ref
    )
    done = begun + len(IN_EMBED) + len(IN_TIME)
    for step in range(done, second + 2):
        advance(step)
    done = max(done, second + 2)
    for k in range(first, second):
        from_planes(k)
        paired(k)
    fetch(4, 5).start()
    fetch(4, 5).wait()

    def space(o, x, fill, *outs):
        space_kernel(o, x, *ws[4:9], v_ref, fill, *outs)

        for s, place in enumerate(IN_SPACE):
            @pl.when(pl.program_id(0) == place)
            def _():
                advance(done + s)

    pltpu.emit_pipeline(space, grid=(steps,), in_specs=[FRAMES, FRAMES, per_frame(1, SP)], out_specs=[FRAMES] * 7 + [per_frame(8, D)])(
        ot_ref, x0_ref, sfill_ref, yt_ref, xs_ref, as_ref, qs_ref, ks_ref, vs_ref, mix_ref, cls_ref
    )
    for step in range(done + len(IN_SPACE), len(order) + 1):
        advance(step)
    for k in range(second, K):
        paired(k)
    for make, sems, at_ in pending:
        ref = make()
        pltpu.make_async_remote_copy(
            src_ref=ref, dst_ref=ref, send_sem=sems.at[at_], recv_sem=sems.at[at_], device_id=here, device_id_type=MESH
        ).wait_send()


class Weight:
    def __init__(self, ref):
        self.ref = ref

    def __getitem__(self, unused):
        value = self.ref[...]
        if value.shape[1] % 16:
            return value.astype(FULL).reshape(D, D).astype(HALF)
        return value.reshape(D, D)


def front(lay, shard, small, patches, time_fill, space_fill):
    A, B, K, Y = lay.outer, lay.inner, lay.handled, lay.planes
    dma = pltpu.SemaphoreType.DMA
    kept = max(lay.split, 1)
    vmem = pl.BlockSpec(memory_space=pltpu.VMEM)
    full = functools.partial(shape, dtype=FULL)
    slots = K + 1 + max(Y - 1, 0) * lay.split
    return pl.pallas_call(
        functools.partial(front_kernel, lay),
        in_specs=[ANY] * 5,
        out_specs=[ANY] * 17 + [vmem],
        out_shape=[
            shape(NMAT, lay.n, lay.rows, D), shape(2, lay.n, *small.shape[1:]),
            ROWS16, ROWS32, ROWS16, ROWS16, ROWS16, ROWS16, ROWS16, ROWS16, ROWS32, ROWS16, ROWS16, ROWS16, ROWS16, ROWS16,
            full(F, 8, D), full(256, D),
        ],
        scratch_shapes=[
            pltpu.VMEM((9, lay.n, lay.rows, D), HALF), pltpu.VMEM((lay.n,) + small.shape[1:], HALF), pltpu.VMEM((SP, D), FULL), pltpu.VMEM((F, 1, D), FULL),
            dma((lay.half + 1,)), dma((K + 1, A)), dma((K + 1, A)), dma((K + 1, B, A)), dma((K + 1, B, A)),
            dma((kept, Y, A, B)), dma((kept, Y, A, B)), dma((slots,)), dma((slots,)), dma((lay.half + 1,)),
        ],
        compiler_params=pltpu.CompilerParams(collective_id=0, has_side_effects=True, vmem_limit_bytes=60 * 2**20),
    )(shard, small, patches, time_fill, space_fill)


def forward(lay, shard, small, patches, mask):
    alive = jnp.pad(mask[0] > 0, ((0, 0), (0, SP - S)))
    kept = jnp.where(alive, 0.0, MASKED).astype(FULL)
    places = jnp.arange(SP)[None]
    space_fill = jnp.where(places < S, kept, jnp.where(places == S, 0.0, NEVER))
    time_keys = kept.reshape(F, SP // GROUP, GROUP).transpose(1, 0, 2).reshape(SP // GROUP, F * GROUP)
    spot = jnp.arange(F * GROUP) % GROUP
    same = spot[:, None] == spot[None]
    time_fill = jnp.where(same[None], time_keys[:, None, :], NEVER)
    time_fill_back = jnp.where(same[None], time_keys[:, :, None], NEVER)
    one = jnp.where(places[0] < S, 1.0, jnp.where(places[0] == S, 1.0 / F, 0.0)).astype(FULL)
    share = jnp.broadcast_to(jnp.tile(one, FB)[:, None], (FB * SP, 1))
    mats, rest, padded, x0, at, qt, kt, vt, ot, yt, xs, as_, qs, ks, vs, os_, cls, table = front(
        lay, shard, small, patches, time_fill, space_fill[:, None]
    )
    mats = mats.reshape(NMAT, D, D)
    tab = whole(*table.shape)
    steps = F // FB
    cls = jnp.mean(cls[:, 0], 0, keepdims=True)
    of, x2, a2, g, e, x3, pool = call(
        mlp_kernel, steps,
        [FRAMES, whole(1, D), FRAMES] + matrices(9, 9) + [tab, whole(FB * SP, 1)],
        [FRAMES] * 3 + [HIDDEN] * 2 + [FRAMES, summed(8)],
        [ROWS16, ROWS32, ROWS16, HIDDEN32, HIDDEN16, ROWS32, shape(8, D, dtype=FULL)],
    )(os_, cls, xs, *[mats] * 9, table, share)
    pooled = (pool[:1] / (F * S + 1)).astype(HALF)
    head = rest[1][:, : 2 * lay.rows].reshape(lay.n, 2, lay.rows, 128).transpose(0, 2, 1, 3).reshape(D, 256)
    saved = (table, share, space_fill, time_fill_back, padded, x0, at, qt, kt, vt, ot, yt, xs, as_, qs, ks, vs, of, x2, a2, g, e, x3)
    return pooled, mats, head, saved


def backward(lay, mats, saved, back_pooled):
    (table, share, space_fill, time_fill, padded, x0, at, qt, kt, vt, ot, yt, xs, as_, qs, ks, vs, of, x2, a2, g, e, x3) = saved
    tab = whole(*table.shape)
    steps = F // FB
    top = back_pooled / (F * S + 1)
    column = jnp.broadcast_to(space_fill[:, :, None], (F, SP, 128))
    r3, dg, d2, r2, dq, dk, dv, cq, ck, cv, sums1 = call(
        mlp_back_kernel, steps,
        [FRAMES, FRAMES, HIDDEN, whole(1, D)] + matrices(9, 9) + [tab, whole(FB * SP, 1), FRAMES, FRAMES, FRAMES, per_frame(SP, 128)],
        [FRAMES, HIDDEN] + [FRAMES] * 5 + [per_frame(8, D)] * 3 + [summed(16)],
        [ROWS16, HIDDEN16, ROWS32] + [ROWS16] * 4 + [shape(F, 8, D, dtype=FULL)] * 3 + [shape(16, D, dtype=FULL)],
        [pltpu.VMEM((FB, SP, D), HALF)],
    )(x3, x2, g, top, *[mats] * 9, table, share, qs, ks, vs, column)
    cls = jnp.concatenate([jnp.sum(part[:, 0], 0, keepdims=True) for part in (cq, ck, cv)], 0)
    cls = cls.astype(HALF).astype(FULL) / F
    first = Part(lay, 10, 4, 1 if lay.planes <= 4 else 0)
    pairs = [((2, 0), (3, k)) for k in range(4)] + [((0, k), (1, 0)) for k in range(4)]
    upper, fq, fk, fv, d1, r1, dy, do, tq, tk, tv, rp, sums2, pos, time, sums3, squares = early(
        lay, first, pairs, (e, r3, a2, dg, dq, dk, dv, xs, d2, qt, kt, vt, time_fill, x0, mats), cls, table
    )
    class_grad = sums2[4:5]
    grad_vecs = jnp.concatenate(
        [
            class_grad, time[:, 0], sums3[4:5], sums3[0:2], sums2[6:7], sums2[5:6], sums2[0:2], sums1[9:10], sums1[3:7], sums1[2:3],
            sums3[2:4], sums2[2:4], sums1[7:9], sums1[0:2], class_grad, pos[:S],
        ],
        0,
    )
    second = Part(lay, 0, 5, 1 if lay.planes <= 4 else 0)
    operands = (padded, rp, at, tq, tk, tv, ot, dy, yt, r1, as_, fq, fk, fv, of, r2)
    pairs = [(0, 1), (2, 3), (2, 4), (2, 5), (6, 7), (8, 9), (10, 11), (10, 12), (10, 13), (14, 15)]
    pairs = [((left, 0), (right, 0)) for left, right in pairs]

    def finish(small):
        return late(lay, second, pairs, small, squares, upper, operands)

    return finish, grad_vecs


def project(inputs, weight):
    return jnp.einsum("...a,ab->...b", inputs, weight, preferred_element_type=jnp.float32)


def project_back(inputs, weight, cotangent):
    rounded = cotangent.astype(jnp.bfloat16)
    back_in = jnp.einsum("...b,ab->...a", rounded, weight, preferred_element_type=jnp.float32)
    flat_in = inputs.reshape(-1, inputs.shape[-1])
    flat_back = rounded.reshape(-1, rounded.shape[-1])
    grad_weight = jnp.einsum("na,nb->ab", flat_in, flat_back, preferred_element_type=jnp.float32)
    return (back_in, grad_weight, jnp.sum(flat_back, 0, dtype=jnp.float32))


def normalize(projected):
    return projected * lax.rsqrt(jnp.sum(projected * projected, -1, keepdims=True) + 1e-06)


def adamw_step(weight, first, second, average, gradient, factor, rate):
    clipped = gradient * factor
    first = BETA_ONE * first + (1.0 - BETA_ONE) * clipped
    second = BETA_TWO * second + (1.0 - BETA_TWO) * clipped * clipped
    first_hat = first / (1.0 - BETA_ONE**STEP)
    second_hat = second / (1.0 - BETA_TWO**STEP)
    weight = weight - rate * (first_hat / (jnp.sqrt(second_hat) + ADAM_EPSILON) + DECAY * weight)
    average = AVERAGE_KEEP * average + (1.0 - AVERAGE_KEEP) * weight
    return (weight, first, second, average)


def pack(lay, head, vecs):
    tall = -(-NVEC // 16) * 16
    first = jnp.pad(vecs, ((0, tall - NVEC), (0, 128 - lay.rows)))
    second = jnp.concatenate([head[:, :128], head[:, 128:]], 0)
    return jnp.stack([first, jnp.pad(second, ((0, tall - second.shape[0]), (0, 0)))])


def pack_all(head, vecs, n):
    rows = D // n
    first = head.reshape(n, 3, rows // 3, D // 3).transpose(0, 2, 1, 3).reshape(n, rows // 3, D)
    tall = jnp.pad(vecs, ((0, D // 3 - vecs.shape[0]), (0, 0)))
    second = tall.reshape(n, rows // 3, n, rows).transpose(2, 1, 0, 3).reshape(n, rows // 3, D)
    fill = -(rows // 3) % 16
    return jnp.pad(jnp.stack([first, second]), ((0, 0), (0, 0), (0, fill), (0, 0)))


def unpack_shard(blocks, n):
    rows = D // n
    first, second = blocks[0, : rows // 3], blocks[1, : rows // 3]
    head = jnp.concatenate([first[:, : D // 3], first[:, D // 3 : 2 * D // 3], first[:, 2 * D // 3 :]], 0)
    vecs = second.reshape(rows // 3, n, rows).transpose(1, 0, 2).reshape(D // 3, rows)
    return head, vecs[:NVEC]


def local(
    lay,
    patches,
    patch_keep_mask,
    partner,
    matrices,
    matrix_first,
    matrix_second,
    matrix_average,
    head_weight,
    head_first,
    head_second,
    head_average,
    vectors,
    array_running_mean,
    vector_second,
    vector_average,
):
    n = lay.n
    pooled, mats16, head16, saved = forward(
        lay,
        matrices.astype(jnp.bfloat16),
        pack(lay, head_weight.astype(jnp.bfloat16), vectors.astype(jnp.bfloat16)),
        patches,
        patch_keep_mask,
    )
    projected = project(pooled, head16)
    unit_length_lines, unit_back = jax.vjp(normalize, projected)
    clip_count, width = unit_length_lines.shape
    lines = unit_length_lines.reshape(-1, 128)
    tile = jnp.pad(lines, ((0, -lines.shape[0] % 8), (0, 0)))
    everyone = spread(lay.dp, n, tile, 2)
    gathered = everyone[:, : lines.shape[0]].reshape(-1, width)

    def contrast(gathered_rows):
        pairwise_affinity_scores_raw = (
            jnp.dot(gathered_rows, gathered_rows.T, precision=lax.Precision.HIGHEST)
            / SCORE_SHARPNESS
        )
        clip_total = pairwise_affinity_scores_raw.shape[0]
        column = jnp.arange(clip_total)[None, :]
        pairwise_affinity_scores_raw = jnp.where(
            jnp.arange(clip_total)[:, None] == column, -1000000000.0, pairwise_affinity_scores_raw
        )
        positive = jnp.sum(
            jnp.where(column == partner[:, None], pairwise_affinity_scores_raw, 0.0), -1
        )
        return jnp.mean(jax.nn.logsumexp(pairwise_affinity_scores_raw, -1) - positive)

    contrastive_loss, objective_cotangent_flow = jax.vjp(contrast, gathered)
    (back_gathered,) = objective_cotangent_flow(jnp.ones_like(contrastive_loss))
    clip_count = projected.shape[0]
    offset = lax.axis_index(("dp", "fsdp")) * clip_count
    back_unit = lax.dynamic_slice_in_dim(back_gathered, offset, clip_count, 0)
    (back_projected,) = unit_back(back_unit)
    back_pooled, grad_head, unused_bias = project_back(pooled, head16, back_projected)
    finish, grad_vecs = backward(lay, mats16, saved, back_pooled)
    small = pack_all(grad_head, grad_vecs, n).astype(jnp.bfloat16)
    grad_mats, grad_small, tiles = finish(small)
    squared_norm = jnp.sum(tiles)
    grad_head, grad_vecs = unpack_shard(grad_small, n)
    factor = CLIP_AT / jnp.maximum(jnp.sqrt(squared_norm), CLIP_AT)
    mats_out = adamw_step(
        matrices, matrix_first, matrix_second, matrix_average, grad_mats, factor, RATE
    )
    head_out = adamw_step(
        head_weight, head_first, head_second, head_average, grad_head, factor, RATE
    )
    vecs_out = adamw_step(
        vectors, array_running_mean, vector_second, vector_average, grad_vecs, factor, VECTOR_RATE
    )
    return (
        contrastive_loss,
        squared_norm,
        mats_out[0],
        mats_out[1],
        mats_out[2],
        mats_out[3],
        head_out[0],
        head_out[1],
        head_out[2],
        head_out[3],
        vecs_out[0],
        vecs_out[1],
        vecs_out[2],
        vecs_out[3],
    )


def solution(mesh):
    planes = mesh.shape["dp"] // 2
    lay = Layout(mesh.shape["dp"], mesh.shape["fsdp"], 2 if planes == 2 else 0)
    placed = (
        P(("dp", "fsdp"), None, None, None),
        P(("dp", "fsdp"), None, None),
        P(),
        P(None, "fsdp", None),
        P(None, "fsdp", None),
        P(None, "fsdp", None),
        P(None, "fsdp", None),
        P("fsdp", None),
        P("fsdp", None),
        P("fsdp", None),
        P("fsdp", None),
        P(None, "fsdp"),
        P(None, "fsdp"),
        P(None, "fsdp"),
        P(None, "fsdp"),
    )
    return jax.shard_map(
        functools.partial(local, lay),
        mesh=mesh,
        in_specs=placed,
        out_specs=(
            P(),
            P(),
            P(None, "fsdp", None),
            P(None, "fsdp", None),
            P(None, "fsdp", None),
            P(None, "fsdp", None),
            P("fsdp", None),
            P("fsdp", None),
            P("fsdp", None),
            P("fsdp", None),
            P(None, "fsdp"),
            P(None, "fsdp"),
            P(None, "fsdp"),
            P(None, "fsdp"),
        ),
        check_vma=False,
    )
```

```python
import functools
import jax
import jax.numpy as jnp
from jax import lax
from jax.experimental import pallas as pl
from jax.experimental.pallas import tpu as pltpu
from jax.sharding import PartitionSpec as P

D = 768
H = 12
HD = 64
F = 8
S = 196
SP = 208
NMAT = 18
NVEC = 227
STEP = 10

SCORE_SHARPNESS = 0.07
CLIP_AT = 0.05
RATE = 0.01
VECTOR_RATE = 0.1
BETA_ONE = 0.9
BETA_TWO = 0.95
ADAM_EPSILON = 1e-08
DECAY = 0.05
AVERAGE_KEEP = 0.9

MESH = pl.DeviceIdType.MESH
ANY = pl.BlockSpec(memory_space=pl.ANY)


class Layout:
    def __init__(self, dp, fsdp, split):
        self.dp, self.n = dp, fsdp
        self.outer = 4 if fsdp % 4 == 0 else 1
        self.inner = fsdp // self.outer
        self.planes = dp // 2
        self.half = NMAT // 2
        self.split = split
        self.common = self.half - split * self.planes
        self.handled = self.common + split
        self.rows = D // fsdp

    def place(self):
        i = lax.axis_index("fsdp")
        d = lax.axis_index("dp")
        return i, lax.div(i, self.inner), lax.rem(i, self.inner), lax.div(d, 2), lax.rem(d, 2)

    def peer(self, i, y, c):
        return {"fsdp": i, "dp": y * 2 + c}

    def matrix(self, c, y, k):
        if k < self.common:
            return c * self.half + k
        return c * self.half + self.common + y * self.split + (k - self.common)


def turn(x, t, size):
    return lax.rem(x + t + size, size)


def greet(lay, i, a, b, y, c):
    barrier = pltpu.get_barrier_semaphore()
    others = [lay.peer(turn(a, t, lay.outer) * lay.inner + b, y, c) for t in range(1, lay.outer)]
    others += [lay.peer(a * lay.inner + turn(b, u, lay.inner), y, c) for u in range(1, lay.inner)]
    others += [lay.peer(i, turn(y, v, lay.planes), c) for v in range(1, lay.planes)]
    others += [lay.peer(i, y, 1 - c)]
    for other in others:
        pl.semaphore_signal(barrier, inc=1, device_id=other, device_id_type=MESH)
    pl.semaphore_wait(barrier, len(others))


def spread_kernel(dp, n, x_ref, o_ref, ssem, rsem):
    i, d = lax.axis_index("fsdp"), lax.axis_index("dp")
    me = d * n + i
    total = dp * n
    barrier = pltpu.get_barrier_semaphore()

    def other(t):
        j = lax.rem(me + t, total)
        return {"fsdp": lax.rem(j, n), "dp": lax.div(j, n)}

    @pl.loop(1, total)
    def _(t):
        pl.semaphore_signal(barrier, inc=1, device_id=other(t), device_id_type=MESH)

    pl.semaphore_wait(barrier, total - 1)

    @pl.loop(1, total)
    def _(t):
        pltpu.make_async_remote_copy(
            src_ref=x_ref, dst_ref=o_ref.at[me], send_sem=ssem.at[t], recv_sem=rsem.at[t], device_id=other(t), device_id_type=MESH
        ).start()

    o_ref[me] = x_ref[...]

    @pl.loop(1, total)
    def _(t):
        pltpu.make_async_remote_copy(
            src_ref=x_ref, dst_ref=o_ref.at[lax.rem(me - t + total, total)], send_sem=ssem.at[t], recv_sem=rsem.at[t], device_id=other(t), device_id_type=MESH
        ).wait()


def spread(dp, n, tile, number):
    vmem = pl.BlockSpec(memory_space=pltpu.VMEM)
    return pl.pallas_call(
        functools.partial(spread_kernel, dp, n),
        out_shape=jax.ShapeDtypeStruct((dp * n,) + tile.shape, tile.dtype),
        in_specs=[vmem],
        out_specs=vmem,
        scratch_shapes=[pltpu.SemaphoreType.DMA((dp * n,)), pltpu.SemaphoreType.DMA((dp * n,))],
        compiler_params=pltpu.CompilerParams(collective_id=number, has_side_effects=True),
    )(tile)


FB = 2
GROUP = 16
HALF = jnp.bfloat16
FULL = jnp.float32
NORM_EPS = 1e-06
MASKED = -1000000000.0
NEVER = -3e38


def dot(a, b):
    return lax.dot_general(a, b, (((1,), (0,)), ((), ())), preferred_element_type=FULL)


def dot_back(a, b):
    return lax.dot_general(a, b, (((1,), (1,)), ((), ())), preferred_element_type=FULL)


def dot_rows(a, b):
    return lax.dot_general(a, b, (((0,), (0,)), ((), ())), preferred_element_type=FULL)


def mean(x):
    return jnp.sum(x, -1, keepdims=True) * (1.0 / D)


def norm(x, gain, shift):
    centred = x - mean(x)
    scale = lax.rsqrt(mean(centred * centred) + NORM_EPS)
    return centred * scale * gain + shift


def norm_back(x, gain, back):
    centred = x - mean(x)
    scale = lax.rsqrt(mean(centred * centred) + NORM_EPS)
    unit = centred * scale
    inner = back * gain
    return scale * (inner - mean(inner) - unit * mean(inner * unit)), back * unit


def normal_cdf(x):
    size = jnp.abs(x) * 0.7071067811865476
    t = pl.reciprocal(1.0 + 0.3275911 * size)
    bell = jnp.exp(-0.5 * x * x)
    poly = ((((1.061405429 * t - 1.453152027) * t + 1.421413741) * t - 0.284496736) * t + 0.254829592) * t
    tail = 0.5 * poly * bell
    return jnp.where(x < 0, tail, 1.0 - tail), bell


def gelu(x):
    below, bell = normal_cdf(x)
    return x * below, below + x * bell * 0.3989422804014327


def column_sum(x):
    return jnp.sum(x.astype(FULL), 0, keepdims=True)


def flat(ref):
    x = ref[...]
    return x.reshape(-1, x.shape[-1])


def row_of(rows):
    return lax.rem(lax.broadcasted_iota(jnp.int32, (rows, 1), 0), SP)


def row_share(rows):
    place = row_of(rows)
    return jnp.where(place < S, 1.0, jnp.where(place == S, 1.0 / F, 0.0))


def first_step():
    return pl.program_id(0) == 0


def add_rows(ref, values):
    @pl.when(first_step())
    def _():
        ref[...] = jnp.zeros_like(ref)

    for k, value in enumerate(values):
        if value is not None:
            ref[k : k + 1, :] += value


def pair_lanes(x, low):
    zero = jnp.zeros_like(x)
    return jnp.concatenate([jnp.where(low, x, zero), jnp.where(low, zero, x)], 0)


def attend(q, k, v, fill):
    rows = q.shape[0]
    low = lax.broadcasted_iota(jnp.int32, (rows, 128), 1) < HD
    stacked = pair_lanes(q * jnp.asarray(HD ** (-0.5), HALF), low)
    scores = dot_back(stacked, k)
    if fill.shape[0] != 1:
        fill = jnp.concatenate([fill, fill], 0)
    scores = jnp.where(fill == 0.0, scores, fill)
    expanded = jnp.exp(scores - jnp.max(scores, -1, keepdims=True))
    share = pl.reciprocal(jnp.sum(expanded, -1, keepdims=True))
    mixed = dot((expanded * share).astype(HALF), v)
    return jnp.where(low, mixed[:rows], mixed[rows:])


def attend_back(q, k, v, back, fill):
    rows = q.shape[0]
    low = lax.broadcasted_iota(jnp.int32, (rows, 128), 1) < HD
    stacked = pair_lanes(q * jnp.asarray(HD ** (-0.5), HALF), low)
    backs = pair_lanes(back, low)
    scores = dot_back(k, stacked)
    scores = jnp.where(fill == 0.0, scores, fill)
    expanded = jnp.exp(scores - jnp.max(scores, 0, keepdims=True))
    chances = expanded * pl.reciprocal(jnp.sum(expanded, 0, keepdims=True))
    back_chances = dot_back(v, backs)
    inner = jnp.sum(back_chances * chances, 0, keepdims=True)
    back_scores = (chances * (back_chances - inner)).astype(HALF)
    back_keys = dot(back_scores, stacked)
    back_values = dot(chances.astype(HALF), backs)
    queries = dot_rows(back_scores, k) * HD ** (-0.5)
    return jnp.where(low, queries[:rows], queries[rows:]), back_keys, back_values


def embed_kernel(p_ref, w0, w1, w2, w3, v_ref, pos_ref, time_ref, pad_ref, x_ref, a_ref, q_ref, k_ref, b_ref):
    pad_ref[:, SP - GROUP :, :] = jnp.zeros((FB, GROUP, D), HALF)
    for f in range(FB):
        pad_ref[f, :S, :] = p_ref[0, f]
    pos = pos_ref[...]
    here = jnp.concatenate([pos + time_ref[f] for f in range(FB)], 0)
    x = dot(flat(pad_ref), w0[0]) + v_ref[9:10] + here
    x_ref[...] = x.reshape(FB, SP, D)
    a = norm(x, v_ref[22:23], v_ref[23:24]).astype(HALF)
    a_ref[...] = a.reshape(FB, SP, D)
    q_ref[...] = (dot(a, w1[0]) + v_ref[10:11]).astype(HALF).reshape(FB, SP, D)
    k_ref[...] = dot(a, w2[0]).astype(HALF).reshape(FB, SP, D)
    b_ref[...] = (dot(a, w3[0]) + v_ref[11:12]).astype(HALF).reshape(FB, SP, D)


def time_kernel(q_ref, k_ref, v_ref, fill_ref, o_ref):
    rows = F * GROUP
    for p in range(H // 2):
        lanes = slice(128 * p, 128 * p + 128)
        q, k, v = (ref[:, :, lanes].reshape(rows, 128) for ref in (q_ref, k_ref, v_ref))
        o_ref[:, :, lanes] = attend(q, k, v, fill_ref[0]).astype(HALF).reshape(F, GROUP, 128)


def space_kernel(o_ref, x_ref, w0, w1, w2, w3, w4, v_ref, fill_ref, y_ref, xs_ref, a_ref, q_ref, k_ref, b_ref, os_ref, cls_ref):
    rows = FB * SP
    y = (dot(flat(o_ref), w0[0]) + v_ref[12:13]).astype(HALF)
    y_ref[...] = y.reshape(FB, SP, D)
    x = flat(x_ref) + dot(y, w1[0]) + v_ref[13:14]
    x = jnp.where(row_of(rows) == S, v_ref[0:1] + v_ref[30:31], x)
    xs_ref[...] = x.reshape(FB, SP, D)
    a = norm(x, v_ref[24:25], v_ref[25:26]).astype(HALF)
    a_ref[...] = a.reshape(FB, SP, D)
    q_ref[...] = (dot(a, w2[0]) + v_ref[14:15]).astype(HALF).reshape(FB, SP, D)
    k_ref[...] = dot(a, w3[0]).astype(HALF).reshape(FB, SP, D)
    b_ref[...] = (dot(a, w4[0]) + v_ref[15:16]).astype(HALF).reshape(FB, SP, D)
    for f in range(FB):
        for p in range(H // 2):
            lanes = slice(128 * p, 128 * p + 128)
            mixed = attend(q_ref[f, :, lanes], k_ref[f, :, lanes], b_ref[f, :, lanes], fill_ref[f])
            os_ref[f, :, lanes] = mixed.astype(HALF)
            cls_ref[f, :, lanes] = mixed[S : S + 8]


def mlp_kernel(o_ref, cls_ref, xs_ref, wp_ref, u0, u1, u2, u3, e0, e1, e2, e3, v_ref, of_ref, x2_ref, a_ref, g_ref, e_ref, x3_ref, pool_ref):
    rows = FB * SP
    middle = sum(cls_ref[f, 0:1, :] for f in range(F)) * (1.0 / F)
    o = jnp.where(row_of(rows) == S, middle, flat(o_ref).astype(FULL)).astype(HALF)
    of_ref[...] = o.reshape(FB, SP, D)
    x2 = flat(xs_ref) + dot(o, wp_ref[0]) + v_ref[16:17]
    x2_ref[...] = x2.reshape(FB, SP, D)
    a = norm(x2, v_ref[26:27], v_ref[27:28]).astype(HALF)
    a_ref[...] = a.reshape(FB, SP, D)
    x3 = x2 + v_ref[21:22]
    for k in range(4):
        g = dot(a, (u0, u1, u2, u3)[k][0]) + v_ref[17 + k : 18 + k]
        e, slope = gelu(g)
        g_ref[k] = slope.reshape(FB, SP, D)
        e = e.astype(HALF)
        e_ref[k] = e.reshape(FB, SP, D)
        x3 = x3 + dot(e, (e0, e1, e2, e3)[k][0])
    x3_ref[...] = x3.reshape(FB, SP, D)
    final = norm(x3, v_ref[28:29], v_ref[29:30]) * row_share(FB * SP)
    add_rows(pool_ref, [column_sum(final)])


def mlp_back_kernel(x3_ref, x2_ref, g_ref, d_ref, wp_ref, u0, u1, u2, u3, e0, e1, e2, e3, v_ref, q_ref, k_ref, b_ref, fill_ref,
                    r3_ref, dg_ref, d2_ref, r2_ref, dq_ref, dk_ref, dv_ref, cq_ref, ck_ref, cv_ref, sum_ref, do_ref):
    top = d_ref[0:1] * row_share(FB * SP)
    d3, unit = norm_back(flat(x3_ref), v_ref[28:29], top)
    sums = [column_sum(unit), column_sum(top)]
    r3 = d3.astype(HALF)
    r3_ref[...] = r3.reshape(FB, SP, D)
    sums.append(column_sum(r3))
    back = None
    for k in range(4):
        dg = (dot_back(r3, (e0, e1, e2, e3)[k][0]) * flat(g_ref.at[k])).astype(HALF)
        dg_ref[k] = dg.reshape(FB, SP, D)
        sums.append(column_sum(dg))
        part = dot_back(dg, (u0, u1, u2, u3)[k][0])
        back = part if back is None else back + part
    d2, unit = norm_back(flat(x2_ref), v_ref[26:27], back)
    sums += [column_sum(unit), column_sum(back)]
    d2 = d2 + d3
    d2_ref[...] = d2.reshape(FB, SP, D)
    r2 = d2.astype(HALF)
    r2_ref[...] = r2.reshape(FB, SP, D)
    sums.append(column_sum(r2))
    add_rows(sum_ref, sums)
    do_ref[...] = dot_back(r2, wp_ref[0]).astype(HALF).reshape(FB, SP, D)
    for f in range(FB):
        for p in range(H // 2):
            lanes = slice(128 * p, 128 * p + 128)
            outs = attend_back(q_ref[f, :, lanes], k_ref[f, :, lanes], b_ref[f, :, lanes], do_ref[f, :, lanes], fill_ref[f][:, 0:1])
            for value, ref, cls in zip(outs, (dq_ref, dk_ref, dv_ref), (cq_ref, ck_ref, cv_ref)):
                ref[f, :, lanes] = value.astype(HALF)
                cls[f, :, lanes] = value[S : S + 8]


def space_back_kernel(dq_ref, dk_ref, dv_ref, cls_ref, xs_ref, d2_ref, w0, w1, w2, w3, w4, v_ref, fq_ref, fk_ref, fv_ref, d1_ref, r1_ref, dy_ref, do_ref, sum_ref):
    frames = xs_ref.shape[0]
    rows = frames * SP
    is_class = row_of(rows) == S
    grads = []
    for k, (ref, out) in enumerate(zip((dq_ref, dk_ref, dv_ref), (fq_ref, fk_ref, fv_ref))):
        grad = jnp.where(is_class, cls_ref[k : k + 1], flat(ref).astype(FULL)).astype(HALF)
        out[...] = grad.reshape(frames, SP, D)
        grads.append(grad)
    back = dot_back(grads[0], w2[0]) + dot_back(grads[1], w3[0]) + dot_back(grads[2], w4[0])
    d, unit = norm_back(flat(xs_ref), v_ref[24:25], back)
    sums = [column_sum(grads[0]), column_sum(grads[2]), column_sum(unit), column_sum(back)]
    d = d + flat(d2_ref)
    kept = jnp.where(is_class, d, 0.0)
    sums.append(column_sum(kept))
    d = d - kept
    d1_ref[...] = d.reshape(frames, SP, D)
    r1 = d.astype(HALF)
    r1_ref[...] = r1.reshape(frames, SP, D)
    sums.append(column_sum(r1))
    dy = dot_back(r1, w1[0]).astype(HALF)
    dy_ref[...] = dy.reshape(frames, SP, D)
    sums.append(column_sum(dy))
    do_ref[...] = dot_back(dy, w0[0]).astype(HALF).reshape(frames, SP, D)
    add_rows(sum_ref, sums)


def time_back_kernel(q_ref, k_ref, v_ref, d_ref, fill_ref, dq_ref, dk_ref, dv_ref):
    rows = F * GROUP
    fill = jnp.concatenate([fill_ref[0], fill_ref[0]], 1)
    for p in range(H // 2):
        lanes = slice(128 * p, 128 * p + 128)
        q, k, v, d = (ref[:, :, lanes].reshape(rows, 128) for ref in (q_ref, k_ref, v_ref, d_ref))
        for value, ref in zip(attend_back(q, k, v, d, fill), (dq_ref, dk_ref, dv_ref)):
            ref[:, :, lanes] = value.astype(HALF).reshape(F, GROUP, 128)


def embed_back_kernel(dq_ref, dk_ref, dv_ref, x_ref, d1_ref, w1, w2, w3, v_ref, r_ref, pos_ref, time_ref, sum_ref):
    q, v = flat(dq_ref), flat(dv_ref)
    back = dot_back(q, w1[0]) + dot_back(flat(dk_ref), w2[0]) + dot_back(v, w3[0])
    d, unit = norm_back(flat(x_ref), v_ref[22:23], back)
    d = d + flat(d1_ref)
    rounded = d.astype(HALF)
    r_ref[...] = rounded.reshape(FB, SP, D)
    add_rows(sum_ref, [column_sum(q), column_sum(v), column_sum(unit), column_sum(back), column_sum(rounded)])

    @pl.when(first_step())
    def _():
        pos_ref[...] = jnp.zeros_like(pos_ref)

    total = jnp.zeros((SP, D), FULL)
    for f in range(FB):
        part = d[f * SP : (f + 1) * SP]
        time_ref[f] = column_sum(part)
        total = total + part
    pos_ref[...] += total


def shape(*dims, dtype=HALF):
    return jax.ShapeDtypeStruct(dims, dtype)


FRAMES = pl.BlockSpec((FB, SP, D), lambda i: (i, 0, 0))
HIDDEN = pl.BlockSpec((4, FB, SP, D), lambda i: (0, i, 0, 0))
SLAB = pl.BlockSpec((F, GROUP, D), lambda i: (0, i, 0))
ROWS16 = shape(F, SP, D)
ROWS32 = shape(F, SP, D, dtype=FULL)
HIDDEN16 = shape(4, F, SP, D)
HIDDEN32 = shape(4, F, SP, D, dtype=FULL)


def whole(*dims):
    return pl.BlockSpec(dims, lambda i: (0,) * len(dims), pipeline_mode=pl.Buffered(1))


def matrix(m):
    return pl.BlockSpec((1, D, D), lambda i: (m, 0, 0), pipeline_mode=pl.Buffered(1))


def matrices(first, count):
    return [matrix(m) for m in range(first, first + count)]


def summed(rows):
    return pl.BlockSpec((rows, D), lambda i: (0, 0))


def call(kernel, steps, in_specs, out_specs, out_shape, scratch=()):
    return pl.pallas_call(
        kernel,
        grid=(steps,),
        in_specs=in_specs,
        out_specs=out_specs,
        out_shape=out_shape,
        scratch_shapes=list(scratch),
        compiler_params=pltpu.CompilerParams(vmem_limit_bytes=60 * 2**20),
    )


def per_frame(*tail):
    return pl.BlockSpec((FB,) + tail, lambda i: (i,) + (0,) * len(tail))


class Part:
    def __init__(self, lay, first, half, split):
        self.first, self.half, self.split = first, half, split
        self.common = half - split * lay.planes

    def order(self):
        return list(range(self.common, self.half)) + list(range(self.common))


class Sums:
    def __init__(self, refs, common, split):
        (self.g, self.r, self.ys, self.yr, self.xs, self.xr, self.zs, self.zr, self.fin, self.every) = refs[:10]
        (self.rs, self.rr, self.yss, self.yrs, self.xss, self.xrs, self.zss, self.zrs, self.fsem) = refs[10:]
        self.common, self.split = common, split


SUMS = 19


def sums_scratch(lay, rows, common, split):
    A, B, Y, n = lay.outer, lay.inner, lay.planes, lay.n
    slots, kept, passed, K = common + split * Y, max(split, 1), max(Y - 1, 1), common + split
    dma = pltpu.SemaphoreType.DMA
    width, depth = (rows, n) if split else (16, 1)
    crossed, along = max(B - 1, 1), max(A - 1, 1)
    return [
        pltpu.VMEM((slots, 2, n, rows, D), HALF), pltpu.VMEM((slots, n, rows, D), HALF),
        pltpu.VMEM((passed, kept, depth, width, D), HALF), pltpu.VMEM((passed, kept, depth, width, D), HALF),
        pltpu.VMEM((K, crossed, A, rows, D), HALF), pltpu.VMEM((K, crossed, A, rows, D), HALF),
        pltpu.VMEM((K, along, rows, D), HALF), pltpu.VMEM((K, along, rows, D), HALF),
        pltpu.VMEM((K, rows, D), FULL), pltpu.VMEM((Y, common, rows, D), FULL),
        dma((slots,)), dma((slots,)), dma((passed, kept)), dma((passed, kept)),
        dma((K, crossed, A)), dma((K, crossed, A)), dma((K, along)), dma((K, along)), dma((5, K, Y)),
    ]


def other_device(lay, me, t):
    j = lax.rem(me + t, lay.dp * lay.n)
    return {"fsdp": lax.rem(j, lay.n), "dp": lax.div(j, lay.n)}


def greet_all(lay, me):
    barrier = pltpu.get_barrier_semaphore()

    @pl.loop(1, lay.dp * lay.n)
    def _(t):
        pl.semaphore_signal(barrier, inc=1, device_id=other_device(lay, me, t), device_id_type=MESH)

    pl.semaphore_wait(barrier, lay.dp * lay.n - 1)


class Reducer:
    def __init__(self, lay, squares, everyone):
        self.lay = lay
        self.squares = squares
        self.i, self.a, self.b, self.y, self.c = lay.place()
        self.here = lay.peer(self.i, self.y, 1 - self.c)
        self.pending = []
        if everyone:
            greet_all(lay, lax.axis_index("dp") * lay.n + self.i)
        else:
            greet(lay, self.i, self.a, self.b, self.y, self.c)

    def square(self, value, share):
        self.squares[...] += jnp.sum((value * value).reshape(-1, 8, D), 0) * share

    def remote(self, src, dst, sends, at, recvs, dev, like):
        pltpu.make_async_remote_copy(
            src_ref=src, dst_ref=dst, send_sem=sends.at[at], recv_sem=recvs[0].at[recvs[1]], device_id=dev, device_id_type=MESH
        ).start()
        self.pending.append((like, sends, at, True))

    def wait_all(self):
        for make, sems, at, remote in self.pending:
            like = make()
            if remote:
                pltpu.make_async_remote_copy(
                    src_ref=like, dst_ref=like, send_sem=sems.at[at], recv_sem=sems.at[at], device_id=self.here, device_id_type=MESH
                ).wait_send()
            else:
                pltpu.make_async_copy(like, like, sems.at[at]).wait()

    def landed(self, dst, sems, *at):
        pltpu.make_async_remote_copy(
            src_ref=dst, dst_ref=dst, send_sem=sems.at[at], recv_sem=sems.at[at], device_id=self.here, device_id_type=MESH
        ).wait_recv()

    def slot(self, st, v, q):
        if v is None:
            return q
        return st.common + turn(self.y, v, self.lay.planes) * st.split + q

    def hand(self, st, h):
        self.remote(st.g.at[h, 1 - self.c], st.r.at[h], st.rs, (h,), (st.rr, (h,)), self.here, lambda: st.r.at[h])

    def base(self, st, v, q, j):
        n = self.slot(st, v, q)
        total = st.g[n, self.c, j].astype(FULL) + st.r[n, j].astype(FULL)
        if v == 0:
            for w in range(1, self.lay.planes):
                total = total + st.yr[w - 1, q, j].astype(FULL)
        return total

    def pass_on(self, st, v, q):
        n = self.slot(st, v, q)
        self.landed(st.r.at[n], st.rr, n)

        @pl.loop(0, self.lay.n)
        def _(j):
            st.ys[v - 1, q, j] = self.base(st, v, q, j).astype(HALF)

        self.remote(
            st.ys.at[v - 1, q], st.yr.at[v - 1, q], st.yss, (v - 1, q), (st.yrs, (v - 1, q)),
            self.lay.peer(self.i, turn(self.y, v, self.lay.planes), self.c), lambda: st.ys.at[v - 1, q],
        )

    def item(self, st, v, q):
        return q if v is None else st.common + q

    def cross(self, st, target, v, q):
        k, n = self.item(st, v, q), self.slot(st, v, q)
        self.landed(st.r.at[n], st.rr, n)
        if v == 0:
            for w in range(1, self.lay.planes):
                self.landed(st.yr.at[w - 1, q], st.yrs, w - 1, q)
        outer, inner = self.lay.outer, self.lay.inner
        for t in list(range(1, outer)) + [0]:
            e = turn(self.a, t, outer)
            for u in range(1, inner):
                other = turn(self.b, u, inner)
                st.xs[k, u - 1, e] = self.base(st, v, q, e * inner + other).astype(HALF)
                self.remote(
                    st.xs.at[k, u - 1, e], st.xr.at[k, u - 1, e], st.xss, (k, u - 1, t), (st.xrs, (k, u - 1, t)),
                    self.lay.peer(self.a * inner + other, self.y, self.c), lambda u=u: st.xs.at[k, u - 1, 0],
                )

    def along(self, st, target, v, q):
        k = self.item(st, v, q)
        inner, outer = self.lay.inner, self.lay.outer
        for t in list(range(1, outer)) + [0]:
            e = turn(self.a, t, outer)
            value = self.base(st, v, q, e * inner + self.b)
            for u in range(1, inner):
                self.landed(st.xr.at[k, u - 1, e], st.xrs, k, u - 1, t)
                value = value + st.xr[k, u - 1, e].astype(FULL)
            if t == 0:
                st.fin[k] = value
                continue
            st.zs[k, t - 1] = value.astype(HALF)
            self.remote(
                st.zs.at[k, t - 1], st.zr.at[k, t - 1], st.zss, (k, t - 1), (st.zrs, (k, t - 1)),
                self.lay.peer(e * inner + self.b, self.y, self.c), lambda t=t: st.zs.at[k, t - 1],
            )

    def close(self, st, target, v, q):
        k, Y = self.item(st, v, q), self.lay.planes
        for t in range(1, self.lay.outer):
            self.landed(st.zr.at[k, t - 1], st.zrs, k, t - 1)
        value = st.fin[k]
        for t in range(1, self.lay.outer):
            value = value + st.zr[k, t - 1].astype(FULL)
        if v is None:
            st.every[self.y, k] = value
            source, landing = st.every.at[self.y, k], st.every.at[self.y, k]
            like = lambda: st.every.at[0, k]
        else:
            st.fin[k] = value
            self.square(value, 1.0)
            source = st.fin.at[k]
            like = lambda: st.fin.at[k]
            landing = target(self.c, self.slot(st, v, q))
        for w in range(1, Y):
            self.remote(source, landing, st.fsem, (0, k, w), (st.fsem, (1, k, w)), self.lay.peer(self.i, turn(self.y, w, Y), self.c), like)
        if v is not None:
            self.finish(st, k, landing)

    def finish(self, st, k, landing):
        pltpu.make_async_copy(st.fin.at[k], landing, st.fsem.at[2, k, 0]).start()
        self.pending.append((lambda: st.fin.at[k], st.fsem, (2, k, 0), False))
        self.remote(st.fin.at[k], landing, st.fsem, (3, k, 0), (st.fsem, (4, k, 0)), self.here, lambda: st.fin.at[k])

    def merge(self, st, target, v, q):
        k, Y = self.item(st, v, q), self.lay.planes
        if v is None:
            for w in range(1, Y):
                self.landed(st.every.at[turn(self.y, -w, Y), k], st.fsem, 1, k, w)
            value = st.every[0, k]
            for w in range(1, Y):
                value = value + st.every[w, k]
            st.fin[k] = value
            self.square(value, 1.0 / Y)
            self.finish(st, k, target(self.c, q))
        else:
            for w in range(1, Y):
                back = target(self.c, self.slot(st, -w, q))
                self.landed(back, st.fsem, 1, k, w)
                self.remote(back, back, st.fsem, (3, k, w), (st.fsem, (4, k, w)), self.here, lambda: target(0, 0))

    def last(self, st, target, v, q):
        k = self.item(st, v, q)
        self.landed(target(1 - self.c, self.slot(st, v, q)), st.fsem, 4, k, 0)
        if v is not None:
            for w in range(1, self.lay.planes):
                self.landed(target(1 - self.c, self.slot(st, -w, q)), st.fsem, 4, k, w)

    def progress(self, work, step):
        for lag, stage in enumerate((self.cross, self.along, self.close, self.merge)):
            if 0 <= step - lag < len(work):
                stage(*work[step - lag])

    def done(self, work):
        for job in work:
            self.last(*job)
        self.wait_all()


def outer_products(rows, operands, jobs, st, after, a_buf, b_buf, sems):
    n = st.g.shape[2]
    lefts, rights, plan = [], [], []
    for slot, core, left, right in jobs:
        fresh = [not lefts or lefts[-1] != left, not rights or rights[-1] != right]
        if fresh[0]:
            lefts.append(left)
        if fresh[1]:
            rights.append(right)
        plan.append((slot, core, len(lefts) - 1, len(rights) - 1, fresh))

    def load(kind, loads, k):
        number, block = loads[k]
        buf = (a_buf, b_buf)[kind]
        return pltpu.make_async_copy(operands[number].at[pl.ds(block * rows, rows)], buf.at[k % 2], sems.at[kind, k % 2])

    load(0, lefts, 0).start()
    load(1, rights, 0).start()
    for slot, core, left, right, fresh in plan:
        if fresh[0]:
            load(0, lefts, left).wait()
        if fresh[1]:
            load(1, rights, right).wait()
        if fresh[0] and left + 1 < len(lefts):
            load(0, lefts, left + 1).start()
        if fresh[1] and right + 1 < len(rights):
            load(1, rights, right + 1).start()
        value = dot_rows(a_buf[left % 2], b_buf[right % 2])
        st.g[slot, core] = value.reshape(n, -1, D).astype(HALF)
        if core == 1:
            after(slot)


def product_buffers(rows):
    return [
        pltpu.VMEM((2, rows, D), HALF), pltpu.VMEM((2, rows, D), HALF), pltpu.SemaphoreType.DMA((2, 2)),
    ]


def product_jobs(part, pairs):
    return [(h, core, *pairs[2 * h + core]) for h in part.order() for core in range(2)]


def part_work(lay, part, st, target):
    return [(st, target, None, k) for k in range(part.common)] + [(st, target, 0, q) for q in range(part.split)]


def products_and_hand(red, part, st, work, operands, jobs, buffers):
    passed = [(v, q) for v in range(1, red.lay.planes) for q in range(part.split)]
    order = part.order()
    ahead = len(work) - part.common - part.split

    def after(h):
        red.hand(st, h)
        place = order.index(h) - (part.half - part.common)
        if place == 0 or part.common == 0 and h == order[-1]:
            for v, q in passed:
                red.pass_on(st, v, q)
        if place >= 1 - ahead and place + ahead - 1 < steps_beside(part, ahead):
            red.progress(work, place + ahead - 1)

    outer_products(F * SP, operands, jobs, st, after, *buffers)


def steps_beside(part, ahead):
    return max(part.common + ahead - 1, 0)


def early_kernel(lay, part, pairs, *refs):
    (e_ref, r3_ref, a2_ref, dg_ref, dq_ref, dk_ref, dv_ref, cq_ref, ck_ref, cv_ref, sum1_ref, xs_ref, d2_ref, qt_ref, kt_ref, vt_ref, fill_ref, x0_ref, mats_ref, v_ref) = refs[:20]
    (og_ref, fq_ref, fk_ref, fv_ref, d1_ref, r1_ref, dy_ref, do_ref, tq_ref, tk_ref, tv_ref, rp_ref, vec_ref, sq_ref) = refs[20:34]
    red = Reducer(lay, sq_ref, False)
    sq_ref[...] = jnp.zeros_like(sq_ref)
    st = Sums(refs[34 : 34 + SUMS], part.common, part.split)
    w_buf, w_sem, cls_ref, sum2_ref, pos_ref, time_ref, sum3_ref = refs[34 + SUMS :]
    for k, ref in enumerate((cq_ref, ck_ref, cv_ref)):
        total = sum(ref[f, 0:1, :] for f in range(F))
        cls_ref[k : k + 1, :] = total.astype(HALF).astype(FULL) * (1.0 / F)
    load = pltpu.make_async_copy(mats_ref.at[pl.ds(1, 8)], w_buf, w_sem.at[0])
    load.start()

    def target(core, h):
        return og_ref.at[part.first + 2 * h + core]

    work = part_work(lay, part, st, target)
    rows = F * SP
    jobs = product_jobs(part, pairs)
    pl.run_scoped(lambda *buffers: products_and_hand(red, part, st, work, (e_ref, r3_ref, a2_ref, dg_ref), jobs, buffers), *product_buffers(rows))
    begun = steps_beside(part, 0)
    load.wait()
    ws = [w_buf.at[pl.ds(k, 1)] for k in range(8)]

    steps = F // FB

    def space(dq, dk, dv, xs, d2, fq, fk, fv, d1, r1, dy, do):
        space_back_kernel(dq, dk, dv, cls_ref, xs, d2, ws[3], ws[4], ws[5], ws[6], ws[7], v_ref, fq, fk, fv, d1, r1, dy, do, sum2_ref)
        for s, place in enumerate((1, 3)):
            @pl.when(pl.program_id(0) == place)
            def _():
                red.progress(work, begun + s)

    pltpu.emit_pipeline(space, grid=(steps,), in_specs=[FRAMES] * 5, out_specs=[FRAMES] * 7)(
        dq_ref, dk_ref, dv_ref, xs_ref, d2_ref, fq_ref, fk_ref, fv_ref, d1_ref, r1_ref, dy_ref, do_ref
    )

    def time(q, k, v, d, fill, dq, dk, dv):
        time_back_kernel(q, k, v, d, fill, dq, dk, dv)

        for s, place in enumerate((6, 12)):
            @pl.when(pl.program_id(0) == place)
            def _():
                red.progress(work, begun + 2 + s)

    pltpu.emit_pipeline(time, grid=(SP // GROUP,), in_specs=[SLAB] * 4 + [FILL], out_specs=[SLAB] * 3)(
        qt_ref, kt_ref, vt_ref, do_ref, fill_ref, tq_ref, tk_ref, tv_ref
    )

    def embed(dq, dk, dv, x, d1, r):
        place = time_ref.at[pl.ds(pl.program_id(0) * FB, FB)]
        embed_back_kernel(dq, dk, dv, x, d1, ws[0], ws[1], ws[2], v_ref, r, pos_ref, place, sum3_ref)

        @pl.when(pl.program_id(0) == 3)
        def _():
            red.progress(work, begun + 4)

    pltpu.emit_pipeline(embed, grid=(steps,), in_specs=[FRAMES] * 5, out_specs=[FRAMES])(
        tq_ref, tk_ref, tv_ref, x0_ref, d1_ref, rp_ref
    )
    vec_ref[...] = jnp.zeros_like(vec_ref)
    for row, ref, first, count in (
        (0, sum2_ref, 4, 1), (9, sum3_ref, 4, 1), (10, sum3_ref, 0, 2), (12, sum2_ref, 6, 1), (13, sum2_ref, 5, 1), (14, sum2_ref, 0, 2),
        (16, sum1_ref, 9, 1), (17, sum1_ref, 3, 4), (21, sum1_ref, 2, 1), (22, sum3_ref, 2, 2), (24, sum2_ref, 2, 2), (26, sum1_ref, 7, 2),
        (28, sum1_ref, 0, 2), (30, sum2_ref, 4, 1), (31, pos_ref, 0, S),
    ):
        vec_ref[row : row + count, :] = ref[first : first + count, :]
    for f in range(F):
        vec_ref[1 + f : 2 + f, :] = time_ref[f]
    for s in range(begun + 5, len(work) + 3):
        red.progress(work, s)
    red.done(work)


FILL = pl.BlockSpec((1, F * GROUP, F * GROUP), lambda i: (i, 0, 0))


def early(lay, part, pairs, arrays, classes, table):
    vmem = pl.BlockSpec(memory_space=pltpu.VMEM)
    e, r3, a2, dg, dq, dk, dv, xs, d2, qt, kt, vt, fill, x0, mats = arrays
    two = lambda x: x.reshape(-1, D)
    full = functools.partial(shape, dtype=FULL)
    return pl.pallas_call(
        functools.partial(early_kernel, lay, part, pairs),
        in_specs=[ANY] * 7 + [vmem] * 4 + [ANY] * 8 + [vmem],
        out_specs=[ANY] * 12 + [vmem, vmem],
        out_shape=[full(NMAT, lay.rows, D), ROWS16, ROWS16, ROWS16, ROWS32] + [ROWS16] * 7 + [full(D // 3, D), full(8, D)],
        scratch_shapes=sums_scratch(lay, lay.rows, part.common, part.split) + [pltpu.VMEM((8, D, D), HALF), pltpu.SemaphoreType.DMA((1,))]
        + [pltpu.VMEM(dims, FULL) for dims in ((8, D), (16, D), (SP, D), (F, 1, D), (16, D))],
        compiler_params=pltpu.CompilerParams(collective_id=1, has_side_effects=True, vmem_limit_bytes=62 * 2**20),
    )(two(e), two(r3), two(a2), two(dg), dq, dk, dv, *classes, xs, d2, qt, kt, vt, fill, x0, mats, table)


def late_kernel(lay, part, pairs, count, *refs):
    s_ref, sq_ref, operands = refs[0], refs[1], refs[3 : 3 + count]
    og_ref, os_ref, tiles_ref = refs[3 + count : 6 + count]
    rest = refs[6 + count : -4]
    squares, tile, tile_sent, tile_come = refs[-4:]
    red = Reducer(lay, squares, True)
    squares[...] = sq_ref[...]
    st = Sums(rest[:SUMS], part.common, part.split)
    little = Sums(rest[SUMS : 2 * SUMS], 1, 0)
    small_sem = rest[2 * SUMS]
    load = pltpu.make_async_copy(s_ref, little.g.at[0], small_sem.at[0])
    load.start()

    def target(core, h):
        return og_ref.at[part.first + 2 * h + core]

    work = part_work(lay, part, st, target)
    work = [(little, lambda core, h: os_ref.at[core], None, 0)] + work
    rows = F * SP
    jobs = product_jobs(part, pairs)
    load.wait()
    red.hand(little, 0)
    pl.run_scoped(lambda *buffers: products_and_hand(red, part, st, work, operands, jobs, buffers), *product_buffers(rows))
    for s in range(steps_beside(part, 1), len(work) + 3):
        red.progress(work, s)
    tile[...] = sum(squares[:, e * 128 : e * 128 + 128] for e in range(D // 128))
    me, total = lax.axis_index("dp") * lay.n + red.i, lay.dp * lay.n

    def swap(t, place):
        return pltpu.make_async_remote_copy(
            src_ref=tile, dst_ref=tiles_ref.at[place], send_sem=tile_sent.at[t], recv_sem=tile_come.at[t],
            device_id=other_device(lay, me, t), device_id_type=MESH,
        )

    @pl.loop(1, total)
    def _(t):
        swap(t, me).start()

    tiles_ref[me] = tile[...]
    red.done(work)

    @pl.loop(1, total)
    def _(t):
        swap(t, lax.rem(me - t + total, total)).wait()


def late(lay, part, pairs, small, squares, sums, arrays):
    full = functools.partial(shape, dtype=FULL)
    vmem = pl.BlockSpec(memory_space=pltpu.VMEM)
    everyone = lay.dp * lay.n
    dma = pltpu.SemaphoreType.DMA
    return pl.pallas_call(
        functools.partial(late_kernel, lay, part, pairs, len(arrays)),
        in_specs=[ANY, vmem] + [ANY] * (1 + len(arrays)),
        out_specs=[ANY, ANY, vmem],
        out_shape=[full(NMAT, lay.rows, D), full(2, small.shape[2], D), full(everyone, 8, 128)],
        scratch_shapes=sums_scratch(lay, lay.rows, part.common, part.split) + sums_scratch(lay, small.shape[2], 1, 0)
        + [dma((1,)), pltpu.VMEM((8, D), FULL), pltpu.VMEM((8, 128), FULL), dma((everyone,)), dma((everyone,))],
        input_output_aliases={2: 0},
        compiler_params=pltpu.CompilerParams(collective_id=4, has_side_effects=True, vmem_limit_bytes=62 * 2**20),
    )(small, squares, sums, *[x.reshape(-1, D) for x in arrays])


AHEAD = 1
IN_EMBED = (2,)
IN_TIME = (4, 12)
IN_SPACE = (0, 2)


def front_kernel(lay, w_ref, s_ref, p_ref, tfill_ref, sfill_ref, *refs):
    (ow_ref, os_ref, pad_ref, x0_ref, at_ref, qt_ref, kt_ref, vt_ref, ot_ref, yt_ref, xs_ref, as_ref, qs_ref, ks_ref, vs_ref, mix_ref, cls_ref, v_ref) = refs[:18]
    (w_buf, piece, pos_buf, time_buf, own, zs, zr, xs, xr, ys, yr, cs, cr, wsem) = refs[18:]
    i, a, b, y, c = lay.place()
    A, B, Y, K = lay.outer, lay.inner, lay.planes, lay.handled
    greet(lay, i, a, b, y, c)
    here = lay.peer(i, y, 1 - c)
    pending = []

    def remote(src, dst, sends, at, recvs, dev, like):
        pltpu.make_async_remote_copy(
            src_ref=src, dst_ref=dst, send_sem=sends.at[at], recv_sem=recvs.at[at], device_id=dev, device_id_type=MESH
        ).start()
        pending.append((like, sends, at))

    def landed(dst, sems, *at):
        pltpu.make_async_remote_copy(
            src_ref=dst, dst_ref=dst, send_sem=sems.at[at], recv_sem=sems.at[at], device_id=here, device_id_type=MESH
        ).wait_recv()

    def matrix_of(core, k, v=0):
        h = k * Y + turn(y, v, Y) if k < lay.split else lay.split * (Y - 1) + k
        return 2 * h + core

    def source(k):
        return s_ref.at[c] if k < 0 else w_ref.at[lax.div(matrix_of(c, k), 2)]

    def at(k, j):
        return os_ref.at[c, j] if k < 0 else ow_ref.at[matrix_of(c, k), j]

    def like(k):
        return (lambda: s_ref.at[0]) if k < 0 else (lambda: w_ref.at[0])

    order = [-1] + list(range(K))

    def local(k):
        if k < 0:
            return pltpu.make_async_copy(s_ref.at[c], os_ref.at[c, i], own.at[0])
        return pltpu.make_async_copy(w_ref.at[k], ow_ref.at[2 * k + c, i], own.at[k + 1])

    def send_along(step):
        if step < len(order):
            k = order[step]
            for t in range(1, A):
                remote(source(k), at(k, i), zs, (k + 1, t), zr, lay.peer(turn(a, t, A) * B + b, y, c), like(k))

    def send_over(k):
        for u in range(1, B):
            remote(source(k), at(k, i), xs, (k + 1, u, 0), xr, lay.peer(a * B + turn(b, u, B), y, c), like(k))

    for step in range(AHEAD):
        send_along(step)
    for k in order:
        send_over(k)
    for k in range(-1, lay.half):
        local(k).start()

    def over(k, j, t, u):
        if 0 <= k < lay.split:
            for v in range(1, Y):
                remote(at(k, j), at(k, j), ys, (k, v, t, u), yr, lay.peer(i, turn(y, v, Y), c), like(k))

    def cross(k):
        send_along(order.index(k) + AHEAD)
        for t in range(1, A):
            j = turn(a, -t, A) * B + b
            landed(at(k, j), zr, k + 1, t)
            for u in range(1, B):
                remote(at(k, j), at(k, j), xs, (k + 1, u, t), xr, lay.peer(a * B + turn(b, u, B), y, c), like(k))
            over(k, j, t, 0)

    def share(k):
        for t in range(A):
            for u in range(1, B):
                j = turn(a, -t, A) * B + turn(b, -u, B)
                landed(at(k, j), xr, k + 1, u, t)
                over(k, j, t, u)
        if k < 0:
            local(k).wait()
            remote(os_ref.at[c], os_ref.at[c], cs, (0,), cr, here, lambda: os_ref.at[0])
        else:
            own_wait(k, 0)
            m = matrix_of(c, k)
            remote(ow_ref.at[m], ow_ref.at[m], cs, (k + 1,), cr, here, lambda: ow_ref.at[0])

    def own_wait(k, v):
        m = matrix_of(c, k, v)
        pltpu.make_async_copy(w_ref.at[lax.div(m, 2)], ow_ref.at[m, i], own.at[lax.div(m, 2) + 1]).wait()

    def slot(q, v):
        return K + 1 + (v - 1) * lay.split + q

    def from_planes(k):
        if k in closed or not 0 <= k < lay.split:
            return
        closed.append(k)
        for v in range(1, Y):
            m = matrix_of(c, k, -v)
            for t in range(A):
                for u in range(B):
                    if t or u:
                        j = turn(a, -t, A) * B + turn(b, -u, B)
                        landed(ow_ref.at[m, j], yr, k, v, t, u)
            own_wait(k, -v)
            remote(ow_ref.at[m], ow_ref.at[m], cs, (slot(k, v),), cr, here, lambda: ow_ref.at[0])

    def paired(k):
        if k < 0:
            landed(os_ref.at[1 - c], cr, 0)
        else:
            landed(ow_ref.at[matrix_of(1 - c, k)], cr, k + 1)
            if k < lay.split:
                for v in range(1, Y):
                    landed(ow_ref.at[matrix_of(1 - c, k, -v)], cr, slot(k, v))

    def fetch(first, count):
        span = pl.ds(first, count)
        return pltpu.make_async_copy(ow_ref.at[span], w_buf.at[span], wsem.at[first])

    closed = []

    def advance(step):
        if step < len(order):
            cross(order[step])
        if 0 <= step - 1 < len(order):
            share(order[step - 1])
        if 0 <= step - 2 < len(order):
            from_planes(order[step - 2])

    first, second = (1, 3) if lay.split else (2, 5)
    begun = first + 2
    for step in range(begun):
        advance(step)
    from_planes(first - 1)
    for k in range(-1, first):
        paired(k)
    fetch(0, 4).start()
    table = pltpu.make_async_copy(os_ref.at[0], piece, wsem.at[lay.half])
    table.start()
    v_ref[...] = jnp.zeros_like(v_ref)
    table.wait()
    for j in range(lay.n):
        lane = min(lay.rows * j // 128 * 128, D - 256)
        wide = jnp.concatenate([piece[j].astype(FULL), jnp.zeros(piece.shape[1:], FULL)], 1)
        v_ref[: piece.shape[1], lane : lane + 256] += pltpu.roll(wide, lay.rows * j - lane, 1)
    pos_buf[...] = v_ref[31 : 31 + SP, :]
    for f in range(F):
        time_buf[f] = v_ref[1 + f : 2 + f, :]
    fetch(0, 4).wait()
    ws = [Weight(w_buf.at[k]) for k in range(9)]
    steps = F // FB

    def embed(p, *outs):
        now = pl.program_id(0)
        embed_kernel(p, *ws[:4], v_ref, pos_buf, time_buf.at[pl.ds(now * FB, FB)], *outs)
        for s, place in enumerate(IN_EMBED):
            @pl.when(now == place)
            def _():
                advance(begun + s)

    pltpu.emit_pipeline(embed, grid=(steps,), in_specs=[pl.BlockSpec((1, FB, S, D), lambda i: (0, i, 0, 0))], out_specs=[FRAMES] * 6)(
        p_ref, pad_ref, x0_ref, at_ref, qt_ref, kt_ref, vt_ref
    )

    def time(q, k, v, fill, o):
        time_kernel(q, k, v, fill, o)
        for s, place in enumerate(IN_TIME):
            @pl.when(pl.program_id(0) == place)
            def _():
                advance(begun + len(IN_EMBED) + s)

    pltpu.emit_pipeline(time, grid=(SP // GROUP,), in_specs=[SLAB] * 3 + [FILL], out_specs=[SLAB])(
        qt_ref, kt_ref, vt_ref, tfill_ref, ot_ref
    )
    done = begun + len(IN_EMBED) + len(IN_TIME)
    for step in range(done, second + 2):
        advance(step)
    done = max(done, second + 2)
    for k in range(first, second):
        from_planes(k)
        paired(k)
    fetch(4, 5).start()
    fetch(4, 5).wait()

    def space(o, x, fill, *outs):
        space_kernel(o, x, *ws[4:9], v_ref, fill, *outs)

        for s, place in enumerate(IN_SPACE):
            @pl.when(pl.program_id(0) == place)
            def _():
                advance(done + s)

    pltpu.emit_pipeline(space, grid=(steps,), in_specs=[FRAMES, FRAMES, per_frame(1, SP)], out_specs=[FRAMES] * 7 + [per_frame(8, D)])(
        ot_ref, x0_ref, sfill_ref, yt_ref, xs_ref, as_ref, qs_ref, ks_ref, vs_ref, mix_ref, cls_ref
    )
    for step in range(done + len(IN_SPACE), len(order) + 1):
        advance(step)
    for k in range(second, K):
        paired(k)
    for make, sems, at_ in pending:
        ref = make()
        pltpu.make_async_remote_copy(
            src_ref=ref, dst_ref=ref, send_sem=sems.at[at_], recv_sem=sems.at[at_], device_id=here, device_id_type=MESH
        ).wait_send()


class Weight:
    def __init__(self, ref):
        self.ref = ref

    def __getitem__(self, unused):
        value = self.ref[...]
        if value.shape[1] % 16:
            return value.astype(FULL).reshape(D, D).astype(HALF)
        return value.reshape(D, D)


def front(lay, shard, small, patches, time_fill, space_fill):
    A, B, K, Y = lay.outer, lay.inner, lay.handled, lay.planes
    dma = pltpu.SemaphoreType.DMA
    kept = max(lay.split, 1)
    vmem = pl.BlockSpec(memory_space=pltpu.VMEM)
    full = functools.partial(shape, dtype=FULL)
    slots = K + 1 + max(Y - 1, 0) * lay.split
    return pl.pallas_call(
        functools.partial(front_kernel, lay),
        in_specs=[ANY] * 5,
        out_specs=[ANY] * 17 + [vmem],
        out_shape=[
            shape(NMAT, lay.n, lay.rows, D), shape(2, lay.n, *small.shape[1:]),
            ROWS16, ROWS32, ROWS16, ROWS16, ROWS16, ROWS16, ROWS16, ROWS16, ROWS32, ROWS16, ROWS16, ROWS16, ROWS16, ROWS16,
            full(F, 8, D), full(256, D),
        ],
        scratch_shapes=[
            pltpu.VMEM((9, lay.n, lay.rows, D), HALF), pltpu.VMEM((lay.n,) + small.shape[1:], HALF), pltpu.VMEM((SP, D), FULL), pltpu.VMEM((F, 1, D), FULL),
            dma((lay.half + 1,)), dma((K + 1, A)), dma((K + 1, A)), dma((K + 1, B, A)), dma((K + 1, B, A)),
            dma((kept, Y, A, B)), dma((kept, Y, A, B)), dma((slots,)), dma((slots,)), dma((lay.half + 1,)),
        ],
        compiler_params=pltpu.CompilerParams(collective_id=0, has_side_effects=True, vmem_limit_bytes=60 * 2**20),
    )(shard, small, patches, time_fill, space_fill)


def forward(lay, shard, small, patches, mask):
    alive = jnp.pad(mask[0] > 0, ((0, 0), (0, SP - S)))
    kept = jnp.where(alive, 0.0, MASKED).astype(FULL)
    places = jnp.arange(SP)[None]
    space_fill = jnp.where(places < S, kept, jnp.where(places == S, 0.0, NEVER))
    time_keys = kept.reshape(F, SP // GROUP, GROUP).transpose(1, 0, 2).reshape(SP // GROUP, F * GROUP)
    spot = jnp.arange(F * GROUP) % GROUP
    same = spot[:, None] == spot[None]
    time_fill = jnp.where(same[None], time_keys[:, None, :], NEVER)
    time_fill_back = jnp.where(same[None], time_keys[:, :, None], NEVER)
    mats, rest, padded, x0, at, qt, kt, vt, ot, yt, xs, as_, qs, ks, vs, os_, cls, table = front(
        lay, shard, small, patches, time_fill, space_fill[:, None]
    )
    mats = mats.reshape(NMAT, D, D)
    tab = whole(*table.shape)
    steps = F // FB
    of, x2, a2, g, e, x3, pool = call(
        mlp_kernel, steps,
        [FRAMES, whole(F, 8, D), FRAMES] + matrices(9, 9) + [tab],
        [FRAMES] * 3 + [HIDDEN] * 2 + [FRAMES, summed(8)],
        [ROWS16, ROWS32, ROWS16, HIDDEN32, HIDDEN16, ROWS32, shape(8, D, dtype=FULL)],
    )(os_, cls, xs, *[mats] * 9, table)
    pooled = (pool[:1] / (F * S + 1)).astype(HALF)
    head = rest[1][:, : 2 * lay.rows].reshape(lay.n, 2, lay.rows, 128).transpose(0, 2, 1, 3).reshape(D, 256)
    saved = (table, space_fill, time_fill_back, padded, x0, at, qt, kt, vt, ot, yt, xs, as_, qs, ks, vs, of, x2, a2, g, e, x3)
    return pooled, mats, head, saved


def backward(lay, mats, saved, back_pooled):
    (table, space_fill, time_fill, padded, x0, at, qt, kt, vt, ot, yt, xs, as_, qs, ks, vs, of, x2, a2, g, e, x3) = saved
    tab = whole(*table.shape)
    steps = F // FB
    top = back_pooled / (F * S + 1)
    column = jnp.broadcast_to(space_fill[:, :, None], (F, SP, 128))
    r3, dg, d2, r2, dq, dk, dv, cq, ck, cv, sums1 = call(
        mlp_back_kernel, steps,
        [FRAMES, FRAMES, HIDDEN, whole(1, D)] + matrices(9, 9) + [tab, FRAMES, FRAMES, FRAMES, per_frame(SP, 128)],
        [FRAMES, HIDDEN] + [FRAMES] * 5 + [per_frame(8, D)] * 3 + [summed(16)],
        [ROWS16, HIDDEN16, ROWS32] + [ROWS16] * 4 + [shape(F, 8, D, dtype=FULL)] * 3 + [shape(16, D, dtype=FULL)],
        [pltpu.VMEM((FB, SP, D), HALF)],
    )(x3, x2, g, top, *[mats] * 9, table, qs, ks, vs, column)
    first = Part(lay, 10, 4, 1 if lay.planes <= 4 else 0)
    pairs = [((2, 0), (3, k)) for k in range(4)] + [((0, k), (1, 0)) for k in range(4)]
    upper, fq, fk, fv, d1, r1, dy, do, tq, tk, tv, rp, grad_vecs, squares = early(
        lay, first, pairs, (e, r3, a2, dg, dq, dk, dv, xs, d2, qt, kt, vt, time_fill, x0, mats), (cq, ck, cv, sums1), table
    )
    second = Part(lay, 0, 5, 1 if lay.planes <= 4 else 0)
    operands = (padded, rp, at, tq, tk, tv, ot, dy, yt, r1, as_, fq, fk, fv, of, r2)
    pairs = [(0, 1), (2, 3), (2, 4), (2, 5), (6, 7), (8, 9), (10, 11), (10, 12), (10, 13), (14, 15)]
    pairs = [((left, 0), (right, 0)) for left, right in pairs]

    def finish(small):
        return late(lay, second, pairs, small, squares, upper, operands)

    return finish, grad_vecs


def project(inputs, weight):
    return jnp.einsum("...a,ab->...b", inputs, weight, preferred_element_type=jnp.float32)


def project_back(inputs, weight, cotangent):
    rounded = cotangent.astype(jnp.bfloat16)
    back_in = jnp.einsum("...b,ab->...a", rounded, weight, preferred_element_type=jnp.float32)
    flat_in = inputs.reshape(-1, inputs.shape[-1])
    flat_back = rounded.reshape(-1, rounded.shape[-1])
    grad_weight = jnp.einsum("na,nb->ab", flat_in, flat_back, preferred_element_type=jnp.float32)
    return (back_in, grad_weight, jnp.sum(flat_back, 0, dtype=jnp.float32))


def normalize(projected):
    return projected * lax.rsqrt(jnp.sum(projected * projected, -1, keepdims=True) + 1e-06)


def adamw_step(weight, first, second, average, gradient, factor, rate):
    clipped = gradient * factor
    first = BETA_ONE * first + (1.0 - BETA_ONE) * clipped
    second = BETA_TWO * second + (1.0 - BETA_TWO) * clipped * clipped
    first_hat = first / (1.0 - BETA_ONE**STEP)
    second_hat = second / (1.0 - BETA_TWO**STEP)
    weight = weight - rate * (first_hat / (jnp.sqrt(second_hat) + ADAM_EPSILON) + DECAY * weight)
    average = AVERAGE_KEEP * average + (1.0 - AVERAGE_KEEP) * weight
    return (weight, first, second, average)


def own_matrices(lay, matrices):
    pairs = matrices.reshape(NMAT // 2, 2, lay.rows, D)
    return lax.dynamic_index_in_dim(pairs, lax.rem(lax.axis_index("dp"), 2), 1, keepdims=False)


def pack(lay, head, vecs):
    tall = -(-NVEC // 16) * 16
    first = jnp.pad(vecs, ((0, tall - NVEC), (0, 128 - lay.rows)))
    second = jnp.concatenate([head[:, :128], head[:, 128:]], 0)
    return jnp.stack([first, jnp.pad(second, ((0, tall - second.shape[0]), (0, 0)))])


def pack_all(head, vecs, n):
    rows = D // n
    first = head.reshape(n, 3, rows // 3, D // 3).transpose(0, 2, 1, 3).reshape(n, rows // 3, D)
    tall = jnp.pad(vecs, ((0, D // 3 - vecs.shape[0]), (0, 0)))
    second = tall.reshape(n, rows // 3, n, rows).transpose(2, 1, 0, 3).reshape(n, rows // 3, D)
    fill = -(rows // 3) % 16
    return jnp.pad(jnp.stack([first, second]), ((0, 0), (0, 0), (0, fill), (0, 0)))


def unpack_shard(blocks, n):
    rows = D // n
    first, second = blocks[0, : rows // 3], blocks[1, : rows // 3]
    head = jnp.concatenate([first[:, : D // 3], first[:, D // 3 : 2 * D // 3], first[:, 2 * D // 3 :]], 0)
    vecs = second.reshape(rows // 3, n, rows).transpose(1, 0, 2).reshape(D // 3, rows)
    return head, vecs[:NVEC]


def local(
    lay,
    patches,
    patch_keep_mask,
    partner,
    matrices,
    matrix_first,
    matrix_second,
    matrix_average,
    head_weight,
    head_first,
    head_second,
    head_average,
    vectors,
    array_running_mean,
    vector_second,
    vector_average,
):
    n = lay.n
    pooled, mats16, head16, saved = forward(
        lay,
        own_matrices(lay, matrices).astype(jnp.bfloat16),
        pack(lay, head_weight.astype(jnp.bfloat16), vectors.astype(jnp.bfloat16)),
        patches,
        patch_keep_mask,
    )
    projected = project(pooled, head16)
    unit_length_lines, unit_back = jax.vjp(normalize, projected)
    clip_count, width = unit_length_lines.shape
    lines = unit_length_lines.reshape(-1, 128)
    tile = jnp.pad(lines, ((0, -lines.shape[0] % 8), (0, 0)))
    everyone = spread(lay.dp, n, tile, 2)
    gathered = everyone[:, : lines.shape[0]].reshape(-1, width)

    def contrast(gathered_rows):
        pairwise_affinity_scores_raw = (
            jnp.dot(gathered_rows, gathered_rows.T, precision=lax.Precision.HIGHEST)
            / SCORE_SHARPNESS
        )
        clip_total = pairwise_affinity_scores_raw.shape[0]
        column = jnp.arange(clip_total)[None, :]
        pairwise_affinity_scores_raw = jnp.where(
            jnp.arange(clip_total)[:, None] == column, -1000000000.0, pairwise_affinity_scores_raw
        )
        positive = jnp.sum(
            jnp.where(column == partner[:, None], pairwise_affinity_scores_raw, 0.0), -1
        )
        return jnp.mean(jax.nn.logsumexp(pairwise_affinity_scores_raw, -1) - positive)

    contrastive_loss, objective_cotangent_flow = jax.vjp(contrast, gathered)
    (back_gathered,) = objective_cotangent_flow(jnp.ones_like(contrastive_loss))
    clip_count = projected.shape[0]
    offset = lax.axis_index(("dp", "fsdp")) * clip_count
    back_unit = lax.dynamic_slice_in_dim(back_gathered, offset, clip_count, 0)
    (back_projected,) = unit_back(back_unit)
    back_pooled, grad_head, unused_bias = project_back(pooled, head16, back_projected)
    finish, grad_vecs = backward(lay, mats16, saved, back_pooled)
    small = pack_all(grad_head, grad_vecs, n).astype(jnp.bfloat16)
    grad_mats, grad_small, tiles = finish(small)
    squared_norm = jnp.sum(tiles)
    grad_head, grad_vecs = unpack_shard(grad_small, n)
    factor = CLIP_AT / jnp.maximum(jnp.sqrt(squared_norm), CLIP_AT)
    mats_out = adamw_step(
        matrices, matrix_first, matrix_second, matrix_average, grad_mats, factor, RATE
    )
    head_out = adamw_step(
        head_weight, head_first, head_second, head_average, grad_head, factor, RATE
    )
    vecs_out = adamw_step(
        vectors, array_running_mean, vector_second, vector_average, grad_vecs, factor, VECTOR_RATE
    )
    return (
        contrastive_loss,
        squared_norm,
        mats_out[0],
        mats_out[1],
        mats_out[2],
        mats_out[3],
        head_out[0],
        head_out[1],
        head_out[2],
        head_out[3],
        vecs_out[0],
        vecs_out[1],
        vecs_out[2],
        vecs_out[3],
    )


def solution(mesh):
    planes = mesh.shape["dp"] // 2
    lay = Layout(mesh.shape["dp"], mesh.shape["fsdp"], 2 if planes == 2 else 0)
    placed = (
        P(("dp", "fsdp"), None, None, None),
        P(("dp", "fsdp"), None, None),
        P(),
        P(None, "fsdp", None),
        P(None, "fsdp", None),
        P(None, "fsdp", None),
        P(None, "fsdp", None),
        P("fsdp", None),
        P("fsdp", None),
        P("fsdp", None),
        P("fsdp", None),
        P(None, "fsdp"),
        P(None, "fsdp"),
        P(None, "fsdp"),
        P(None, "fsdp"),
    )
    return jax.shard_map(
        functools.partial(local, lay),
        mesh=mesh,
        in_specs=placed,
        out_specs=(
            P(),
            P(),
            P(None, "fsdp", None),
            P(None, "fsdp", None),
            P(None, "fsdp", None),
            P(None, "fsdp", None),
            P("fsdp", None),
            P("fsdp", None),
            P("fsdp", None),
            P("fsdp", None),
            P(None, "fsdp"),
            P(None, "fsdp"),
            P(None, "fsdp"),
            P(None, "fsdp"),
        ),
        check_vma=False,
    )
```

```python
import functools
import jax
import jax.numpy as jnp
from jax import lax
from jax.experimental import pallas as pl
from jax.experimental.pallas import tpu as pltpu
from jax.sharding import PartitionSpec as P

D = 768
H = 12
HD = 64
F = 8
S = 196
SP = 208
NMAT = 18
NVEC = 227
STEP = 10

SCORE_SHARPNESS = 0.07
CLIP_AT = 0.05
RATE = 0.01
VECTOR_RATE = 0.1
BETA_ONE = 0.9
BETA_TWO = 0.95
ADAM_EPSILON = 1e-08
DECAY = 0.05
AVERAGE_KEEP = 0.9

MESH = pl.DeviceIdType.MESH
ANY = pl.BlockSpec(memory_space=pl.ANY)


class Layout:
    def __init__(self, dp, fsdp, split):
        self.dp, self.n = dp, fsdp
        self.outer = 4 if fsdp % 4 == 0 else 1
        self.inner = fsdp // self.outer
        self.planes = dp // 2
        self.half = NMAT // 2
        self.split = split
        self.common = self.half - split * self.planes
        self.handled = self.common + split
        self.rows = D // fsdp

    def place(self):
        i = lax.axis_index("fsdp")
        d = lax.axis_index("dp")
        return i, lax.div(i, self.inner), lax.rem(i, self.inner), lax.div(d, 2), lax.rem(d, 2)

    def peer(self, i, y, c):
        return {"fsdp": i, "dp": y * 2 + c}

    def matrix(self, c, y, k):
        if k < self.common:
            return c * self.half + k
        return c * self.half + self.common + y * self.split + (k - self.common)


def turn(x, t, size):
    return lax.rem(x + t + size, size)


def greet(lay, i, a, b, y, c):
    barrier = pltpu.get_barrier_semaphore()
    others = [lay.peer(turn(a, t, lay.outer) * lay.inner + b, y, c) for t in range(1, lay.outer)]
    others += [lay.peer(a * lay.inner + turn(b, u, lay.inner), y, c) for u in range(1, lay.inner)]
    others += [lay.peer(i, turn(y, v, lay.planes), c) for v in range(1, lay.planes)]
    others += [lay.peer(i, y, 1 - c)]
    for other in others:
        pl.semaphore_signal(barrier, inc=1, device_id=other, device_id_type=MESH)
    pl.semaphore_wait(barrier, len(others))


def spread_kernel(dp, n, x_ref, o_ref, ssem, rsem):
    i, d = lax.axis_index("fsdp"), lax.axis_index("dp")
    me = d * n + i
    total = dp * n
    barrier = pltpu.get_barrier_semaphore()

    def other(t):
        j = lax.rem(me + t, total)
        return {"fsdp": lax.rem(j, n), "dp": lax.div(j, n)}

    @pl.loop(1, total)
    def _(t):
        pl.semaphore_signal(barrier, inc=1, device_id=other(t), device_id_type=MESH)

    pl.semaphore_wait(barrier, total - 1)

    @pl.loop(1, total)
    def _(t):
        pltpu.make_async_remote_copy(
            src_ref=x_ref, dst_ref=o_ref.at[me], send_sem=ssem.at[t], recv_sem=rsem.at[t], device_id=other(t), device_id_type=MESH
        ).start()

    o_ref[me] = x_ref[...]

    @pl.loop(1, total)
    def _(t):
        pltpu.make_async_remote_copy(
            src_ref=x_ref, dst_ref=o_ref.at[lax.rem(me - t + total, total)], send_sem=ssem.at[t], recv_sem=rsem.at[t], device_id=other(t), device_id_type=MESH
        ).wait()


def spread(dp, n, tile, number):
    vmem = pl.BlockSpec(memory_space=pltpu.VMEM)
    return pl.pallas_call(
        functools.partial(spread_kernel, dp, n),
        out_shape=jax.ShapeDtypeStruct((dp * n,) + tile.shape, tile.dtype),
        in_specs=[vmem],
        out_specs=vmem,
        scratch_shapes=[pltpu.SemaphoreType.DMA((dp * n,)), pltpu.SemaphoreType.DMA((dp * n,))],
        compiler_params=pltpu.CompilerParams(collective_id=number, has_side_effects=True),
    )(tile)


FB = 2
GROUP = 16
HALF = jnp.bfloat16
FULL = jnp.float32
NORM_EPS = 1e-06
MASKED = -1000000000.0
NEVER = -3e38


def dot(a, b):
    return lax.dot_general(a, b, (((1,), (0,)), ((), ())), preferred_element_type=FULL)


def dot_back(a, b):
    return lax.dot_general(a, b, (((1,), (1,)), ((), ())), preferred_element_type=FULL)


def dot_rows(a, b):
    return lax.dot_general(a, b, (((0,), (0,)), ((), ())), preferred_element_type=FULL)


def mean(x):
    return jnp.sum(x, -1, keepdims=True) * (1.0 / D)


def norm(x, gain, shift):
    centred = x - mean(x)
    scale = lax.rsqrt(mean(centred * centred) + NORM_EPS)
    return centred * scale * gain + shift


def norm_back(x, gain, back):
    centred = x - mean(x)
    scale = lax.rsqrt(mean(centred * centred) + NORM_EPS)
    unit = centred * scale
    inner = back * gain
    return scale * (inner - mean(inner) - unit * mean(inner * unit)), back * unit


def normal_cdf(x):
    size = jnp.abs(x) * 0.7071067811865476
    t = pl.reciprocal(1.0 + 0.3275911 * size)
    bell = jnp.exp(-0.5 * x * x)
    poly = ((((1.061405429 * t - 1.453152027) * t + 1.421413741) * t - 0.284496736) * t + 0.254829592) * t
    tail = 0.5 * poly * bell
    return jnp.where(x < 0, tail, 1.0 - tail), bell


def gelu(x):
    below, bell = normal_cdf(x)
    return x * below, below + x * bell * 0.3989422804014327


def column_sum(x):
    return jnp.sum(x.astype(FULL), 0, keepdims=True)


def flat(ref):
    x = ref[...]
    return x.reshape(-1, x.shape[-1])


def row_of(rows):
    return lax.rem(lax.broadcasted_iota(jnp.int32, (rows, 1), 0), SP)


def row_share(rows):
    place = row_of(rows)
    return jnp.where(place < S, 1.0, jnp.where(place == S, 1.0 / F, 0.0))


def first_step():
    return pl.program_id(0) == 0


def add_rows(ref, values):
    @pl.when(first_step())
    def _():
        ref[...] = jnp.zeros_like(ref)

    for k, value in enumerate(values):
        if value is not None:
            ref[k : k + 1, :] += value


def pair_lanes(x, low):
    zero = jnp.zeros_like(x)
    return jnp.concatenate([jnp.where(low, x, zero), jnp.where(low, zero, x)], 0)


def attend(q, k, v, fill):
    rows = q.shape[0]
    low = lax.broadcasted_iota(jnp.int32, (rows, 128), 1) < HD
    stacked = pair_lanes(q * jnp.asarray(HD ** (-0.5), HALF), low)
    scores = dot_back(stacked, k)
    if fill.shape[0] != 1:
        fill = jnp.concatenate([fill, fill], 0)
    scores = jnp.where(fill == 0.0, scores, fill)
    expanded = jnp.exp(scores - jnp.max(scores, -1, keepdims=True))
    share = pl.reciprocal(jnp.sum(expanded, -1, keepdims=True))
    mixed = dot((expanded * share).astype(HALF), v)
    return jnp.where(low, mixed[:rows], mixed[rows:])


def attend_back(q, k, v, back, fill):
    rows = q.shape[0]
    low = lax.broadcasted_iota(jnp.int32, (rows, 128), 1) < HD
    stacked = pair_lanes(q * jnp.asarray(HD ** (-0.5), HALF), low)
    backs = pair_lanes(back, low)
    scores = dot_back(k, stacked)
    scores = jnp.where(fill == 0.0, scores, fill)
    expanded = jnp.exp(scores - jnp.max(scores, 0, keepdims=True))
    chances = expanded * pl.reciprocal(jnp.sum(expanded, 0, keepdims=True))
    back_chances = dot_back(v, backs)
    inner = jnp.sum(back_chances * chances, 0, keepdims=True)
    back_scores = (chances * (back_chances - inner)).astype(HALF)
    back_keys = dot(back_scores, stacked)
    back_values = dot(chances.astype(HALF), backs)
    queries = dot_rows(back_scores, k) * HD ** (-0.5)
    return jnp.where(low, queries[:rows], queries[rows:]), back_keys, back_values


def embed_kernel(p_ref, w0, w1, w2, w3, v_ref, pos_ref, time_ref, pad_ref, x_ref, a_ref, q_ref, k_ref, b_ref):
    pad_ref[:, SP - GROUP :, :] = jnp.zeros((FB, GROUP, D), HALF)
    for f in range(FB):
        pad_ref[f, :S, :] = p_ref[0, f]
    pos = pos_ref[...]
    here = jnp.concatenate([pos + time_ref[f] for f in range(FB)], 0)
    x = dot(flat(pad_ref), w0[0]) + v_ref[9:10] + here
    x_ref[...] = x.reshape(FB, SP, D)
    a = norm(x, v_ref[22:23], v_ref[23:24]).astype(HALF)
    a_ref[...] = a.reshape(FB, SP, D)
    q_ref[...] = (dot(a, w1[0]) + v_ref[10:11]).astype(HALF).reshape(FB, SP, D)
    k_ref[...] = dot(a, w2[0]).astype(HALF).reshape(FB, SP, D)
    b_ref[...] = (dot(a, w3[0]) + v_ref[11:12]).astype(HALF).reshape(FB, SP, D)


def time_kernel(q_ref, k_ref, v_ref, fill_ref, o_ref):
    rows = F * GROUP
    for p in range(H // 2):
        lanes = slice(128 * p, 128 * p + 128)
        q, k, v = (ref[:, :, lanes].reshape(rows, 128) for ref in (q_ref, k_ref, v_ref))
        o_ref[:, :, lanes] = attend(q, k, v, fill_ref[0]).astype(HALF).reshape(F, GROUP, 128)


def space_kernel(o_ref, x_ref, w0, w1, w2, w3, w4, v_ref, fill_ref, y_ref, xs_ref, a_ref, q_ref, k_ref, b_ref, os_ref, cls_ref):
    rows = FB * SP
    y = (dot(flat(o_ref), w0[0]) + v_ref[12:13]).astype(HALF)
    y_ref[...] = y.reshape(FB, SP, D)
    x = flat(x_ref) + dot(y, w1[0]) + v_ref[13:14]
    x = jnp.where(row_of(rows) == S, v_ref[0:1] + v_ref[30:31], x)
    xs_ref[...] = x.reshape(FB, SP, D)
    a = norm(x, v_ref[24:25], v_ref[25:26]).astype(HALF)
    a_ref[...] = a.reshape(FB, SP, D)
    q_ref[...] = (dot(a, w2[0]) + v_ref[14:15]).astype(HALF).reshape(FB, SP, D)
    k_ref[...] = dot(a, w3[0]).astype(HALF).reshape(FB, SP, D)
    b_ref[...] = (dot(a, w4[0]) + v_ref[15:16]).astype(HALF).reshape(FB, SP, D)
    for f in range(FB):
        for p in range(H // 2):
            lanes = slice(128 * p, 128 * p + 128)
            mixed = attend(q_ref[f, :, lanes], k_ref[f, :, lanes], b_ref[f, :, lanes], fill_ref[f])
            os_ref[f, :, lanes] = mixed.astype(HALF)
            cls_ref[f, :, lanes] = mixed[S : S + 8]


def mlp_kernel(o_ref, cls_ref, xs_ref, wp_ref, u0, u1, u2, u3, e0, e1, e2, e3, v_ref, of_ref, x2_ref, a_ref, g_ref, e_ref, x3_ref, pool_ref):
    rows = FB * SP
    middle = sum(cls_ref[f, 0:1, :] for f in range(F)) * (1.0 / F)
    o = jnp.where(row_of(rows) == S, middle, flat(o_ref).astype(FULL)).astype(HALF)
    of_ref[...] = o.reshape(FB, SP, D)
    x2 = flat(xs_ref) + dot(o, wp_ref[0]) + v_ref[16:17]
    x2_ref[...] = x2.reshape(FB, SP, D)
    a = norm(x2, v_ref[26:27], v_ref[27:28]).astype(HALF)
    a_ref[...] = a.reshape(FB, SP, D)
    x3 = x2 + v_ref[21:22]
    for k in range(4):
        g = dot(a, (u0, u1, u2, u3)[k][0]) + v_ref[17 + k : 18 + k]
        e, slope = gelu(g)
        g_ref[k] = slope.reshape(FB, SP, D)
        e = e.astype(HALF)
        e_ref[k] = e.reshape(FB, SP, D)
        x3 = x3 + dot(e, (e0, e1, e2, e3)[k][0])
    x3_ref[...] = x3.reshape(FB, SP, D)
    final = norm(x3, v_ref[28:29], v_ref[29:30]) * row_share(FB * SP)
    add_rows(pool_ref, [column_sum(final)])


def mlp_back_kernel(x3_ref, x2_ref, g_ref, d_ref, wp_ref, u0, u1, u2, u3, e0, e1, e2, e3, v_ref, q_ref, k_ref, b_ref, fill_ref,
                    r3_ref, dg_ref, d2_ref, r2_ref, dq_ref, dk_ref, dv_ref, cq_ref, ck_ref, cv_ref, sum_ref, do_ref):
    top = d_ref[0:1] * row_share(FB * SP)
    d3, unit = norm_back(flat(x3_ref), v_ref[28:29], top)
    sums = [column_sum(unit), column_sum(top)]
    r3 = d3.astype(HALF)
    r3_ref[...] = r3.reshape(FB, SP, D)
    sums.append(column_sum(r3))
    back = None
    for k in range(4):
        dg = (dot_back(r3, (e0, e1, e2, e3)[k][0]) * flat(g_ref.at[k])).astype(HALF)
        dg_ref[k] = dg.reshape(FB, SP, D)
        sums.append(column_sum(dg))
        part = dot_back(dg, (u0, u1, u2, u3)[k][0])
        back = part if back is None else back + part
    d2, unit = norm_back(flat(x2_ref), v_ref[26:27], back)
    sums += [column_sum(unit), column_sum(back)]
    d2 = d2 + d3
    d2_ref[...] = d2.reshape(FB, SP, D)
    r2 = d2.astype(HALF)
    r2_ref[...] = r2.reshape(FB, SP, D)
    sums.append(column_sum(r2))
    add_rows(sum_ref, sums)
    do_ref[...] = dot_back(r2, wp_ref[0]).astype(HALF).reshape(FB, SP, D)
    for f in range(FB):
        for p in range(H // 2):
            lanes = slice(128 * p, 128 * p + 128)
            outs = attend_back(q_ref[f, :, lanes], k_ref[f, :, lanes], b_ref[f, :, lanes], do_ref[f, :, lanes], fill_ref[f][:, 0:1])
            for value, ref, cls in zip(outs, (dq_ref, dk_ref, dv_ref), (cq_ref, ck_ref, cv_ref)):
                ref[f, :, lanes] = value.astype(HALF)
                cls[f, :, lanes] = value[S : S + 8]


def space_back_kernel(dq_ref, dk_ref, dv_ref, cls_ref, xs_ref, d2_ref, w0, w1, w2, w3, w4, v_ref, fq_ref, fk_ref, fv_ref, d1_ref, r1_ref, dy_ref, do_ref, sum_ref):
    frames = xs_ref.shape[0]
    rows = frames * SP
    is_class = row_of(rows) == S
    grads = []
    for k, (ref, out) in enumerate(zip((dq_ref, dk_ref, dv_ref), (fq_ref, fk_ref, fv_ref))):
        grad = jnp.where(is_class, cls_ref[k : k + 1], flat(ref).astype(FULL)).astype(HALF)
        out[...] = grad.reshape(frames, SP, D)
        grads.append(grad)
    back = dot_back(grads[0], w2[0]) + dot_back(grads[1], w3[0]) + dot_back(grads[2], w4[0])
    d, unit = norm_back(flat(xs_ref), v_ref[24:25], back)
    sums = [column_sum(grads[0]), column_sum(grads[2]), column_sum(unit), column_sum(back)]
    d = d + flat(d2_ref)
    kept = jnp.where(is_class, d, 0.0)
    sums.append(column_sum(kept))
    d = d - kept
    d1_ref[...] = d.reshape(frames, SP, D)
    r1 = d.astype(HALF)
    r1_ref[...] = r1.reshape(frames, SP, D)
    sums.append(column_sum(r1))
    dy = dot_back(r1, w1[0]).astype(HALF)
    dy_ref[...] = dy.reshape(frames, SP, D)
    sums.append(column_sum(dy))
    do_ref[...] = dot_back(dy, w0[0]).astype(HALF).reshape(frames, SP, D)
    add_rows(sum_ref, sums)


def time_back_kernel(q_ref, k_ref, v_ref, d_ref, fill_ref, dq_ref, dk_ref, dv_ref):
    rows = F * GROUP
    fill = jnp.concatenate([fill_ref[0], fill_ref[0]], 1)
    for p in range(H // 2):
        lanes = slice(128 * p, 128 * p + 128)
        q, k, v, d = (ref[:, :, lanes].reshape(rows, 128) for ref in (q_ref, k_ref, v_ref, d_ref))
        for value, ref in zip(attend_back(q, k, v, d, fill), (dq_ref, dk_ref, dv_ref)):
            ref[:, :, lanes] = value.astype(HALF).reshape(F, GROUP, 128)


def embed_back_kernel(dq_ref, dk_ref, dv_ref, x_ref, d1_ref, w1, w2, w3, v_ref, r_ref, pos_ref, time_ref, sum_ref):
    q, v = flat(dq_ref), flat(dv_ref)
    back = dot_back(q, w1[0]) + dot_back(flat(dk_ref), w2[0]) + dot_back(v, w3[0])
    d, unit = norm_back(flat(x_ref), v_ref[22:23], back)
    d = d + flat(d1_ref)
    rounded = d.astype(HALF)
    r_ref[...] = rounded.reshape(FB, SP, D)
    add_rows(sum_ref, [column_sum(q), column_sum(v), column_sum(unit), column_sum(back), column_sum(rounded)])

    @pl.when(first_step())
    def _():
        pos_ref[...] = jnp.zeros_like(pos_ref)

    total = jnp.zeros((SP, D), FULL)
    for f in range(FB):
        part = d[f * SP : (f + 1) * SP]
        time_ref[f] = column_sum(part)
        total = total + part
    pos_ref[...] += total


def shape(*dims, dtype=HALF):
    return jax.ShapeDtypeStruct(dims, dtype)


FRAMES = pl.BlockSpec((FB, SP, D), lambda i: (i, 0, 0))
HIDDEN = pl.BlockSpec((4, FB, SP, D), lambda i: (0, i, 0, 0))
SLAB = pl.BlockSpec((F, GROUP, D), lambda i: (0, i, 0))
ROWS16 = shape(F, SP, D)
ROWS32 = shape(F, SP, D, dtype=FULL)
HIDDEN16 = shape(4, F, SP, D)
HIDDEN32 = shape(4, F, SP, D, dtype=FULL)


def whole(*dims):
    return pl.BlockSpec(dims, lambda i: (0,) * len(dims), pipeline_mode=pl.Buffered(1))


def matrix(m):
    return pl.BlockSpec((1, D, D), lambda i: (m, 0, 0), pipeline_mode=pl.Buffered(1))


def matrices(first, count):
    return [matrix(m) for m in range(first, first + count)]


def summed(rows):
    return pl.BlockSpec((rows, D), lambda i: (0, 0))


def call(kernel, steps, in_specs, out_specs, out_shape, scratch=()):
    return pl.pallas_call(
        kernel,
        grid=(steps,),
        in_specs=in_specs,
        out_specs=out_specs,
        out_shape=out_shape,
        scratch_shapes=list(scratch),
        compiler_params=pltpu.CompilerParams(vmem_limit_bytes=60 * 2**20),
    )


def per_frame(*tail):
    return pl.BlockSpec((FB,) + tail, lambda i: (i,) + (0,) * len(tail))


class Part:
    def __init__(self, lay, first, half, split):
        self.first, self.half, self.split = first, half, split
        self.common = half - split * lay.planes

    def order(self):
        return list(range(self.common, self.half)) + list(range(self.common))


class Sums:
    def __init__(self, refs, common, split):
        (self.g, self.r, self.ys, self.yr, self.xs, self.xr, self.zs, self.zr, self.fin, self.every) = refs[:10]
        (self.rs, self.rr, self.yss, self.yrs, self.xss, self.xrs, self.zss, self.zrs, self.fsem) = refs[10:]
        self.common, self.split = common, split


SUMS = 19


def sums_scratch(lay, rows, common, split):
    A, B, Y, n = lay.outer, lay.inner, lay.planes, lay.n
    slots, kept, passed, K = common + split * Y, max(split, 1), max(Y - 1, 1), common + split
    dma = pltpu.SemaphoreType.DMA
    width, depth = (rows, n) if split else (16, 1)
    crossed, along = max(B - 1, 1), max(A - 1, 1)
    return [
        pltpu.VMEM((slots, 2, n, rows, D), HALF), pltpu.VMEM((slots, n, rows, D), HALF),
        pltpu.VMEM((passed, kept, depth, width, D), HALF), pltpu.VMEM((passed, kept, depth, width, D), HALF),
        pltpu.VMEM((K, crossed, A, rows, D), HALF), pltpu.VMEM((K, crossed, A, rows, D), HALF),
        pltpu.VMEM((K, along, rows, D), HALF), pltpu.VMEM((K, along, rows, D), HALF),
        pltpu.VMEM((K, rows, D), FULL), pltpu.VMEM((Y, common, rows, D), FULL),
        dma((slots,)), dma((slots,)), dma((passed, kept)), dma((passed, kept)),
        dma((K, crossed, A)), dma((K, crossed, A)), dma((K, along)), dma((K, along)), dma((5, K, Y)),
    ]


def other_device(lay, me, t):
    j = lax.rem(me + t, lay.dp * lay.n)
    return {"fsdp": lax.rem(j, lay.n), "dp": lax.div(j, lay.n)}


def greet_all(lay, me):
    barrier = pltpu.get_barrier_semaphore()

    @pl.loop(1, lay.dp * lay.n)
    def _(t):
        pl.semaphore_signal(barrier, inc=1, device_id=other_device(lay, me, t), device_id_type=MESH)

    pl.semaphore_wait(barrier, lay.dp * lay.n - 1)


class Reducer:
    def __init__(self, lay, squares, everyone):
        self.lay = lay
        self.squares = squares
        self.i, self.a, self.b, self.y, self.c = lay.place()
        self.here = lay.peer(self.i, self.y, 1 - self.c)
        self.pending = []
        if everyone:
            greet_all(lay, lax.axis_index("dp") * lay.n + self.i)
        else:
            greet(lay, self.i, self.a, self.b, self.y, self.c)

    def square(self, value, share):
        self.squares[...] += jnp.sum((value * value).reshape(-1, 8, D), 0) * share

    def remote(self, src, dst, sends, at, recvs, dev, like):
        pltpu.make_async_remote_copy(
            src_ref=src, dst_ref=dst, send_sem=sends.at[at], recv_sem=recvs[0].at[recvs[1]], device_id=dev, device_id_type=MESH
        ).start()
        self.pending.append((like, sends, at, True))

    def wait_all(self):
        for make, sems, at, remote in self.pending:
            like = make()
            if remote:
                pltpu.make_async_remote_copy(
                    src_ref=like, dst_ref=like, send_sem=sems.at[at], recv_sem=sems.at[at], device_id=self.here, device_id_type=MESH
                ).wait_send()
            else:
                pltpu.make_async_copy(like, like, sems.at[at]).wait()

    def landed(self, dst, sems, *at):
        pltpu.make_async_remote_copy(
            src_ref=dst, dst_ref=dst, send_sem=sems.at[at], recv_sem=sems.at[at], device_id=self.here, device_id_type=MESH
        ).wait_recv()

    def slot(self, st, v, q):
        if v is None:
            return q
        return st.common + turn(self.y, v, self.lay.planes) * st.split + q

    def hand(self, st, h):
        self.remote(st.g.at[h, 1 - self.c], st.r.at[h], st.rs, (h,), (st.rr, (h,)), self.here, lambda: st.r.at[h])

    def base(self, st, v, q, j):
        n = self.slot(st, v, q)
        total = st.g[n, self.c, j].astype(FULL) + st.r[n, j].astype(FULL)
        if v == 0:
            for w in range(1, self.lay.planes):
                total = total + st.yr[w - 1, q, j].astype(FULL)
        return total

    def pass_on(self, st, v, q):
        n = self.slot(st, v, q)
        self.landed(st.r.at[n], st.rr, n)

        @pl.loop(0, self.lay.n)
        def _(j):
            st.ys[v - 1, q, j] = self.base(st, v, q, j).astype(HALF)

        self.remote(
            st.ys.at[v - 1, q], st.yr.at[v - 1, q], st.yss, (v - 1, q), (st.yrs, (v - 1, q)),
            self.lay.peer(self.i, turn(self.y, v, self.lay.planes), self.c), lambda: st.ys.at[v - 1, q],
        )

    def item(self, st, v, q):
        return q if v is None else st.common + q

    def cross(self, st, target, v, q):
        k, n = self.item(st, v, q), self.slot(st, v, q)
        self.landed(st.r.at[n], st.rr, n)
        if v == 0:
            for w in range(1, self.lay.planes):
                self.landed(st.yr.at[w - 1, q], st.yrs, w - 1, q)
        outer, inner = self.lay.outer, self.lay.inner
        for t in list(range(1, outer)) + [0]:
            e = turn(self.a, t, outer)
            for u in range(1, inner):
                other = turn(self.b, u, inner)
                st.xs[k, u - 1, e] = self.base(st, v, q, e * inner + other).astype(HALF)
                self.remote(
                    st.xs.at[k, u - 1, e], st.xr.at[k, u - 1, e], st.xss, (k, u - 1, t), (st.xrs, (k, u - 1, t)),
                    self.lay.peer(self.a * inner + other, self.y, self.c), lambda u=u: st.xs.at[k, u - 1, 0],
                )

    def along(self, st, target, v, q):
        k = self.item(st, v, q)
        inner, outer = self.lay.inner, self.lay.outer
        for t in list(range(1, outer)) + [0]:
            e = turn(self.a, t, outer)
            value = self.base(st, v, q, e * inner + self.b)
            for u in range(1, inner):
                self.landed(st.xr.at[k, u - 1, e], st.xrs, k, u - 1, t)
                value = value + st.xr[k, u - 1, e].astype(FULL)
            if t == 0:
                st.fin[k] = value
                continue
            st.zs[k, t - 1] = value.astype(HALF)
            self.remote(
                st.zs.at[k, t - 1], st.zr.at[k, t - 1], st.zss, (k, t - 1), (st.zrs, (k, t - 1)),
                self.lay.peer(e * inner + self.b, self.y, self.c), lambda t=t: st.zs.at[k, t - 1],
            )

    def close(self, st, target, v, q):
        k, Y = self.item(st, v, q), self.lay.planes
        for t in range(1, self.lay.outer):
            self.landed(st.zr.at[k, t - 1], st.zrs, k, t - 1)
        value = st.fin[k]
        for t in range(1, self.lay.outer):
            value = value + st.zr[k, t - 1].astype(FULL)
        if v is None:
            st.every[self.y, k] = value
            source, landing = st.every.at[self.y, k], st.every.at[self.y, k]
            like = lambda: st.every.at[0, k]
        else:
            st.fin[k] = value
            self.square(value, 1.0)
            source = st.fin.at[k]
            like = lambda: st.fin.at[k]
            landing = target(self.c, self.slot(st, v, q))
        for w in range(1, Y):
            self.remote(source, landing, st.fsem, (0, k, w), (st.fsem, (1, k, w)), self.lay.peer(self.i, turn(self.y, w, Y), self.c), like)
        if v is not None:
            self.finish(st, k, landing)

    def finish(self, st, k, landing):
        pltpu.make_async_copy(st.fin.at[k], landing, st.fsem.at[2, k, 0]).start()
        self.pending.append((lambda: st.fin.at[k], st.fsem, (2, k, 0), False))
        self.remote(st.fin.at[k], landing, st.fsem, (3, k, 0), (st.fsem, (4, k, 0)), self.here, lambda: st.fin.at[k])

    def merge(self, st, target, v, q):
        k, Y = self.item(st, v, q), self.lay.planes
        if v is None:
            for w in range(1, Y):
                self.landed(st.every.at[turn(self.y, -w, Y), k], st.fsem, 1, k, w)
            value = st.every[0, k]
            for w in range(1, Y):
                value = value + st.every[w, k]
            st.fin[k] = value
            self.square(value, 1.0 / Y)
            self.finish(st, k, target(self.c, q))
        else:
            for w in range(1, Y):
                back = target(self.c, self.slot(st, -w, q))
                self.landed(back, st.fsem, 1, k, w)
                self.remote(back, back, st.fsem, (3, k, w), (st.fsem, (4, k, w)), self.here, lambda: target(0, 0))

    def last(self, st, target, v, q):
        k = self.item(st, v, q)
        self.landed(target(1 - self.c, self.slot(st, v, q)), st.fsem, 4, k, 0)
        if v is not None:
            for w in range(1, self.lay.planes):
                self.landed(target(1 - self.c, self.slot(st, -w, q)), st.fsem, 4, k, w)

    def progress(self, work, step):
        for lag, stage in enumerate((self.cross, self.along, self.close, self.merge)):
            if 0 <= step - lag < len(work):
                stage(*work[step - lag])

    def done(self, work):
        for job in work:
            self.last(*job)
        self.wait_all()


def outer_products(rows, operands, jobs, st, after, a_buf, b_buf, sems):
    n = st.g.shape[2]
    lefts, rights, plan = [], [], []
    for slot, core, left, right in jobs:
        fresh = [not lefts or lefts[-1] != left, not rights or rights[-1] != right]
        if fresh[0]:
            lefts.append(left)
        if fresh[1]:
            rights.append(right)
        plan.append((slot, core, len(lefts) - 1, len(rights) - 1, fresh))

    def load(kind, loads, k):
        number, block = loads[k]
        buf = (a_buf, b_buf)[kind]
        return pltpu.make_async_copy(operands[number].at[pl.ds(block * rows, rows)], buf.at[k % 2], sems.at[kind, k % 2])

    load(0, lefts, 0).start()
    load(1, rights, 0).start()
    for slot, core, left, right, fresh in plan:
        if fresh[0]:
            load(0, lefts, left).wait()
        if fresh[1]:
            load(1, rights, right).wait()
        if fresh[0] and left + 1 < len(lefts):
            load(0, lefts, left + 1).start()
        if fresh[1] and right + 1 < len(rights):
            load(1, rights, right + 1).start()
        value = dot_rows(a_buf[left % 2], b_buf[right % 2])
        st.g[slot, core] = value.reshape(n, -1, D).astype(HALF)
        if core == 1:
            after(slot)


def product_buffers(rows):
    return [
        pltpu.VMEM((2, rows, D), HALF), pltpu.VMEM((2, rows, D), HALF), pltpu.SemaphoreType.DMA((2, 2)),
    ]


def product_jobs(part, pairs):
    return [(h, core, *pairs[2 * h + core]) for h in part.order() for core in range(2)]


def part_work(lay, part, st, target):
    return [(st, target, None, k) for k in range(part.common)] + [(st, target, 0, q) for q in range(part.split)]


def products_and_hand(red, part, st, work, operands, jobs, buffers):
    passed = [(v, q) for v in range(1, red.lay.planes) for q in range(part.split)]
    order = part.order()
    ahead = len(work) - part.common - part.split

    def after(h):
        red.hand(st, h)
        place = order.index(h) - (part.half - part.common)
        if place == 0 or part.common == 0 and h == order[-1]:
            for v, q in passed:
                red.pass_on(st, v, q)
        if place >= 1 - ahead and place + ahead - 1 < steps_beside(part, ahead):
            red.progress(work, place + ahead - 1)

    outer_products(F * SP, operands, jobs, st, after, *buffers)


def steps_beside(part, ahead):
    return max(part.common + ahead - 1, 0)


def early_kernel(lay, part, pairs, *refs):
    (e_ref, r3_ref, a2_ref, dg_ref, dq_ref, dk_ref, dv_ref, cq_ref, ck_ref, cv_ref, sum1_ref, xs_ref, d2_ref, qt_ref, kt_ref, vt_ref, fill_ref, x0_ref, mats_ref, v_ref) = refs[:20]
    (og_ref, fq_ref, fk_ref, fv_ref, d1_ref, r1_ref, dy_ref, do_ref, tq_ref, tk_ref, tv_ref, rp_ref, vec_ref, sq_ref) = refs[20:34]
    red = Reducer(lay, sq_ref, False)
    sq_ref[...] = jnp.zeros_like(sq_ref)
    st = Sums(refs[34 : 34 + SUMS], part.common, part.split)
    w_buf, w_sem, cls_ref, sum2_ref, pos_ref, time_ref, sum3_ref = refs[34 + SUMS :]
    for k, ref in enumerate((cq_ref, ck_ref, cv_ref)):
        total = sum(ref[f, 0:1, :] for f in range(F))
        cls_ref[k : k + 1, :] = total.astype(HALF).astype(FULL) * (1.0 / F)
    load = pltpu.make_async_copy(mats_ref.at[pl.ds(1, 8)], w_buf, w_sem.at[0])
    load.start()

    def target(core, h):
        return og_ref.at[part.first + 2 * h + core]

    work = part_work(lay, part, st, target)
    rows = F * SP
    jobs = product_jobs(part, pairs)
    pl.run_scoped(lambda *buffers: products_and_hand(red, part, st, work, (e_ref, r3_ref, a2_ref, dg_ref), jobs, buffers), *product_buffers(rows))
    begun = steps_beside(part, 0)
    load.wait()
    ws = [w_buf.at[pl.ds(k, 1)] for k in range(8)]

    steps = F // FB

    def space(dq, dk, dv, xs, d2, fq, fk, fv, d1, r1, dy, do):
        space_back_kernel(dq, dk, dv, cls_ref, xs, d2, ws[3], ws[4], ws[5], ws[6], ws[7], v_ref, fq, fk, fv, d1, r1, dy, do, sum2_ref)
        for s, place in enumerate((1, 3)):
            @pl.when(pl.program_id(0) == place)
            def _():
                red.progress(work, begun + s)

    pltpu.emit_pipeline(space, grid=(steps,), in_specs=[FRAMES] * 5, out_specs=[FRAMES] * 7)(
        dq_ref, dk_ref, dv_ref, xs_ref, d2_ref, fq_ref, fk_ref, fv_ref, d1_ref, r1_ref, dy_ref, do_ref
    )

    def time(q, k, v, d, fill, dq, dk, dv):
        time_back_kernel(q, k, v, d, fill, dq, dk, dv)

        for s, place in enumerate((6, 12)):
            @pl.when(pl.program_id(0) == place)
            def _():
                red.progress(work, begun + 2 + s)

    pltpu.emit_pipeline(time, grid=(SP // GROUP,), in_specs=[SLAB] * 4 + [FILL], out_specs=[SLAB] * 3)(
        qt_ref, kt_ref, vt_ref, do_ref, fill_ref, tq_ref, tk_ref, tv_ref
    )

    def embed(dq, dk, dv, x, d1, r):
        place = time_ref.at[pl.ds(pl.program_id(0) * FB, FB)]
        embed_back_kernel(dq, dk, dv, x, d1, ws[0], ws[1], ws[2], v_ref, r, pos_ref, place, sum3_ref)

        @pl.when(pl.program_id(0) == 3)
        def _():
            red.progress(work, begun + 4)

    pltpu.emit_pipeline(embed, grid=(steps,), in_specs=[FRAMES] * 5, out_specs=[FRAMES])(
        tq_ref, tk_ref, tv_ref, x0_ref, d1_ref, rp_ref
    )
    vec_ref[...] = jnp.zeros_like(vec_ref)
    for row, ref, first, count in (
        (0, sum2_ref, 4, 1), (9, sum3_ref, 4, 1), (10, sum3_ref, 0, 2), (12, sum2_ref, 6, 1), (13, sum2_ref, 5, 1), (14, sum2_ref, 0, 2),
        (16, sum1_ref, 9, 1), (17, sum1_ref, 3, 4), (21, sum1_ref, 2, 1), (22, sum3_ref, 2, 2), (24, sum2_ref, 2, 2), (26, sum1_ref, 7, 2),
        (28, sum1_ref, 0, 2), (30, sum2_ref, 4, 1), (31, pos_ref, 0, S),
    ):
        vec_ref[row : row + count, :] = ref[first : first + count, :]
    for f in range(F):
        vec_ref[1 + f : 2 + f, :] = time_ref[f]
    for s in range(begun + 5, len(work) + 3):
        red.progress(work, s)
    red.done(work)


FILL = pl.BlockSpec((1, F * GROUP, F * GROUP), lambda i: (i, 0, 0))


def early(lay, part, pairs, arrays, classes, table):
    vmem = pl.BlockSpec(memory_space=pltpu.VMEM)
    e, r3, a2, dg, dq, dk, dv, xs, d2, qt, kt, vt, fill, x0, mats = arrays
    two = lambda x: x.reshape(-1, D)
    full = functools.partial(shape, dtype=FULL)
    return pl.pallas_call(
        functools.partial(early_kernel, lay, part, pairs),
        in_specs=[ANY] * 7 + [vmem] * 4 + [ANY] * 8 + [vmem],
        out_specs=[ANY] * 12 + [vmem, vmem],
        out_shape=[full(NMAT, lay.rows, D), ROWS16, ROWS16, ROWS16, ROWS32] + [ROWS16] * 7 + [full(D // 3, D), full(8, D)],
        scratch_shapes=sums_scratch(lay, lay.rows, part.common, part.split) + [pltpu.VMEM((8, D, D), HALF), pltpu.SemaphoreType.DMA((1,))]
        + [pltpu.VMEM(dims, FULL) for dims in ((8, D), (16, D), (SP, D), (F, 1, D), (16, D))],
        compiler_params=pltpu.CompilerParams(collective_id=1, has_side_effects=True, vmem_limit_bytes=62 * 2**20),
    )(two(e), two(r3), two(a2), two(dg), dq, dk, dv, *classes, xs, d2, qt, kt, vt, fill, x0, mats, table)


def late_kernel(lay, part, pairs, count, *refs):
    s_ref, sq_ref, operands = refs[0], refs[1], refs[3 : 3 + count]
    og_ref, os_ref, tiles_ref = refs[3 + count : 6 + count]
    rest = refs[6 + count : -4]
    squares, tile, tile_sent, tile_come = refs[-4:]
    red = Reducer(lay, squares, True)
    squares[...] = sq_ref[...]
    st = Sums(rest[:SUMS], part.common, part.split)
    little = Sums(rest[SUMS : 2 * SUMS], 1, 0)
    small_sem = rest[2 * SUMS]
    load = pltpu.make_async_copy(s_ref, little.g.at[0], small_sem.at[0])
    load.start()

    def target(core, h):
        return og_ref.at[part.first + 2 * h + core]

    work = part_work(lay, part, st, target)
    work = [(little, lambda core, h: os_ref.at[core], None, 0)] + work
    rows = F * SP
    jobs = product_jobs(part, pairs)
    load.wait()
    red.hand(little, 0)
    pl.run_scoped(lambda *buffers: products_and_hand(red, part, st, work, operands, jobs, buffers), *product_buffers(rows))
    for s in range(steps_beside(part, 1), len(work) + 3):
        red.progress(work, s)
    tile[...] = sum(squares[:, e * 128 : e * 128 + 128] for e in range(D // 128))
    me, total = lax.axis_index("dp") * lay.n + red.i, lay.dp * lay.n

    def swap(t, place):
        return pltpu.make_async_remote_copy(
            src_ref=tile, dst_ref=tiles_ref.at[place], send_sem=tile_sent.at[t], recv_sem=tile_come.at[t],
            device_id=other_device(lay, me, t), device_id_type=MESH,
        )

    @pl.loop(1, total)
    def _(t):
        swap(t, me).start()

    tiles_ref[me] = tile[...]
    red.done(work)

    @pl.loop(1, total)
    def _(t):
        swap(t, lax.rem(me - t + total, total)).wait()


def late(lay, part, pairs, small, squares, sums, arrays):
    full = functools.partial(shape, dtype=FULL)
    vmem = pl.BlockSpec(memory_space=pltpu.VMEM)
    everyone = lay.dp * lay.n
    dma = pltpu.SemaphoreType.DMA
    return pl.pallas_call(
        functools.partial(late_kernel, lay, part, pairs, len(arrays)),
        in_specs=[ANY, vmem] + [ANY] * (1 + len(arrays)),
        out_specs=[ANY, ANY, vmem],
        out_shape=[full(NMAT, lay.rows, D), full(2, small.shape[2], D), full(everyone, 8, 128)],
        scratch_shapes=sums_scratch(lay, lay.rows, part.common, part.split) + sums_scratch(lay, small.shape[2], 1, 0)
        + [dma((1,)), pltpu.VMEM((8, D), FULL), pltpu.VMEM((8, 128), FULL), dma((everyone,)), dma((everyone,))],
        input_output_aliases={2: 0},
        compiler_params=pltpu.CompilerParams(collective_id=4, has_side_effects=True, vmem_limit_bytes=62 * 2**20),
    )(small, squares, sums, *[x.reshape(-1, D) for x in arrays])


AHEAD = 1
IN_EMBED = (0, 3)
IN_TIME = (6, 12)
IN_SPACE = (0, 2)


def front_kernel(lay, w_ref, s_ref, p_ref, tfill_ref, sfill_ref, *refs):
    (ow_ref, os_ref, pad_ref, x0_ref, at_ref, qt_ref, kt_ref, vt_ref, ot_ref, yt_ref, xs_ref, as_ref, qs_ref, ks_ref, vs_ref, mix_ref, cls_ref, v_ref) = refs[:18]
    (w_buf, piece, pos_buf, time_buf, own, zs, zr, xs, xr, ys, yr, cs, cr, wsem) = refs[18:]
    i, a, b, y, c = lay.place()
    A, B, Y, K = lay.outer, lay.inner, lay.planes, lay.handled
    greet(lay, i, a, b, y, c)
    here = lay.peer(i, y, 1 - c)
    pending = []

    def remote(src, dst, sends, at, recvs, dev, like):
        pltpu.make_async_remote_copy(
            src_ref=src, dst_ref=dst, send_sem=sends.at[at], recv_sem=recvs.at[at], device_id=dev, device_id_type=MESH
        ).start()
        pending.append((like, sends, at))

    def landed(dst, sems, *at):
        pltpu.make_async_remote_copy(
            src_ref=dst, dst_ref=dst, send_sem=sems.at[at], recv_sem=sems.at[at], device_id=here, device_id_type=MESH
        ).wait_recv()

    def matrix_of(core, k, v=0):
        h = k * Y + turn(y, v, Y) if k < lay.split else lay.split * (Y - 1) + k
        return 2 * h + core

    def source(k):
        return s_ref.at[c] if k < 0 else w_ref.at[lax.div(matrix_of(c, k), 2)]

    def at(k, j):
        return os_ref.at[c, j] if k < 0 else ow_ref.at[matrix_of(c, k), j]

    def like(k):
        return (lambda: s_ref.at[0]) if k < 0 else (lambda: w_ref.at[0])

    order = [-1] + list(range(K))

    def local(k):
        if k < 0:
            return pltpu.make_async_copy(s_ref.at[c], os_ref.at[c, i], own.at[0])
        return pltpu.make_async_copy(w_ref.at[k], ow_ref.at[2 * k + c, i], own.at[k + 1])

    def send_along(step):
        if step < len(order):
            k = order[step]
            for t in range(1, A):
                remote(source(k), at(k, i), zs, (k + 1, t), zr, lay.peer(turn(a, t, A) * B + b, y, c), like(k))

    def send_over(k):
        for u in range(1, B):
            remote(source(k), at(k, i), xs, (k + 1, u, 0), xr, lay.peer(a * B + turn(b, u, B), y, c), like(k))

    for step in range(AHEAD):
        send_along(step)
    for k in order:
        send_over(k)
    for k in range(-1, lay.half):
        local(k).start()

    def over(k, j, t, u):
        if 0 <= k < lay.split:
            for v in range(1, Y):
                remote(at(k, j), at(k, j), ys, (k, v, t, u), yr, lay.peer(i, turn(y, v, Y), c), like(k))

    def cross(k):
        send_along(order.index(k) + AHEAD)
        for t in range(1, A):
            j = turn(a, -t, A) * B + b
            landed(at(k, j), zr, k + 1, t)
            for u in range(1, B):
                remote(at(k, j), at(k, j), xs, (k + 1, u, t), xr, lay.peer(a * B + turn(b, u, B), y, c), like(k))
            over(k, j, t, 0)

    def share(k):
        for t in range(A):
            for u in range(1, B):
                j = turn(a, -t, A) * B + turn(b, -u, B)
                landed(at(k, j), xr, k + 1, u, t)
                over(k, j, t, u)
        if k < 0:
            local(k).wait()
            remote(os_ref.at[c], os_ref.at[c], cs, (0,), cr, here, lambda: os_ref.at[0])
        else:
            own_wait(k, 0)
            m = matrix_of(c, k)
            remote(ow_ref.at[m], ow_ref.at[m], cs, (k + 1,), cr, here, lambda: ow_ref.at[0])

    def own_wait(k, v):
        m = matrix_of(c, k, v)
        pltpu.make_async_copy(w_ref.at[lax.div(m, 2)], ow_ref.at[m, i], own.at[lax.div(m, 2) + 1]).wait()

    def slot(q, v):
        return K + 1 + (v - 1) * lay.split + q

    def from_planes(k):
        if k in closed or not 0 <= k < lay.split:
            return
        closed.append(k)
        for v in range(1, Y):
            m = matrix_of(c, k, -v)
            for t in range(A):
                for u in range(B):
                    if t or u:
                        j = turn(a, -t, A) * B + turn(b, -u, B)
                        landed(ow_ref.at[m, j], yr, k, v, t, u)
            own_wait(k, -v)
            remote(ow_ref.at[m], ow_ref.at[m], cs, (slot(k, v),), cr, here, lambda: ow_ref.at[0])

    def paired(k):
        if k < 0:
            landed(os_ref.at[1 - c], cr, 0)
        else:
            landed(ow_ref.at[matrix_of(1 - c, k)], cr, k + 1)
            if k < lay.split:
                for v in range(1, Y):
                    landed(ow_ref.at[matrix_of(1 - c, k, -v)], cr, slot(k, v))

    def fetch(first, count):
        span = pl.ds(first, count)
        return pltpu.make_async_copy(ow_ref.at[span], w_buf.at[span], wsem.at[first])

    closed = []

    def advance(step):
        if step < len(order):
            cross(order[step])
        if 0 <= step - 1 < len(order):
            share(order[step - 1])
        if 0 <= step - 2 < len(order):
            from_planes(order[step - 2])

    first, second = (1, 3) if lay.split else (2, 5)
    begun = first + 2
    for step in range(begun):
        advance(step)
    from_planes(first - 1)
    for k in range(-1, first):
        paired(k)
    fetch(0, 4).start()
    table = pltpu.make_async_copy(os_ref.at[0], piece, wsem.at[lay.half])
    table.start()
    v_ref[...] = jnp.zeros_like(v_ref)
    table.wait()
    for j in range(lay.n):
        lane = min(lay.rows * j // 128 * 128, D - 256)
        wide = jnp.concatenate([piece[j].astype(FULL), jnp.zeros(piece.shape[1:], FULL)], 1)
        v_ref[: piece.shape[1], lane : lane + 256] += pltpu.roll(wide, lay.rows * j - lane, 1)
    pos_buf[...] = v_ref[31 : 31 + SP, :]
    for f in range(F):
        time_buf[f] = v_ref[1 + f : 2 + f, :]
    fetch(0, 4).wait()
    ws = [Weight(w_buf.at[k]) for k in range(9)]
    steps = F // FB

    def embed(p, *outs):
        now = pl.program_id(0)
        embed_kernel(p, *ws[:4], v_ref, pos_buf, time_buf.at[pl.ds(now * FB, FB)], *outs)
        for s, place in enumerate(IN_EMBED):
            @pl.when(now == place)
            def _():
                advance(begun + s)

    pltpu.emit_pipeline(embed, grid=(steps,), in_specs=[pl.BlockSpec((1, FB, S, D), lambda i: (0, i, 0, 0))], out_specs=[FRAMES] * 6)(
        p_ref, pad_ref, x0_ref, at_ref, qt_ref, kt_ref, vt_ref
    )

    def time(q, k, v, fill, o):
        time_kernel(q, k, v, fill, o)
        for s, place in enumerate(IN_TIME):
            @pl.when(pl.program_id(0) == place)
            def _():
                advance(begun + len(IN_EMBED) + s)

    pltpu.emit_pipeline(time, grid=(SP // GROUP,), in_specs=[SLAB] * 3 + [FILL], out_specs=[SLAB])(
        qt_ref, kt_ref, vt_ref, tfill_ref, ot_ref
    )
    done = begun + len(IN_EMBED) + len(IN_TIME)
    for step in range(done, second + 2):
        advance(step)
    done = max(done, second + 2)
    for k in range(first, second):
        from_planes(k)
        paired(k)
    fetch(4, 5).start()
    fetch(4, 5).wait()

    def space(o, x, fill, *outs):
        space_kernel(o, x, *ws[4:9], v_ref, fill, *outs)

        for s, place in enumerate(IN_SPACE):
            @pl.when(pl.program_id(0) == place)
            def _():
                advance(done + s)

    pltpu.emit_pipeline(space, grid=(steps,), in_specs=[FRAMES, FRAMES, per_frame(1, SP)], out_specs=[FRAMES] * 7 + [per_frame(8, D)])(
        ot_ref, x0_ref, sfill_ref, yt_ref, xs_ref, as_ref, qs_ref, ks_ref, vs_ref, mix_ref, cls_ref
    )
    for step in range(done + len(IN_SPACE), len(order) + 1):
        advance(step)
    for k in range(second, K):
        paired(k)
    for make, sems, at_ in pending:
        ref = make()
        pltpu.make_async_remote_copy(
            src_ref=ref, dst_ref=ref, send_sem=sems.at[at_], recv_sem=sems.at[at_], device_id=here, device_id_type=MESH
        ).wait_send()


class Weight:
    def __init__(self, ref):
        self.ref = ref

    def __getitem__(self, unused):
        value = self.ref[...]
        if value.shape[1] % 16:
            return value.astype(FULL).reshape(D, D).astype(HALF)
        return value.reshape(D, D)


def front(lay, shard, small, patches, time_fill, space_fill):
    A, B, K, Y = lay.outer, lay.inner, lay.handled, lay.planes
    dma = pltpu.SemaphoreType.DMA
    kept = max(lay.split, 1)
    vmem = pl.BlockSpec(memory_space=pltpu.VMEM)
    full = functools.partial(shape, dtype=FULL)
    slots = K + 1 + max(Y - 1, 0) * lay.split
    return pl.pallas_call(
        functools.partial(front_kernel, lay),
        in_specs=[ANY] * 5,
        out_specs=[ANY] * 17 + [vmem],
        out_shape=[
            shape(NMAT, lay.n, lay.rows, D), shape(2, lay.n, *small.shape[1:]),
            ROWS16, ROWS32, ROWS16, ROWS16, ROWS16, ROWS16, ROWS16, ROWS16, ROWS32, ROWS16, ROWS16, ROWS16, ROWS16, ROWS16,
            full(F, 8, D), full(256, D),
        ],
        scratch_shapes=[
            pltpu.VMEM((9, lay.n, lay.rows, D), HALF), pltpu.VMEM((lay.n,) + small.shape[1:], HALF), pltpu.VMEM((SP, D), FULL), pltpu.VMEM((F, 1, D), FULL),
            dma((lay.half + 1,)), dma((K + 1, A)), dma((K + 1, A)), dma((K + 1, B, A)), dma((K + 1, B, A)),
            dma((kept, Y, A, B)), dma((kept, Y, A, B)), dma((slots,)), dma((slots,)), dma((lay.half + 1,)),
        ],
        compiler_params=pltpu.CompilerParams(collective_id=0, has_side_effects=True, vmem_limit_bytes=60 * 2**20),
    )(shard, small, patches, time_fill, space_fill)


def forward(lay, shard, small, patches, mask):
    alive = jnp.pad(mask[0] > 0, ((0, 0), (0, SP - S)))
    kept = jnp.where(alive, 0.0, MASKED).astype(FULL)
    places = jnp.arange(SP)[None]
    space_fill = jnp.where(places < S, kept, jnp.where(places == S, 0.0, NEVER))
    time_keys = kept.reshape(F, SP // GROUP, GROUP).transpose(1, 0, 2).reshape(SP // GROUP, F * GROUP)
    spot = jnp.arange(F * GROUP) % GROUP
    same = spot[:, None] == spot[None]
    time_fill = jnp.where(same[None], time_keys[:, None, :], NEVER)
    time_fill_back = jnp.where(same[None], time_keys[:, :, None], NEVER)
    mats, rest, padded, x0, at, qt, kt, vt, ot, yt, xs, as_, qs, ks, vs, os_, cls, table = front(
        lay, shard, small, patches, time_fill, space_fill[:, None]
    )
    mats = mats.reshape(NMAT, D, D)
    tab = whole(*table.shape)
    steps = F // FB
    of, x2, a2, g, e, x3, pool = call(
        mlp_kernel, steps,
        [FRAMES, whole(F, 8, D), FRAMES] + matrices(9, 9) + [tab],
        [FRAMES] * 3 + [HIDDEN] * 2 + [FRAMES, summed(8)],
        [ROWS16, ROWS32, ROWS16, HIDDEN32, HIDDEN16, ROWS32, shape(8, D, dtype=FULL)],
    )(os_, cls, xs, *[mats] * 9, table)
    pooled = (pool[:1] / (F * S + 1)).astype(HALF)
    head = rest[1][:, : 2 * lay.rows].reshape(lay.n, 2, lay.rows, 128).transpose(0, 2, 1, 3).reshape(D, 256)
    saved = (table, space_fill, time_fill_back, padded, x0, at, qt, kt, vt, ot, yt, xs, as_, qs, ks, vs, of, x2, a2, g, e, x3)
    return pooled, mats, head, saved


def backward(lay, mats, saved, back_pooled):
    (table, space_fill, time_fill, padded, x0, at, qt, kt, vt, ot, yt, xs, as_, qs, ks, vs, of, x2, a2, g, e, x3) = saved
    tab = whole(*table.shape)
    steps = F // FB
    top = back_pooled / (F * S + 1)
    column = jnp.broadcast_to(space_fill[:, :, None], (F, SP, 128))
    r3, dg, d2, r2, dq, dk, dv, cq, ck, cv, sums1 = call(
        mlp_back_kernel, steps,
        [FRAMES, FRAMES, HIDDEN, whole(1, D)] + matrices(9, 9) + [tab, FRAMES, FRAMES, FRAMES, per_frame(SP, 128)],
        [FRAMES, HIDDEN] + [FRAMES] * 5 + [per_frame(8, D)] * 3 + [summed(16)],
        [ROWS16, HIDDEN16, ROWS32] + [ROWS16] * 4 + [shape(F, 8, D, dtype=FULL)] * 3 + [shape(16, D, dtype=FULL)],
        [pltpu.VMEM((FB, SP, D), HALF)],
    )(x3, x2, g, top, *[mats] * 9, table, qs, ks, vs, column)
    first = Part(lay, 10, 4, 1 if lay.planes <= 4 else 0)
    pairs = [((2, 0), (3, k)) for k in range(4)] + [((0, k), (1, 0)) for k in range(4)]
    upper, fq, fk, fv, d1, r1, dy, do, tq, tk, tv, rp, grad_vecs, squares = early(
        lay, first, pairs, (e, r3, a2, dg, dq, dk, dv, xs, d2, qt, kt, vt, time_fill, x0, mats), (cq, ck, cv, sums1), table
    )
    second = Part(lay, 0, 5, 1 if lay.planes <= 4 else 0)
    operands = (padded, rp, at, tq, tk, tv, ot, dy, yt, r1, as_, fq, fk, fv, of, r2)
    pairs = [(0, 1), (2, 3), (2, 4), (2, 5), (6, 7), (8, 9), (10, 11), (10, 12), (10, 13), (14, 15)]
    pairs = [((left, 0), (right, 0)) for left, right in pairs]

    def finish(small):
        return late(lay, second, pairs, small, squares, upper, operands)

    return finish, grad_vecs


def project(inputs, weight):
    return jnp.einsum("...a,ab->...b", inputs, weight, preferred_element_type=jnp.float32)


def project_back(inputs, weight, cotangent):
    rounded = cotangent.astype(jnp.bfloat16)
    back_in = jnp.einsum("...b,ab->...a", rounded, weight, preferred_element_type=jnp.float32)
    flat_in = inputs.reshape(-1, inputs.shape[-1])
    flat_back = rounded.reshape(-1, rounded.shape[-1])
    grad_weight = jnp.einsum("na,nb->ab", flat_in, flat_back, preferred_element_type=jnp.float32)
    return (back_in, grad_weight, jnp.sum(flat_back, 0, dtype=jnp.float32))


def normalize(projected):
    return projected * lax.rsqrt(jnp.sum(projected * projected, -1, keepdims=True) + 1e-06)


def adamw_step(weight, first, second, average, gradient, factor, rate):
    clipped = gradient * factor
    first = BETA_ONE * first + (1.0 - BETA_ONE) * clipped
    second = BETA_TWO * second + (1.0 - BETA_TWO) * clipped * clipped
    first_hat = first / (1.0 - BETA_ONE**STEP)
    second_hat = second / (1.0 - BETA_TWO**STEP)
    weight = weight - rate * (first_hat / (jnp.sqrt(second_hat) + ADAM_EPSILON) + DECAY * weight)
    average = AVERAGE_KEEP * average + (1.0 - AVERAGE_KEEP) * weight
    return (weight, first, second, average)


def own_matrices(lay, matrices):
    pairs = matrices.reshape(NMAT // 2, 2, lay.rows, D)
    return lax.dynamic_index_in_dim(pairs, lax.rem(lax.axis_index("dp"), 2), 1, keepdims=False)


def pack(lay, head, vecs):
    tall = -(-NVEC // 16) * 16
    first = jnp.pad(vecs, ((0, tall - NVEC), (0, 128 - lay.rows)))
    second = jnp.concatenate([head[:, :128], head[:, 128:]], 0)
    return jnp.stack([first, jnp.pad(second, ((0, tall - second.shape[0]), (0, 0)))])


def pack_all(head, vecs, n):
    rows = D // n
    first = head.reshape(n, 3, rows // 3, D // 3).transpose(0, 2, 1, 3).reshape(n, rows // 3, D)
    tall = jnp.pad(vecs, ((0, D // 3 - vecs.shape[0]), (0, 0)))
    second = tall.reshape(n, rows // 3, n, rows).transpose(2, 1, 0, 3).reshape(n, rows // 3, D)
    fill = -(rows // 3) % 16
    return jnp.pad(jnp.stack([first, second]), ((0, 0), (0, 0), (0, fill), (0, 0)))


def unpack_shard(blocks, n):
    rows = D // n
    first, second = blocks[0, : rows // 3], blocks[1, : rows // 3]
    head = jnp.concatenate([first[:, : D // 3], first[:, D // 3 : 2 * D // 3], first[:, 2 * D // 3 :]], 0)
    vecs = second.reshape(rows // 3, n, rows).transpose(1, 0, 2).reshape(D // 3, rows)
    return head, vecs[:NVEC]


def local(
    lay,
    patches,
    patch_keep_mask,
    partner,
    matrices,
    matrix_first,
    matrix_second,
    matrix_average,
    head_weight,
    head_first,
    head_second,
    head_average,
    vectors,
    array_running_mean,
    vector_second,
    vector_average,
):
    n = lay.n
    pooled, mats16, head16, saved = forward(
        lay,
        own_matrices(lay, matrices).astype(jnp.bfloat16),
        pack(lay, head_weight.astype(jnp.bfloat16), vectors.astype(jnp.bfloat16)),
        patches,
        patch_keep_mask,
    )
    projected = project(pooled, head16)
    unit_length_lines, unit_back = jax.vjp(normalize, projected)
    clip_count, width = unit_length_lines.shape
    lines = unit_length_lines.reshape(-1, 128)
    tile = jnp.pad(lines, ((0, -lines.shape[0] % 8), (0, 0)))
    everyone = spread(lay.dp, n, tile, 2)
    gathered = everyone[:, : lines.shape[0]].reshape(-1, width)

    def contrast(gathered_rows):
        pairwise_affinity_scores_raw = (
            jnp.dot(gathered_rows, gathered_rows.T, precision=lax.Precision.HIGHEST)
            / SCORE_SHARPNESS
        )
        clip_total = pairwise_affinity_scores_raw.shape[0]
        column = jnp.arange(clip_total)[None, :]
        pairwise_affinity_scores_raw = jnp.where(
            jnp.arange(clip_total)[:, None] == column, -1000000000.0, pairwise_affinity_scores_raw
        )
        positive = jnp.sum(
            jnp.where(column == partner[:, None], pairwise_affinity_scores_raw, 0.0), -1
        )
        return jnp.mean(jax.nn.logsumexp(pairwise_affinity_scores_raw, -1) - positive)

    contrastive_loss, objective_cotangent_flow = jax.vjp(contrast, gathered)
    (back_gathered,) = objective_cotangent_flow(jnp.ones_like(contrastive_loss))
    clip_count = projected.shape[0]
    offset = lax.axis_index(("dp", "fsdp")) * clip_count
    back_unit = lax.dynamic_slice_in_dim(back_gathered, offset, clip_count, 0)
    (back_projected,) = unit_back(back_unit)
    back_pooled, grad_head, unused_bias = project_back(pooled, head16, back_projected)
    finish, grad_vecs = backward(lay, mats16, saved, back_pooled)
    small = pack_all(grad_head, grad_vecs, n).astype(jnp.bfloat16)
    grad_mats, grad_small, tiles = finish(small)
    squared_norm = jnp.sum(tiles)
    grad_head, grad_vecs = unpack_shard(grad_small, n)
    factor = CLIP_AT / jnp.maximum(jnp.sqrt(squared_norm), CLIP_AT)
    mats_out = adamw_step(
        matrices, matrix_first, matrix_second, matrix_average, grad_mats, factor, RATE
    )
    head_out = adamw_step(
        head_weight, head_first, head_second, head_average, grad_head, factor, RATE
    )
    vecs_out = adamw_step(
        vectors, array_running_mean, vector_second, vector_average, grad_vecs, factor, VECTOR_RATE
    )
    return (
        contrastive_loss,
        squared_norm,
        mats_out[0],
        mats_out[1],
        mats_out[2],
        mats_out[3],
        head_out[0],
        head_out[1],
        head_out[2],
        head_out[3],
        vecs_out[0],
        vecs_out[1],
        vecs_out[2],
        vecs_out[3],
    )


def solution(mesh):
    planes = mesh.shape["dp"] // 2
    lay = Layout(mesh.shape["dp"], mesh.shape["fsdp"], 2 if planes == 2 else 0)
    placed = (
        P(("dp", "fsdp"), None, None, None),
        P(("dp", "fsdp"), None, None),
        P(),
        P(None, "fsdp", None),
        P(None, "fsdp", None),
        P(None, "fsdp", None),
        P(None, "fsdp", None),
        P("fsdp", None),
        P("fsdp", None),
        P("fsdp", None),
        P("fsdp", None),
        P(None, "fsdp"),
        P(None, "fsdp"),
        P(None, "fsdp"),
        P(None, "fsdp"),
    )
    return jax.shard_map(
        functools.partial(local, lay),
        mesh=mesh,
        in_specs=placed,
        out_specs=(
            P(),
            P(),
            P(None, "fsdp", None),
            P(None, "fsdp", None),
            P(None, "fsdp", None),
            P(None, "fsdp", None),
            P("fsdp", None),
            P("fsdp", None),
            P("fsdp", None),
            P("fsdp", None),
            P(None, "fsdp"),
            P(None, "fsdp"),
            P(None, "fsdp"),
            P(None, "fsdp"),
        ),
        check_vma=False,
    )
```
